32 devices in a mesh: dp: 8 (over y, x, core), tensor: 4 (over z).
Axes of the slice: x: 2, y: 2, z: 4, core: 2. Of those that a mesh axis runs over, the one named last changes fastest.
Arguments:
- residual: bfloat16 [8192, 2048], P(('dp', 'tensor')), may hold values from -6 to 6
- segments: int32 [8, 1024], P('dp'), may hold values from 0 to 7, never falling along the last dimension, each value on 1 to 512 neighbouring positions
- mixgain: bfloat16 [2048], P(('dp', 'tensor')), may hold values from 0.5 to 1.5
- ffngain: bfloat16 [2048], P(('dp', 'tensor')), may hold values from 0.5 to 1.5
- gateproj: bfloat16 [2048, 3072], P('dp', 'tensor'), may hold values from -0.125 to 0.125
- innerproj: bfloat16 [2048, 3072], P('dp', 'tensor'), may hold values from -0.125 to 0.125
- stepproj: bfloat16 [2048, 48], P('dp', 'tensor'), may hold values from -0.125 to 0.125
- sharedproj: bfloat16 [2048, 512], P(('dp', 'tensor')), may hold values from -0.125 to 0.125
- innerconv: bfloat16 [3072, 4], P('tensor'), may hold values from -1.796875 to 1.796875
- sharedconv: bfloat16 [512, 4], P(('dp', 'tensor')), may hold values from -1.796875 to 1.796875
- stepbias: bfloat16 [48], P('tensor'), may hold values from -6 to -2
- decaylog: bfloat16 [48], P('tensor'), may hold values from -4 to 0
- skipgain: bfloat16 [48], P('tensor'), may hold values from 0.5 to 1.5
- mixerout: bfloat16 [2048, 3072], P('dp', 'tensor'), may hold values from -0.109375 to 0.109375
- queryproj: bfloat16 [2048, 1024], P('dp', 'tensor'), may hold values from -0.125 to 0.125
- keyvalue: bfloat16 [2048, 512], P(('dp', 'tensor')), may hold values from -0.125 to 0.125
- attnout: bfloat16 [2048, 1024], P('dp', 'tensor'), may hold values from -0.375 to 0.375
- ffngate: bfloat16 [2048, 4096], P('dp', 'tensor'), may hold values from -0.125 to 0.125
- upproj: bfloat16 [2048, 4096], P('dp', 'tensor'), may hold values from -0.125 to 0.125
- downproj: bfloat16 [2048, 4096], P('dp', 'tensor'), may hold values from -0.1875 to 0.1875
- cotangent: bfloat16 [8192, 2048], P(('dp', 'tensor')), may hold values from -6 to 6
Outputs:
- layer_out: float32 [8192, 2048], P(('dp', 'tensor'))
- grad_residual: float32 [8192, 2048], P(('dp', 'tensor'))
- grad_mixgain: float32 [2048], P(('dp', 'tensor'))
- grad_ffngain: float32 [2048], P(('dp', 'tensor'))
- grad_gateproj: float32 [2048, 3072], P('dp', 'tensor')
- grad_innerproj: float32 [2048, 3072], P('dp', 'tensor')
- grad_stepproj: float32 [2048, 48], P('dp', 'tensor')
- grad_sharedproj: float32 [2048, 512], P(('dp', 'tensor'))
- grad_innerconv: float32 [3072, 4], P('tensor')
- grad_sharedconv: float32 [512, 4], P(('dp', 'tensor'))
- grad_stepbias: float32 [48], P('tensor')
- grad_decaylog: float32 [48], P('tensor')
- grad_skipgain: float32 [48], P('tensor')
- grad_mixerout: float32 [2048, 3072], P('dp', 'tensor')
- grad_queryproj: float32 [2048, 1024], P('dp', 'tensor')
- grad_keyvalue: float32 [2048, 512], P(('dp', 'tensor'))
- grad_attnout: float32 [2048, 1024], P('dp', 'tensor')
- grad_ffngate: float32 [2048, 4096], P('dp', 'tensor')
- grad_upproj: float32 [2048, 4096], P('dp', 'tensor')
- grad_downproj: float32 [2048, 4096], P('dp', 'tensor')
The draws below stay inside these ranges and needn't reach their ends.
Inputs may be any that keep to these rules, and one draw needn't show every extreme that they name: `segments`: within each sequence the document numbers never fall; a document has 1 to 512 tokens.
All inputs are finite; a program needn't handle non-finite values.
Results may differ from the reference program's by a relative error of at most 0.023.
Values may be sent and summed in bfloat16 or wider, within the bound.
A program may use at most 256 MiB of HBM per device.

```python
import math
import jax
import jax.numpy as jnp
import numpy as np
from jax import lax

MODEL_WIDTH = 2048
DI = 3072
MH = 48
NS = 256
QUERY_HEADS = 8
KEY_VALUE_HEADS = 2
HEAD_SIZE = 128
FF = 4096
KC = 4
SPAN = 256
SEQ = 1024
NSEQ = 8
TOKENS = 8192
N_TENSOR = 4


def steps_of(key, extent, pieces, least, high):
    level, own = 1.0, jax.random.fold_in(key, 6)
    for position, blocks in pieces:
        heights = jnp.exp(jax.random.uniform(jax.random.fold_in(own, position), (blocks,), jnp.float32, least / len(pieces), high / len(pieces)))
        level = level * jnp.repeat(heights, extent[position] // blocks).reshape([-1 if axis == position else 1 for axis in range(len(extent))])
    return level


def split_up(number_of, total, most, slope):
    weights = [(1 << 20) // math.isqrt(rank ** slope) + 1 for rank in range(2, number_of + 1)]
    rest, holding = total - most - (number_of - 1), [1] * (number_of - 1)
    while rest > 0:
        free = [i for i in range(number_of - 1) if holding[i] < most]
        mass, remaining = sum([weights[i] for i in free]), rest
        for i in free:
            extra = min(most - holding[i], max(1, remaining * weights[i] // mass), rest)
            holding[i] = holding[i] + extra
            rest = rest - extra
    return np.array([most] + holding)


def uneven(key, number_of, total, limit, lean):
    if number_of == 2:
        one = jax.random.randint(key, (), max(1, total - limit), min(limit, total - 1) + 1)
        return jnp.stack([one, total - one])
    tallies = jnp.asarray(split_up(number_of, total, limit, lean), jnp.int32)
    couples = (number_of - 1) // 2
    donor, receiver = tallies[1:1 + 2 * couples:2], tallies[2:2 + 2 * couples:2]
    margin = jnp.minimum(donor - 1, limit - receiver)
    moved = jax.random.randint(jax.random.fold_in(key, 1), (couples,), 0, 1 << 20) % (margin + 1)
    tallies = tallies.at[1:1 + 2 * couples:2].set(donor - moved).at[2:2 + 2 * couples:2].set(receiver + moved)
    return tallies[jax.random.permutation(jax.random.fold_in(key, 2), number_of)]


def bell_draw(own_key, shape, scale, most, cuts=(), dtype=jnp.bfloat16):
    values = jax.random.normal(own_key, shape, jnp.float32) * scale
    if len(cuts) > 0:
        values = steps_of(own_key, shape, cuts, -0.22, 0.18) * values
    return jnp.clip(values, min=-most, max=most).astype(dtype)


def setup_inputs(seed: int = 0) -> dict:
    key_list = jax.random.split(jax.random.key(seed), 22)
    return {
        "residual": bell_draw(key_list[0], (TOKENS, MODEL_WIDTH), 1.0, 6.0, ((0, 32),)),
        "segments": jax.vmap(lambda own: jnp.searchsorted(jnp.cumsum(uneven(own, 8, SEQ, SEQ // 2, 1)), jnp.arange(SEQ), side="right"))(jax.random.split(key_list[1], NSEQ)).reshape((NSEQ, SEQ)).astype(jnp.int32),
        "mixgain": jnp.clip(1.0 + 0.1 * jax.random.normal(key_list[2], (MODEL_WIDTH,), jnp.float32), 0.5, 1.5).astype(jnp.bfloat16),
        "ffngain": jnp.clip(1.0 + 0.1 * jax.random.normal(key_list[3], (MODEL_WIDTH,), jnp.float32), 0.5, 1.5).astype(jnp.bfloat16),
        "gateproj": bell_draw(key_list[4], (MODEL_WIDTH, DI), MODEL_WIDTH ** -0.5, 0.125, ((0, 8), (1, 4))),
        "innerproj": bell_draw(key_list[5], (MODEL_WIDTH, DI), MODEL_WIDTH ** -0.5, 0.125, ((0, 8), (1, 4))),
        "stepproj": bell_draw(key_list[6], (MODEL_WIDTH, MH), MODEL_WIDTH ** -0.5, 0.125, ((0, 8), (1, 4))),
        "sharedproj": bell_draw(key_list[7], (MODEL_WIDTH, 2 * NS), MODEL_WIDTH ** -0.5, 0.125, ((0, 32),)),
        "innerconv": bell_draw(key_list[8], (DI, KC), 0.3, 1.796875, ((0, 4),)),
        "sharedconv": bell_draw(key_list[9], (2 * NS, KC), 0.3, 1.796875, ((0, 32),)),
        "stepbias": jnp.clip(-6.0 + 4.0 * jax.random.uniform(key_list[10], (MH,), jnp.float32) ** steps_of(key_list[10], (MH,), ((0, 4),), -0.2, 0.2), -6.0, -2.0).astype(jnp.bfloat16),
        "decaylog": jnp.clip(-4.0 + 4.0 * jax.random.uniform(key_list[11], (MH,), jnp.float32) ** steps_of(key_list[11], (MH,), ((0, 4),), -0.2, 0.2), -4.0, 0.0).astype(jnp.bfloat16),
        "skipgain": jnp.clip(0.5 + 1.0 * jax.random.uniform(key_list[12], (MH,), jnp.float32) ** steps_of(key_list[12], (MH,), ((0, 4),), -0.2, 0.2), 0.5, 1.5).astype(jnp.bfloat16),
        "mixerout": bell_draw(key_list[13], (MODEL_WIDTH, DI), DI ** -0.5, 0.109375, ((0, 8), (1, 4))),
        "queryproj": bell_draw(key_list[14], (MODEL_WIDTH, QUERY_HEADS * HEAD_SIZE), MODEL_WIDTH ** -0.5, 0.125, ((0, 8), (1, 4))),
        "keyvalue": bell_draw(key_list[15], (MODEL_WIDTH, 2 * KEY_VALUE_HEADS * HEAD_SIZE), MODEL_WIDTH ** -0.5, 0.125, ((0, 32),)),
        "attnout": bell_draw(key_list[16], (MODEL_WIDTH, QUERY_HEADS * HEAD_SIZE), (QUERY_HEADS * HEAD_SIZE // 4) ** -0.5, 0.375, ((0, 8), (1, 4))),
        "ffngate": bell_draw(key_list[17], (MODEL_WIDTH, FF), MODEL_WIDTH ** -0.5, 0.125, ((0, 8), (1, 4))),
        "upproj": bell_draw(key_list[18], (MODEL_WIDTH, FF), MODEL_WIDTH ** -0.5, 0.125, ((0, 8), (1, 4))),
        "downproj": bell_draw(key_list[19], (MODEL_WIDTH, FF), (FF // 4) ** -0.5, 0.1875, ((0, 8), (1, 4))),
        "cotangent": bell_draw(key_list[20], (TOKENS, MODEL_WIDTH), 1.0, 6.0, ((0, 32),)),
    }


HIGH = lax.Precision.HIGHEST
eps = 1e-05
rope_base = 10000.0

@jax.custom_vjp
def low(v):
    return lax.optimization_barrier(v.astype(jnp.bfloat16)).astype(jnp.float32)

@jax.custom_vjp
def low_back(v):
    return v

def low_keep(v):
    return (low(v), None)

def low_pass(kept, grad):
    return (grad,)

def back_keep(v):
    return (v, None)

def back_low(kept, grad):
    return (low(grad),)
low.defvjp(low_keep, low_pass)
low_back.defvjp(back_keep, back_low)

def matrix_product(left, right):
    return jnp.dot(left, right, precision=HIGH, preferred_element_type=jnp.float32)

def rmsnorm(value, gain):
    return value * lax.rsqrt(lax.optimization_barrier(jnp.mean(value * value, axis=-1, keepdims=True)) + eps) * gain

def rotate(tensor_array, sign):
    half = tensor_array.shape[-1] // 2
    places = jnp.arange(tensor_array.shape[1]).astype(jnp.float32)
    freqs = rope_base ** (-jnp.arange(half).astype(jnp.float32) / half)
    angle = (places[:, None] * freqs[None, :]).reshape((tensor_array.shape[1],) + (1,) * (tensor_array.ndim - 3) + (half,))
    cosine = jnp.cos(angle)
    sine = sign * jnp.sin(angle)
    first = tensor_array[..., :half]
    second = tensor_array[..., half:]
    return jnp.concatenate([first * cosine - second * sine, first * sine + second * cosine], axis=-1)

def causal_conv(values, kernel, segs):
    total = values * kernel[:, 0]
    for lag in range(1, kernel.shape[1]):
        moved = jnp.pad(values, ((0, 0), (lag, 0), (0, 0)))[:, :-lag]
        prior = jnp.pad(segs, ((0, 0), (lag, 0)), constant_values=-1)[:, :-lag]
        total = total + jnp.where((prior == segs)[..., None], moved, 0.0) * kernel[:, lag]
    return total

def state_scan(inner, step, logdec, bmat, cmat, segs, span):
    groups, length, heads, width = inner.shape
    count = length // span
    scaled = (inner * step[..., None]).reshape(groups, count, span, heads, width)
    cumul = jnp.cumsum(logdec.reshape(groups, count, span, heads), axis=2)
    bmat = bmat.reshape(groups, count, span, -1)
    cmat = cmat.reshape(groups, count, span, -1)
    segc = segs.reshape(groups, count, span)
    order = jnp.arange(span)
    inside = (order[:, None] >= order[None, :]) & (segc[..., :, None] == segc[..., None, :])
    spread = cumul[:, :, :, None, :] - cumul[:, :, None, :, :]
    decay = jnp.exp(jnp.where(inside[..., None], spread, -jnp.inf))
    intersection = jnp.einsum('gctn,gcsn->gcts', cmat, bmat, precision=HIGH)
    result = jnp.einsum('gcts,gctsh,gcshp->gcthp', intersection, decay, scaled, precision=HIGH)
    ending = cumul[:, :, -1, :]
    seglast = segc[:, :, -1]
    tail = jnp.where((segc == seglast[..., None])[..., None], jnp.exp(ending[:, :, None, :] - cumul), 0.0)
    states = jnp.einsum('gcsh,gcshp,gcsn->gchpn', tail, scaled, bmat, precision=HIGH)
    carried = states[:, 0]
    outputs = [result[:, 0]]
    for number in range(1, count):
        reach = jnp.where((segc[:, number] == seglast[:, number - 1][:, None])[..., None], jnp.exp(cumul[:, number]), 0.0)
        outputs.append(result[:, number] + jnp.einsum('gth,gtn,ghpn->gthp', reach, cmat[:, number], carried, precision=HIGH))
        keeping = jnp.where((seglast[:, number] == seglast[:, number - 1])[:, None], jnp.exp(ending[:, number]), 0.0)
        carried = states[:, number] + keeping[:, :, None, None] * carried
    return jnp.stack(outputs, axis=1).reshape(groups, length, heads, width)

def mamba_mix(gate_raw, inner_raw, step_raw, shared_raw, conv_inner, conv_shared, step_bias, decay_log, skip, segs, span):
    groups, length = segs.shape
    heads = step_raw.shape[-1]
    inner = jax.nn.silu(causal_conv(inner_raw.reshape(groups, length, -1), conv_inner, segs))
    shared = jax.nn.silu(causal_conv(shared_raw.reshape(groups, length, -1), conv_shared, segs))
    half = shared.shape[-1] // 2
    step = jax.nn.softplus(step_raw.reshape(groups, length, heads) + step_bias)
    logdec = -step * jnp.exp(decay_log)
    inner = inner.reshape(groups, length, heads, -1)
    mixed = state_scan(inner, step, logdec, shared[..., :half], shared[..., half:], segs, span) + skip[:, None] * inner
    return mixed.reshape(groups * length, -1) * jax.nn.silu(gate_raw)

def attend(query, key_in, value_input, segs):
    groups, length = segs.shape
    width = key_in.shape[-1]
    query_r = low(rotate(query.reshape(groups, length, -1, width), 1.0))
    key_r = low(rotate(key_in.reshape(groups, length, width), 1.0))
    value_r = low(value_input.reshape(groups, length, width))
    scores = low_back(jnp.einsum('gthd,gsd->ghts', query_r, key_r, precision=HIGH) / math.sqrt(width))
    order = jnp.arange(length)
    allowed = (order[:, None] >= order[None, :]) & (segs[:, :, None] == segs[:, None, :])
    masked = jnp.where(allowed[:, None], scores, -jnp.inf)
    peak = lax.optimization_barrier(jnp.max(masked, axis=-1, keepdims=True))
    expo = jnp.exp(masked - peak)
    probs = low(expo / lax.optimization_barrier(jnp.sum(expo, axis=-1, keepdims=True)))
    result = jnp.einsum('ghts,gsd->gthd', probs, value_r, precision=HIGH)
    return low(low_back(result.reshape(groups * length, -1)))

def layer(params, resid, segs):
    mixgain, ffngain, gateproj, innerproj, stepproj, sharedproj, innerconv, sharedconv, stepbias, decaylog, skipgain, mixerout, queryproj, keyvalue, attnout, ffngate, upproj, downproj = params
    normalized_rows = low(rmsnorm(resid, mixgain))
    gate_raw = low_back(matrix_product(normalized_rows, gateproj))
    inner_raw = low_back(matrix_product(normalized_rows, innerproj))
    step_raw = low_back(matrix_product(normalized_rows, stepproj))
    query = low_back(matrix_product(normalized_rows, queryproj))
    mheads = stepproj.shape[1] // N_TENSOR
    channels = gateproj.shape[1] // N_TENSOR
    query_head_count = QUERY_HEADS // N_TENSOR
    mamba_parts = []
    attn_parts = []
    for query_group in range(N_TENSOR):
        shared_raw = low_back(matrix_product(normalized_rows, sharedproj))
        key_value_head = query_group * query_head_count // (QUERY_HEADS // KEY_VALUE_HEADS)
        key_in = low_back(matrix_product(normalized_rows, keyvalue[:, key_value_head * HEAD_SIZE:(key_value_head + 1) * HEAD_SIZE]))
        value_input = low_back(matrix_product(normalized_rows, keyvalue[:, (KEY_VALUE_HEADS + key_value_head) * HEAD_SIZE:(KEY_VALUE_HEADS + key_value_head + 1) * HEAD_SIZE]))
        chan = slice(query_group * channels, (query_group + 1) * channels)
        hsel = slice(query_group * mheads, (query_group + 1) * mheads)
        mamba_parts.append(low(mamba_mix(gate_raw[:, chan], inner_raw[:, chan], step_raw[:, hsel], shared_raw, innerconv[chan], sharedconv, stepbias[hsel], decaylog[hsel], skipgain[hsel], segs, SPAN)))
        attn_parts.append(attend(query[:, query_group * query_head_count * HEAD_SIZE:(query_group + 1) * query_head_count * HEAD_SIZE], key_in, value_input, segs))
    mixed = matrix_product(jnp.concatenate(mamba_parts, axis=1), mixerout.T) + matrix_product(jnp.concatenate(attn_parts, axis=1), attnout.T)
    middle = resid + low_back(mixed)
    normed2 = low(rmsnorm(middle, ffngain))
    gate = low_back(matrix_product(normed2, ffngate))
    upper = low_back(matrix_product(normed2, upproj))
    hidden = low(jax.nn.silu(gate) * upper)
    return middle + low_back(matrix_product(hidden, downproj.T))

def reference(residual, segments, mixgain, ffngain, gateproj, innerproj, stepproj, sharedproj, innerconv, sharedconv, stepbias, decaylog, skipgain, mixerout, queryproj, keyvalue, attnout, ffngate, upproj, downproj, cotangent):
    weights = tuple((arr.astype(jnp.float32) for arr in (mixgain, ffngain, gateproj, innerproj, stepproj, sharedproj, innerconv, sharedconv, stepbias, decaylog, skipgain, mixerout, queryproj, keyvalue, attnout, ffngate, upproj, downproj)))
    seq_total = segments.shape[0]
    batch = math.gcd(seq_total, 4)
    rounds = seq_total // batch
    width = residual.shape[1]
    resid_b = residual.astype(jnp.float32).reshape(rounds, batch * SEQ, width)
    cot_b = cotangent.astype(jnp.float32).reshape(rounds, batch * SEQ, width)
    seg_b = segments.reshape(rounds, batch, SEQ)

    def one_round(carry, item):
        resid_in, seg_in, cot_in = item
        result, pull = jax.vjp(lambda params, rows: layer(params, rows, seg_in), weights, resid_in)
        grad_w, grad_r = pull(cot_in)
        return (jax.tree.map(jnp.add, carry, grad_w), (result, grad_r))
    zeros = jax.tree.map(jnp.zeros_like, weights)
    grads, (results, grad_rows) = lax.scan(one_round, zeros, (resid_b, seg_b, cot_b))
    return (results.reshape(-1, width), grad_rows.reshape(-1, width), grads[0], grads[1], grads[2], grads[3], grads[4], grads[5], grads[6], grads[7], grads[8], grads[9], grads[10], grads[11], grads[12], grads[13], grads[14], grads[15], grads[16], grads[17])
```

```python
import functools
import math

import jax
import jax.numpy as jnp
from jax import lax
from jax.sharding import PartitionSpec as P

QUERY_HEADS = 8
KEY_VALUE_HEADS = 2
HEAD_SIZE = 128
SPAN = 256


HIGH = lax.Precision.HIGHEST
eps = 1e-05
rope_base = 10000.0


def rmsnorm(value, gain):
    return value * lax.rsqrt(jnp.mean(value * value, axis=-1, keepdims=True) + eps) * gain


def rotate(tensor_array, sign):
    half = tensor_array.shape[-1] // 2
    places = jnp.arange(tensor_array.shape[1]).astype(jnp.float32)
    freqs = rope_base ** (-jnp.arange(half).astype(jnp.float32) / half)
    angle = (places[:, None] * freqs[None, :]).reshape(
        (tensor_array.shape[1],) + (1,) * (tensor_array.ndim - 3) + (half,)
    )
    cosine = jnp.cos(angle)
    sine = sign * jnp.sin(angle)
    first = tensor_array[..., :half]
    second = tensor_array[..., half:]
    return jnp.concatenate(
        [first * cosine - second * sine, first * sine + second * cosine], axis=-1
    )


def causal_conv(values, kernel, segs):
    total = values * kernel[:, 0]
    for lag in range(1, kernel.shape[1]):
        moved = jnp.pad(values, ((0, 0), (lag, 0), (0, 0)))[:, :-lag]
        prior = jnp.pad(segs, ((0, 0), (lag, 0)), constant_values=-1)[:, :-lag]
        total = total + jnp.where((prior == segs)[..., None], moved, 0.0) * kernel[:, lag]
    return total


def state_scan(inner, step, logdec, bmat, cmat, segs, span):
    groups, length, heads, width = inner.shape
    count = length // span
    scaled = (inner * step[..., None]).reshape(groups, count, span, heads, width)
    cumul = jnp.cumsum(logdec.reshape(groups, count, span, heads), axis=2)
    bmat = bmat.reshape(groups, count, span, -1)
    cmat = cmat.reshape(groups, count, span, -1)
    segc = segs.reshape(groups, count, span)
    order = jnp.arange(span)
    inside = (order[:, None] >= order[None, :]) & (segc[..., :, None] == segc[..., None, :])
    spread = cumul[:, :, :, None, :] - cumul[:, :, None, :, :]
    decay = jnp.exp(jnp.where(inside[..., None], spread, -jnp.inf))
    intersection = jnp.einsum("gctn,gcsn->gcts", cmat, bmat, precision=HIGH)
    result = jnp.einsum("gcts,gctsh,gcshp->gcthp", intersection, decay, scaled, precision=HIGH)
    ending = cumul[:, :, -1, :]
    seglast = segc[:, :, -1]
    tail = jnp.where(
        (segc == seglast[..., None])[..., None], jnp.exp(ending[:, :, None, :] - cumul), 0.0
    )
    states = jnp.einsum("gcsh,gcshp,gcsn->gchpn", tail, scaled, bmat, precision=HIGH)
    carried = states[:, 0]
    outputs = [result[:, 0]]
    for number in range(1, count):
        reach = jnp.where(
            (segc[:, number] == seglast[:, number - 1][:, None])[..., None],
            jnp.exp(cumul[:, number]),
            0.0,
        )
        outputs.append(
            result[:, number]
            + jnp.einsum("gth,gtn,ghpn->gthp", reach, cmat[:, number], carried, precision=HIGH)
        )
        keeping = jnp.where(
            (seglast[:, number] == seglast[:, number - 1])[:, None], jnp.exp(ending[:, number]), 0.0
        )
        carried = states[:, number] + keeping[:, :, None, None] * carried
    return jnp.stack(outputs, axis=1).reshape(groups, length, heads, width)


def mamba_mix(
    gate_raw,
    inner_raw,
    step_raw,
    shared_raw,
    conv_inner,
    conv_shared,
    step_bias,
    decay_log,
    skip,
    segs,
    span,
):
    groups, length = segs.shape
    heads = step_raw.shape[-1]
    inner = jax.nn.silu(causal_conv(inner_raw.reshape(groups, length, -1), conv_inner, segs))
    shared = jax.nn.silu(causal_conv(shared_raw.reshape(groups, length, -1), conv_shared, segs))
    half = shared.shape[-1] // 2
    step = jax.nn.softplus(step_raw.reshape(groups, length, heads) + step_bias)
    logdec = -step * jnp.exp(decay_log)
    inner = inner.reshape(groups, length, heads, -1)
    mixed = (
        state_scan(inner, step, logdec, shared[..., :half], shared[..., half:], segs, span)
        + skip[:, None] * inner
    )
    return mixed.reshape(groups * length, -1) * jax.nn.silu(gate_raw)


def matrix_product(left, right):
    return jnp.dot(left, right, preferred_element_type=jnp.float32)


def contract_leading_axis(left, right):
    return lax.dot_general(
        left, right, (((0,), (0,)), ((), ())), preferred_element_type=jnp.float32
    )


def contract_last(left, right):
    return lax.dot_general(
        left, right, (((1,), (1,)), ((), ())), preferred_element_type=jnp.float32
    )


def partner(value, axis, size, bit):
    return lax.ppermute(value, axis, [(i, i ^ (1 << bit)) for i in range(size)])


def bit_orders(size):
    high = list(range(size.bit_length() - 2, 0, -1))
    return high, high[:2][::-1] + high[2:]


def relative_blocks(size):
    both = []
    for half, order in enumerate(bit_orders(size)):
        chain = [0]
        for bit in order:
            chain = chain + [other ^ (1 << bit) for other in chain]
        both = both + [(other, half) for other in chain]
    return both + [(other ^ 1, half) for other, half in both]


def gather_dp(own, size):
    half = own.shape[0] // 2
    pieces = []
    for piece, order in zip((own[:half], own[half:]), bit_orders(size)):
        for bit in order:
            piece = jnp.concatenate([piece, partner(piece, "dp", size, bit)])
        pieces.append(piece)
    same = jnp.concatenate(pieces)
    return jnp.concatenate([same, partner(same, "dp", size, 0)])


def scatter_dp(parts, size, dtype):
    half = parts.shape[0] // 2
    same = parts[:half].astype(jnp.float32) + partner(parts[half:], "dp", size, 0).astype(jnp.float32)
    pieces = []
    for piece, order in zip((same[: half // 2], same[half // 2 :]), bit_orders(size)):
        for bit in order[::-1]:
            keep = piece.shape[0] // 2
            away = partner(piece[keep:].astype(dtype), "dp", size, bit)
            piece = piece[:keep] + away.astype(jnp.float32)
        pieces.append(piece)
    return jnp.concatenate(pieces)


def to_relative(value, axis, size):
    me = lax.axis_index("dp")
    width = value.shape[axis] // (2 * size)
    return jnp.concatenate(
        [
            lax.dynamic_slice_in_dim(value, ((me ^ other) * 2 + half) * width, width, axis)
            for other, half in relative_blocks(size)
        ],
        axis,
    )


def from_relative(value, axis, size):
    me = lax.axis_index("dp")
    width = value.shape[axis] // (2 * size)
    blocks = relative_blocks(size)
    place = jnp.asarray([blocks.index((other, half)) for other in range(size) for half in range(2)], jnp.int32)
    return jnp.concatenate(
        [
            lax.dynamic_slice_in_dim(value, place[(me ^ number) * 2 + half] * width, width, axis)
            for number in range(size)
            for half in range(2)
        ],
        axis,
    )


def up(value, size, low, high):
    return lax.ppermute(value, "tensor", [(i, i + 1) for i in range(low, high)])


def down(value, size, low, high):
    return lax.ppermute(value, "tensor", [(i + 1, i) for i in range(low, high)])


def gather_line(own, size):
    me = lax.axis_index("tensor")
    below, above = [own], [own]
    for step in range(size - 1):
        below.append(up(below[-1], size, step, size - 1))
        above.append(down(above[-1], size, 0, size - 1 - step))
    return [own] + [jnp.where(me + r < size, above[r], below[size - r]) for r in range(1, size)]


def scatter_line(parts, size):
    rising, falling = None, None
    for step in range(size - 1):
        first = parts[size - 1 - step].astype(jnp.float32)
        second = parts[step + 1].astype(jnp.float32)
        if rising is not None:
            first = first + rising.astype(jnp.float32)
            second = second + falling.astype(jnp.float32)
        rising = up(first.astype(jnp.bfloat16), size, 0, step + 1)
        falling = down(second.astype(jnp.bfloat16), size, size - 2 - step, size - 1)
    return parts[0].astype(jnp.float32) + rising.astype(jnp.float32) + falling.astype(jnp.float32)


def absolute_rows(blocks, size):
    me = lax.axis_index("tensor")
    rows = blocks[0].shape[0]
    total = jnp.zeros((rows * size,) + blocks[0].shape[1:], blocks[0].dtype)
    for r, block in enumerate(blocks):
        total = lax.dynamic_update_slice_in_dim(total, block, lax.rem(me + r, size) * rows, 0)
    return total


def relative_parts(value, size):
    me = lax.axis_index("tensor")
    rows = value.shape[0] // size
    return [lax.dynamic_slice_in_dim(value, lax.rem(me + r, size) * rows, rows, 0) for r in range(size)]


def sum_small(value, axis, size):
    for bit in range(size.bit_length() - 1):
        value = value + partner(value, axis, size, bit)
    return value


def after(value, *others):
    return lax.optimization_barrier((value,) + others)[0]


def per_device(
    nd,
    nt,
    residual,
    segments,
    mixgain,
    ffngain,
    gateproj,
    innerproj,
    stepproj,
    sharedproj,
    innerconv,
    sharedconv,
    stepbias,
    decaylog,
    skipgain,
    mixerout,
    queryproj,
    keyvalue,
    attnout,
    ffngate,
    upproj,
    downproj,
    cotangent,
):
    bfloat = jnp.bfloat16
    single = jnp.float32
    width = residual.shape[1]
    query_head_rows = queryproj.shape[1] // HEAD_SIZE
    zed = lax.axis_index("tensor")
    kv_head = zed * query_head_rows // (QUERY_HEADS // KEY_VALUE_HEADS)
    seq_count, length = segments.shape
    token_count = seq_count * length
    channels = innerproj.shape[1]
    state_columns = sharedproj.shape[1]
    heads = stepproj.shape[1]
    query_columns = queryproj.shape[1]
    ffn_columns = ffngate.shape[1]
    small_rows = sharedproj.shape[0]
    conv_rows = sharedconv.shape[0]
    taps = sharedconv.shape[1]

    side_width = 128 * (-(-(heads + 2 + taps) // 128))
    gains = jnp.concatenate(
        [
            mixgain[:, None],
            ffngain[:, None],
            jnp.pad(sharedconv, ((0, small_rows - conv_rows), (0, 0))),
            jnp.zeros((small_rows, side_width - heads - 2 - taps), bfloat),
        ],
        axis=1,
    )
    common = absolute_rows(gather_line(jnp.concatenate([sharedproj, keyvalue, gains], axis=1), nt), nt)
    key_at = state_columns + kv_head * HEAD_SIZE
    value_at = state_columns + (KEY_VALUE_HEADS + kv_head) * HEAD_SIZE
    side_own = jnp.concatenate(
        [
            common[:, :state_columns],
            lax.dynamic_slice_in_dim(common, key_at, HEAD_SIZE, 1),
            lax.dynamic_slice_in_dim(common, value_at, HEAD_SIZE, 1),
            stepproj,
            common[:, state_columns + keyvalue.shape[1] :],
        ],
        axis=1,
    )
    side = gather_dp(side_own, nd)
    main = gather_dp(jnp.concatenate([gateproj, innerproj, queryproj], axis=1), nd)
    out_own = after(jnp.concatenate([mixerout, attnout], axis=1), main)
    out_w = gather_dp(out_own, nd)
    ffn_own = after(jnp.concatenate([ffngate, upproj, downproj], axis=1), out_w)
    ffn_w = gather_dp(ffn_own, nd)
    gate_up_w = ffn_w[:, : 2 * ffn_columns]
    down_w = ffn_w[:, 2 * ffn_columns :]
    extra = side[:, state_columns + 2 * HEAD_SIZE + heads :]
    gain_one = extra[:, 0].astype(single)
    gain_two = extra[:, 1].astype(single)
    conv_shared = from_relative(extra[:, 2 : 2 + taps], 0, nd)
    conv_shared = conv_shared.reshape(nd * nt, small_rows, taps)[:, :conv_rows].reshape(-1, taps)
    conv_shared = conv_shared.astype(single)
    side_used = side[:, : state_columns + 2 * HEAD_SIZE + heads]

    resid_own = to_relative(residual, 1, nd)
    cot_own = to_relative(cotangent, 1, nd)
    resid_rows = absolute_rows(gather_line(resid_own, nt), nt).astype(single)
    normed = (rmsnorm(resid_rows, gain_one)).astype(bfloat)
    resid_f = resid_own.astype(single)
    _, norm_one_pull = jax.vjp(rmsnorm, resid_f, gain_one)
    main_raw = matrix_product(normed, main)
    side_raw = matrix_product(normed, side_used)
    gate_raw = main_raw[:, :channels]
    inner_raw = main_raw[:, channels : 2 * channels]
    query_raw = main_raw[:, 2 * channels :]
    shared_raw = side_raw[:, :state_columns]
    key_raw = side_raw[:, state_columns : state_columns + HEAD_SIZE]
    value_raw = side_raw[:, state_columns + HEAD_SIZE : state_columns + 2 * HEAD_SIZE]
    step_raw = side_raw[:, state_columns + 2 * HEAD_SIZE :]

    def mamba_local(
        gate_in, inner_in, step_in, shared_in, conv_in, conv_sh, bias_in, decay_in, skip_in
    ):
        return mamba_mix(
            gate_in,
            inner_in,
            step_in,
            shared_in,
            conv_in,
            conv_sh,
            bias_in,
            decay_in,
            skip_in,
            segments,
            SPAN,
        )

    mamba_value, mamba_pull = jax.vjp(
        mamba_local,
        gate_raw,
        inner_raw,
        step_raw,
        shared_raw,
        innerconv.astype(single),
        conv_shared,
        stepbias.astype(single),
        decaylog.astype(single),
        skipgain.astype(single),
    )
    mamba_y = mamba_value.astype(bfloat)
    query_r = rotate(query_raw.reshape(seq_count, length, query_head_rows, HEAD_SIZE), 1.0).astype(
        bfloat
    )
    key_r = rotate(key_raw.reshape(seq_count, length, HEAD_SIZE), 1.0).astype(bfloat)
    value_b = value_raw.reshape(seq_count, length, HEAD_SIZE).astype(bfloat)
    order = jnp.arange(length)
    allowed = ((order[:, None] >= order[None, :]) & (segments[:, :, None] == segments[:, None, :]))[
        :, None
    ]
    scale = math.sqrt(HEAD_SIZE)
    scores = jnp.einsum("gthd,gsd->ghts", query_r, key_r, preferred_element_type=single) / scale
    masked = jnp.where(allowed, scores, -jnp.inf)
    peak = jnp.max(masked, axis=-1, keepdims=True)
    expo = jnp.exp(masked - peak)
    totals = jnp.sum(expo, axis=-1, keepdims=True)
    probs = (expo / totals).astype(bfloat)
    logsum = peak + jnp.log(totals)
    attn_o = (
        jnp.einsum("ghts,gsd->gthd", probs, value_b, preferred_element_type=single)
        .reshape(token_count, -1)
        .astype(bfloat)
    )
    mixed_in = jnp.concatenate([mamba_y, attn_o], axis=1)
    mix_part = contract_last(mixed_in, out_w).astype(bfloat)
    middle = resid_f + scatter_line(relative_parts(mix_part, nt), nt)
    norm_two, norm_two_pull = jax.vjp(rmsnorm, middle, gain_two)
    rows_two = jnp.concatenate(gather_line(norm_two.astype(bfloat), nt))
    gate_up = matrix_product(rows_two, gate_up_w)
    gate = gate_up[:, :ffn_columns]
    upper = gate_up[:, ffn_columns:]
    sigma = jax.nn.sigmoid(gate)
    hidden = (gate * sigma * upper).astype(bfloat)
    grad_rows = jnp.concatenate(gather_line(after(cot_own, resid_rows), nt))
    grad_hidden = matrix_product(grad_rows, down_w)
    grad_gate = (grad_hidden * upper * sigma * (1.0 + gate * (1.0 - sigma))).astype(bfloat)
    grad_upper = (grad_hidden * gate * sigma).astype(bfloat)
    grad_gate_up = jnp.concatenate([grad_gate, grad_upper], axis=1)
    two_part = contract_last(grad_gate_up, gate_up_w).astype(bfloat)
    grad_norm_two = scatter_line(jnp.split(two_part, nt), nt)
    grad_middle_n, grad_gain_two = norm_two_pull(grad_norm_two)
    grad_middle = cot_own.astype(single) + grad_middle_n
    grad_mix_own = grad_middle.astype(bfloat)
    grad_mix_rows = absolute_rows(gather_line(grad_mix_own, nt), nt)
    ffn_part = contract_last(hidden, down_w).astype(bfloat)
    ffn_parts = [after(part, grad_mix_rows) for part in jnp.split(ffn_part, nt)]
    layer_out = from_relative(middle + scatter_line(ffn_parts, nt), 1, nd)
    grad_mixed_in = matrix_product(grad_mix_rows, out_w)
    grad_mamba = grad_mixed_in[:, :channels]
    grad_attn_o = (
        grad_mixed_in[:, channels:]
        .astype(bfloat)
        .reshape(seq_count, length, query_head_rows, HEAD_SIZE)
    )
    probs_full = jnp.exp(jnp.where(allowed, scores - logsum, -jnp.inf))
    grad_probs = jnp.einsum("gthd,gsd->ghts", grad_attn_o, value_b, preferred_element_type=single)
    delta = jnp.sum(grad_probs * probs_full, axis=-1, keepdims=True)
    grad_scores = (probs_full * (grad_probs - delta)).astype(bfloat)
    grad_query_r = (
        jnp.einsum("ghts,gsd->gthd", grad_scores, key_r, preferred_element_type=single) / scale
    )
    grad_key_r = (
        jnp.einsum("ghts,gthd->gsd", grad_scores, query_r, preferred_element_type=single) / scale
    )
    grad_value = jnp.einsum("ghts,gthd->gsd", probs, grad_attn_o, preferred_element_type=single)
    grad_query = rotate(grad_query_r, -1.0).reshape(token_count, -1).astype(bfloat)
    grad_key = rotate(grad_key_r, -1.0).reshape(token_count, HEAD_SIZE).astype(bfloat)
    value_gradient = grad_value.reshape(token_count, HEAD_SIZE).astype(bfloat)
    (
        grad_gate_raw,
        grad_inner_raw,
        grad_step_raw,
        grad_shared_raw,
        grad_convi,
        grad_convs,
        grad_bias,
        grad_decay,
        grad_skip,
    ) = mamba_pull(grad_mamba)
    grad_main = jnp.concatenate(
        [grad_gate_raw.astype(bfloat), grad_inner_raw.astype(bfloat), grad_query], axis=1
    )
    grad_side = jnp.concatenate(
        [grad_shared_raw.astype(bfloat), grad_key, value_gradient, grad_step_raw.astype(bfloat)],
        axis=1,
    )
    one_part = (contract_last(grad_main, main) + contract_last(grad_side, side_used)).astype(bfloat)
    grad_norm_one = scatter_line(relative_parts(one_part, nt), nt)
    grad_resid_n, grad_gain_one = norm_one_pull(grad_norm_one)
    grad_residual = from_relative(grad_middle + grad_resid_n, 1, nd)

    down_g = scatter_dp(contract_leading_axis(grad_rows, hidden).astype(bfloat), nd, bfloat)
    gate_up_g = scatter_dp(contract_leading_axis(rows_two, grad_gate_up).astype(bfloat), nd, bfloat)
    out_g = scatter_dp(contract_leading_axis(grad_mix_rows, mixed_in).astype(bfloat), nd, bfloat)
    side_g = scatter_dp(contract_leading_axis(normed, grad_side).astype(bfloat), nd, bfloat)
    main_g = scatter_dp(contract_leading_axis(normed, grad_main).astype(bfloat), nd, bfloat)

    key_value_g = jnp.zeros((side_g.shape[0], keyvalue.shape[1]), single)
    key_value_g = lax.dynamic_update_slice_in_dim(
        key_value_g, side_g[:, state_columns : state_columns + HEAD_SIZE], kv_head * HEAD_SIZE, 1
    )
    key_value_g = lax.dynamic_update_slice_in_dim(
        key_value_g,
        side_g[:, state_columns + HEAD_SIZE : state_columns + 2 * HEAD_SIZE],
        (KEY_VALUE_HEADS + kv_head) * HEAD_SIZE,
        1,
    )
    common_g = jnp.concatenate([side_g[:, :state_columns], key_value_g], axis=1).astype(bfloat)
    common_g = scatter_line(relative_parts(common_g, nt), nt)

    everywhere = jnp.concatenate(
        [
            from_relative(grad_gain_one, 0, nd),
            from_relative(grad_gain_two, 0, nd),
            grad_convs.reshape(-1),
        ]
    )
    local = jnp.concatenate([grad_convi.reshape(-1), grad_bias, grad_decay, grad_skip])
    local = jnp.pad(local, (0, -local.shape[0] % 128))
    split = everywhere.shape[0]
    small = sum_small(jnp.concatenate([everywhere, local]).reshape(-1, 128), "dp", nd).reshape(-1)
    local = small[split:]
    everywhere = sum_small(small[:split].reshape(-1, 128), "tensor", nt).reshape(-1)
    place = lax.axis_index("dp") * nt + zed
    gain_one_g = lax.dynamic_slice_in_dim(everywhere, place * small_rows, small_rows, 0)
    gain_two_g = lax.dynamic_slice_in_dim(everywhere, width + place * small_rows, small_rows, 0)
    conv_g = lax.dynamic_slice_in_dim(
        everywhere[2 * width :].reshape(-1, taps), place * conv_rows, conv_rows, 0
    )
    counts = channels * innerconv.shape[1]
    return (
        layer_out,
        grad_residual,
        gain_one_g,
        gain_two_g,
        main_g[:, :channels],
        main_g[:, channels : 2 * channels],
        side_g[:, state_columns + 2 * HEAD_SIZE :],
        common_g[:, :state_columns],
        local[:counts].reshape(channels, -1),
        conv_g,
        local[counts : counts + heads],
        local[counts + heads : counts + 2 * heads],
        local[counts + 2 * heads : counts + 3 * heads],
        out_g[:, :channels],
        main_g[:, 2 * channels :],
        common_g[:, state_columns:],
        out_g[:, channels:],
        gate_up_g[:, :ffn_columns],
        gate_up_g[:, ffn_columns:],
        down_g,
    )


def solution(mesh):
    return jax.shard_map(
        functools.partial(per_device, mesh.shape["dp"], mesh.shape["tensor"]),
        mesh=mesh,
        in_specs=(
            P(("dp", "tensor"), None),
            P("dp", None),
            P(("dp", "tensor")),
            P(("dp", "tensor")),
            P("dp", "tensor"),
            P("dp", "tensor"),
            P("dp", "tensor"),
            P(("dp", "tensor"), None),
            P("tensor", None),
            P(("dp", "tensor"), None),
            P("tensor"),
            P("tensor"),
            P("tensor"),
            P("dp", "tensor"),
            P("dp", "tensor"),
            P(("dp", "tensor"), None),
            P("dp", "tensor"),
            P("dp", "tensor"),
            P("dp", "tensor"),
            P("dp", "tensor"),
            P(("dp", "tensor"), None),
        ),
        out_specs=(
            P(("dp", "tensor"), None),
            P(("dp", "tensor"), None),
            P(("dp", "tensor")),
            P(("dp", "tensor")),
            P("dp", "tensor"),
            P("dp", "tensor"),
            P("dp", "tensor"),
            P(("dp", "tensor"), None),
            P("tensor", None),
            P(("dp", "tensor"), None),
            P("tensor"),
            P("tensor"),
            P("tensor"),
            P("dp", "tensor"),
            P("dp", "tensor"),
            P(("dp", "tensor"), None),
            P("dp", "tensor"),
            P("dp", "tensor"),
            P("dp", "tensor"),
            P("dp", "tensor"),
        ),
        check_vma=False,
    )
```

```python
import functools
import math

import jax
import jax.numpy as jnp
from jax import lax
from jax.experimental import pallas as pl
from jax.experimental.pallas import tpu as pltpu
from jax.sharding import PartitionSpec as P

QUERY_HEADS = 8
KEY_VALUE_HEADS = 2
HEAD_SIZE = 128
SPAN = 256


HIGH = lax.Precision.HIGHEST
eps = 1e-05
rope_base = 10000.0


def rmsnorm(value, gain):
    return value * lax.rsqrt(jnp.mean(value * value, axis=-1, keepdims=True) + eps) * gain


def rotate(tensor_array, sign):
    half = tensor_array.shape[-1] // 2
    places = jnp.arange(tensor_array.shape[1]).astype(jnp.float32)
    freqs = rope_base ** (-jnp.arange(half).astype(jnp.float32) / half)
    angle = (places[:, None] * freqs[None, :]).reshape(
        (tensor_array.shape[1],) + (1,) * (tensor_array.ndim - 3) + (half,)
    )
    cosine = jnp.cos(angle)
    sine = sign * jnp.sin(angle)
    first = tensor_array[..., :half]
    second = tensor_array[..., half:]
    return jnp.concatenate(
        [first * cosine - second * sine, first * sine + second * cosine], axis=-1
    )


def causal_conv(values, kernel, segs):
    total = values * kernel[:, 0]
    for lag in range(1, kernel.shape[1]):
        moved = jnp.pad(values, ((0, 0), (lag, 0), (0, 0)))[:, :-lag]
        prior = jnp.pad(segs, ((0, 0), (lag, 0)), constant_values=-1)[:, :-lag]
        total = total + jnp.where((prior == segs)[..., None], moved, 0.0) * kernel[:, lag]
    return total


def state_scan(inner, step, logdec, bmat, cmat, segs, span):
    groups, length, heads, width = inner.shape
    count = length // span
    scaled = (inner * step[..., None]).reshape(groups, count, span, heads, width)
    cumul = jnp.cumsum(logdec.reshape(groups, count, span, heads), axis=2)
    bmat = bmat.reshape(groups, count, span, -1)
    cmat = cmat.reshape(groups, count, span, -1)
    segc = segs.reshape(groups, count, span)
    order = jnp.arange(span)
    inside = (order[:, None] >= order[None, :]) & (segc[..., :, None] == segc[..., None, :])
    spread = cumul[:, :, :, None, :] - cumul[:, :, None, :, :]
    decay = jnp.exp(jnp.where(inside[..., None], spread, -jnp.inf))
    intersection = jnp.einsum("gctn,gcsn->gcts", cmat, bmat, precision=HIGH)
    result = jnp.einsum("gcts,gctsh,gcshp->gcthp", intersection, decay, scaled, precision=HIGH)
    ending = cumul[:, :, -1, :]
    seglast = segc[:, :, -1]
    tail = jnp.where(
        (segc == seglast[..., None])[..., None], jnp.exp(ending[:, :, None, :] - cumul), 0.0
    )
    states = jnp.einsum("gcsh,gcshp,gcsn->gchpn", tail, scaled, bmat, precision=HIGH)
    carried = states[:, 0]
    outputs = [result[:, 0]]
    for number in range(1, count):
        reach = jnp.where(
            (segc[:, number] == seglast[:, number - 1][:, None])[..., None],
            jnp.exp(cumul[:, number]),
            0.0,
        )
        outputs.append(
            result[:, number]
            + jnp.einsum("gth,gtn,ghpn->gthp", reach, cmat[:, number], carried, precision=HIGH)
        )
        keeping = jnp.where(
            (seglast[:, number] == seglast[:, number - 1])[:, None], jnp.exp(ending[:, number]), 0.0
        )
        carried = states[:, number] + keeping[:, :, None, None] * carried
    return jnp.stack(outputs, axis=1).reshape(groups, length, heads, width)


def mamba_mix(
    gate_raw,
    inner_raw,
    step_raw,
    shared_raw,
    conv_inner,
    conv_shared,
    step_bias,
    decay_log,
    skip,
    segs,
    span,
):
    groups, length = segs.shape
    heads = step_raw.shape[-1]
    inner = jax.nn.silu(causal_conv(inner_raw.reshape(groups, length, -1), conv_inner, segs))
    shared = jax.nn.silu(causal_conv(shared_raw.reshape(groups, length, -1), conv_shared, segs))
    half = shared.shape[-1] // 2
    step = jax.nn.softplus(step_raw.reshape(groups, length, heads) + step_bias)
    logdec = -step * jnp.exp(decay_log)
    inner = inner.reshape(groups, length, heads, -1)
    mixed = (
        state_scan(inner, step, logdec, shared[..., :half], shared[..., half:], segs, span)
        + skip[:, None] * inner
    )
    return mixed.reshape(groups * length, -1) * jax.nn.silu(gate_raw)


def matrix_product(left, right):
    return jnp.dot(left, right, preferred_element_type=jnp.float32)


def contract_leading_axis(left, right):
    return lax.dot_general(
        left, right, (((0,), (0,)), ((), ())), preferred_element_type=jnp.float32
    )


def contract_last(left, right):
    return lax.dot_general(
        left, right, (((1,), (1,)), ((), ())), preferred_element_type=jnp.float32
    )


def partner(value, axis, size, bit):
    return lax.ppermute(value, axis, [(i, i ^ (1 << bit)) for i in range(size)])


def bit_orders(size):
    high = list(range(size.bit_length() - 2, 0, -1))
    return high, high[:2][::-1] + high[2:]


def relative_blocks(size):
    both = []
    for half, order in enumerate(bit_orders(size)):
        chain = [0]
        for bit in order:
            chain = chain + [other ^ (1 << bit) for other in chain]
        both = both + [(other, half) for other in chain]
    return both + [(other ^ 1, half) for other, half in both]


def to_relative(value, axis, size):
    me = lax.axis_index("dp")
    width = value.shape[axis] // (2 * size)
    return jnp.concatenate(
        [
            lax.dynamic_slice_in_dim(value, ((me ^ other) * 2 + half) * width, width, axis)
            for other, half in relative_blocks(size)
        ],
        axis,
    )


def from_relative(value, axis, size):
    me = lax.axis_index("dp")
    width = value.shape[axis] // (2 * size)
    blocks = relative_blocks(size)
    place = jnp.asarray([blocks.index((other, half)) for other in range(size) for half in range(2)], jnp.int32)
    return jnp.concatenate(
        [
            lax.dynamic_slice_in_dim(value, place[(me ^ number) * 2 + half] * width, width, axis)
            for number in range(size)
            for half in range(2)
        ],
        axis,
    )


def sum_small(value, axis, size):
    for bit in range(size.bit_length() - 1):
        value = value + partner(value, axis, size, bit)
    return value


def line_sums(value, size):
    me = lax.axis_index("tensor")
    rows = value.shape[0] // size
    total = lax.dynamic_slice_in_dim(value, me * rows, rows, 0).astype(jnp.float32)
    for other in range(1, size):
        away = lax.dynamic_slice_in_dim(value, lax.rem(me + other, size) * rows, rows, 0)
        came = lax.ppermute(away, "tensor", [(i, (i + other) % size) for i in range(size)])
        total = total + came.astype(jnp.float32)
    return total


def after(value, *others):
    return lax.optimization_barrier((value,) + others)[0]


MESH = pl.DeviceIdType.MESH
VMEM_LIMIT = 56 * 1024 * 1024


def flip(value, bit):
    unit = 1 << bit
    return value + unit * (1 - 2 * ((value // unit) % 2))


def mixed_with(value, other, bits):
    for bit in range(bits):
        if (other >> bit) & 1:
            value = flip(value, bit)
    return value


def enter(nt, bits):
    me, zed = lax.axis_index("dp"), lax.axis_index("tensor")
    barrier = pltpu.get_barrier_semaphore()

    @pl.when(zed > 0)
    def _():
        pl.semaphore_signal(barrier, inc=1, device_id=(me, zed - 1), device_id_type=MESH)

    @pl.when(zed < nt - 1)
    def _():
        pl.semaphore_signal(barrier, inc=1, device_id=(me, zed + 1), device_id_type=MESH)

    for bit in range(bits):
        pl.semaphore_signal(barrier, inc=1, device_id=(flip(me, bit), zed), device_id_type=MESH)
    below = jnp.where(zed > 0, 1, 0)
    above = jnp.where(zed < nt - 1, 1, 0)
    pl.semaphore_wait(barrier, bits + below + above)
    return me, zed


def aligned(start, size):
    return pl.ds(pl.multiple_of(start, 16), size)


def together(*flows):
    flows = [list(flow) for flow in flows]
    order = sorted(
        ((place + 0.5) / len(flow), number, place)
        for number, flow in enumerate(flows)
        for place in range(len(flow))
    )
    for _, number, place in order:
        flows[number][place]()


def gather_steps(nd, me, zed, own, everything, send, recv, local):
    half = own.shape[0] // 2
    blocks = relative_blocks(nd)
    place = {block: number for number, block in enumerate(blocks)}

    def rows(block):
        return everything.at[pl.ds(place[block] * half, half)]

    def source(block):
        return own.at[pl.ds(block[1] * half, half)] if block[0] == 0 else rows(block)

    hops = []
    for part, order in enumerate(bit_orders(nd)):
        chain = [0]
        for bit in order:
            hops = hops + [((other, part), bit) for other in chain]
            chain = chain + [other ^ (1 << bit) for other in chain]
    hops = hops + [(block, 0) for block in blocks[:nd]]

    def copy(number):
        block, bit = hops[number]
        landed = (block[0] ^ (1 << bit), block[1])
        return pltpu.make_async_remote_copy(
            src_ref=source(block),
            dst_ref=rows(landed),
            send_sem=send.at[number],
            recv_sem=recv.at[place[landed]],
            device_id=(flip(me, bit), zed),
            device_id_type=MESH,
        )

    def arrival(block):
        return pltpu.make_async_remote_copy(
            src_ref=rows(block),
            dst_ref=rows(block),
            send_sem=send.at[0],
            recv_sem=recv.at[place[block]],
            device_id=(flip(me, 0), zed),
            device_id_type=MESH,
        )

    def begin():
        for number, (block, bit) in enumerate(hops):
            if block[0] == 0:
                copy(number).start()
        for part in range(2):
            pltpu.make_async_copy(source((0, part)), rows((0, part)), local.at[part]).start()

    def forward(block):
        def step():
            arrival(block).wait_recv()
            for number, (origin, bit) in enumerate(hops):
                if origin == block:
                    copy(number).start()

        return step

    def end():
        for block in blocks[nd:]:
            arrival(block).wait_recv()
        for number in range(len(hops)):
            copy(number).wait_send()
        for part in range(2):
            pltpu.make_async_copy(source((0, part)), rows((0, part)), local.at[part]).wait()

    first, second = blocks[1 : nd // 2], blocks[nd // 2 + 1 : nd]
    middle = [forward(block) for pair in zip(first, second) for block in pair]
    return [begin] + middle + [end]


def gather_hops(nd):
    return 2 * (nd // 2 - 1) + nd


def gather_semaphores(nd):
    return [
        pltpu.SemaphoreType.DMA((gather_hops(nd),)),
        pltpu.SemaphoreType.DMA((2 * nd,)),
        pltpu.SemaphoreType.DMA((2,)),
    ]


def each_rows(rows, body, unit=16):
    def step(number, carry):
        body(aligned(number * unit, unit))
        return carry

    lax.fori_loop(0, rows // unit, step, 0)


def scatter_steps(nd, me, zed, parts, total, mine, held, landed, core_send, core_recv, send, recv, local):
    half = total.shape[0] // 2
    chain_length = nd // 2

    def piece(ref, number):
        return ref.at[pl.ds(number * half, half)]

    rounds, slot = [], 0
    for part, order in enumerate(bit_orders(nd)):
        length, own_rounds = chain_length, []
        for bit in order[::-1]:
            length = length // 2
            own_rounds.append((bit, length, slot))
            slot = slot + length
        rounds.append(own_rounds)

    def core_copy(number):
        return pltpu.make_async_remote_copy(
            src_ref=piece(parts, nd + number),
            dst_ref=piece(held, number),
            send_sem=core_send.at[number],
            recv_sem=core_recv.at[number],
            device_id=(flip(me, 0), zed),
            device_id_type=MESH,
        )

    def hop(part, bit, number, where):
        return pltpu.make_async_remote_copy(
            src_ref=piece(held, number),
            dst_ref=piece(landed, where),
            send_sem=send.at[where],
            recv_sem=recv.at[where],
            device_id=(flip(me, bit), zed),
            device_id_type=MESH,
        )

    wanted = []
    for number in range(chain_length - 1, -1, -1):
        wanted = wanted + [number, chain_length + number]

    def load(number):
        return pltpu.make_async_copy(piece(parts, number), piece(mine, number), local.at[number])

    def begin():
        for number in wanted:
            core_copy(number).start()
        for number in wanted:
            load(number).start()

    def core_sum(number):
        part, spot = number // chain_length, number % chain_length

        def step():
            load(number).wait()
            core_copy(number).wait_recv()

            def body(rows):
                spot_rows = piece(held, number)
                value = spot_rows[rows].astype(jnp.float32) + piece(mine, number)[rows].astype(jnp.float32)
                spot_rows[rows] = value.astype(jnp.bfloat16)

            each_rows(half, body)
            if rounds[part]:
                bit, length, first = rounds[part][0]
                if spot >= length:
                    hop(part, bit, number, first + spot - length).start()

        return step

    def later_sum(part, turn, spot):
        bit, length, first = rounds[part][turn]
        number = part * chain_length + spot

        def step():
            hop(part, bit, number, first + spot).wait_recv()
            last = turn == len(rounds[part]) - 1

            def body(rows):
                value = piece(held, number)[rows].astype(jnp.float32) + piece(landed, first + spot)[rows].astype(
                    jnp.float32
                )
                if last:
                    piece(total, part)[rows] = value
                else:
                    piece(held, number)[rows] = value.astype(jnp.bfloat16)

            each_rows(half, body)
            if not last:
                next_bit, next_length, next_first = rounds[part][turn + 1]
                if spot >= next_length:
                    hop(part, next_bit, number, next_first + spot - next_length).start()

        return step

    steps = [begin] + [core_sum(number) for number in wanted]
    for turn in range(len(rounds[0])):
        length = rounds[0][turn][1]
        for spot in range(length - 1, -1, -1):
            for part in range(2):
                steps.append(later_sum(part, turn, spot))

    def end():
        for number in range(nd):
            core_copy(number).wait_send()
        for part in range(2):
            for bit, length, first in rounds[part]:
                for spot in range(length):
                    hop(part, bit, part * chain_length + length + spot, first + spot).wait_send()

    return steps + [end]


def scatter_scratch(nd, rows, columns):
    slots = nd - 2
    return [
        pltpu.VMEM((nd * rows // 2, columns), jnp.bfloat16),
        pltpu.VMEM((nd * rows // 2, columns), jnp.bfloat16),
        pltpu.VMEM((slots * rows // 2, columns), jnp.bfloat16),
        pltpu.SemaphoreType.DMA((nd,)),
        pltpu.SemaphoreType.DMA((nd,)),
        pltpu.SemaphoreType.DMA((slots,)),
        pltpu.SemaphoreType.DMA((slots,)),
        pltpu.SemaphoreType.DMA((nd,)),
    ]


def line_gather(nt, me, zed, chunks, own, everything, send, recv):
    size = own.shape[0] // chunks

    def own_rows(chunk):
        return own.at[pl.ds(chunk * size, size)]

    def rows(block, chunk):
        return everything.at[aligned(block * (size * chunks) + chunk * size, size)]

    def copy(source, block, chunk, side):
        return pltpu.make_async_remote_copy(
            src_ref=source,
            dst_ref=rows(block, chunk),
            send_sem=send.at[side, block, chunk],
            recv_sem=recv.at[block, chunk],
            device_id=(me, zed + 1 - 2 * side),
            device_id_type=MESH,
        )

    def keep(chunk):
        return pltpu.make_async_copy(own_rows(chunk), rows(zed, chunk), recv.at[zed, chunk])

    def first(chunk):
        for side, condition in ((0, zed < nt - 1), (1, zed > 0)):

            @pl.when(condition)
            def _(side=side):
                copy(own_rows(chunk), zed, chunk, side).start()

        keep(chunk).start()

    def onward(chunk, distance):
        for side, block in ((0, zed - distance), (1, zed + distance)):
            inside = (block >= 0) if side == 0 else (block < nt)
            open_end = (zed < nt - 1) if side == 0 else (zed > 0)

            @pl.when(inside)
            def _(block=block, side=side):
                copy(rows(block, chunk), block, chunk, side).wait_recv()

            @pl.when(jnp.logical_and(inside, open_end))
            def _(block=block, side=side):
                copy(rows(block, chunk), block, chunk, side).start()

    def end(chunk):
        keep(chunk).wait()
        for side, condition in ((0, zed < nt - 1), (1, zed > 0)):

            @pl.when(condition)
            def _(side=side):
                copy(own_rows(chunk), zed, chunk, side).wait_send()

            for distance in range(1, nt - 1):
                block = zed - distance if side == 0 else zed + distance
                inside = (block >= 0) if side == 0 else (block < nt)

                @pl.when(jnp.logical_and(inside, condition))
                def _(block=block, side=side):
                    copy(rows(block, chunk), block, chunk, side).wait_send()

    return first, onward, end


def line_gather_semaphores(nt, chunks):
    return [pltpu.SemaphoreType.DMA((2, nt, chunks)), pltpu.SemaphoreType.DMA((nt, chunks))]


def line_reduce(nt, me, zed, chunks, parts, rising, falling, send, recv):
    block_rows = parts.shape[0] // nt
    size = block_rows // chunks
    sides = ((0, rising), (1, falling))

    def rows(block, chunk):
        return aligned(block * block_rows + chunk * size, size)

    def copy(source, side, held, block, chunk):
        return pltpu.make_async_remote_copy(
            src_ref=source.at[rows(block, chunk)],
            dst_ref=held.at[rows(block, chunk)],
            send_sem=send.at[side, block, chunk],
            recv_sem=recv.at[side, block, chunk],
            device_id=(me, zed + 1 - 2 * side),
            device_id_type=MESH,
        )

    def roles(side, block):
        if side == 0:
            return zed == 0, jnp.logical_and(zed > 0, zed < block)
        return zed == nt - 1, jnp.logical_and(zed < nt - 1, zed > block)

    def pass_on(chunk):
        for turn in range(nt - 1):
            for side, held in sides:
                block = nt - 1 - turn if side == 0 else turn
                source, between = roles(side, block)

                @pl.when(source)
                def _(side=side, held=held, block=block):
                    copy(parts, side, held, block, chunk).start()

                @pl.when(between)
                def _(side=side, held=held, block=block):
                    copy(held, side, held, block, chunk).wait_recv()

                    def body(inner):
                        where = aligned(block * block_rows + chunk * size + inner.start, inner.size)
                        value = parts[where].astype(jnp.float32) + held[where].astype(jnp.float32)
                        held[where] = value.astype(jnp.bfloat16)

                    each_rows(size, body)
                    copy(held, side, held, block, chunk).start()

    def own_sum(chunk, total):
        where = rows(zed, chunk)
        total[...] = parts[where].astype(jnp.float32)
        for side, held in sides:

            @pl.when(zed > 0 if side == 0 else zed < nt - 1)
            def _(side=side, held=held):
                copy(held, side, held, zed, chunk).wait_recv()
                total[...] += held[where].astype(jnp.float32)

    def end(chunk):
        for turn in range(nt - 1):
            for side, held in sides:
                block = nt - 1 - turn if side == 0 else turn
                source, between = roles(side, block)

                @pl.when(jnp.logical_or(source, between))
                def _(side=side, held=held, block=block):
                    copy(held, side, held, block, chunk).wait_send()

    return pass_on, own_sum, end


def line_reduce_scratch(nt, block_rows, columns, chunks):
    return [
        pltpu.VMEM((nt * block_rows, columns), jnp.bfloat16),
        pltpu.VMEM((nt * block_rows, columns), jnp.bfloat16),
        pltpu.VMEM((block_rows // chunks, columns), jnp.float32),
        pltpu.SemaphoreType.DMA((2, nt, chunks)),
        pltpu.SemaphoreType.DMA((2, nt, chunks)),
    ]


HBM = pl.BlockSpec(memory_space=pl.ANY)
ONCHIP = pl.BlockSpec(memory_space=pltpu.VMEM)


def first_gathers(nd, nt, rows, small, groups):
    chunks = 2
    bits = nd.bit_length() - 1
    count = len(groups)

    def kernel(rows_ref, small_ref, *refs):
        group_refs, refs = refs[:count], refs[count:]
        rows_all, small_line, small_all = refs[:3]
        group_all, refs = refs[3 : 3 + count], refs[3 + count :]
        row_sems, small_sems, small_dp, refs = refs[:2], refs[2:4], refs[4:7], refs[7:]
        me, zed = enter(nt, bits)
        small_first, small_onward, small_end = line_gather(nt, me, zed, 1, small_ref, small_line, *small_sems)
        row_first, row_onward, row_end = line_gather(nt, me, zed, chunks, rows_ref, rows_all, *row_sems)
        flows = [
            gather_steps(nd, me, zed, group_refs[n], group_all[n], *refs[3 * n : 3 * n + 3]) for n in range(count)
        ]
        last = gather_steps(nd, me, zed, small_line, small_all, *small_dp)
        small_first(0)
        flows[0][0]()
        for chunk in range(chunks):
            row_first(chunk)
        for flow in flows[1:]:
            flow[0]()
        for distance in range(1, nt):
            small_onward(0, distance)
        small_end(0)
        last[0]()
        along = [
            functools.partial(row_onward, chunk, distance) for distance in range(1, nt) for chunk in range(chunks)
        ]
        over = [step for flow in flows for step in flow[1:-1]]
        over = over + last[1:-1] + [flow[-1] for flow in flows] + [last[-1]]
        together(along, over)
        for chunk in range(chunks):
            row_end(chunk)

    def widened(array, times):
        return jax.ShapeDtypeStruct((array.shape[0] * times, array.shape[1]), array.dtype)

    semaphores = line_gather_semaphores(nt, chunks) + line_gather_semaphores(nt, 1) + gather_semaphores(nd)
    return pl.pallas_call(
        kernel,
        out_shape=[widened(rows, nt), widened(small, nt), widened(small, nt * nd)]
        + [widened(group, nd) for group in groups],
        in_specs=[HBM] * (2 + count),
        out_specs=[HBM] * (3 + count),
        scratch_shapes=semaphores + gather_semaphores(nd) * count,
        compiler_params=pltpu.CompilerParams(
            collective_id=0, has_side_effects=True, vmem_limit_bytes=VMEM_LIMIT
        ),
        name="first_gathers",
    )(rows, small, *groups)


def middle_rows(nd, nt, parts, resid, gain, groups):
    chunks = 4
    bits = nd.bit_length() - 1
    count = len(groups)
    block_rows, width = resid.shape
    size = block_rows // chunks

    def kernel(parts_ref, resid_ref, gain_ref, *refs):
        group_refs, refs = refs[:count], refs[count:]
        middle_ref, rows_all = refs[:2]
        group_all, refs = refs[2 : 2 + count], refs[2 + count :]
        own, rising, falling, total, send, recv = refs[:6]
        gather_sems, refs = refs[6:8], refs[8:]
        me, zed = enter(nt, bits)
        pass_on, own_sum, reduce_end = line_reduce(nt, me, zed, chunks, parts_ref, rising, falling, send, recv)
        first, onward, gather_end = line_gather(nt, me, zed, chunks, own, rows_all, *gather_sems)
        flows = [
            gather_steps(nd, me, zed, group_refs[n], group_all[n], *refs[3 * n : 3 * n + 3]) for n in range(count)
        ]

        def finish(chunk):
            own_sum(chunk, total)
            where = pl.ds(chunk * size, size)
            value = resid_ref[where].astype(jnp.float32) + total[...]
            middle_ref[where] = value
            scale = lax.rsqrt(jnp.mean(value * value, axis=-1, keepdims=True) + eps)
            own[where] = (value * scale * gain_ref[...]).astype(jnp.bfloat16)
            first(chunk)

        line_schedule(nt, chunks, pass_on, finish, onward, [step for flow in flows for step in flow])
        for chunk in range(chunks):
            reduce_end(chunk)
            gather_end(chunk)

    return pl.pallas_call(
        kernel,
        out_shape=[
            jax.ShapeDtypeStruct((block_rows, width), jnp.float32),
            jax.ShapeDtypeStruct((block_rows * nt, width), jnp.bfloat16),
        ]
        + [jax.ShapeDtypeStruct((group.shape[0] * nd, group.shape[1]), group.dtype) for group in groups],
        in_specs=[ONCHIP] * 3 + [HBM] * count,
        out_specs=[ONCHIP] + [HBM] * (1 + count),
        scratch_shapes=[pltpu.VMEM((block_rows, width), jnp.bfloat16)]
        + line_reduce_scratch(nt, block_rows, width, chunks)
        + line_gather_semaphores(nt, chunks)
        + gather_semaphores(nd) * count,
        compiler_params=pltpu.CompilerParams(
            collective_id=1, has_side_effects=True, vmem_limit_bytes=VMEM_LIMIT
        ),
        name="middle_rows",
    )(parts, resid, gain, *groups)


def line_schedule(nt, chunks, pass_on, finish, onward, others):
    steps = []
    lead = 1
    for turn in range(chunks + lead + 1):
        if turn < chunks:
            steps.append(functools.partial(pass_on, turn))
        chunk = turn - lead
        if 0 <= chunk < chunks and finish is not None:
            steps.append(functools.partial(finish, chunk))
        chunk = turn - lead - 1
        if 0 <= chunk < chunks and onward is not None:
            steps = steps + [functools.partial(onward, chunk, distance) for distance in range(1, nt)]
    together(steps, others)


def norm_pull(value, gain, grad):
    scale = lax.rsqrt(jnp.mean(value * value, axis=-1, keepdims=True) + eps)
    scaled = grad * gain
    inner = jnp.mean(scaled * value, axis=-1, keepdims=True)
    return scale * (scaled - value * (inner * scale * scale)), grad * value * scale


def middle_back(nd, nt, parts, middle, cot, gain, groups):
    chunks = 4
    bits = nd.bit_length() - 1
    count = len(groups)
    block_rows, width = middle.shape
    size = block_rows // chunks
    per_group = 8

    def kernel(parts_ref, middle_ref, cot_ref, gain_ref, *refs):
        group_refs, refs = refs[:count], refs[count:]
        grad_ref, gain_grad, rows_all = refs[:3]
        totals, refs = refs[3 : 3 + count], refs[3 + count :]
        own, rising, falling, total, send, recv = refs[:6]
        gather_sems, refs = refs[6:8], refs[8:]
        me, zed = enter(nt, bits)
        pass_on, own_sum, reduce_end = line_reduce(nt, me, zed, chunks, parts_ref, rising, falling, send, recv)
        first, onward, gather_end = line_gather(nt, me, zed, chunks, own, rows_all, *gather_sems)
        flows = [
            scatter_steps(nd, me, zed, group_refs[n], totals[n], *refs[per_group * n : per_group * (n + 1)])
            for n in range(count)
        ]
        gain_grad[...] = jnp.zeros_like(gain_grad)

        def finish(chunk):
            own_sum(chunk, total)
            where = pl.ds(chunk * size, size)
            through, gained = norm_pull(middle_ref[where], gain_ref[...], total[...])
            value = cot_ref[where].astype(jnp.float32) + through
            gain_grad[...] += jnp.sum(gained, axis=0, keepdims=True)
            grad_ref[where] = value
            own[where] = value.astype(jnp.bfloat16)
            first(chunk)

        line_schedule(nt, chunks, pass_on, finish, onward, [step for flow in flows for step in flow])
        for chunk in range(chunks):
            reduce_end(chunk)
            gather_end(chunk)

    scratch = []
    for group in groups:
        scratch = scratch + scatter_scratch(nd, group.shape[0] // nd, group.shape[1])
    return pl.pallas_call(
        kernel,
        out_shape=[
            jax.ShapeDtypeStruct((block_rows, width), jnp.float32),
            jax.ShapeDtypeStruct((1, width), jnp.float32),
            jax.ShapeDtypeStruct((block_rows * nt, width), jnp.bfloat16),
        ]
        + [jax.ShapeDtypeStruct((group.shape[0] // nd, group.shape[1]), jnp.float32) for group in groups],
        in_specs=[ONCHIP] * 4 + [HBM] * count,
        out_specs=[ONCHIP, ONCHIP, HBM] + [ONCHIP] * count,
        scratch_shapes=[pltpu.VMEM((block_rows, width), jnp.bfloat16)]
        + line_reduce_scratch(nt, block_rows, width, chunks)
        + line_gather_semaphores(nt, chunks)
        + scratch,
        compiler_params=pltpu.CompilerParams(
            collective_id=2, has_side_effects=True, vmem_limit_bytes=VMEM_LIMIT
        ),
        name="middle_back",
    )(parts, middle, cot, gain, *groups)


def last_sums(nd, nt, parts, resid, before, gain, groups):
    chunks = 4
    bits = nd.bit_length() - 1
    count = len(groups)
    block_rows, width = resid.shape
    size = block_rows // chunks
    per_group = 8
    blocks = relative_blocks(nd)
    lane = width // len(blocks)

    def kernel(parts_ref, resid_ref, before_ref, gain_ref, *refs):
        group_refs, refs = refs[:count], refs[count:]
        grad_ref, gain_grad = refs[:2]
        totals, refs = refs[2 : 2 + count], refs[2 + count :]
        rising, falling, total, send, recv = refs[:5]
        refs = refs[5:]
        me, zed = enter(nt, bits)
        pass_on, own_sum, reduce_end = line_reduce(nt, me, zed, chunks, parts_ref, rising, falling, send, recv)
        flows = [
            scatter_steps(nd, me, zed, group_refs[n], totals[n], *refs[per_group * n : per_group * (n + 1)])
            for n in range(count)
        ]
        gain_grad[...] = jnp.zeros_like(gain_grad)

        def finish(chunk):
            own_sum(chunk, total)
            where = pl.ds(chunk * size, size)
            through, gained = norm_pull(resid_ref[where].astype(jnp.float32), gain_ref[...], total[...])
            gain_grad[...] += jnp.sum(gained, axis=0, keepdims=True)
            value = before_ref[where] + through
            if lane % 128:
                grad_ref[where] = value
                return
            for number, (other, part) in enumerate(blocks):
                start = (mixed_with(me, other, bits) * 2 + part) * lane
                grad_ref[where, pl.ds(pl.multiple_of(start, lane), lane)] = value[:, number * lane : (number + 1) * lane]

        line_schedule(nt, chunks, pass_on, finish, None, [step for flow in flows for step in flow])
        for chunk in range(chunks):
            reduce_end(chunk)

    scratch = []
    for group in groups:
        scratch = scratch + scatter_scratch(nd, group.shape[0] // nd, group.shape[1])
    results = pl.pallas_call(
        kernel,
        out_shape=[
            jax.ShapeDtypeStruct((block_rows, width), jnp.float32),
            jax.ShapeDtypeStruct((1, width), jnp.float32),
        ]
        + [jax.ShapeDtypeStruct((group.shape[0] // nd, group.shape[1]), jnp.float32) for group in groups],
        in_specs=[ONCHIP] * 4 + [HBM] * count,
        out_specs=[ONCHIP, ONCHIP] + [ONCHIP] * count,
        scratch_shapes=line_reduce_scratch(nt, block_rows, width, chunks) + scratch,
        compiler_params=pltpu.CompilerParams(
            collective_id=3, has_side_effects=True, vmem_limit_bytes=VMEM_LIMIT
        ),
        name="last_sums",
    )(parts, resid, before, gain, *groups)
    if lane % 128:
        results = (from_relative(results[0], 1, nd), *results[1:])
    return results


def per_device(
    nd,
    nt,
    residual,
    segments,
    mixgain,
    ffngain,
    gateproj,
    innerproj,
    stepproj,
    sharedproj,
    innerconv,
    sharedconv,
    stepbias,
    decaylog,
    skipgain,
    mixerout,
    queryproj,
    keyvalue,
    attnout,
    ffngate,
    upproj,
    downproj,
    cotangent,
):
    bfloat = jnp.bfloat16
    single = jnp.float32
    width = residual.shape[1]
    query_head_rows = queryproj.shape[1] // HEAD_SIZE
    zed = lax.axis_index("tensor")
    kv_head = zed * query_head_rows // (QUERY_HEADS // KEY_VALUE_HEADS)
    seq_count, length = segments.shape
    token_count = seq_count * length
    channels = innerproj.shape[1]
    state_columns = sharedproj.shape[1]
    heads = stepproj.shape[1]
    query_columns = queryproj.shape[1]
    ffn_columns = ffngate.shape[1]
    small_rows = sharedproj.shape[0]
    conv_rows = sharedconv.shape[0]
    taps = sharedconv.shape[1]

    gains = jnp.concatenate(
        [
            mixgain[:, None],
            ffngain[:, None],
            jnp.pad(sharedconv, ((0, small_rows - conv_rows), (0, 0))),
            jnp.zeros((small_rows, 128 - 2 - taps), bfloat),
        ],
        axis=1,
    )
    main_used = 2 * channels + query_columns + heads
    main_own = jnp.concatenate(
        [
            gateproj,
            innerproj,
            queryproj,
            stepproj,
            jnp.zeros((gateproj.shape[0], -main_used % 128), bfloat),
        ],
        axis=1,
    )
    resid_own = to_relative(residual, 1, nd)
    cot_own = to_relative(cotangent, 1, nd)
    resid_rows, _, common, main, out_w = first_gathers(
        nd,
        nt,
        resid_own,
        jnp.concatenate([sharedproj, keyvalue, gains], axis=1),
        [main_own, jnp.concatenate([mixerout, attnout], axis=1)],
    )
    grad_rows = lax.all_gather(after(cot_own, resid_rows), "tensor", axis=0, tiled=True)
    extra = common[:, state_columns + keyvalue.shape[1] :]
    gain_one = extra[:, 0].astype(single)
    gain_two = extra[:, 1].astype(single)
    conv_shared = from_relative(extra[:, 2 : 2 + taps], 0, nd)
    conv_shared = conv_shared.reshape(nd * nt, small_rows, taps)[:, :conv_rows].reshape(-1, taps)
    conv_shared = conv_shared.astype(single)
    key_at = state_columns + kv_head * HEAD_SIZE
    value_at = state_columns + (KEY_VALUE_HEADS + kv_head) * HEAD_SIZE
    side = jnp.concatenate(
        [
            common[:, :state_columns],
            lax.dynamic_slice_in_dim(common, key_at, HEAD_SIZE, 1),
            lax.dynamic_slice_in_dim(common, value_at, HEAD_SIZE, 1),
        ],
        axis=1,
    )

    resid_rows = resid_rows.astype(single)
    normed = (rmsnorm(resid_rows, gain_one)).astype(bfloat)
    main_raw = matrix_product(normed, main)
    side_raw = matrix_product(normed, side)
    gate_raw = main_raw[:, :channels]
    inner_raw = main_raw[:, channels : 2 * channels]
    query_raw = main_raw[:, 2 * channels : 2 * channels + query_columns]
    step_raw = main_raw[:, 2 * channels + query_columns : main_used]
    shared_raw = side_raw[:, :state_columns]
    key_raw = side_raw[:, state_columns : state_columns + HEAD_SIZE]
    value_raw = side_raw[:, state_columns + HEAD_SIZE :]

    def mamba_local(
        gate_in, inner_in, step_in, shared_in, conv_in, conv_sh, bias_in, decay_in, skip_in
    ):
        return mamba_mix(
            gate_in,
            inner_in,
            step_in,
            shared_in,
            conv_in,
            conv_sh,
            bias_in,
            decay_in,
            skip_in,
            segments,
            SPAN,
        )

    mamba_value, mamba_pull = jax.vjp(
        mamba_local,
        gate_raw,
        inner_raw,
        step_raw,
        shared_raw,
        innerconv.astype(single),
        conv_shared,
        stepbias.astype(single),
        decaylog.astype(single),
        skipgain.astype(single),
    )
    mamba_y = mamba_value.astype(bfloat)
    query_r = rotate(query_raw.reshape(seq_count, length, query_head_rows, HEAD_SIZE), 1.0).astype(
        bfloat
    )
    key_r = rotate(key_raw.reshape(seq_count, length, HEAD_SIZE), 1.0).astype(bfloat)
    value_b = value_raw.reshape(seq_count, length, HEAD_SIZE).astype(bfloat)
    order = jnp.arange(length)
    allowed = ((order[:, None] >= order[None, :]) & (segments[:, :, None] == segments[:, None, :]))[
        :, None
    ]
    scale = math.sqrt(HEAD_SIZE)
    scores = jnp.einsum("gthd,gsd->ghts", query_r, key_r, preferred_element_type=single) / scale
    masked = jnp.where(allowed, scores, -jnp.inf)
    peak = jnp.max(masked, axis=-1, keepdims=True)
    expo = jnp.exp(masked - peak)
    totals = jnp.sum(expo, axis=-1, keepdims=True)
    probs = (expo / totals).astype(bfloat)
    logsum = peak + jnp.log(totals)
    attn_o = (
        jnp.einsum("ghts,gsd->gthd", probs, value_b, preferred_element_type=single)
        .reshape(token_count, -1)
        .astype(bfloat)
    )
    mixed_in = jnp.concatenate([mamba_y, attn_o], axis=1)
    mix_part = contract_last(mixed_in, out_w).astype(bfloat)
    middle, rows_two, ffn_w = middle_rows(
        nd,
        nt,
        mix_part,
        resid_own,
        gain_two[None],
        [jnp.concatenate([ffngate, upproj, downproj], axis=1)],
    )
    gate_up_w = ffn_w[:, : 2 * ffn_columns]
    down_w = ffn_w[:, 2 * ffn_columns :]
    gate_up = matrix_product(rows_two, gate_up_w)
    gate = gate_up[:, :ffn_columns]
    upper = gate_up[:, ffn_columns:]
    sigma = jax.nn.sigmoid(gate)
    hidden = (gate * sigma * upper).astype(bfloat)
    grad_hidden = matrix_product(grad_rows, down_w)
    grad_gate = (grad_hidden * upper * sigma * (1.0 + gate * (1.0 - sigma))).astype(bfloat)
    grad_upper = (grad_hidden * gate * sigma).astype(bfloat)
    grad_gate_up = jnp.concatenate([grad_gate, grad_upper], axis=1)
    two_part = contract_last(grad_gate_up, gate_up_w).astype(bfloat)
    grad_middle, grad_gain_two, grad_mix_rows, down_g, gate_up_g = middle_back(
        nd,
        nt,
        two_part,
        middle,
        cot_own,
        gain_two[None],
        [
            contract_leading_axis(grad_rows, hidden).astype(bfloat),
            contract_leading_axis(rows_two, grad_gate_up).astype(bfloat),
        ],
    )
    ffn_part = after(contract_last(hidden, down_w).astype(bfloat), grad_mix_rows)
    ffn_out = lax.psum_scatter(ffn_part, "tensor", scatter_dimension=0, tiled=True)
    layer_out = from_relative(middle + ffn_out.astype(single), 1, nd)
    grad_mixed_in = matrix_product(grad_mix_rows, out_w)
    grad_mamba = grad_mixed_in[:, :channels]
    grad_attn_o = (
        grad_mixed_in[:, channels:]
        .astype(bfloat)
        .reshape(seq_count, length, query_head_rows, HEAD_SIZE)
    )
    probs_full = jnp.exp(jnp.where(allowed, scores - logsum, -jnp.inf))
    grad_probs = jnp.einsum("gthd,gsd->ghts", grad_attn_o, value_b, preferred_element_type=single)
    delta = jnp.sum(grad_probs * probs_full, axis=-1, keepdims=True)
    grad_scores = (probs_full * (grad_probs - delta)).astype(bfloat)
    grad_query_r = (
        jnp.einsum("ghts,gsd->gthd", grad_scores, key_r, preferred_element_type=single) / scale
    )
    grad_key_r = (
        jnp.einsum("ghts,gthd->gsd", grad_scores, query_r, preferred_element_type=single) / scale
    )
    grad_value = jnp.einsum("ghts,gthd->gsd", probs, grad_attn_o, preferred_element_type=single)
    grad_query = rotate(grad_query_r, -1.0).reshape(token_count, -1).astype(bfloat)
    grad_key = rotate(grad_key_r, -1.0).reshape(token_count, HEAD_SIZE).astype(bfloat)
    value_gradient = grad_value.reshape(token_count, HEAD_SIZE).astype(bfloat)
    (
        grad_gate_raw,
        grad_inner_raw,
        grad_step_raw,
        grad_shared_raw,
        grad_convi,
        grad_convs,
        grad_bias,
        grad_decay,
        grad_skip,
    ) = mamba_pull(grad_mamba)
    grad_main = jnp.concatenate(
        [
            grad_gate_raw.astype(bfloat),
            grad_inner_raw.astype(bfloat),
            grad_query,
            grad_step_raw.astype(bfloat),
            jnp.zeros((token_count, -main_used % 128), bfloat),
        ],
        axis=1,
    )
    grad_side = jnp.concatenate([grad_shared_raw.astype(bfloat), grad_key, value_gradient], axis=1)
    one_part = (contract_last(grad_main, main) + contract_last(grad_side, side)).astype(bfloat)
    grad_residual, grad_gain_one, main_g, side_g, out_g = last_sums(
        nd,
        nt,
        one_part,
        resid_own,
        grad_middle,
        gain_one[None],
        [
            contract_leading_axis(normed, grad_main).astype(bfloat),
            contract_leading_axis(normed, grad_side).astype(bfloat),
            contract_leading_axis(grad_mix_rows, mixed_in).astype(bfloat),
        ],
    )
    key_value_g = jnp.zeros((side_g.shape[0], keyvalue.shape[1]), single)
    key_value_g = lax.dynamic_update_slice_in_dim(
        key_value_g, side_g[:, state_columns : state_columns + HEAD_SIZE], kv_head * HEAD_SIZE, 1
    )
    key_value_g = lax.dynamic_update_slice_in_dim(
        key_value_g,
        side_g[:, state_columns + HEAD_SIZE :],
        (KEY_VALUE_HEADS + kv_head) * HEAD_SIZE,
        1,
    )
    common_g = jnp.concatenate([side_g[:, :state_columns], key_value_g], axis=1)
    common_g = line_sums(common_g.astype(bfloat), nt)

    everywhere = jnp.concatenate(
        [
            from_relative(grad_gain_one[0], 0, nd),
            from_relative(grad_gain_two[0], 0, nd),
            grad_convs.reshape(-1),
        ]
    )
    local = jnp.concatenate([grad_convi.reshape(-1), grad_bias, grad_decay, grad_skip])
    local = jnp.pad(local, (0, -local.shape[0] % 128))
    split = everywhere.shape[0]
    small = sum_small(jnp.concatenate([everywhere, local]).reshape(-1, 128), "dp", nd).reshape(-1)
    local = small[split:]
    everywhere = sum_small(small[:split].reshape(-1, 128), "tensor", nt).reshape(-1)
    place = lax.axis_index("dp") * nt + zed
    gain_one_g = lax.dynamic_slice_in_dim(everywhere, place * small_rows, small_rows, 0)
    gain_two_g = lax.dynamic_slice_in_dim(everywhere, width + place * small_rows, small_rows, 0)
    conv_g = lax.dynamic_slice_in_dim(
        everywhere[2 * width :].reshape(-1, taps), place * conv_rows, conv_rows, 0
    )
    counts = channels * innerconv.shape[1]
    return (
        layer_out,
        grad_residual,
        gain_one_g,
        gain_two_g,
        main_g[:, :channels],
        main_g[:, channels : 2 * channels],
        main_g[:, 2 * channels + query_columns : main_used],
        common_g[:, :state_columns],
        local[:counts].reshape(channels, -1),
        conv_g,
        local[counts : counts + heads],
        local[counts + heads : counts + 2 * heads],
        local[counts + 2 * heads : counts + 3 * heads],
        out_g[:, :channels],
        main_g[:, 2 * channels : 2 * channels + query_columns],
        common_g[:, state_columns:],
        out_g[:, channels:],
        gate_up_g[:, :ffn_columns],
        gate_up_g[:, ffn_columns:],
        down_g,
    )


def solution(mesh):
    return jax.shard_map(
        functools.partial(per_device, mesh.shape["dp"], mesh.shape["tensor"]),
        mesh=mesh,
        in_specs=(
            P(("dp", "tensor"), None),
            P("dp", None),
            P(("dp", "tensor")),
            P(("dp", "tensor")),
            P("dp", "tensor"),
            P("dp", "tensor"),
            P("dp", "tensor"),
            P(("dp", "tensor"), None),
            P("tensor", None),
            P(("dp", "tensor"), None),
            P("tensor"),
            P("tensor"),
            P("tensor"),
            P("dp", "tensor"),
            P("dp", "tensor"),
            P(("dp", "tensor"), None),
            P("dp", "tensor"),
            P("dp", "tensor"),
            P("dp", "tensor"),
            P("dp", "tensor"),
            P(("dp", "tensor"), None),
        ),
        out_specs=(
            P(("dp", "tensor"), None),
            P(("dp", "tensor"), None),
            P(("dp", "tensor")),
            P(("dp", "tensor")),
            P("dp", "tensor"),
            P("dp", "tensor"),
            P("dp", "tensor"),
            P(("dp", "tensor"), None),
            P("tensor", None),
            P(("dp", "tensor"), None),
            P("tensor"),
            P("tensor"),
            P("tensor"),
            P("dp", "tensor"),
            P("dp", "tensor"),
            P(("dp", "tensor"), None),
            P("dp", "tensor"),
            P("dp", "tensor"),
            P("dp", "tensor"),
            P("dp", "tensor"),
        ),
        check_vma=False,
    )
```

```python
import functools
import math

import jax
import jax.numpy as jnp
import numpy as np
from jax import lax
from jax.experimental import pallas as pl
from jax.experimental.pallas import tpu as pltpu
from jax.sharding import PartitionSpec as P

QUERY_HEADS = 8
KEY_VALUE_HEADS = 2
HEAD_SIZE = 128
SPAN = 256


eps = 1e-05
rope_base = 10000.0


def rmsnorm(value, gain):
    return value * lax.rsqrt(jnp.mean(value * value, axis=-1, keepdims=True) + eps) * gain


def matrix_product(left, right):
    return jnp.dot(left, right, preferred_element_type=jnp.float32)


def contract_leading_axis(left, right):
    return lax.dot_general(
        left, right, (((0,), (0,)), ((), ())), preferred_element_type=jnp.float32
    )


def contract_last(left, right):
    return lax.dot_general(
        left, right, (((1,), (1,)), ((), ())), preferred_element_type=jnp.float32
    )


def partner(value, axis, size, bit):
    return lax.ppermute(value, axis, [(i, i ^ (1 << bit)) for i in range(size)])


def bit_orders(size):
    high = list(range(size.bit_length() - 2, 0, -1))
    return high, high[:2][::-1] + high[2:]


def relative_blocks(size):
    both = []
    for half, order in enumerate(bit_orders(size)):
        chain = [0]
        for bit in order:
            chain = chain + [other ^ (1 << bit) for other in chain]
        both = both + [(other, half) for other in chain]
    return both + [(other ^ 1, half) for other, half in both]


def to_relative(value, axis, size):
    me = lax.axis_index("dp")
    width = value.shape[axis] // (2 * size)
    return jnp.concatenate(
        [
            lax.dynamic_slice_in_dim(value, ((me ^ other) * 2 + half) * width, width, axis)
            for other, half in relative_blocks(size)
        ],
        axis,
    )


def from_relative(value, axis, size):
    me = lax.axis_index("dp")
    width = value.shape[axis] // (2 * size)
    blocks = relative_blocks(size)
    place = jnp.asarray([blocks.index((other, half)) for other in range(size) for half in range(2)], jnp.int32)
    return jnp.concatenate(
        [
            lax.dynamic_slice_in_dim(value, place[(me ^ number) * 2 + half] * width, width, axis)
            for number in range(size)
            for half in range(2)
        ],
        axis,
    )


def sum_small(value, axis, size):
    for bit in range(size.bit_length() - 1):
        value = value + partner(value, axis, size, bit)
    return value


def line_sums(value, size):
    me = lax.axis_index("tensor")
    rows = value.shape[0] // size
    total = lax.dynamic_slice_in_dim(value, me * rows, rows, 0).astype(jnp.float32)
    for other in range(1, size):
        away = lax.dynamic_slice_in_dim(value, lax.rem(me + other, size) * rows, rows, 0)
        came = lax.ppermute(away, "tensor", [(i, (i + other) % size) for i in range(size)])
        total = total + came.astype(jnp.float32)
    return total


def after(value, *others):
    return lax.optimization_barrier((value,) + others)[0]


MESH = pl.DeviceIdType.MESH
VMEM_LIMIT = 56 * 1024 * 1024


def flip(value, bit):
    unit = 1 << bit
    return value + unit * (1 - 2 * ((value // unit) % 2))


def mixed_with(value, other, bits):
    for bit in range(bits):
        if (other >> bit) & 1:
            value = flip(value, bit)
    return value


def enter(nt, bits):
    me, zed = lax.axis_index("dp"), lax.axis_index("tensor")
    barrier = pltpu.get_barrier_semaphore()

    @pl.when(zed > 0)
    def _():
        pl.semaphore_signal(barrier, inc=1, device_id=(me, zed - 1), device_id_type=MESH)

    @pl.when(zed < nt - 1)
    def _():
        pl.semaphore_signal(barrier, inc=1, device_id=(me, zed + 1), device_id_type=MESH)

    for bit in range(bits):
        pl.semaphore_signal(barrier, inc=1, device_id=(flip(me, bit), zed), device_id_type=MESH)
    below = jnp.where(zed > 0, 1, 0)
    above = jnp.where(zed < nt - 1, 1, 0)
    pl.semaphore_wait(barrier, bits + below + above)
    return me, zed


def aligned(start, size):
    return pl.ds(pl.multiple_of(start, 16), size)


def together(*flows):
    flows = [list(flow) for flow in flows]
    order = sorted(
        ((place + 0.5) / len(flow), number, place)
        for number, flow in enumerate(flows)
        for place in range(len(flow))
    )
    for _, number, place in order:
        flows[number][place]()


def gather_steps(nd, me, zed, own, everything, send, recv, local):
    half = own.shape[0] // 2
    blocks = relative_blocks(nd)
    place = {block: number for number, block in enumerate(blocks)}

    def rows(block):
        return everything.at[pl.ds(place[block] * half, half)]

    def source(block):
        return own.at[pl.ds(block[1] * half, half)] if block[0] == 0 else rows(block)

    hops = []
    for part, order in enumerate(bit_orders(nd)):
        chain = [0]
        for bit in order:
            hops = hops + [((other, part), bit) for other in chain]
            chain = chain + [other ^ (1 << bit) for other in chain]
    hops = hops + [(block, 0) for block in blocks[:nd]]

    def copy(number):
        block, bit = hops[number]
        landed = (block[0] ^ (1 << bit), block[1])
        return pltpu.make_async_remote_copy(
            src_ref=source(block),
            dst_ref=rows(landed),
            send_sem=send.at[number],
            recv_sem=recv.at[place[landed]],
            device_id=(flip(me, bit), zed),
            device_id_type=MESH,
        )

    def arrival(block):
        return pltpu.make_async_remote_copy(
            src_ref=rows(block),
            dst_ref=rows(block),
            send_sem=send.at[0],
            recv_sem=recv.at[place[block]],
            device_id=(flip(me, 0), zed),
            device_id_type=MESH,
        )

    def begin():
        for number, (block, bit) in enumerate(hops):
            if block[0] == 0:
                copy(number).start()
        for part in range(2):
            pltpu.make_async_copy(source((0, part)), rows((0, part)), local.at[part]).start()

    def forward(block):
        def step():
            arrival(block).wait_recv()
            for number, (origin, bit) in enumerate(hops):
                if origin == block:
                    copy(number).start()

        return step

    def end():
        for block in blocks[nd:]:
            arrival(block).wait_recv()
        for number in range(len(hops)):
            copy(number).wait_send()
        for part in range(2):
            pltpu.make_async_copy(source((0, part)), rows((0, part)), local.at[part]).wait()

    first, second = blocks[1 : nd // 2], blocks[nd // 2 + 1 : nd]
    middle = [forward(block) for pair in zip(first, second) for block in pair]
    return [begin] + middle + [end]


def gather_hops(nd):
    return 2 * (nd // 2 - 1) + nd


def gather_semaphores(nd):
    return [
        pltpu.SemaphoreType.DMA((gather_hops(nd),)),
        pltpu.SemaphoreType.DMA((2 * nd,)),
        pltpu.SemaphoreType.DMA((2,)),
    ]


def each_rows(rows, body, unit=16):
    def step(number, carry):
        body(aligned(number * unit, unit))
        return carry

    lax.fori_loop(0, rows // unit, step, 0)


def scatter_steps(nd, me, zed, parts, total, mine, held, landed, core_send, core_recv, send, recv, local):
    half = total.shape[0] // 2
    chain_length = nd // 2

    def piece(ref, number):
        return ref.at[pl.ds(number * half, half)]

    rounds, slot = [], 0
    for part, order in enumerate(bit_orders(nd)):
        length, own_rounds = chain_length, []
        for bit in order[::-1]:
            length = length // 2
            own_rounds.append((bit, length, slot))
            slot = slot + length
        rounds.append(own_rounds)

    def core_copy(number):
        return pltpu.make_async_remote_copy(
            src_ref=piece(parts, nd + number),
            dst_ref=piece(held, number),
            send_sem=core_send.at[number],
            recv_sem=core_recv.at[number],
            device_id=(flip(me, 0), zed),
            device_id_type=MESH,
        )

    def hop(part, bit, number, where):
        return pltpu.make_async_remote_copy(
            src_ref=piece(held, number),
            dst_ref=piece(landed, where),
            send_sem=send.at[where],
            recv_sem=recv.at[where],
            device_id=(flip(me, bit), zed),
            device_id_type=MESH,
        )

    wanted = []
    for number in range(chain_length - 1, -1, -1):
        wanted = wanted + [number, chain_length + number]

    def load(number):
        return pltpu.make_async_copy(piece(parts, number), piece(mine, number), local.at[number])

    def begin():
        for number in wanted:
            core_copy(number).start()
        for number in wanted:
            load(number).start()

    def core_sum(number):
        part, spot = number // chain_length, number % chain_length

        def step():
            load(number).wait()
            core_copy(number).wait_recv()

            def body(rows):
                spot_rows = piece(held, number)
                value = spot_rows[rows].astype(jnp.float32) + piece(mine, number)[rows].astype(jnp.float32)
                spot_rows[rows] = value.astype(jnp.bfloat16)

            each_rows(half, body)
            if rounds[part]:
                bit, length, first = rounds[part][0]
                if spot >= length:
                    hop(part, bit, number, first + spot - length).start()

        return step

    def later_sum(part, turn, spot):
        bit, length, first = rounds[part][turn]
        number = part * chain_length + spot

        def step():
            hop(part, bit, number, first + spot).wait_recv()
            last = turn == len(rounds[part]) - 1

            def body(rows):
                value = piece(held, number)[rows].astype(jnp.float32) + piece(landed, first + spot)[rows].astype(
                    jnp.float32
                )
                if last:
                    piece(total, part)[rows] = value
                else:
                    piece(held, number)[rows] = value.astype(jnp.bfloat16)

            each_rows(half, body)
            if not last:
                next_bit, next_length, next_first = rounds[part][turn + 1]
                if spot >= next_length:
                    hop(part, next_bit, number, next_first + spot - next_length).start()

        return step

    steps = [begin] + [core_sum(number) for number in wanted]
    for turn in range(len(rounds[0])):
        length = rounds[0][turn][1]
        for spot in range(length - 1, -1, -1):
            for part in range(2):
                steps.append(later_sum(part, turn, spot))

    def end():
        for number in range(nd):
            core_copy(number).wait_send()
        for part in range(2):
            for bit, length, first in rounds[part]:
                for spot in range(length):
                    hop(part, bit, part * chain_length + length + spot, first + spot).wait_send()

    return steps + [end]


def scatter_scratch(nd, rows, columns):
    slots = nd - 2
    return [
        pltpu.VMEM((nd * rows // 2, columns), jnp.bfloat16),
        pltpu.VMEM((nd * rows // 2, columns), jnp.bfloat16),
        pltpu.VMEM((slots * rows // 2, columns), jnp.bfloat16),
        pltpu.SemaphoreType.DMA((nd,)),
        pltpu.SemaphoreType.DMA((nd,)),
        pltpu.SemaphoreType.DMA((slots,)),
        pltpu.SemaphoreType.DMA((slots,)),
        pltpu.SemaphoreType.DMA((nd,)),
    ]


def line_gather(nt, me, zed, chunks, own, everything, send, recv):
    size = own.shape[0] // chunks

    def own_rows(chunk):
        return own.at[pl.ds(chunk * size, size)]

    def rows(block, chunk):
        return everything.at[aligned(block * (size * chunks) + chunk * size, size)]

    def copy(source, block, chunk, side):
        return pltpu.make_async_remote_copy(
            src_ref=source,
            dst_ref=rows(block, chunk),
            send_sem=send.at[side, block, chunk],
            recv_sem=recv.at[block, chunk],
            device_id=(me, zed + 1 - 2 * side),
            device_id_type=MESH,
        )

    def keep(chunk):
        return pltpu.make_async_copy(own_rows(chunk), rows(zed, chunk), recv.at[zed, chunk])

    def first(chunk):
        for side, condition in ((0, zed < nt - 1), (1, zed > 0)):

            @pl.when(condition)
            def _(side=side):
                copy(own_rows(chunk), zed, chunk, side).start()

        keep(chunk).start()

    def onward(chunk, distance):
        for side, block in ((0, zed - distance), (1, zed + distance)):
            inside = (block >= 0) if side == 0 else (block < nt)
            open_end = (zed < nt - 1) if side == 0 else (zed > 0)

            @pl.when(inside)
            def _(block=block, side=side):
                copy(rows(block, chunk), block, chunk, side).wait_recv()

            @pl.when(jnp.logical_and(inside, open_end))
            def _(block=block, side=side):
                copy(rows(block, chunk), block, chunk, side).start()

    def end(chunk):
        keep(chunk).wait()
        for side, condition in ((0, zed < nt - 1), (1, zed > 0)):

            @pl.when(condition)
            def _(side=side):
                copy(own_rows(chunk), zed, chunk, side).wait_send()

            for distance in range(1, nt - 1):
                block = zed - distance if side == 0 else zed + distance
                inside = (block >= 0) if side == 0 else (block < nt)

                @pl.when(jnp.logical_and(inside, condition))
                def _(block=block, side=side):
                    copy(rows(block, chunk), block, chunk, side).wait_send()

    return first, onward, end


def line_gather_semaphores(nt, chunks):
    return [pltpu.SemaphoreType.DMA((2, nt, chunks)), pltpu.SemaphoreType.DMA((nt, chunks))]


def line_reduce(nt, me, zed, chunks, parts, rising, falling, send, recv):
    block_rows = parts.shape[0] // nt
    size = block_rows // chunks
    sides = ((0, rising), (1, falling))

    def rows(block, chunk):
        return aligned(block * block_rows + chunk * size, size)

    def copy(source, side, held, block, chunk):
        return pltpu.make_async_remote_copy(
            src_ref=source.at[rows(block, chunk)],
            dst_ref=held.at[rows(block, chunk)],
            send_sem=send.at[side, block, chunk],
            recv_sem=recv.at[side, block, chunk],
            device_id=(me, zed + 1 - 2 * side),
            device_id_type=MESH,
        )

    def role(side, turn):
        away = nt - 1 - turn
        if side == 0:
            return zed + away, zed + away < nt, zed == 0
        return zed - away, zed - away >= 0, zed == nt - 1

    def pass_on(chunk, turn):
        for side, held in sides:
            block, active, source = role(side, turn)

            @pl.when(jnp.logical_and(active, source))
            def _(side=side, held=held, block=block):
                copy(parts, side, held, block, chunk).start()

            @pl.when(jnp.logical_and(active, jnp.logical_not(source)))
            def _(side=side, held=held, block=block):
                copy(held, side, held, block, chunk).wait_recv()

                def body(inner):
                    where = aligned(block * block_rows + chunk * size + inner.start, inner.size)
                    value = parts[where].astype(jnp.float32) + held[where].astype(jnp.float32)
                    held[where] = value.astype(jnp.bfloat16)

                each_rows(size, body)
                copy(held, side, held, block, chunk).start()

    def own_sum(chunk, total):
        where = rows(zed, chunk)
        total[...] = parts[where].astype(jnp.float32)
        for side, held in sides:

            @pl.when(zed > 0 if side == 0 else zed < nt - 1)
            def _(side=side, held=held):
                copy(held, side, held, zed, chunk).wait_recv()
                total[...] += held[where].astype(jnp.float32)

    def end(chunk):
        for turn in range(nt - 1):
            for side, held in sides:
                block, active, source = role(side, turn)

                @pl.when(active)
                def _(side=side, held=held, block=block):
                    copy(held, side, held, block, chunk).wait_send()

    return pass_on, own_sum, end


def line_reduce_scratch(nt, block_rows, columns, chunks):
    return [
        pltpu.VMEM((nt * block_rows, columns), jnp.bfloat16),
        pltpu.VMEM((nt * block_rows, columns), jnp.bfloat16),
        pltpu.VMEM((block_rows // chunks, columns), jnp.float32),
        pltpu.SemaphoreType.DMA((2, nt, chunks)),
        pltpu.SemaphoreType.DMA((2, nt, chunks)),
    ]


HBM = pl.BlockSpec(memory_space=pl.ANY)
ONCHIP = pl.BlockSpec(memory_space=pltpu.VMEM)


def first_gathers(nd, nt, rows, grad, small, groups):
    chunks = 2
    bits = nd.bit_length() - 1
    count = len(groups)
    blocks = relative_blocks(nd)
    lane = rows.shape[1] // len(blocks)
    if lane % 128:
        rows, grad = to_relative(rows, 1, nd), to_relative(grad, 1, nd)

    def reorder(me, source, target):
        if lane % 128:
            target[...] = source[...]
            return
        for number, (other, part) in enumerate(blocks):
            start = (mixed_with(me, other, bits) * 2 + part) * lane
            target[:, number * lane : (number + 1) * lane] = source[:, pl.ds(pl.multiple_of(start, lane), lane)]

    def kernel(rows_in, grad_in, small_ref, *refs):
        group_refs, refs = refs[:count], refs[count:]
        rows_ref, grad_ref, rows_all, small_line, small_all = refs[:5]
        group_all, refs = refs[5 : 5 + count], refs[5 + count :]
        row_sems, small_sems, small_dp, refs = refs[:2], refs[2:4], refs[4:7], refs[7:]
        me, zed = enter(nt, bits)
        small_first, small_onward, small_end = line_gather(nt, me, zed, 1, small_ref, small_line, *small_sems)
        row_first, row_onward, row_end = line_gather(nt, me, zed, chunks, rows_ref, rows_all, *row_sems)
        flows = [
            gather_steps(nd, me, zed, group_refs[n], group_all[n], *refs[3 * n : 3 * n + 3]) for n in range(count)
        ]
        last = gather_steps(nd, me, zed, small_line, small_all, *small_dp)
        small_first(0)
        flows[0][0]()
        reorder(me, rows_in, rows_ref)
        for chunk in range(chunks):
            row_first(chunk)
        for flow in flows[1:]:
            flow[0]()
        for distance in range(1, nt):
            small_onward(0, distance)
        small_end(0)
        last[0]()
        along = [
            functools.partial(row_onward, chunk, distance) for distance in range(1, nt) for chunk in range(chunks)
        ]
        over = [step for flow in flows for step in flow[1:-1]]
        over = over + last[1:-1] + [flow[-1] for flow in flows] + [last[-1]]
        reorder(me, grad_in, grad_ref)
        together(along, over)
        for chunk in range(chunks):
            row_end(chunk)

    def widened(array, times):
        return jax.ShapeDtypeStruct((array.shape[0] * times, array.shape[1]), array.dtype)

    semaphores = line_gather_semaphores(nt, chunks) + line_gather_semaphores(nt, 1) + gather_semaphores(nd)
    return pl.pallas_call(
        kernel,
        out_shape=[widened(rows, 1), widened(grad, 1), widened(rows, nt), widened(small, nt), widened(small, nt * nd)]
        + [widened(group, nd) for group in groups],
        in_specs=[ONCHIP] * 2 + [HBM] * (1 + count),
        out_specs=[ONCHIP] * 2 + [HBM] * (3 + count),
        scratch_shapes=semaphores + gather_semaphores(nd) * count,
        compiler_params=pltpu.CompilerParams(
            collective_id=0, has_side_effects=True, vmem_limit_bytes=VMEM_LIMIT
        ),
        name="first_gathers",
    )(rows, grad, small, *groups)


def middle_rows(nd, nt, parts, resid, gain, groups):
    chunks = 4
    bits = nd.bit_length() - 1
    count = len(groups)
    block_rows, width = resid.shape
    size = block_rows // chunks

    def kernel(parts_ref, resid_ref, gain_ref, *refs):
        group_refs, refs = refs[:count], refs[count:]
        middle_ref, rows_all = refs[:2]
        group_all, refs = refs[2 : 2 + count], refs[2 + count :]
        own, rising, falling, total, send, recv = refs[:6]
        gather_sems, refs = refs[6:8], refs[8:]
        me, zed = enter(nt, bits)
        pass_on, own_sum, reduce_end = line_reduce(nt, me, zed, chunks, parts_ref, rising, falling, send, recv)
        first, onward, gather_end = line_gather(nt, me, zed, chunks, own, rows_all, *gather_sems)
        flows = [
            gather_steps(nd, me, zed, group_refs[n], group_all[n], *refs[3 * n : 3 * n + 3]) for n in range(count)
        ]

        def finish(chunk):
            own_sum(chunk, total)
            where = pl.ds(chunk * size, size)
            value = resid_ref[where].astype(jnp.float32) + total[...]
            middle_ref[where] = value
            scale = lax.rsqrt(jnp.mean(value * value, axis=-1, keepdims=True) + eps)
            own[where] = (value * scale * gain_ref[...]).astype(jnp.bfloat16)
            first(chunk)

        line_schedule(nt, chunks, pass_on, finish, onward, [step for flow in flows for step in flow])
        for chunk in range(chunks):
            reduce_end(chunk)
            gather_end(chunk)

    return pl.pallas_call(
        kernel,
        out_shape=[
            jax.ShapeDtypeStruct((block_rows, width), jnp.float32),
            jax.ShapeDtypeStruct((block_rows * nt, width), jnp.bfloat16),
        ]
        + [jax.ShapeDtypeStruct((group.shape[0] * nd, group.shape[1]), group.dtype) for group in groups],
        in_specs=[ONCHIP] * 3 + [HBM] * count,
        out_specs=[ONCHIP] + [HBM] * (1 + count),
        scratch_shapes=[pltpu.VMEM((block_rows, width), jnp.bfloat16)]
        + line_reduce_scratch(nt, block_rows, width, chunks)
        + line_gather_semaphores(nt, chunks)
        + gather_semaphores(nd) * count,
        compiler_params=pltpu.CompilerParams(
            collective_id=1, has_side_effects=True, vmem_limit_bytes=VMEM_LIMIT
        ),
        name="middle_rows",
    )(parts, resid, gain, *groups)


def line_schedule(nt, chunks, pass_on, finish, onward, others):
    steps = []

    def add(function, chunk, *rest):
        if function is not None and 0 <= chunk < chunks:
            steps.append(functools.partial(function, chunk, *rest))

    for chunk in range(chunks + 2):
        add(pass_on, chunk, 0)
        add(finish, chunk - 1)
        add(onward, chunk - 2, nt - 1)
        for turn in range(1, nt - 1):
            add(pass_on, chunk, turn)
            add(onward, chunk - 1, turn)
    together(steps, others)


def absolute_lanes(me, bits, blocks, source, target):
    lane = source.shape[1] // len(blocks)
    for number, (other, part) in enumerate(blocks):
        start = (mixed_with(me, other, bits) * 2 + part) * lane
        target[:, pl.ds(pl.multiple_of(start, lane), lane)] = source[:, number * lane : (number + 1) * lane]


def norm_pull(value, gain, grad):
    scale = lax.rsqrt(jnp.mean(value * value, axis=-1, keepdims=True) + eps)
    scaled = grad * gain
    inner = jnp.mean(scaled * value, axis=-1, keepdims=True)
    return scale * (scaled - value * (inner * scale * scale)), grad * value * scale


def middle_back(nd, nt, parts, middle, cot, gain, groups):
    chunks = 4
    bits = nd.bit_length() - 1
    count = len(groups)
    block_rows, width = middle.shape
    size = block_rows // chunks
    per_group = 8

    def kernel(parts_ref, middle_ref, cot_ref, gain_ref, *refs):
        group_refs, refs = refs[:count], refs[count:]
        grad_ref, gain_grad, rows_all = refs[:3]
        totals, refs = refs[3 : 3 + count], refs[3 + count :]
        own, rising, falling, total, send, recv = refs[:6]
        gather_sems, refs = refs[6:8], refs[8:]
        me, zed = enter(nt, bits)
        pass_on, own_sum, reduce_end = line_reduce(nt, me, zed, chunks, parts_ref, rising, falling, send, recv)
        first, onward, gather_end = line_gather(nt, me, zed, chunks, own, rows_all, *gather_sems)
        flows = [
            scatter_steps(nd, me, zed, group_refs[n], totals[n], *refs[per_group * n : per_group * (n + 1)])
            for n in range(count)
        ]
        gain_grad[...] = jnp.zeros_like(gain_grad)

        def finish(chunk):
            own_sum(chunk, total)
            where = pl.ds(chunk * size, size)
            through, gained = norm_pull(middle_ref[where], gain_ref[...], total[...])
            value = cot_ref[where].astype(jnp.float32) + through
            gain_grad[...] += jnp.sum(gained, axis=0, keepdims=True)
            grad_ref[where] = value
            own[where] = value.astype(jnp.bfloat16)
            first(chunk)

        line_schedule(nt, chunks, pass_on, finish, onward, [step for flow in flows for step in flow])
        for chunk in range(chunks):
            reduce_end(chunk)
            gather_end(chunk)

    scratch = []
    for group in groups:
        scratch = scratch + scatter_scratch(nd, group.shape[0] // nd, group.shape[1])
    return pl.pallas_call(
        kernel,
        out_shape=[
            jax.ShapeDtypeStruct((block_rows, width), jnp.float32),
            jax.ShapeDtypeStruct((1, width), jnp.float32),
            jax.ShapeDtypeStruct((block_rows * nt, width), jnp.bfloat16),
        ]
        + [jax.ShapeDtypeStruct((group.shape[0] // nd, group.shape[1]), jnp.float32) for group in groups],
        in_specs=[ONCHIP] * 4 + [HBM] * count,
        out_specs=[ONCHIP, ONCHIP, HBM] + [ONCHIP] * count,
        scratch_shapes=[pltpu.VMEM((block_rows, width), jnp.bfloat16)]
        + line_reduce_scratch(nt, block_rows, width, chunks)
        + line_gather_semaphores(nt, chunks)
        + scratch,
        compiler_params=pltpu.CompilerParams(
            collective_id=2, has_side_effects=True, vmem_limit_bytes=VMEM_LIMIT
        ),
        name="middle_back",
    )(parts, middle, cot, gain, *groups)


def last_sums(nd, nt, parts, resid, before, gain, groups):
    chunks = 4
    bits = nd.bit_length() - 1
    count = len(groups)
    block_rows, width = resid.shape
    size = block_rows // chunks
    per_group = 8
    blocks = relative_blocks(nd)
    lane = width // len(blocks)

    def kernel(parts_ref, resid_ref, before_ref, gain_ref, *refs):
        group_refs, refs = refs[:count], refs[count:]
        grad_ref, gain_grad = refs[:2]
        totals, refs = refs[2 : 2 + count], refs[2 + count :]
        rising, falling, total, send, recv = refs[:5]
        refs = refs[5:]
        me, zed = enter(nt, bits)
        pass_on, own_sum, reduce_end = line_reduce(nt, me, zed, chunks, parts_ref, rising, falling, send, recv)
        flows = [
            scatter_steps(nd, me, zed, group_refs[n], totals[n], *refs[per_group * n : per_group * (n + 1)])
            for n in range(count)
        ]
        gain_grad[...] = jnp.zeros_like(gain_grad)

        def finish(chunk):
            own_sum(chunk, total)
            where = pl.ds(chunk * size, size)
            through, gained = norm_pull(resid_ref[where].astype(jnp.float32), gain_ref[...], total[...])
            gain_grad[...] += jnp.sum(gained, axis=0, keepdims=True)
            value = before_ref[where] + through
            if lane % 128:
                grad_ref[where] = value
                return
            for number, (other, part) in enumerate(blocks):
                start = (mixed_with(me, other, bits) * 2 + part) * lane
                grad_ref[where, pl.ds(pl.multiple_of(start, lane), lane)] = value[:, number * lane : (number + 1) * lane]

        line_schedule(nt, chunks, pass_on, finish, None, [step for flow in flows for step in flow])
        for chunk in range(chunks):
            reduce_end(chunk)

    scratch = []
    for group in groups:
        scratch = scratch + scatter_scratch(nd, group.shape[0] // nd, group.shape[1])
    results = pl.pallas_call(
        kernel,
        out_shape=[
            jax.ShapeDtypeStruct((block_rows, width), jnp.float32),
            jax.ShapeDtypeStruct((1, width), jnp.float32),
        ]
        + [jax.ShapeDtypeStruct((group.shape[0] // nd, group.shape[1]), jnp.float32) for group in groups],
        in_specs=[ONCHIP] * 4 + [HBM] * count,
        out_specs=[ONCHIP, ONCHIP] + [ONCHIP] * count,
        scratch_shapes=line_reduce_scratch(nt, block_rows, width, chunks) + scratch,
        compiler_params=pltpu.CompilerParams(
            collective_id=3, has_side_effects=True, vmem_limit_bytes=VMEM_LIMIT
        ),
        name="last_sums",
    )(parts, resid, before, gain, *groups)
    if lane % 128:
        results = (from_relative(results[0], 1, nd), *results[1:])
    return results


def silu_slope(value, sig):
    return sig * (1.0 + value * (1.0 - sig))


def split_dot(value, constant, dims, terms):
    total = None
    for _ in range(terms):
        piece = value.astype(jnp.bfloat16)
        value = value - piece.astype(jnp.float32)
        part = lax.dot_general(*((piece, constant) if dims[0] else (constant, piece)), dims[1], preferred_element_type=jnp.float32)
        total = part if total is None else total + part
    return total


PLAIN = (((1,), (0,)), ((), ()))
LAST = (((1,), (1,)), ((), ()))
FIRST = (((0,), (0,)), ((), ()))


def product(left, right, dims=PLAIN):
    return lax.dot_general(left, right, dims, preferred_element_type=jnp.float32)


def turned(value, cosine, sine):
    return value * cosine + pltpu.roll(value, value.shape[-1] // 2, 1) * sine


class Sizes:
    def __init__(self, channels, state_columns, query_columns, heads, length):
        self.channels, self.states = channels, state_columns // 2
        self.query, self.heads, self.length = query_columns, heads, length
        self.span = SPAN
        self.count = length // SPAN
        self.wide = channels + state_columns
        self.head_width = channels // heads
        self.step_at = 2 * channels + query_columns
        self.main = self.step_at + heads + (-(self.step_at + heads)) % 128
        self.step_lanes = self.main - self.step_at
        self.side = state_columns + 2 * HEAD_SIZE
        self.window = min(length, 3 * SPAN)


def spread_heads(size):
    table = np.zeros((size.step_lanes, size.channels), np.float32)
    for head in range(size.heads):
        table[head, head * size.head_width : (head + 1) * size.head_width] = 1.0
    return table.astype(jnp.bfloat16)


def turn_tables(length):
    half = HEAD_SIZE // 2
    angle = np.arange(length, dtype=np.float64)[:, None] * rope_base ** (-np.arange(half) / half)[None]
    cosine, sine = np.cos(angle), np.sin(angle)
    return (
        np.concatenate([cosine, cosine], 1).astype(np.float32),
        np.concatenate([-sine, sine], 1).astype(np.float32),
    )


def token_flags(segments, taps):
    seg = segments[0]
    length = seg.shape[0]
    columns = [jnp.ones((length,), bool)]
    ahead = []
    for lag in range(1, taps):
        columns.append(jnp.concatenate([jnp.zeros((lag,), bool), seg[lag:] == seg[:-lag]]))
        ahead.append(jnp.concatenate([seg[lag:] == seg[:-lag], jnp.zeros((lag,), bool)]))
    ends = seg.reshape(-1, SPAN)[:, -1]
    before = jnp.concatenate([jnp.full((1,), -1, seg.dtype), ends[:-1]])
    columns.append(seg == jnp.repeat(before, SPAN))
    columns.append(seg == jnp.repeat(ends, SPAN))
    columns = columns + ahead
    return jnp.pad(jnp.stack(columns, 1).astype(jnp.float32), ((0, 0), (0, 16 - len(columns))))


def chunk_values(size, taps, main_ref, wide_ref, flags, spread, taps_ref, heads_ref, segc, segr):
    span = size.span
    pre = wide_ref[pl.ds(8, span), :] * taps_ref[0:1, :]
    for lag in range(1, taps):
        pre = pre + wide_ref[pl.ds(8 - lag, span), :] * (flags[:, lag : lag + 1] * taps_ref[lag : lag + 1, :])
    sig = jax.nn.sigmoid(pre)
    act = pre * sig
    inner = act[:, : size.channels]
    bmat = act[:, size.channels : size.channels + size.states].astype(jnp.bfloat16)
    cmat = act[:, size.channels + size.states :].astype(jnp.bfloat16)
    step_in = main_ref[:, size.step_at :] + heads_ref[0:1, :]
    step = jnp.maximum(step_in, 0.0) + jnp.log1p(jnp.exp(-jnp.abs(step_in)))
    logdec = -step * heads_ref[1:2, :]
    rows = lax.broadcasted_iota(jnp.int32, (span, span), 0)
    columns = lax.broadcasted_iota(jnp.int32, (span, span), 1)
    later = jnp.where(rows >= columns, 1.0, 0.0).astype(jnp.bfloat16)
    cumul = split_dot(logdec, later, (False, PLAIN), 3)
    inside = jnp.logical_and(rows >= columns, segc == segr)
    ending = cumul[span - 1 : span, :]
    reach = jnp.exp(cumul) * flags[:, 4:5]
    tail = jnp.exp(ending - cumul) * flags[:, 5:6]
    step_wide = split_dot(step, spread, (True, PLAIN), 2)
    scaled = inner * step_wide
    return dict(
        pre=pre, sig=sig, inner=inner, bmat=bmat, cmat=cmat, step_in=step_in, step=step, logdec=logdec, later=later,
        cumul=cumul, turned=jnp.transpose(cumul), inside=inside, step_wide=step_wide, scaled=scaled,
        scaled_b=scaled.astype(jnp.bfloat16), meeting=product(cmat, bmat, LAST),
        reach_wide=split_dot(reach, spread, (True, PLAIN), 2), tail_wide=split_dot(tail, spread, (True, PLAIN), 2),
        skip_wide=split_dot(jnp.broadcast_to(heads_ref[2:3, :], (8, size.step_lanes)), spread, (True, PLAIN), 2)[0:1],
    )


def decay_of(values, head):
    spread = values["cumul"][:, head : head + 1] - values["turned"][head : head + 1, :]
    return jnp.exp(jnp.where(values["inside"], spread, -1e30))


def softmax_of(size, query, keys, chunk, start, segc, seg_all):
    scores = product(query, keys, LAST) * (1.0 / math.sqrt(HEAD_SIZE))
    rows = lax.broadcasted_iota(jnp.int32, scores.shape, 0) + chunk * size.span
    columns = lax.broadcasted_iota(jnp.int32, scores.shape, 1) + start
    allowed = jnp.logical_and(rows >= columns, segc == seg_all)
    masked = jnp.where(allowed, scores, -1e30)
    expo = jnp.exp(masked - jnp.max(masked, axis=-1, keepdims=True))
    return expo / jnp.sum(expo, axis=-1, keepdims=True)


def mixers_forward(size, taps, main_raw, side_raw, segments, flags, tap_rows, head_rows):
    span = size.span
    per_head = size.head_width

    def kernel(
        main_ref, side_ref, segc_ref, segr_ref, flags_ref, taps_ref, heads_ref, cos_ref, sin_ref, spread_ref,
        mixed_ref, y_ref, state_ref, keys_ref, values_ref, wide, state,
    ):
        chunk = pl.program_id(0)

        @pl.when(chunk == 0)
        def _():
            wide[0:8, :] = jnp.zeros((8, size.wide), jnp.float32)
            state[...] = jnp.zeros_like(state)
            keys_ref[...] = jnp.zeros_like(keys_ref)
            values_ref[...] = jnp.zeros_like(values_ref)

        wide[pl.ds(8, span), : size.channels] = main_ref[:, size.channels : 2 * size.channels]
        wide[pl.ds(8, span), size.channels :] = side_ref[:, : 2 * size.states]
        flags, spread, segc = flags_ref[...], spread_ref[...], segc_ref[...]
        segr = segr_ref[:, pl.ds(pl.multiple_of(chunk * span, span), span)]
        val = chunk_values(size, taps, main_ref, wide, flags, spread, taps_ref, heads_ref, segc, segr)
        wide[0:8, :] = wide[pl.ds(span, 8), :]
        held = state[...]
        held_b = held.astype(jnp.bfloat16)
        state_ref[...] = held
        across = val["reach_wide"] * product(val["cmat"], held_b)
        lane = lax.broadcasted_iota(jnp.int32, (span, 2 * per_head), 1)
        for pair in range(size.heads // 2):
            where = slice(pair * 2 * per_head, (pair + 1) * 2 * per_head)
            both = []
            for head in (2 * pair, 2 * pair + 1):
                weights = (val["meeting"] * decay_of(val, head)).astype(jnp.bfloat16)
                both.append(product(weights, val["scaled_b"][:, where]))
            result = jnp.where(lane < per_head, both[0], both[1])
            result = result + across[:, where] + val["skip_wide"][:, where] * val["inner"][:, where]
            y_ref[:, where] = result
            gate = main_ref[:, where]
            mixed_ref[:, where] = (result * (gate * jax.nn.sigmoid(gate))).astype(jnp.bfloat16)
        keep = jnp.broadcast_to(val["reach_wide"][span - 1 : span, :], (1, size.channels))
        state[...] = keep * held + product(
            val["bmat"], (val["tail_wide"] * val["scaled"]).astype(jnp.bfloat16), FIRST
        )

        cosine, sine = cos_ref[...], sin_ref[...]
        own = pl.ds(pl.multiple_of(chunk * span, span), span)
        key_at = 2 * size.states
        keys_ref[own, :] = turned(side_ref[:, key_at : key_at + HEAD_SIZE], cosine, sine).astype(jnp.bfloat16)
        values_ref[own, :] = side_ref[:, key_at + HEAD_SIZE :].astype(jnp.bfloat16)
        start = pl.multiple_of(jnp.maximum(chunk + 1 - size.window // span, 0) * span, span)
        seen = pl.ds(start, size.window)
        for head in range(size.query // HEAD_SIZE):
            at = 2 * size.channels + head * HEAD_SIZE
            query = turned(main_ref[:, at : at + HEAD_SIZE], cosine, sine).astype(jnp.bfloat16)
            probs = softmax_of(size, query, keys_ref[seen, :], chunk, start, segc, segr_ref[:, seen])
            result = product(probs.astype(jnp.bfloat16), values_ref[seen, :])
            at = size.channels + head * HEAD_SIZE
            mixed_ref[:, at : at + HEAD_SIZE] = result.astype(jnp.bfloat16)

    def rows(columns):
        return pl.BlockSpec((span, columns), lambda i: (i, 0))

    def whole(array):
        return pl.BlockSpec(array.shape, lambda i: (0, 0))

    cosine, sine = turn_tables(size.length)
    spread = spread_heads(size)
    tokens = size.length
    return pl.pallas_call(
        kernel,
        grid=(size.count,),
        in_specs=[
            rows(size.main), rows(size.side), rows(1), whole(segments), rows(16), whole(tap_rows), whole(head_rows),
            rows(HEAD_SIZE), rows(HEAD_SIZE), whole(spread),
        ],
        out_specs=[
            rows(size.channels + size.query), rows(size.channels),
            pl.BlockSpec((size.states, size.channels), lambda i: (i, 0)),
            pl.BlockSpec((tokens, HEAD_SIZE), lambda i: (0, 0)), pl.BlockSpec((tokens, HEAD_SIZE), lambda i: (0, 0)),
        ],
        out_shape=[
            jax.ShapeDtypeStruct((tokens, size.channels + size.query), jnp.bfloat16),
            jax.ShapeDtypeStruct((tokens, size.channels), jnp.float32),
            jax.ShapeDtypeStruct((size.count * size.states, size.channels), jnp.float32),
            jax.ShapeDtypeStruct((tokens, HEAD_SIZE), jnp.bfloat16),
            jax.ShapeDtypeStruct((tokens, HEAD_SIZE), jnp.bfloat16),
        ],
        scratch_shapes=[
            pltpu.VMEM((span + 8, size.wide), jnp.float32),
            pltpu.VMEM((size.states, size.channels), jnp.float32),
        ],
        compiler_params=pltpu.CompilerParams(
            dimension_semantics=("arbitrary",), vmem_limit_bytes=VMEM_LIMIT
        ),
        name="mixers_forward",
    )(main_raw, side_raw, segments.reshape(tokens, 1), segments, flags, tap_rows, head_rows,
      jnp.asarray(cosine), jnp.asarray(sine), jnp.asarray(spread))


def mixers_backward(
    size, taps, grad_mixed, main_raw, side_raw, segments, flags, tap_rows, head_rows, y_value, states, keys, values
):
    span = size.span
    per_head = size.head_width
    count = size.count

    def kernel(
        grad_ref, main_ref, side_ref, before_ref, side_before_ref, segc_ref, segr_ref, flags_ref, taps_ref, heads_ref,
        cos_ref, sin_ref, spread_ref, y_ref, state_ref, keys_ref, values_ref,
        grad_main, grad_side, tap_sums, head_sums, wide, back, grad_state, grad_keys, grad_values,
    ):
        turn = pl.program_id(0)
        chunk = count - 1 - turn

        @pl.when(turn == 0)
        def _():
            back[pl.ds(span, 8), :] = jnp.zeros((8, size.wide), jnp.float32)
            grad_state[...] = jnp.zeros_like(grad_state)
            grad_keys[...] = jnp.zeros_like(grad_keys)
            grad_values[...] = jnp.zeros_like(grad_values)
            tap_sums[...] = jnp.zeros_like(tap_sums)
            head_sums[...] = jnp.zeros_like(head_sums)

        wide[0:8, : size.channels] = before_ref[...]
        wide[0:8, size.channels :] = side_before_ref[...]
        wide[pl.ds(8, span), : size.channels] = main_ref[:, size.channels : 2 * size.channels]
        wide[pl.ds(8, span), size.channels :] = side_ref[:, : 2 * size.states]
        flags, spread, segc = flags_ref[...], spread_ref[...], segc_ref[...]
        segr = segr_ref[:, pl.ds(pl.multiple_of(chunk * span, span), span)]
        val = chunk_values(size, taps, main_ref, wide, flags, spread, taps_ref, heads_ref, segc, segr)
        inner, scaled = val["inner"], val["scaled"]

        gate = main_ref[:, : size.channels]
        gate_sig = jax.nn.sigmoid(gate)
        grad = grad_ref[:, : size.channels]
        grad_main[:, : size.channels] = (grad * y_ref[...] * silu_slope(gate, gate_sig)).astype(jnp.bfloat16)
        grad_y = grad * (gate * gate_sig)
        grad_y_b = grad_y.astype(jnp.bfloat16)
        tap_sums[4:5, : size.channels] += jnp.sum(grad_y * inner, axis=0, keepdims=True)

        lane = lax.broadcasted_iota(jnp.int32, (span, 2 * per_head), 1)
        head_lane = lax.broadcasted_iota(jnp.int32, (span, size.step_lanes), 1)
        head_row = lax.broadcasted_iota(jnp.int32, (size.step_lanes, span), 0)
        grad_meeting = jnp.zeros((span, span), jnp.float32)
        by_row = jnp.zeros((span, size.step_lanes), jnp.float32)
        by_column = jnp.zeros((size.step_lanes, span), jnp.float32)
        pieces = []
        for pair in range(size.heads // 2):
            where = slice(pair * 2 * per_head, (pair + 1) * 2 * per_head)
            both = []
            for side in range(2):
                head = 2 * pair + side
                decay = decay_of(val, head)
                weights = val["meeting"] * decay
                mine = (lane < per_head) if side == 0 else (lane >= per_head)
                grad_own = jnp.where(mine, grad_y_b[:, where], jnp.zeros((), jnp.bfloat16))
                grad_weights = product(grad_own, val["scaled_b"][:, where], LAST)
                both.append(product(weights.astype(jnp.bfloat16), grad_y_b[:, where], FIRST))
                grad_meeting = grad_meeting + grad_weights * decay
                moved = grad_weights * weights
                by_row = jnp.where(head_lane == head, jnp.sum(moved, axis=1, keepdims=True), by_row)
                by_column = jnp.where(head_row == head, jnp.sum(moved, axis=0, keepdims=True), by_column)
            pieces.append(jnp.where(lane < per_head, both[0], both[1]))
        grad_scaled = jnp.concatenate(pieces, axis=1)
        grad_cumul = by_row - jnp.transpose(by_column)

        held = state_ref[...]
        held_b = held.astype(jnp.bfloat16)
        grad_held = grad_state[...]
        grad_held_b = grad_held.astype(jnp.bfloat16)
        grad_meeting_b = grad_meeting.astype(jnp.bfloat16)
        reached = val["reach_wide"] * grad_y
        reached_b = reached.astype(jnp.bfloat16)
        grad_cumul = grad_cumul + split_dot(reached * product(val["cmat"], held_b), spread, (True, LAST), 2)
        grad_c = product(reached_b, held_b, LAST) + product(grad_meeting_b, val["bmat"])
        from_state = val["tail_wide"] * product(val["bmat"], grad_held_b)
        grad_b = product(grad_meeting_b, val["cmat"], FIRST) + product(
            (val["tail_wide"] * scaled).astype(jnp.bfloat16), grad_held_b, LAST
        )
        grad_scaled = grad_scaled + from_state
        ended = split_dot(scaled * from_state, spread, (True, LAST), 2)
        keep = val["reach_wide"][span - 1 : span, :]
        kept = jnp.sum(grad_held * held, axis=0, keepdims=True) * keep
        kept = split_dot(jnp.broadcast_to(kept, (8, size.channels)), spread, (True, LAST), 2)[0:1]
        at_end = jnp.sum(ended, axis=0, keepdims=True) + kept
        grad_logdec = split_dot(grad_cumul - ended, val["later"], (False, FIRST), 3) + at_end
        grad_state[...] = keep * grad_held + product(val["cmat"], reached_b, FIRST)

        grad_inner = grad_scaled * val["step_wide"] + grad_y * val["skip_wide"]
        grad_step = split_dot(grad_scaled * inner, spread, (True, LAST), 2) - grad_logdec * heads_ref[1:2, :]
        grad_step_raw = grad_step * jax.nn.sigmoid(val["step_in"])
        head_sums[0:1, :] += jnp.sum(grad_step_raw, axis=0, keepdims=True)
        head_sums[1:2, :] += jnp.sum(grad_logdec * val["logdec"], axis=0, keepdims=True)
        grad_main[:, size.step_at :] = grad_step_raw.astype(jnp.bfloat16)

        slope = silu_slope(val["pre"], val["sig"])
        grad_pre = jnp.concatenate([grad_inner, grad_b, grad_c], axis=1) * slope
        back[pl.ds(0, span), :] = grad_pre
        raw = grad_pre * taps_ref[0:1, :]
        tap_sums[0:1, :] += jnp.sum(grad_pre * wide[pl.ds(8, span), :], axis=0, keepdims=True)
        for lag in range(1, taps):
            tap_sums[lag : lag + 1, :] += jnp.sum(
                grad_pre * (wide[pl.ds(8 - lag, span), :] * flags[:, lag : lag + 1]), axis=0, keepdims=True
            )
            raw = raw + back[pl.ds(lag, span), :] * (flags[:, 5 + lag : 6 + lag] * taps_ref[lag : lag + 1, :])
        back[pl.ds(span, 8), :] = back[0:8, :]
        grad_main[:, size.channels : 2 * size.channels] = raw[:, : size.channels].astype(jnp.bfloat16)
        grad_side[:, : 2 * size.states] = raw[:, size.channels :].astype(jnp.bfloat16)

        cosine, sine = cos_ref[...], sin_ref[...]
        start = pl.multiple_of(jnp.maximum(chunk + 1 - size.window // span, 0) * span, span)
        seen = pl.ds(start, size.window)
        seen_keys, seen_values = keys_ref[seen, :], values_ref[seen, :]
        scale = 1.0 / math.sqrt(HEAD_SIZE)
        for head in range(size.query // HEAD_SIZE):
            at = 2 * size.channels + head * HEAD_SIZE
            query = turned(main_ref[:, at : at + HEAD_SIZE], cosine, sine).astype(jnp.bfloat16)
            probs = softmax_of(size, query, seen_keys, chunk, start, segc, segr_ref[:, seen])
            out_at = size.channels + head * HEAD_SIZE
            grad_out = grad_ref[:, out_at : out_at + HEAD_SIZE].astype(jnp.bfloat16)
            grad_probs = product(grad_out, seen_values, LAST)
            delta = jnp.sum(grad_probs * probs, axis=-1, keepdims=True)
            grad_scores = (probs * (grad_probs - delta)).astype(jnp.bfloat16)
            grad_query = product(grad_scores, seen_keys) * scale
            grad_main[:, at : at + HEAD_SIZE] = turned(grad_query, cosine, -sine).astype(jnp.bfloat16)
            grad_keys[seen, :] += product(grad_scores, query, FIRST) * scale
            grad_values[seen, :] += product(probs.astype(jnp.bfloat16), grad_out, FIRST)
        own = pl.ds(pl.multiple_of(chunk * span, span), span)
        key_at = 2 * size.states
        grad_side[:, key_at : key_at + HEAD_SIZE] = turned(grad_keys[own, :], cosine, -sine).astype(jnp.bfloat16)
        grad_side[:, key_at + HEAD_SIZE :] = grad_values[own, :].astype(jnp.bfloat16)

    def rows(columns):
        return pl.BlockSpec((span, columns), lambda i: (count - 1 - i, 0))

    def previous(columns, column):
        return pl.BlockSpec((8, columns), lambda i: (jnp.maximum((count - 1 - i) * (span // 8) - 1, 0), column))

    def whole(array):
        return pl.BlockSpec(array.shape, lambda i: (0, 0))

    cosine, sine = turn_tables(size.length)
    spread = spread_heads(size)
    tokens = size.length
    return pl.pallas_call(
        kernel,
        grid=(count,),
        in_specs=[
            rows(size.channels + size.query), rows(size.main), rows(size.side), previous(size.channels, 1),
            previous(2 * size.states, 0), rows(1), whole(segments), rows(16), whole(tap_rows), whole(head_rows),
            rows(HEAD_SIZE), rows(HEAD_SIZE), whole(spread), rows(size.channels),
            pl.BlockSpec((size.states, size.channels), lambda i: (count - 1 - i, 0)), whole(keys), whole(values),
        ],
        out_specs=[
            rows(size.main), rows(size.side), pl.BlockSpec((8, size.wide), lambda i: (0, 0)),
            pl.BlockSpec((8, size.step_lanes), lambda i: (0, 0)),
        ],
        out_shape=[
            jax.ShapeDtypeStruct((tokens, size.main), jnp.bfloat16),
            jax.ShapeDtypeStruct((tokens, size.side), jnp.bfloat16),
            jax.ShapeDtypeStruct((8, size.wide), jnp.float32),
            jax.ShapeDtypeStruct((8, size.step_lanes), jnp.float32),
        ],
        scratch_shapes=[
            pltpu.VMEM((span + 8, size.wide), jnp.float32),
            pltpu.VMEM((span + 8, size.wide), jnp.float32),
            pltpu.VMEM((size.states, size.channels), jnp.float32),
            pltpu.VMEM((tokens, HEAD_SIZE), jnp.float32),
            pltpu.VMEM((tokens, HEAD_SIZE), jnp.float32),
        ],
        compiler_params=pltpu.CompilerParams(
            dimension_semantics=("arbitrary",), vmem_limit_bytes=VMEM_LIMIT
        ),
        name="mixers_backward",
    )(grad_mixed, main_raw, side_raw, main_raw, side_raw, segments.reshape(tokens, 1), segments, flags, tap_rows,
      head_rows, jnp.asarray(cosine), jnp.asarray(sine), jnp.asarray(spread), y_value, states, keys, values)


def per_device(
    nd,
    nt,
    residual,
    segments,
    mixgain,
    ffngain,
    gateproj,
    innerproj,
    stepproj,
    sharedproj,
    innerconv,
    sharedconv,
    stepbias,
    decaylog,
    skipgain,
    mixerout,
    queryproj,
    keyvalue,
    attnout,
    ffngate,
    upproj,
    downproj,
    cotangent,
):
    bfloat = jnp.bfloat16
    single = jnp.float32
    width = residual.shape[1]
    query_head_rows = queryproj.shape[1] // HEAD_SIZE
    zed = lax.axis_index("tensor")
    kv_head = zed * query_head_rows // (QUERY_HEADS // KEY_VALUE_HEADS)
    seq_count, length = segments.shape
    token_count = seq_count * length
    channels = innerproj.shape[1]
    state_columns = sharedproj.shape[1]
    heads = stepproj.shape[1]
    query_columns = queryproj.shape[1]
    ffn_columns = ffngate.shape[1]
    small_rows = sharedproj.shape[0]
    conv_rows = sharedconv.shape[0]
    taps = sharedconv.shape[1]

    gains = jnp.concatenate(
        [
            mixgain[:, None],
            ffngain[:, None],
            jnp.pad(sharedconv, ((0, small_rows - conv_rows), (0, 0))),
            jnp.zeros((small_rows, 128 - 2 - taps), bfloat),
        ],
        axis=1,
    )
    main_used = 2 * channels + query_columns + heads
    main_own = jnp.concatenate(
        [
            gateproj,
            innerproj,
            queryproj,
            stepproj,
            jnp.zeros((gateproj.shape[0], -main_used % 128), bfloat),
        ],
        axis=1,
    )
    resid_own, cot_own, resid_rows, _, common, main, out_w = first_gathers(
        nd,
        nt,
        residual,
        cotangent,
        jnp.concatenate([sharedproj, keyvalue, gains], axis=1),
        [main_own, jnp.concatenate([mixerout, attnout], axis=1)],
    )
    grad_rows = lax.all_gather(cot_own, "tensor", axis=0, tiled=True)
    extra = common[:, state_columns + keyvalue.shape[1] :]
    gain_one = extra[:, 0].astype(single)
    gain_two = extra[:, 1].astype(single)
    conv_shared = from_relative(extra[:, 2 : 2 + taps], 0, nd)
    conv_shared = conv_shared.reshape(nd * nt, small_rows, taps)[:, :conv_rows].reshape(-1, taps)
    conv_shared = conv_shared.astype(single)
    key_at = state_columns + kv_head * HEAD_SIZE
    value_at = state_columns + (KEY_VALUE_HEADS + kv_head) * HEAD_SIZE
    side = jnp.concatenate(
        [
            common[:, :state_columns],
            lax.dynamic_slice_in_dim(common, key_at, HEAD_SIZE, 1),
            lax.dynamic_slice_in_dim(common, value_at, HEAD_SIZE, 1),
        ],
        axis=1,
    )

    resid_rows = resid_rows.astype(single)
    normed = (rmsnorm(resid_rows, gain_one)).astype(bfloat)
    main_raw = matrix_product(normed, main)
    side_raw = matrix_product(normed, side)
    size = Sizes(channels, state_columns, query_columns, heads, length)
    flags = token_flags(segments, taps)
    tap_rows = jnp.concatenate([innerconv.astype(single), conv_shared]).T
    tap_rows = jnp.pad(tap_rows, ((0, 8 - taps), (0, 0)))
    head_rows = jnp.stack([stepbias.astype(single), jnp.exp(decaylog.astype(single)), skipgain.astype(single)])
    head_rows = jnp.pad(head_rows, ((0, 5), (0, size.step_lanes - heads)))
    mixed_in, y_value, states, keys, values = mixers_forward(
        size, taps, main_raw, side_raw, segments, flags, tap_rows, head_rows
    )
    mix_part = contract_last(mixed_in, out_w).astype(bfloat)
    middle, rows_two, ffn_w = middle_rows(
        nd,
        nt,
        mix_part,
        resid_own,
        gain_two[None],
        [jnp.concatenate([ffngate, upproj, downproj], axis=1)],
    )
    gate_up_w = ffn_w[:, : 2 * ffn_columns]
    down_w = ffn_w[:, 2 * ffn_columns :]
    gate_up = matrix_product(rows_two, gate_up_w)
    gate = gate_up[:, :ffn_columns]
    upper = gate_up[:, ffn_columns:]
    sigma = jax.nn.sigmoid(gate)
    hidden = (gate * sigma * upper).astype(bfloat)
    grad_hidden = matrix_product(grad_rows, down_w)
    grad_gate = (grad_hidden * upper * sigma * (1.0 + gate * (1.0 - sigma))).astype(bfloat)
    grad_upper = (grad_hidden * gate * sigma).astype(bfloat)
    grad_gate_up = jnp.concatenate([grad_gate, grad_upper], axis=1)
    two_part = contract_last(grad_gate_up, gate_up_w).astype(bfloat)
    grad_middle, grad_gain_two, grad_mix_rows, down_g, gate_up_g = middle_back(
        nd,
        nt,
        two_part,
        middle,
        cot_own,
        gain_two[None],
        [
            contract_leading_axis(grad_rows, hidden).astype(bfloat),
            contract_leading_axis(rows_two, grad_gate_up).astype(bfloat),
        ],
    )
    ffn_part = after(contract_last(hidden, down_w).astype(bfloat), grad_mix_rows)
    ffn_out = lax.psum_scatter(ffn_part, "tensor", scatter_dimension=0, tiled=True)
    layer_out = from_relative(middle + ffn_out.astype(single), 1, nd)
    grad_mixed_in = matrix_product(grad_mix_rows, out_w)
    grad_main, grad_side, tap_sums, head_sums = mixers_backward(
        size, taps, grad_mixed_in, main_raw, side_raw, segments, flags, tap_rows, head_rows, y_value, states, keys, values
    )
    grad_convi = tap_sums[:taps, :channels].T
    grad_convs = tap_sums[:taps, channels:].T
    grad_bias = head_sums[0, :heads]
    grad_decay = head_sums[1, :heads]
    grad_skip = tap_sums[4, :channels].reshape(heads, -1).sum(axis=1)
    one_part = (contract_last(grad_main, main) + contract_last(grad_side, side)).astype(bfloat)
    grad_residual, grad_gain_one, main_g, side_g, out_g = last_sums(
        nd,
        nt,
        one_part,
        resid_own,
        grad_middle,
        gain_one[None],
        [
            contract_leading_axis(normed, grad_main).astype(bfloat),
            contract_leading_axis(normed, grad_side).astype(bfloat),
            contract_leading_axis(grad_mix_rows, mixed_in).astype(bfloat),
        ],
    )
    key_value_g = jnp.zeros((side_g.shape[0], keyvalue.shape[1]), single)
    key_value_g = lax.dynamic_update_slice_in_dim(
        key_value_g, side_g[:, state_columns : state_columns + HEAD_SIZE], kv_head * HEAD_SIZE, 1
    )
    key_value_g = lax.dynamic_update_slice_in_dim(
        key_value_g,
        side_g[:, state_columns + HEAD_SIZE :],
        (KEY_VALUE_HEADS + kv_head) * HEAD_SIZE,
        1,
    )
    common_g = jnp.concatenate([side_g[:, :state_columns], key_value_g], axis=1)
    common_g = line_sums(common_g.astype(bfloat), nt)

    everywhere = jnp.concatenate(
        [
            from_relative(grad_gain_one[0], 0, nd),
            from_relative(grad_gain_two[0], 0, nd),
            grad_convs.reshape(-1),
        ]
    )
    local = jnp.concatenate([grad_convi.reshape(-1), grad_bias, grad_decay, grad_skip])
    local = jnp.pad(local, (0, -local.shape[0] % 128))
    split = everywhere.shape[0]
    small = sum_small(jnp.concatenate([everywhere, local]).reshape(-1, 128), "dp", nd).reshape(-1)
    local = small[split:]
    everywhere = sum_small(small[:split].reshape(-1, 128), "tensor", nt).reshape(-1)
    place = lax.axis_index("dp") * nt + zed
    gain_one_g = lax.dynamic_slice_in_dim(everywhere, place * small_rows, small_rows, 0)
    gain_two_g = lax.dynamic_slice_in_dim(everywhere, width + place * small_rows, small_rows, 0)
    conv_g = lax.dynamic_slice_in_dim(
        everywhere[2 * width :].reshape(-1, taps), place * conv_rows, conv_rows, 0
    )
    counts = channels * innerconv.shape[1]
    return (
        layer_out,
        grad_residual,
        gain_one_g,
        gain_two_g,
        main_g[:, :channels],
        main_g[:, channels : 2 * channels],
        main_g[:, 2 * channels + query_columns : main_used],
        common_g[:, :state_columns],
        local[:counts].reshape(channels, -1),
        conv_g,
        local[counts : counts + heads],
        local[counts + heads : counts + 2 * heads],
        local[counts + 2 * heads : counts + 3 * heads],
        out_g[:, :channels],
        main_g[:, 2 * channels : 2 * channels + query_columns],
        common_g[:, state_columns:],
        out_g[:, channels:],
        gate_up_g[:, :ffn_columns],
        gate_up_g[:, ffn_columns:],
        down_g,
    )


def solution(mesh):
    return jax.shard_map(
        functools.partial(per_device, mesh.shape["dp"], mesh.shape["tensor"]),
        mesh=mesh,
        in_specs=(
            P(("dp", "tensor"), None),
            P("dp", None),
            P(("dp", "tensor")),
            P(("dp", "tensor")),
            P("dp", "tensor"),
            P("dp", "tensor"),
            P("dp", "tensor"),
            P(("dp", "tensor"), None),
            P("tensor", None),
            P(("dp", "tensor"), None),
            P("tensor"),
            P("tensor"),
            P("tensor"),
            P("dp", "tensor"),
            P("dp", "tensor"),
            P(("dp", "tensor"), None),
            P("dp", "tensor"),
            P("dp", "tensor"),
            P("dp", "tensor"),
            P("dp", "tensor"),
            P(("dp", "tensor"), None),
        ),
        out_specs=(
            P(("dp", "tensor"), None),
            P(("dp", "tensor"), None),
            P(("dp", "tensor")),
            P(("dp", "tensor")),
            P("dp", "tensor"),
            P("dp", "tensor"),
            P("dp", "tensor"),
            P(("dp", "tensor"), None),
            P("tensor", None),
            P(("dp", "tensor"), None),
            P("tensor"),
            P("tensor"),
            P("tensor"),
            P("dp", "tensor"),
            P("dp", "tensor"),
            P(("dp", "tensor"), None),
            P("dp", "tensor"),
            P("dp", "tensor"),
            P("dp", "tensor"),
            P("dp", "tensor"),
        ),
        check_vma=False,
    )
```

```python
import functools
import math

import jax
import jax.numpy as jnp
import numpy as np
from jax import lax
from jax.experimental import pallas as pl
from jax.experimental.pallas import tpu as pltpu
from jax.sharding import PartitionSpec as P

QUERY_HEADS = 8
KEY_VALUE_HEADS = 2
HEAD_SIZE = 128
SPAN = 256


eps = 1e-05
rope_base = 10000.0


def rmsnorm(value, gain):
    return value * lax.rsqrt(jnp.mean(value * value, axis=-1, keepdims=True) + eps) * gain


def matrix_product(left, right):
    return jnp.dot(left, right, preferred_element_type=jnp.float32)


def contract_leading_axis(left, right):
    return lax.dot_general(
        left, right, (((0,), (0,)), ((), ())), preferred_element_type=jnp.float32
    )


def contract_last(left, right):
    return lax.dot_general(
        left, right, (((1,), (1,)), ((), ())), preferred_element_type=jnp.float32
    )


def bit_orders(size):
    high = list(range(size.bit_length() - 2, 0, -1))
    return high, high[:2][::-1] + high[2:]


def relative_blocks(size):
    both = []
    for half, order in enumerate(bit_orders(size)):
        chain = [0]
        for bit in order:
            chain = chain + [other ^ (1 << bit) for other in chain]
        both = both + [(other, half) for other in chain]
    return both + [(other ^ 1, half) for other, half in both]


def to_relative(value, axis, size):
    me = lax.axis_index("dp")
    width = value.shape[axis] // (2 * size)
    return jnp.concatenate(
        [
            lax.dynamic_slice_in_dim(value, ((me ^ other) * 2 + half) * width, width, axis)
            for other, half in relative_blocks(size)
        ],
        axis,
    )


def from_relative(value, axis, size):
    me = lax.axis_index("dp")
    width = value.shape[axis] // (2 * size)
    blocks = relative_blocks(size)
    place = jnp.asarray([blocks.index((other, half)) for other in range(size) for half in range(2)], jnp.int32)
    return jnp.concatenate(
        [
            lax.dynamic_slice_in_dim(value, place[(me ^ number) * 2 + half] * width, width, axis)
            for number in range(size)
            for half in range(2)
        ],
        axis,
    )


def after(value, *others):
    return lax.optimization_barrier((value,) + others)[0]


MESH = pl.DeviceIdType.MESH
VMEM_LIMIT = 56 * 1024 * 1024


def flip(value, bit):
    unit = 1 << bit
    return value + unit * (1 - 2 * ((value // unit) % 2))


def mixed_with(value, other, bits):
    for bit in range(bits):
        if (other >> bit) & 1:
            value = flip(value, bit)
    return value


def enter(nt, bits):
    me, zed = lax.axis_index("dp"), lax.axis_index("tensor")
    barrier = pltpu.get_barrier_semaphore()
    for other in range(nt):

        @pl.when(zed != other)
        def _(other=other):
            pl.semaphore_signal(barrier, inc=1, device_id=(me, other), device_id_type=MESH)

    for bit in range(bits):
        pl.semaphore_signal(barrier, inc=1, device_id=(flip(me, bit), zed), device_id_type=MESH)
    pl.semaphore_wait(barrier, bits + nt - 1)
    return me, zed


def aligned(start, size):
    return pl.ds(pl.multiple_of(start, 16), size)


def together(*flows):
    flows = [list(flow) for flow in flows]
    order = sorted(
        ((place + 0.5) / len(flow), number, place)
        for number, flow in enumerate(flows)
        for place in range(len(flow))
    )
    for _, number, place in order:
        flows[number][place]()


def gather_steps(nd, me, zed, own, everything, send, recv, local):
    half = own.shape[0] // 2
    blocks = relative_blocks(nd)
    place = {block: number for number, block in enumerate(blocks)}

    def rows(block):
        return everything.at[pl.ds(place[block] * half, half)]

    def source(block):
        return own.at[pl.ds(block[1] * half, half)] if block[0] == 0 else rows(block)

    hops = []
    for part, order in enumerate(bit_orders(nd)):
        chain = [0]
        for bit in order:
            hops = hops + [((other, part), bit) for other in chain]
            chain = chain + [other ^ (1 << bit) for other in chain]
    hops = hops + [(block, 0) for block in blocks[:nd]]

    def copy(number):
        block, bit = hops[number]
        landed = (block[0] ^ (1 << bit), block[1])
        return pltpu.make_async_remote_copy(
            src_ref=source(block),
            dst_ref=rows(landed),
            send_sem=send.at[number],
            recv_sem=recv.at[place[landed]],
            device_id=(flip(me, bit), zed),
            device_id_type=MESH,
        )

    def arrival(block):
        return pltpu.make_async_remote_copy(
            src_ref=rows(block),
            dst_ref=rows(block),
            send_sem=send.at[0],
            recv_sem=recv.at[place[block]],
            device_id=(flip(me, 0), zed),
            device_id_type=MESH,
        )

    def begin():
        for number, (block, bit) in enumerate(hops):
            if block[0] == 0:
                copy(number).start()
        for part in range(2):
            pltpu.make_async_copy(source((0, part)), rows((0, part)), local.at[part]).start()

    def forward(block):
        def step():
            arrival(block).wait_recv()
            for number, (origin, bit) in enumerate(hops):
                if origin == block:
                    copy(number).start()

        return step

    def end():
        for block in blocks[nd:]:
            arrival(block).wait_recv()
        for number in range(len(hops)):
            copy(number).wait_send()
        for part in range(2):
            pltpu.make_async_copy(source((0, part)), rows((0, part)), local.at[part]).wait()

    first, second = blocks[1 : nd // 2], blocks[nd // 2 + 1 : nd]
    middle = [forward(block) for pair in zip(first, second) for block in pair]
    return [begin] + middle + [end]


def gather_hops(nd):
    return 2 * (nd // 2 - 1) + nd


def gather_semaphores(nd):
    return [
        pltpu.SemaphoreType.DMA((gather_hops(nd),)),
        pltpu.SemaphoreType.DMA((2 * nd,)),
        pltpu.SemaphoreType.DMA((2,)),
    ]


def each_rows(rows, body, unit=16):
    def step(number, carry):
        body(aligned(number * unit, unit))
        return carry

    lax.fori_loop(0, rows // unit, step, 0)


def scatter_steps(nd, me, zed, parts, total, mine, held, landed, core_send, core_recv, send, recv, local):
    half = total.shape[0] // 2
    chain_length = nd // 2

    def piece(ref, number):
        return ref.at[pl.ds(number * half, half)]

    rounds, slot = [], 0
    for part, order in enumerate(bit_orders(nd)):
        length, own_rounds = chain_length, []
        for bit in order[::-1]:
            length = length // 2
            own_rounds.append((bit, length, slot))
            slot = slot + length
        rounds.append(own_rounds)

    def core_copy(number):
        return pltpu.make_async_remote_copy(
            src_ref=piece(parts, nd + number),
            dst_ref=piece(held, number),
            send_sem=core_send.at[number],
            recv_sem=core_recv.at[number],
            device_id=(flip(me, 0), zed),
            device_id_type=MESH,
        )

    def hop(part, bit, number, where):
        return pltpu.make_async_remote_copy(
            src_ref=piece(held, number),
            dst_ref=piece(landed, where),
            send_sem=send.at[where],
            recv_sem=recv.at[where],
            device_id=(flip(me, bit), zed),
            device_id_type=MESH,
        )

    wanted = []
    for number in range(chain_length - 1, -1, -1):
        wanted = wanted + [number, chain_length + number]

    def load(number):
        return pltpu.make_async_copy(piece(parts, number), piece(mine, number), local.at[number])

    def begin():
        for number in wanted:
            core_copy(number).start()
        for number in wanted:
            load(number).start()

    def core_sum(number):
        part, spot = number // chain_length, number % chain_length

        def step():
            load(number).wait()
            core_copy(number).wait_recv()

            def body(rows):
                spot_rows = piece(held, number)
                spot_rows[rows] = spot_rows[rows] + piece(mine, number)[rows]

            each_rows(half, body)
            if rounds[part]:
                bit, length, first = rounds[part][0]
                if spot >= length:
                    hop(part, bit, number, first + spot - length).start()

        return step

    def later_sum(part, turn, spot):
        bit, length, first = rounds[part][turn]
        number = part * chain_length + spot

        def step():
            hop(part, bit, number, first + spot).wait_recv()
            last = turn == len(rounds[part]) - 1

            def body(rows):
                kept, came = piece(held, number)[rows], piece(landed, first + spot)[rows]
                if last:
                    piece(total, part)[rows] = kept.astype(jnp.float32) + came.astype(jnp.float32)
                else:
                    piece(held, number)[rows] = kept + came

            each_rows(half, body)
            if not last:
                next_bit, next_length, next_first = rounds[part][turn + 1]
                if spot >= next_length:
                    hop(part, next_bit, number, next_first + spot - next_length).start()

        return step

    stages = [[core_sum(number) for number in wanted]]
    for turn in range(len(rounds[0])):
        length = rounds[0][turn][1]
        stages.append([later_sum(part, turn, spot) for spot in range(length - 1, -1, -1) for part in range(2)])

    def end():
        for number in range(nd):
            core_copy(number).wait_send()
        for part in range(2):
            for bit, length, first in rounds[part]:
                for spot in range(length):
                    hop(part, bit, part * chain_length + length + spot, first + spot).wait_send()

    return [[begin]] + stages + [[end]]


def staggered(flows):
    steps = [step for flow in flows for step in flow[0]]
    depth = len(flows[0]) - 2
    for turn in range(depth + len(flows) - 1):
        for number in range(len(flows) - 1, -1, -1):
            if 0 <= turn - number < depth:
                steps = steps + flows[number][1 + turn - number]
    return steps + [step for flow in flows for step in flow[-1]]


def scatter_scratch(nd, rows, columns):
    slots = nd - 2
    return [
        pltpu.VMEM((nd * rows // 2, columns), jnp.bfloat16),
        pltpu.VMEM((nd * rows // 2, columns), jnp.bfloat16),
        pltpu.VMEM((slots * rows // 2, columns), jnp.bfloat16),
        pltpu.SemaphoreType.DMA((nd,)),
        pltpu.SemaphoreType.DMA((nd,)),
        pltpu.SemaphoreType.DMA((slots,)),
        pltpu.SemaphoreType.DMA((slots,)),
        pltpu.SemaphoreType.DMA((nd,)),
    ]


def line_gather(nt, me, zed, chunks, own, everything, send, recv):
    size = own.shape[0] // chunks

    def own_rows(chunk):
        return own.at[pl.ds(chunk * size, size)]

    def rows(block, chunk):
        return everything.at[aligned(block * (size * chunks) + chunk * size, size)]

    def copy(source, block, chunk, side):
        return pltpu.make_async_remote_copy(
            src_ref=source,
            dst_ref=rows(block, chunk),
            send_sem=send.at[side, block, chunk],
            recv_sem=recv.at[block, chunk],
            device_id=(me, zed + 1 - 2 * side),
            device_id_type=MESH,
        )

    def keep(chunk):
        return pltpu.make_async_copy(own_rows(chunk), rows(zed, chunk), recv.at[zed, chunk])

    def first(chunk):
        for side, condition in ((0, zed < nt - 1), (1, zed > 0)):

            @pl.when(condition)
            def _(side=side):
                copy(own_rows(chunk), zed, chunk, side).start()

        keep(chunk).start()

    def onward(chunk, distance):
        for side, block in ((0, zed - distance), (1, zed + distance)):
            inside = (block >= 0) if side == 0 else (block < nt)
            open_end = (zed < nt - 1) if side == 0 else (zed > 0)

            @pl.when(inside)
            def _(block=block, side=side):
                copy(rows(block, chunk), block, chunk, side).wait_recv()

            @pl.when(jnp.logical_and(inside, open_end))
            def _(block=block, side=side):
                copy(rows(block, chunk), block, chunk, side).start()

    def end(chunk):
        keep(chunk).wait()
        for side, condition in ((0, zed < nt - 1), (1, zed > 0)):

            @pl.when(condition)
            def _(side=side):
                copy(own_rows(chunk), zed, chunk, side).wait_send()

            for distance in range(1, nt - 1):
                block = zed - distance if side == 0 else zed + distance
                inside = (block >= 0) if side == 0 else (block < nt)

                @pl.when(jnp.logical_and(inside, condition))
                def _(block=block, side=side):
                    copy(rows(block, chunk), block, chunk, side).wait_send()

    return first, onward, end


def line_gather_semaphores(nt, chunks):
    return [pltpu.SemaphoreType.DMA((2, nt, chunks)), pltpu.SemaphoreType.DMA((nt, chunks))]


def line_reduce(nt, me, zed, chunks, parts, rising, falling, send, recv):
    block_rows = parts.shape[0] // nt
    size = block_rows // chunks
    sides = ((0, rising), (1, falling))

    def rows(block, chunk):
        return aligned(block * block_rows + chunk * size, size)

    def copy(source, side, held, block, chunk):
        return pltpu.make_async_remote_copy(
            src_ref=source.at[rows(block, chunk)],
            dst_ref=held.at[rows(block, chunk)],
            send_sem=send.at[side, block, chunk],
            recv_sem=recv.at[side, block, chunk],
            device_id=(me, zed + 1 - 2 * side),
            device_id_type=MESH,
        )

    def role(side, turn):
        away = nt - 1 - turn
        if side == 0:
            return zed + away, zed + away < nt, zed == 0
        return zed - away, zed - away >= 0, zed == nt - 1

    def pass_on(chunk, turn):
        for side, held in sides:
            block, active, source = role(side, turn)

            @pl.when(jnp.logical_and(active, source))
            def _(side=side, held=held, block=block):
                copy(parts, side, held, block, chunk).start()

            @pl.when(jnp.logical_and(active, jnp.logical_not(source)))
            def _(side=side, held=held, block=block):
                copy(held, side, held, block, chunk).wait_recv()

                def body(inner):
                    where = aligned(block * block_rows + chunk * size + inner.start, inner.size)
                    held[where] = parts[where] + held[where]

                each_rows(size, body)
                copy(held, side, held, block, chunk).start()

    def own_sum(chunk, total):
        where = rows(zed, chunk)
        total[...] = parts[where].astype(jnp.float32)
        for side, held in sides:

            @pl.when(zed > 0 if side == 0 else zed < nt - 1)
            def _(side=side, held=held):
                copy(held, side, held, zed, chunk).wait_recv()
                total[...] += held[where].astype(jnp.float32)

    def end(chunk):
        for turn in range(nt - 1):
            for side, held in sides:
                block, active, source = role(side, turn)

                @pl.when(active)
                def _(side=side, held=held, block=block):
                    copy(held, side, held, block, chunk).wait_send()

    return pass_on, own_sum, end


def line_reduce_scratch(nt, block_rows, columns, chunks):
    return [
        pltpu.VMEM((nt * block_rows, columns), jnp.bfloat16),
        pltpu.VMEM((nt * block_rows, columns), jnp.bfloat16),
        pltpu.VMEM((block_rows // chunks, columns), jnp.float32),
        pltpu.SemaphoreType.DMA((2, nt, chunks)),
        pltpu.SemaphoreType.DMA((2, nt, chunks)),
    ]


HBM = pl.BlockSpec(memory_space=pl.ANY)
ONCHIP = pl.BlockSpec(memory_space=pltpu.VMEM)


def first_gathers(nd, nt, rows, grad, small, groups):
    chunks = 4
    bits = nd.bit_length() - 1
    count = len(groups)
    blocks = relative_blocks(nd)
    lane = rows.shape[1] // len(blocks)
    if lane % 128:
        rows, grad = to_relative(rows, 1, nd), to_relative(grad, 1, nd)

    def reorder(me, source, target):
        if lane % 128:
            target[...] = source[...]
            return
        for number, (other, part) in enumerate(blocks):
            start = (mixed_with(me, other, bits) * 2 + part) * lane
            target[:, number * lane : (number + 1) * lane] = source[:, pl.ds(pl.multiple_of(start, lane), lane)]

    def kernel(rows_in, grad_in, small_ref, *refs):
        group_refs, refs = refs[:count], refs[count:]
        rows_ref, grad_ref, rows_all, small_line, small_all = refs[:5]
        group_all, refs = refs[5 : 5 + count], refs[5 + count :]
        row_sems, small_sems, small_dp, refs = refs[:2], refs[2:4], refs[4:7], refs[7:]
        me, zed = enter(nt, bits)
        small_first, small_onward, small_end = line_gather(nt, me, zed, 1, small_ref, small_line, *small_sems)
        row_first, row_onward, row_end = line_gather(nt, me, zed, chunks, rows_ref, rows_all, *row_sems)
        flows = [
            gather_steps(nd, me, zed, group_refs[n], group_all[n], *refs[3 * n : 3 * n + 3]) for n in range(count)
        ]
        last = gather_steps(nd, me, zed, small_line, small_all, *small_dp)
        small_first(0)
        flows[0][0]()
        reorder(me, rows_in, rows_ref)
        for chunk in range(chunks):
            row_first(chunk)
        for flow in flows[1:]:
            flow[0]()
        for distance in range(1, nt):
            small_onward(0, distance)
        small_end(0)
        last[0]()
        along = [
            functools.partial(row_onward, chunk, distance) for distance in range(1, nt) for chunk in range(chunks)
        ]
        over = [step for flow in flows for step in flow[1:-1]]
        over = over + last[1:-1] + [flow[-1] for flow in flows] + [last[-1]]
        reorder(me, grad_in, grad_ref)
        together(along, over)
        for chunk in range(chunks):
            row_end(chunk)

    def widened(array, times):
        return jax.ShapeDtypeStruct((array.shape[0] * times, array.shape[1]), array.dtype)

    semaphores = line_gather_semaphores(nt, chunks) + line_gather_semaphores(nt, 1) + gather_semaphores(nd)
    return pl.pallas_call(
        kernel,
        out_shape=[widened(rows, 1), widened(grad, 1), widened(rows, nt), widened(small, nt), widened(small, nt * nd)]
        + [widened(group, nd) for group in groups],
        in_specs=[ONCHIP] * 2 + [HBM] * (1 + count),
        out_specs=[ONCHIP] * 2 + [HBM] * (3 + count),
        scratch_shapes=semaphores + gather_semaphores(nd) * count,
        compiler_params=pltpu.CompilerParams(
            collective_id=0, has_side_effects=True, vmem_limit_bytes=VMEM_LIMIT
        ),
        name="first_gathers",
    )(rows, grad, small, *groups)


def middle_rows(nd, nt, parts, resid, gain, groups):
    chunks = 8
    bits = nd.bit_length() - 1
    count = len(groups)
    block_rows, width = resid.shape
    size = block_rows // chunks

    def kernel(parts_ref, resid_ref, gain_ref, *refs):
        group_refs, refs = refs[:count], refs[count:]
        middle_ref, rows_all = refs[:2]
        group_all, refs = refs[2 : 2 + count], refs[2 + count :]
        own, rising, falling, total, send, recv = refs[:6]
        gather_sems, refs = refs[6:8], refs[8:]
        me, zed = enter(nt, bits)
        pass_on, own_sum, reduce_end = line_reduce(nt, me, zed, chunks, parts_ref, rising, falling, send, recv)
        first, onward, gather_end = line_gather(nt, me, zed, chunks, own, rows_all, *gather_sems)
        flows = [
            gather_steps(nd, me, zed, group_refs[n], group_all[n], *refs[3 * n : 3 * n + 3]) for n in range(count)
        ]

        def finish(chunk):
            own_sum(chunk, total)
            where = pl.ds(chunk * size, size)
            value = resid_ref[where].astype(jnp.float32) + total[...]
            middle_ref[where] = value
            scale = lax.rsqrt(jnp.mean(value * value, axis=-1, keepdims=True) + eps)
            own[where] = (value * scale * gain_ref[...]).astype(jnp.bfloat16)
            first(chunk)

        line_schedule(nt, chunks, pass_on, finish, onward, [step for flow in flows for step in flow])
        for chunk in range(chunks):
            reduce_end(chunk)
            gather_end(chunk)

    return pl.pallas_call(
        kernel,
        out_shape=[
            jax.ShapeDtypeStruct((block_rows, width), jnp.float32),
            jax.ShapeDtypeStruct((block_rows * nt, width), jnp.bfloat16),
        ]
        + [jax.ShapeDtypeStruct((group.shape[0] * nd, group.shape[1]), group.dtype) for group in groups],
        in_specs=[ONCHIP] * 3 + [HBM] * count,
        out_specs=[ONCHIP] + [HBM] * (1 + count),
        scratch_shapes=[pltpu.VMEM((block_rows, width), jnp.bfloat16)]
        + line_reduce_scratch(nt, block_rows, width, chunks)
        + line_gather_semaphores(nt, chunks)
        + gather_semaphores(nd) * count,
        compiler_params=pltpu.CompilerParams(
            collective_id=1, has_side_effects=True, vmem_limit_bytes=VMEM_LIMIT
        ),
        name="middle_rows",
    )(parts, resid, gain, *groups)


def line_schedule(nt, chunks, pass_on, finish, onward, others):
    steps = []

    def add(function, chunk, *rest):
        if function is not None and 0 <= chunk < chunks:
            steps.append(functools.partial(function, chunk, *rest))

    for chunk in range(chunks + 2):
        add(pass_on, chunk, 0)
        add(finish, chunk - 1)
        add(onward, chunk - 2, nt - 1)
        for turn in range(1, nt - 1):
            add(pass_on, chunk, turn)
            add(onward, chunk - 1, turn)
    together(steps, others)


def absolute_lanes(me, bits, blocks, source, target):
    lane = source.shape[1] // len(blocks)
    for number, (other, part) in enumerate(blocks):
        start = (mixed_with(me, other, bits) * 2 + part) * lane
        target[:, pl.ds(pl.multiple_of(start, lane), lane)] = source[:, number * lane : (number + 1) * lane]


def norm_pull(value, gain, grad):
    scale = lax.rsqrt(jnp.mean(value * value, axis=-1, keepdims=True) + eps)
    scaled = grad * gain
    inner = jnp.mean(scaled * value, axis=-1, keepdims=True)
    return scale * (scaled - value * (inner * scale * scale)), grad * value * scale


def middle_back(nd, nt, parts, middle, cot, gain, groups):
    chunks = 8
    bits = nd.bit_length() - 1
    count = len(groups)
    block_rows, width = middle.shape
    size = block_rows // chunks
    per_group = 8
    blocks = relative_blocks(nd)
    lane = width // len(blocks)

    def kernel(parts_ref, middle_ref, cot_ref, gain_ref, *refs):
        group_refs, refs = refs[:count], refs[count:]
        grad_ref, gain_out, rows_all = refs[:3]
        totals, refs = refs[3 : 3 + count], refs[3 + count :]
        own, gain_grad, rising, falling, total, send, recv = refs[:7]
        gather_sems, refs = refs[7:9], refs[9:]
        me, zed = enter(nt, bits)
        pass_on, own_sum, reduce_end = line_reduce(nt, me, zed, chunks, parts_ref, rising, falling, send, recv)
        first, onward, gather_end = line_gather(nt, me, zed, chunks, own, rows_all, *gather_sems)
        flows = [
            scatter_steps(nd, me, zed, group_refs[n], totals[n], *refs[per_group * n : per_group * (n + 1)])
            for n in range(count)
        ]
        gain_grad[...] = jnp.zeros_like(gain_grad)

        def finish(chunk):
            own_sum(chunk, total)
            where = pl.ds(chunk * size, size)
            through, gained = norm_pull(middle_ref[where], gain_ref[...], total[...])
            value = cot_ref[where].astype(jnp.float32) + through
            gain_grad[...] += jnp.sum(gained, axis=0, keepdims=True)
            grad_ref[where] = value
            own[where] = value.astype(jnp.bfloat16)
            first(chunk)

        line_schedule(nt, chunks, pass_on, finish, onward, staggered(flows))
        if lane % 128:
            gain_out[...] = gain_grad[...]
        else:
            absolute_lanes(me, bits, blocks, gain_grad, gain_out)
        for chunk in range(chunks):
            reduce_end(chunk)
            gather_end(chunk)

    scratch = []
    for group in groups:
        scratch = scratch + scatter_scratch(nd, group.shape[0] // nd, group.shape[1])
    results = pl.pallas_call(
        kernel,
        out_shape=[
            jax.ShapeDtypeStruct((block_rows, width), jnp.float32),
            jax.ShapeDtypeStruct((1, width), jnp.float32),
            jax.ShapeDtypeStruct((block_rows * nt, width), jnp.bfloat16),
        ]
        + [jax.ShapeDtypeStruct((group.shape[0] // nd, group.shape[1]), jnp.float32) for group in groups],
        in_specs=[ONCHIP] * 4 + [HBM] * count,
        out_specs=[ONCHIP, ONCHIP, HBM] + [ONCHIP] * count,
        scratch_shapes=[pltpu.VMEM((block_rows, width), jnp.bfloat16), pltpu.VMEM((1, width), jnp.float32)]
        + line_reduce_scratch(nt, block_rows, width, chunks)
        + line_gather_semaphores(nt, chunks)
        + scratch,
        compiler_params=pltpu.CompilerParams(
            collective_id=2, has_side_effects=True, vmem_limit_bytes=VMEM_LIMIT
        ),
        name="middle_back",
    )(parts, middle, cot, gain, *groups)
    if lane % 128:
        results = (results[0], from_relative(results[1], 1, nd), *results[2:])
    return results


def last_sums(nd, nt, parts, rows, resid, before, gain, small, shared_rows, groups, side):
    chunks = 8
    bits, line_bits = nd.bit_length() - 1, nt.bit_length() - 1
    block_rows, width = resid.shape
    size = block_rows // chunks
    per_group = 8
    blocks = relative_blocks(nd)
    lane = width // len(blocks)
    groups = [*groups, side]
    count = len(groups)
    side_rows, side_columns = side.shape[0] // nd, side.shape[1]
    shared_columns = side_columns - 2 * HEAD_SIZE
    owned = side_rows // nt
    gain_rows = width // 128
    if lane % 128:
        value = rows.astype(jnp.float32)
        scale = lax.rsqrt(jnp.mean(value * value, axis=-1, keepdims=True) + eps)
        own_gain = from_relative(jnp.sum(parts.astype(jnp.float32) * value * scale, axis=0), 0, nd)
        small = jnp.concatenate([own_gain.reshape(gain_rows, 128), small[gain_rows:]])

    def kernel(parts_ref, rows_ref, resid_ref, before_ref, gain_ref, small_ref, *refs):
        group_refs, refs = refs[:count], refs[count:]
        grad_ref, small_out, common_ref = refs[:3]
        totals, refs = refs[3 : 2 + count], refs[2 + count :]
        side_total, rising, falling, total, send, recv = refs[:6]
        sums, landed, small_send, small_recv, gain_grad = refs[6:11]
        side_out, side_in, side_send, side_recv = refs[11:15]
        refs = refs[15:]
        me, zed = enter(nt, bits)
        pass_on, own_sum, reduce_end = line_reduce(nt, me, zed, chunks, parts_ref, rising, falling, send, recv)
        totals = [*totals, side_total]
        flows = [
            scatter_steps(nd, me, zed, group_refs[n], totals[n], *refs[per_group * n : per_group * (n + 1)])
            for n in range(count)
        ]

        def gain_term(number):
            def step():
                if number == 0:
                    gain_grad[...] = jnp.zeros_like(gain_grad)

                def body(inner, carry):
                    where = aligned(number * block_rows + inner * 16, 16)
                    value = rows_ref[where].astype(jnp.float32)
                    scale = lax.rsqrt(jnp.mean(value * value, axis=-1, keepdims=True) + eps)
                    gain_grad[...] += parts_ref[where].astype(jnp.float32) * (value * scale)
                    return carry

                lax.fori_loop(0, block_rows // 16, body, 0)

            return step

        def gain_end():
            sums[0] = small_ref[...]
            if lane % 128 == 0:
                whole = jnp.sum(gain_grad[...], axis=0, keepdims=True)
                for number, (other, part) in enumerate(blocks):
                    spot = mixed_with(me, other, bits) * 2 + part
                    sums[0, pl.ds(spot, 1), :] = whole[:, number * lane : (number + 1) * lane]

        def small_copy(turn):
            if turn < bits:
                device = (flip(me, turn), zed)
            else:
                device = (me, flip(zed, turn - bits))
            extent = slice(None) if turn < bits else pl.ds(0, shared_rows)
            return pltpu.make_async_remote_copy(
                src_ref=sums.at[turn, extent],
                dst_ref=landed.at[turn, extent],
                send_sem=small_send.at[turn],
                recv_sem=small_recv.at[turn],
                device_id=device,
                device_id_type=MESH,
            )

        def small_step(turn):
            def step():
                small_copy(turn).wait_recv()
                if turn < bits:
                    sums[turn + 1] = sums[turn] + landed[turn]
                else:
                    sums[turn + 1] = sums[turn]
                    sums[turn + 1, pl.ds(0, shared_rows)] = (
                        sums[turn, pl.ds(0, shared_rows)] + landed[turn, pl.ds(0, shared_rows)]
                    )
                if turn + 1 < bits + line_bits:
                    small_copy(turn + 1).start()

            return step

        def small_begin():
            gain_end()
            small_copy(0).start()

        def small_end():
            for turn in range(bits + line_bits):
                small_copy(turn).wait_send()
            small_out[...] = sums[bits + line_bits]

        few = [gain_term(number) for number in range(nt if lane % 128 == 0 else 0)]
        few = few + [small_begin] + [small_step(turn) for turn in range(bits + line_bits)] + [small_end]

        def side_copy(source, target):
            return pltpu.make_async_remote_copy(
                src_ref=side_out.at[pl.ds(target * owned, owned)],
                dst_ref=side_in.at[source],
                send_sem=side_send.at[target],
                recv_sem=side_recv.at[source],
                device_id=(me, target),
                device_id_type=MESH,
            )

        def side_begin():
            side_out[...] = side_total[...].astype(jnp.bfloat16)
            for target in range(nt):

                @pl.when(zed != target)
                def _(target=target):
                    side_copy(zed, target).start()

            side_in[zed] = side_out[aligned(zed * owned, owned)]

        def side_end():
            for source in range(nt):

                @pl.when(zed != source)
                def _(source=source):
                    side_copy(source, source).wait_recv()

            common_ref[...] = jnp.zeros_like(common_ref)
            for source in range(nt):
                value = side_in[source].astype(jnp.float32)
                head = source * (QUERY_HEADS // nt) // (QUERY_HEADS // KEY_VALUE_HEADS)
                common_ref[:, :shared_columns] += value[:, :shared_columns]
                for turn in range(2):
                    at = shared_columns + (turn * KEY_VALUE_HEADS + head) * HEAD_SIZE
                    start = shared_columns + turn * HEAD_SIZE
                    common_ref[:, at : at + HEAD_SIZE] += value[:, start : start + HEAD_SIZE]
            for target in range(nt):

                @pl.when(zed != target)
                def _(target=target):
                    side_copy(zed, target).wait_send()

        def finish(chunk):
            own_sum(chunk, total)
            where = pl.ds(chunk * size, size)
            through, _ = norm_pull(resid_ref[where].astype(jnp.float32), gain_ref[...], total[...])
            value = before_ref[where] + through
            if lane % 128:
                grad_ref[where] = value
                return
            for number, (other, part) in enumerate(blocks):
                start = (mixed_with(me, other, bits) * 2 + part) * lane
                grad_ref[where, pl.ds(pl.multiple_of(start, lane), lane)] = value[:, number * lane : (number + 1) * lane]

        over = staggered([flows[-1]] + flows[:-1])
        first = len(flows)
        over = over[:first] + [step for pair in zip(over[first : first + len(few)], few) for step in pair] + over[
            first + len(few) :
        ]
        over = over[: -len(flows)] + [side_begin] + over[-len(flows) :] + [side_end]
        line_schedule(nt, chunks, pass_on, finish, None, over)
        for chunk in range(chunks):
            reduce_end(chunk)

    scratch = []
    for group in groups:
        scratch = scratch + scatter_scratch(nd, group.shape[0] // nd, group.shape[1])
    turns = bits + line_bits
    common_columns = shared_columns + 2 * KEY_VALUE_HEADS * HEAD_SIZE
    results = pl.pallas_call(
        kernel,
        out_shape=[
            jax.ShapeDtypeStruct((block_rows, width), jnp.float32),
            jax.ShapeDtypeStruct(small.shape, jnp.float32),
            jax.ShapeDtypeStruct((owned, common_columns), jnp.float32),
        ]
        + [jax.ShapeDtypeStruct((group.shape[0] // nd, group.shape[1]), jnp.float32) for group in groups[:-1]],
        in_specs=[ONCHIP] * 6 + [HBM] * count,
        out_specs=[ONCHIP] * (2 + count),
        scratch_shapes=[pltpu.VMEM((side_rows, side_columns), jnp.float32)]
        + line_reduce_scratch(nt, block_rows, width, chunks)
        + [
            pltpu.VMEM((turns + 1, *small.shape), jnp.float32),
            pltpu.VMEM((turns, *small.shape), jnp.float32),
            pltpu.SemaphoreType.DMA((turns,)),
            pltpu.SemaphoreType.DMA((turns,)),
            pltpu.VMEM((16, width), jnp.float32),
            pltpu.VMEM((side_rows, side_columns), jnp.bfloat16),
            pltpu.VMEM((nt, owned, side_columns), jnp.bfloat16),
            pltpu.SemaphoreType.DMA((nt,)),
            pltpu.SemaphoreType.DMA((nt,)),
        ]
        + scratch,
        compiler_params=pltpu.CompilerParams(
            collective_id=3, has_side_effects=True, vmem_limit_bytes=VMEM_LIMIT
        ),
        name="last_sums",
    )(parts, rows, resid, before, gain, small, *groups)
    if lane % 128:
        results = (from_relative(results[0], 1, nd), *results[1:])
    return results


def silu_slope(value, sig):
    return sig * (1.0 + value * (1.0 - sig))


def split_dot(value, constant, dims, terms):
    total = None
    for _ in range(terms):
        piece = value.astype(jnp.bfloat16)
        value = value - piece.astype(jnp.float32)
        part = lax.dot_general(*((piece, constant) if dims[0] else (constant, piece)), dims[1], preferred_element_type=jnp.float32)
        total = part if total is None else total + part
    return total


PLAIN = (((1,), (0,)), ((), ()))
LAST = (((1,), (1,)), ((), ()))
FIRST = (((0,), (0,)), ((), ()))


def product(left, right, dims=PLAIN):
    return lax.dot_general(left, right, dims, preferred_element_type=jnp.float32)


def turned(value, cosine, sine):
    return value * cosine + pltpu.roll(value, value.shape[-1] // 2, 1) * sine


class Sizes:
    def __init__(self, channels, state_columns, query_columns, heads, length):
        self.channels, self.states = channels, state_columns // 2
        self.query, self.heads, self.length = query_columns, heads, length
        self.span = SPAN
        self.count = length // SPAN
        self.wide = channels + state_columns
        self.head_width = channels // heads
        self.step_at = 2 * channels + query_columns
        self.main = self.step_at + heads + (-(self.step_at + heads)) % 128
        self.step_lanes = self.main - self.step_at
        self.side = state_columns + 2 * HEAD_SIZE
        self.window = min(length, 3 * SPAN)


def spread_heads(size):
    table = np.zeros((size.step_lanes, size.channels), np.float32)
    for head in range(size.heads):
        table[head, head * size.head_width : (head + 1) * size.head_width] = 1.0
    return table.astype(jnp.bfloat16)


def turn_tables(length):
    half = HEAD_SIZE // 2
    angle = np.arange(length, dtype=np.float64)[:, None] * rope_base ** (-np.arange(half) / half)[None]
    cosine, sine = np.cos(angle), np.sin(angle)
    return (
        np.concatenate([cosine, cosine], 1).astype(np.float32),
        np.concatenate([-sine, sine], 1).astype(np.float32),
    )


def token_flags(segments, taps):
    seg = segments[0]
    length = seg.shape[0]
    columns = [jnp.ones((length,), bool)]
    ahead = []
    for lag in range(1, taps):
        columns.append(jnp.concatenate([jnp.zeros((lag,), bool), seg[lag:] == seg[:-lag]]))
        ahead.append(jnp.concatenate([seg[lag:] == seg[:-lag], jnp.zeros((lag,), bool)]))
    ends = seg.reshape(-1, SPAN)[:, -1]
    before = jnp.concatenate([jnp.full((1,), -1, seg.dtype), ends[:-1]])
    columns.append(seg == jnp.repeat(before, SPAN))
    columns.append(seg == jnp.repeat(ends, SPAN))
    columns = columns + ahead
    return jnp.pad(jnp.stack(columns, 1).astype(jnp.float32), ((0, 0), (0, 16 - len(columns))))


def chunk_values(size, taps, main_ref, wide_ref, flags, spread, taps_ref, heads_ref, segc, segr):
    span = size.span
    pre = wide_ref[pl.ds(8, span), :] * taps_ref[0:1, :]
    for lag in range(1, taps):
        pre = pre + wide_ref[pl.ds(8 - lag, span), :] * (flags[:, lag : lag + 1] * taps_ref[lag : lag + 1, :])
    sig = jax.nn.sigmoid(pre)
    act = pre * sig
    inner = act[:, : size.channels]
    bmat = act[:, size.channels : size.channels + size.states].astype(jnp.bfloat16)
    cmat = act[:, size.channels + size.states :].astype(jnp.bfloat16)
    step_in = main_ref[:, size.step_at :] + heads_ref[0:1, :]
    step = jnp.maximum(step_in, 0.0) + jnp.log1p(jnp.exp(-jnp.abs(step_in)))
    logdec = -step * heads_ref[1:2, :]
    rows = lax.broadcasted_iota(jnp.int32, (span, span), 0)
    columns = lax.broadcasted_iota(jnp.int32, (span, span), 1)
    later = jnp.where(rows >= columns, 1.0, 0.0).astype(jnp.bfloat16)
    cumul = split_dot(logdec, later, (False, PLAIN), 3)
    inside = jnp.logical_and(rows >= columns, segc == segr)
    ending = cumul[span - 1 : span, :]
    reach = jnp.exp(cumul) * flags[:, 4:5]
    tail = jnp.exp(ending - cumul) * flags[:, 5:6]
    step_wide = split_dot(step, spread, (True, PLAIN), 2)
    scaled = inner * step_wide
    return dict(
        pre=pre, sig=sig, inner=inner, bmat=bmat, cmat=cmat, step_in=step_in, step=step, logdec=logdec, later=later,
        cumul=cumul, turned=jnp.transpose(cumul), inside=inside, step_wide=step_wide, scaled=scaled,
        scaled_b=scaled.astype(jnp.bfloat16), meeting=product(cmat, bmat, LAST),
        reach_wide=split_dot(reach, spread, (True, PLAIN), 2), tail_wide=split_dot(tail, spread, (True, PLAIN), 2),
        skip_wide=split_dot(jnp.broadcast_to(heads_ref[2:3, :], (8, size.step_lanes)), spread, (True, PLAIN), 2)[0:1],
    )


def decay_of(values, head):
    spread = values["cumul"][:, head : head + 1] - values["turned"][head : head + 1, :]
    return jnp.exp(jnp.where(values["inside"], spread, -1e30))


def softmax_of(size, query, keys, chunk, start, segc, seg_all):
    scores = product(query, keys, LAST) * (1.0 / math.sqrt(HEAD_SIZE))
    rows = lax.broadcasted_iota(jnp.int32, scores.shape, 0) + chunk * size.span
    columns = lax.broadcasted_iota(jnp.int32, scores.shape, 1) + start
    allowed = jnp.logical_and(rows >= columns, segc == seg_all)
    masked = jnp.where(allowed, scores, -1e30)
    expo = jnp.exp(masked - jnp.max(masked, axis=-1, keepdims=True))
    return expo / jnp.sum(expo, axis=-1, keepdims=True)


def mixers_forward(size, taps, main_raw, side_raw, segments, flags, tap_rows, head_rows):
    span = size.span
    per_head = size.head_width

    def kernel(
        main_ref, side_ref, segc_ref, segr_ref, flags_ref, taps_ref, heads_ref, cos_ref, sin_ref, spread_ref,
        mixed_ref, y_ref, state_ref, keys_ref, values_ref, wide, state,
    ):
        chunk = pl.program_id(0)

        @pl.when(chunk == 0)
        def _():
            wide[0:8, :] = jnp.zeros((8, size.wide), jnp.float32)
            state[...] = jnp.zeros_like(state)
            keys_ref[...] = jnp.zeros_like(keys_ref)
            values_ref[...] = jnp.zeros_like(values_ref)

        wide[pl.ds(8, span), : size.channels] = main_ref[:, size.channels : 2 * size.channels]
        wide[pl.ds(8, span), size.channels :] = side_ref[:, : 2 * size.states]
        flags, spread, segc = flags_ref[...], spread_ref[...], segc_ref[...]
        segr = segr_ref[:, pl.ds(pl.multiple_of(chunk * span, span), span)]
        val = chunk_values(size, taps, main_ref, wide, flags, spread, taps_ref, heads_ref, segc, segr)
        wide[0:8, :] = wide[pl.ds(span, 8), :]
        held = state[...]
        held_b = held.astype(jnp.bfloat16)
        state_ref[...] = held
        across = val["reach_wide"] * product(val["cmat"], held_b)
        lane = lax.broadcasted_iota(jnp.int32, (span, 2 * per_head), 1)
        for pair in range(size.heads // 2):
            where = slice(pair * 2 * per_head, (pair + 1) * 2 * per_head)
            both = []
            for head in (2 * pair, 2 * pair + 1):
                weights = (val["meeting"] * decay_of(val, head)).astype(jnp.bfloat16)
                both.append(product(weights, val["scaled_b"][:, where]))
            result = jnp.where(lane < per_head, both[0], both[1])
            result = result + across[:, where] + val["skip_wide"][:, where] * val["inner"][:, where]
            y_ref[:, where] = result
            gate = main_ref[:, where]
            mixed_ref[:, where] = (result * (gate * jax.nn.sigmoid(gate))).astype(jnp.bfloat16)
        keep = jnp.broadcast_to(val["reach_wide"][span - 1 : span, :], (1, size.channels))
        state[...] = keep * held + product(
            val["bmat"], (val["tail_wide"] * val["scaled"]).astype(jnp.bfloat16), FIRST
        )

        cosine, sine = cos_ref[...], sin_ref[...]
        own = pl.ds(pl.multiple_of(chunk * span, span), span)
        key_at = 2 * size.states
        keys_ref[own, :] = turned(side_ref[:, key_at : key_at + HEAD_SIZE], cosine, sine).astype(jnp.bfloat16)
        values_ref[own, :] = side_ref[:, key_at + HEAD_SIZE :].astype(jnp.bfloat16)
        start = pl.multiple_of(jnp.maximum(chunk + 1 - size.window // span, 0) * span, span)
        seen = pl.ds(start, size.window)
        for head in range(size.query // HEAD_SIZE):
            at = 2 * size.channels + head * HEAD_SIZE
            query = turned(main_ref[:, at : at + HEAD_SIZE], cosine, sine).astype(jnp.bfloat16)
            probs = softmax_of(size, query, keys_ref[seen, :], chunk, start, segc, segr_ref[:, seen])
            result = product(probs.astype(jnp.bfloat16), values_ref[seen, :])
            at = size.channels + head * HEAD_SIZE
            mixed_ref[:, at : at + HEAD_SIZE] = result.astype(jnp.bfloat16)

    def rows(columns):
        return pl.BlockSpec((span, columns), lambda i: (i, 0))

    def whole(array):
        return pl.BlockSpec(array.shape, lambda i: (0, 0))

    cosine, sine = turn_tables(size.length)
    spread = spread_heads(size)
    tokens = size.length
    return pl.pallas_call(
        kernel,
        grid=(size.count,),
        in_specs=[
            rows(size.main), rows(size.side), rows(1), whole(segments), rows(16), whole(tap_rows), whole(head_rows),
            rows(HEAD_SIZE), rows(HEAD_SIZE), whole(spread),
        ],
        out_specs=[
            rows(size.channels + size.query), rows(size.channels),
            pl.BlockSpec((size.states, size.channels), lambda i: (i, 0)),
            pl.BlockSpec((tokens, HEAD_SIZE), lambda i: (0, 0)), pl.BlockSpec((tokens, HEAD_SIZE), lambda i: (0, 0)),
        ],
        out_shape=[
            jax.ShapeDtypeStruct((tokens, size.channels + size.query), jnp.bfloat16),
            jax.ShapeDtypeStruct((tokens, size.channels), jnp.float32),
            jax.ShapeDtypeStruct((size.count * size.states, size.channels), jnp.float32),
            jax.ShapeDtypeStruct((tokens, HEAD_SIZE), jnp.bfloat16),
            jax.ShapeDtypeStruct((tokens, HEAD_SIZE), jnp.bfloat16),
        ],
        scratch_shapes=[
            pltpu.VMEM((span + 8, size.wide), jnp.float32),
            pltpu.VMEM((size.states, size.channels), jnp.float32),
        ],
        compiler_params=pltpu.CompilerParams(
            dimension_semantics=("arbitrary",), vmem_limit_bytes=VMEM_LIMIT
        ),
        name="mixers_forward",
    )(main_raw, side_raw, segments.reshape(tokens, 1), segments, flags, tap_rows, head_rows,
      jnp.asarray(cosine), jnp.asarray(sine), jnp.asarray(spread))


def mixers_backward(
    size, taps, grad_mixed, main_raw, side_raw, segments, flags, tap_rows, head_rows, y_value, states, keys, values
):
    span = size.span
    per_head = size.head_width
    count = size.count

    def kernel(
        grad_ref, main_ref, side_ref, before_ref, side_before_ref, segc_ref, segr_ref, flags_ref, taps_ref, heads_ref,
        cos_ref, sin_ref, spread_ref, y_ref, state_ref, keys_ref, values_ref,
        grad_main, grad_side, tap_sums, head_sums, wide, back, grad_state, grad_keys, grad_values,
    ):
        turn = pl.program_id(0)
        chunk = count - 1 - turn

        @pl.when(turn == 0)
        def _():
            back[pl.ds(span, 8), :] = jnp.zeros((8, size.wide), jnp.float32)
            grad_state[...] = jnp.zeros_like(grad_state)
            grad_keys[...] = jnp.zeros_like(grad_keys)
            grad_values[...] = jnp.zeros_like(grad_values)
            tap_sums[...] = jnp.zeros_like(tap_sums)
            head_sums[...] = jnp.zeros_like(head_sums)

        wide[0:8, : size.channels] = before_ref[...]
        wide[0:8, size.channels :] = side_before_ref[...]
        wide[pl.ds(8, span), : size.channels] = main_ref[:, size.channels : 2 * size.channels]
        wide[pl.ds(8, span), size.channels :] = side_ref[:, : 2 * size.states]
        flags, spread, segc = flags_ref[...], spread_ref[...], segc_ref[...]
        segr = segr_ref[:, pl.ds(pl.multiple_of(chunk * span, span), span)]
        val = chunk_values(size, taps, main_ref, wide, flags, spread, taps_ref, heads_ref, segc, segr)
        inner, scaled = val["inner"], val["scaled"]

        gate = main_ref[:, : size.channels]
        gate_sig = jax.nn.sigmoid(gate)
        grad = grad_ref[:, : size.channels]
        grad_main[:, : size.channels] = (grad * y_ref[...] * silu_slope(gate, gate_sig)).astype(jnp.bfloat16)
        grad_y = grad * (gate * gate_sig)
        grad_y_b = grad_y.astype(jnp.bfloat16)
        tap_sums[4:5, : size.channels] += jnp.sum(grad_y * inner, axis=0, keepdims=True)

        lane = lax.broadcasted_iota(jnp.int32, (span, 2 * per_head), 1)
        head_lane = lax.broadcasted_iota(jnp.int32, (span, size.step_lanes), 1)
        head_row = lax.broadcasted_iota(jnp.int32, (size.step_lanes, span), 0)
        grad_meeting = jnp.zeros((span, span), jnp.float32)
        by_row = jnp.zeros((span, size.step_lanes), jnp.float32)
        by_column = jnp.zeros((size.step_lanes, span), jnp.float32)
        pieces = []
        for pair in range(size.heads // 2):
            where = slice(pair * 2 * per_head, (pair + 1) * 2 * per_head)
            both = []
            for side in range(2):
                head = 2 * pair + side
                decay = decay_of(val, head)
                weights = val["meeting"] * decay
                mine = (lane < per_head) if side == 0 else (lane >= per_head)
                grad_own = jnp.where(mine, grad_y_b[:, where], jnp.zeros((), jnp.bfloat16))
                grad_weights = product(grad_own, val["scaled_b"][:, where], LAST)
                both.append(product(weights.astype(jnp.bfloat16), grad_y_b[:, where], FIRST))
                grad_meeting = grad_meeting + grad_weights * decay
                moved = grad_weights * weights
                by_row = jnp.where(head_lane == head, jnp.sum(moved, axis=1, keepdims=True), by_row)
                by_column = jnp.where(head_row == head, jnp.sum(moved, axis=0, keepdims=True), by_column)
            pieces.append(jnp.where(lane < per_head, both[0], both[1]))
        grad_scaled = jnp.concatenate(pieces, axis=1)
        grad_cumul = by_row - jnp.transpose(by_column)

        held = state_ref[...]
        held_b = held.astype(jnp.bfloat16)
        grad_held = grad_state[...]
        grad_held_b = grad_held.astype(jnp.bfloat16)
        grad_meeting_b = grad_meeting.astype(jnp.bfloat16)
        reached = val["reach_wide"] * grad_y
        reached_b = reached.astype(jnp.bfloat16)
        grad_cumul = grad_cumul + split_dot(reached * product(val["cmat"], held_b), spread, (True, LAST), 2)
        grad_c = product(reached_b, held_b, LAST) + product(grad_meeting_b, val["bmat"])
        from_state = val["tail_wide"] * product(val["bmat"], grad_held_b)
        grad_b = product(grad_meeting_b, val["cmat"], FIRST) + product(
            (val["tail_wide"] * scaled).astype(jnp.bfloat16), grad_held_b, LAST
        )
        grad_scaled = grad_scaled + from_state
        ended = split_dot(scaled * from_state, spread, (True, LAST), 2)
        keep = val["reach_wide"][span - 1 : span, :]
        kept = jnp.sum(grad_held * held, axis=0, keepdims=True) * keep
        kept = split_dot(jnp.broadcast_to(kept, (8, size.channels)), spread, (True, LAST), 2)[0:1]
        at_end = jnp.sum(ended, axis=0, keepdims=True) + kept
        grad_logdec = split_dot(grad_cumul - ended, val["later"], (False, FIRST), 3) + at_end
        grad_state[...] = keep * grad_held + product(val["cmat"], reached_b, FIRST)

        grad_inner = grad_scaled * val["step_wide"] + grad_y * val["skip_wide"]
        grad_step = split_dot(grad_scaled * inner, spread, (True, LAST), 2) - grad_logdec * heads_ref[1:2, :]
        grad_step_raw = grad_step * jax.nn.sigmoid(val["step_in"])
        head_sums[0:1, :] += jnp.sum(grad_step_raw, axis=0, keepdims=True)
        head_sums[1:2, :] += jnp.sum(grad_logdec * val["logdec"], axis=0, keepdims=True)
        grad_main[:, size.step_at :] = grad_step_raw.astype(jnp.bfloat16)

        slope = silu_slope(val["pre"], val["sig"])
        grad_pre = jnp.concatenate([grad_inner, grad_b, grad_c], axis=1) * slope
        back[pl.ds(0, span), :] = grad_pre
        raw = grad_pre * taps_ref[0:1, :]
        tap_sums[0:1, :] += jnp.sum(grad_pre * wide[pl.ds(8, span), :], axis=0, keepdims=True)
        for lag in range(1, taps):
            tap_sums[lag : lag + 1, :] += jnp.sum(
                grad_pre * (wide[pl.ds(8 - lag, span), :] * flags[:, lag : lag + 1]), axis=0, keepdims=True
            )
            raw = raw + back[pl.ds(lag, span), :] * (flags[:, 5 + lag : 6 + lag] * taps_ref[lag : lag + 1, :])
        back[pl.ds(span, 8), :] = back[0:8, :]
        grad_main[:, size.channels : 2 * size.channels] = raw[:, : size.channels].astype(jnp.bfloat16)
        grad_side[:, : 2 * size.states] = raw[:, size.channels :].astype(jnp.bfloat16)

        cosine, sine = cos_ref[...], sin_ref[...]
        start = pl.multiple_of(jnp.maximum(chunk + 1 - size.window // span, 0) * span, span)
        seen = pl.ds(start, size.window)
        seen_keys, seen_values = keys_ref[seen, :], values_ref[seen, :]
        scale = 1.0 / math.sqrt(HEAD_SIZE)
        for head in range(size.query // HEAD_SIZE):
            at = 2 * size.channels + head * HEAD_SIZE
            query = turned(main_ref[:, at : at + HEAD_SIZE], cosine, sine).astype(jnp.bfloat16)
            probs = softmax_of(size, query, seen_keys, chunk, start, segc, segr_ref[:, seen])
            out_at = size.channels + head * HEAD_SIZE
            grad_out = grad_ref[:, out_at : out_at + HEAD_SIZE].astype(jnp.bfloat16)
            grad_probs = product(grad_out, seen_values, LAST)
            delta = jnp.sum(grad_probs * probs, axis=-1, keepdims=True)
            grad_scores = (probs * (grad_probs - delta)).astype(jnp.bfloat16)
            grad_query = product(grad_scores, seen_keys) * scale
            grad_main[:, at : at + HEAD_SIZE] = turned(grad_query, cosine, -sine).astype(jnp.bfloat16)
            grad_keys[seen, :] += product(grad_scores, query, FIRST) * scale
            grad_values[seen, :] += product(probs.astype(jnp.bfloat16), grad_out, FIRST)
        own = pl.ds(pl.multiple_of(chunk * span, span), span)
        key_at = 2 * size.states
        grad_side[:, key_at : key_at + HEAD_SIZE] = turned(grad_keys[own, :], cosine, -sine).astype(jnp.bfloat16)
        grad_side[:, key_at + HEAD_SIZE :] = grad_values[own, :].astype(jnp.bfloat16)

    def rows(columns):
        return pl.BlockSpec((span, columns), lambda i: (count - 1 - i, 0))

    def previous(columns, column):
        return pl.BlockSpec((8, columns), lambda i: (jnp.maximum((count - 1 - i) * (span // 8) - 1, 0), column))

    def whole(array):
        return pl.BlockSpec(array.shape, lambda i: (0, 0))

    cosine, sine = turn_tables(size.length)
    spread = spread_heads(size)
    tokens = size.length
    return pl.pallas_call(
        kernel,
        grid=(count,),
        in_specs=[
            rows(size.channels + size.query), rows(size.main), rows(size.side), previous(size.channels, 1),
            previous(2 * size.states, 0), rows(1), whole(segments), rows(16), whole(tap_rows), whole(head_rows),
            rows(HEAD_SIZE), rows(HEAD_SIZE), whole(spread), rows(size.channels),
            pl.BlockSpec((size.states, size.channels), lambda i: (count - 1 - i, 0)), whole(keys), whole(values),
        ],
        out_specs=[
            rows(size.main), rows(size.side), pl.BlockSpec((8, size.wide), lambda i: (0, 0)),
            pl.BlockSpec((8, size.step_lanes), lambda i: (0, 0)),
        ],
        out_shape=[
            jax.ShapeDtypeStruct((tokens, size.main), jnp.bfloat16),
            jax.ShapeDtypeStruct((tokens, size.side), jnp.bfloat16),
            jax.ShapeDtypeStruct((8, size.wide), jnp.float32),
            jax.ShapeDtypeStruct((8, size.step_lanes), jnp.float32),
        ],
        scratch_shapes=[
            pltpu.VMEM((span + 8, size.wide), jnp.float32),
            pltpu.VMEM((span + 8, size.wide), jnp.float32),
            pltpu.VMEM((size.states, size.channels), jnp.float32),
            pltpu.VMEM((tokens, HEAD_SIZE), jnp.float32),
            pltpu.VMEM((tokens, HEAD_SIZE), jnp.float32),
        ],
        compiler_params=pltpu.CompilerParams(
            dimension_semantics=("arbitrary",), vmem_limit_bytes=VMEM_LIMIT
        ),
        name="mixers_backward",
    )(grad_mixed, main_raw, side_raw, main_raw, side_raw, segments.reshape(tokens, 1), segments, flags, tap_rows,
      head_rows, jnp.asarray(cosine), jnp.asarray(sine), jnp.asarray(spread), y_value, states, keys, values)


def per_device(
    nd,
    nt,
    residual,
    segments,
    mixgain,
    ffngain,
    gateproj,
    innerproj,
    stepproj,
    sharedproj,
    innerconv,
    sharedconv,
    stepbias,
    decaylog,
    skipgain,
    mixerout,
    queryproj,
    keyvalue,
    attnout,
    ffngate,
    upproj,
    downproj,
    cotangent,
):
    bfloat = jnp.bfloat16
    single = jnp.float32
    width = residual.shape[1]
    query_head_rows = queryproj.shape[1] // HEAD_SIZE
    zed = lax.axis_index("tensor")
    kv_head = zed * query_head_rows // (QUERY_HEADS // KEY_VALUE_HEADS)
    seq_count, length = segments.shape
    token_count = seq_count * length
    channels = innerproj.shape[1]
    state_columns = sharedproj.shape[1]
    heads = stepproj.shape[1]
    query_columns = queryproj.shape[1]
    ffn_columns = ffngate.shape[1]
    small_rows = sharedproj.shape[0]
    conv_rows = sharedconv.shape[0]
    taps = sharedconv.shape[1]

    gains = jnp.concatenate(
        [
            mixgain[:, None],
            ffngain[:, None],
            jnp.pad(sharedconv, ((0, small_rows - conv_rows), (0, 0))),
            jnp.zeros((small_rows, 128 - 2 - taps), bfloat),
        ],
        axis=1,
    )
    main_used = 2 * channels + query_columns + heads
    main_own = jnp.concatenate(
        [
            gateproj,
            innerproj,
            queryproj,
            stepproj,
            jnp.zeros((gateproj.shape[0], -main_used % 128), bfloat),
        ],
        axis=1,
    )
    resid_own, cot_own, resid_rows, _, common, main, out_w = first_gathers(
        nd,
        nt,
        residual,
        cotangent,
        jnp.concatenate([sharedproj, keyvalue, gains], axis=1),
        [main_own, jnp.concatenate([mixerout, attnout], axis=1)],
    )
    grad_rows = lax.all_gather(cot_own, "tensor", axis=0, tiled=True)
    extra = common[:, state_columns + keyvalue.shape[1] :]
    gain_one = extra[:, 0].astype(single)
    gain_two = extra[:, 1].astype(single)
    conv_shared = from_relative(extra[:, 2 : 2 + taps], 0, nd)
    conv_shared = conv_shared.reshape(nd * nt, small_rows, taps)[:, :conv_rows].reshape(-1, taps)
    conv_shared = conv_shared.astype(single)
    key_at = state_columns + kv_head * HEAD_SIZE
    value_at = state_columns + (KEY_VALUE_HEADS + kv_head) * HEAD_SIZE
    side = jnp.concatenate(
        [
            common[:, :state_columns],
            lax.dynamic_slice_in_dim(common, key_at, HEAD_SIZE, 1),
            lax.dynamic_slice_in_dim(common, value_at, HEAD_SIZE, 1),
        ],
        axis=1,
    )

    normed = rmsnorm(resid_rows.astype(single), gain_one).astype(bfloat)
    main_raw = matrix_product(normed, main)
    side_raw = matrix_product(normed, side)
    size = Sizes(channels, state_columns, query_columns, heads, length)
    flags = token_flags(segments, taps)
    tap_rows = jnp.concatenate([innerconv.astype(single), conv_shared]).T
    tap_rows = jnp.pad(tap_rows, ((0, 8 - taps), (0, 0)))
    head_rows = jnp.stack([stepbias.astype(single), jnp.exp(decaylog.astype(single)), skipgain.astype(single)])
    head_rows = jnp.pad(head_rows, ((0, 5), (0, size.step_lanes - heads)))
    mixed_in, y_value, states, keys, values = mixers_forward(
        size, taps, main_raw, side_raw, segments, flags, tap_rows, head_rows
    )
    mix_part = contract_last(mixed_in, out_w).astype(bfloat)
    middle, rows_two, ffn_w = middle_rows(
        nd,
        nt,
        mix_part,
        resid_own,
        gain_two[None],
        [jnp.concatenate([ffngate, upproj, downproj], axis=1)],
    )
    gate_up_w = ffn_w[:, : 2 * ffn_columns]
    down_w = ffn_w[:, 2 * ffn_columns :]
    gate_up = matrix_product(rows_two, gate_up_w)
    gate = gate_up[:, :ffn_columns]
    upper = gate_up[:, ffn_columns:]
    sigma = jax.nn.sigmoid(gate)
    hidden = (gate * sigma * upper).astype(bfloat)
    grad_hidden = matrix_product(grad_rows, down_w)
    grad_gate = (grad_hidden * upper * sigma * (1.0 + gate * (1.0 - sigma))).astype(bfloat)
    grad_upper = (grad_hidden * gate * sigma).astype(bfloat)
    grad_gate_up = jnp.concatenate([grad_gate, grad_upper], axis=1)
    two_part = contract_last(grad_gate_up, gate_up_w).astype(bfloat)
    grad_middle, grad_gain_two, grad_mix_rows, down_g, gate_up_g = middle_back(
        nd,
        nt,
        two_part,
        middle,
        cot_own,
        gain_two[None],
        [
            contract_leading_axis(grad_rows, hidden).astype(bfloat),
            contract_leading_axis(rows_two, grad_gate_up).astype(bfloat),
        ],
    )
    ffn_part = after(contract_last(hidden, down_w).astype(bfloat), grad_mix_rows)
    ffn_out = lax.psum_scatter(ffn_part, "tensor", scatter_dimension=0, tiled=True)
    layer_out = from_relative(middle + ffn_out.astype(single), 1, nd)
    grad_mixed_in = matrix_product(grad_mix_rows, out_w)
    grad_main, grad_side, tap_sums, head_sums = mixers_backward(
        size, taps, grad_mixed_in, main_raw, side_raw, segments, flags, tap_rows, head_rows, y_value, states, keys, values
    )
    one_part = (contract_last(grad_main, main) + contract_last(grad_side, side)).astype(bfloat)
    small = jnp.concatenate(
        [
            jnp.zeros((width,), single),
            grad_gain_two[0],
            tap_sums[:taps, channels:].reshape(-1),
            tap_sums[:taps, :channels].reshape(-1),
            tap_sums[4, :channels],
            head_sums[:2].reshape(-1),
        ]
    )
    shared_length = 2 * width + taps * state_columns
    small = jnp.pad(small, (0, -small.shape[0] % 1024)).reshape(-1, 128)
    grad_residual, small, common_g, main_g, out_g = last_sums(
        nd,
        nt,
        one_part,
        resid_rows,
        resid_own,
        grad_middle,
        gain_one[None],
        small,
        shared_length // 128,
        [
            contract_leading_axis(normed, grad_main).astype(bfloat),
            contract_leading_axis(grad_mix_rows, mixed_in).astype(bfloat),
        ],
        contract_leading_axis(normed, grad_side).astype(bfloat),
    )
    small = small.reshape(-1)
    place = lax.axis_index("dp") * nt + zed
    gain_one_g = lax.dynamic_slice_in_dim(small, place * small_rows, small_rows, 0)
    gain_two_g = lax.dynamic_slice_in_dim(small, width + place * small_rows, small_rows, 0)
    conv_g = lax.dynamic_slice_in_dim(
        small[2 * width : shared_length].reshape(taps, -1), place * conv_rows, conv_rows, 1
    ).T
    local = small[shared_length:]
    skip_at = taps * channels
    head_at = skip_at + channels
    return (
        layer_out,
        grad_residual,
        gain_one_g,
        gain_two_g,
        main_g[:, :channels],
        main_g[:, channels : 2 * channels],
        main_g[:, 2 * channels + query_columns : main_used],
        common_g[:, :state_columns],
        local[:skip_at].reshape(taps, channels).T,
        conv_g,
        local[head_at : head_at + heads],
        local[head_at + size.step_lanes : head_at + size.step_lanes + heads],
        local[skip_at:head_at].reshape(heads, -1).sum(axis=1),
        out_g[:, :channels],
        main_g[:, 2 * channels : 2 * channels + query_columns],
        common_g[:, state_columns:],
        out_g[:, channels:],
        gate_up_g[:, :ffn_columns],
        gate_up_g[:, ffn_columns:],
        down_g,
    )


def solution(mesh):
    return jax.shard_map(
        functools.partial(per_device, mesh.shape["dp"], mesh.shape["tensor"]),
        mesh=mesh,
        in_specs=(
            P(("dp", "tensor"), None),
            P("dp", None),
            P(("dp", "tensor")),
            P(("dp", "tensor")),
            P("dp", "tensor"),
            P("dp", "tensor"),
            P("dp", "tensor"),
            P(("dp", "tensor"), None),
            P("tensor", None),
            P(("dp", "tensor"), None),
            P("tensor"),
            P("tensor"),
            P("tensor"),
            P("dp", "tensor"),
            P("dp", "tensor"),
            P(("dp", "tensor"), None),
            P("dp", "tensor"),
            P("dp", "tensor"),
            P("dp", "tensor"),
            P("dp", "tensor"),
            P(("dp", "tensor"), None),
        ),
        out_specs=(
            P(("dp", "tensor"), None),
            P(("dp", "tensor"), None),
            P(("dp", "tensor")),
            P(("dp", "tensor")),
            P("dp", "tensor"),
            P("dp", "tensor"),
            P("dp", "tensor"),
            P(("dp", "tensor"), None),
            P("tensor", None),
            P(("dp", "tensor"), None),
            P("tensor"),
            P("tensor"),
            P("tensor"),
            P("dp", "tensor"),
            P("dp", "tensor"),
            P(("dp", "tensor"), None),
            P("dp", "tensor"),
            P("dp", "tensor"),
            P("dp", "tensor"),
            P("dp", "tensor"),
        ),
        check_vma=False,
    )
```

```python
import functools
import math

import jax
import jax.numpy as jnp
import numpy as np
from jax import lax
from jax.experimental import pallas as pl
from jax.experimental.pallas import tpu as pltpu
from jax.sharding import PartitionSpec as P

QUERY_HEADS = 8
KEY_VALUE_HEADS = 2
HEAD_SIZE = 128
SPAN = 256


eps = 1e-05
rope_base = 10000.0


def matrix_product(left, right):
    return jnp.dot(left, right, preferred_element_type=jnp.float32)


def contract_leading_axis(left, right):
    return lax.dot_general(
        left, right, (((0,), (0,)), ((), ())), preferred_element_type=jnp.float32
    )


def contract_last(left, right):
    return lax.dot_general(
        left, right, (((1,), (1,)), ((), ())), preferred_element_type=jnp.float32
    )


def bit_orders(size):
    high = list(range(size.bit_length() - 2, 0, -1))
    return high, high[:2][::-1] + high[2:]


def relative_blocks(size):
    both = []
    for half, order in enumerate(bit_orders(size)):
        chain = [0]
        for bit in order:
            chain = chain + [other ^ (1 << bit) for other in chain]
        both = both + [(other, half) for other in chain]
    return both + [(other ^ 1, half) for other, half in both]


def to_relative(value, axis, size):
    me = lax.axis_index("dp")
    width = value.shape[axis] // (2 * size)
    return jnp.concatenate(
        [
            lax.dynamic_slice_in_dim(value, ((me ^ other) * 2 + half) * width, width, axis)
            for other, half in relative_blocks(size)
        ],
        axis,
    )


def from_relative(value, axis, size):
    me = lax.axis_index("dp")
    width = value.shape[axis] // (2 * size)
    blocks = relative_blocks(size)
    place = jnp.asarray([blocks.index((other, half)) for other in range(size) for half in range(2)], jnp.int32)
    return jnp.concatenate(
        [
            lax.dynamic_slice_in_dim(value, place[(me ^ number) * 2 + half] * width, width, axis)
            for number in range(size)
            for half in range(2)
        ],
        axis,
    )


def after(value, *others):
    return lax.optimization_barrier((value,) + others)[0]


MESH = pl.DeviceIdType.MESH
VMEM_LIMIT = 56 * 1024 * 1024


def flip(value, bit):
    unit = 1 << bit
    return value + unit * (1 - 2 * ((value // unit) % 2))


def mixed_with(value, other, bits):
    for bit in range(bits):
        if (other >> bit) & 1:
            value = flip(value, bit)
    return value


def enter(nt, bits):
    me, zed = lax.axis_index("dp"), lax.axis_index("tensor")
    barrier = pltpu.get_barrier_semaphore()
    for other in range(nt):

        @pl.when(zed != other)
        def _(other=other):
            pl.semaphore_signal(barrier, inc=1, device_id=(me, other), device_id_type=MESH)

    for bit in range(bits):
        pl.semaphore_signal(barrier, inc=1, device_id=(flip(me, bit), zed), device_id_type=MESH)
    pl.semaphore_wait(barrier, bits + nt - 1)
    return me, zed


def aligned(start, size):
    return pl.ds(pl.multiple_of(start, 16), size)


def together(*flows):
    flows = [list(flow) for flow in flows]
    order = sorted(
        ((place + 0.5) / len(flow), number, place)
        for number, flow in enumerate(flows)
        for place in range(len(flow))
    )
    for _, number, place in order:
        flows[number][place]()


def gather_steps(nd, me, zed, own, everything, send, recv, local):
    half = own.shape[0] // 2
    blocks = relative_blocks(nd)
    place = {block: number for number, block in enumerate(blocks)}

    def rows(block):
        return everything.at[pl.ds(place[block] * half, half)]

    def source(block):
        return own.at[pl.ds(block[1] * half, half)] if block[0] == 0 else rows(block)

    hops = []
    for part, order in enumerate(bit_orders(nd)):
        chain = [0]
        for bit in order:
            hops = hops + [((other, part), bit) for other in chain]
            chain = chain + [other ^ (1 << bit) for other in chain]
    hops = hops + [(block, 0) for block in blocks[:nd]]

    def copy(number):
        block, bit = hops[number]
        landed = (block[0] ^ (1 << bit), block[1])
        return pltpu.make_async_remote_copy(
            src_ref=source(block),
            dst_ref=rows(landed),
            send_sem=send.at[number],
            recv_sem=recv.at[place[landed]],
            device_id=(flip(me, bit), zed),
            device_id_type=MESH,
        )

    def arrival(block):
        return pltpu.make_async_remote_copy(
            src_ref=rows(block),
            dst_ref=rows(block),
            send_sem=send.at[0],
            recv_sem=recv.at[place[block]],
            device_id=(flip(me, 0), zed),
            device_id_type=MESH,
        )

    def begin():
        for number, (block, bit) in enumerate(hops):
            if block[0] == 0:
                copy(number).start()
        for part in range(2):
            pltpu.make_async_copy(source((0, part)), rows((0, part)), local.at[part]).start()

    def forward(block):
        def step():
            arrival(block).wait_recv()
            for number, (origin, bit) in enumerate(hops):
                if origin == block:
                    copy(number).start()

        return step

    def end():
        for block in blocks[nd:]:
            arrival(block).wait_recv()
        for number in range(len(hops)):
            copy(number).wait_send()
        for part in range(2):
            pltpu.make_async_copy(source((0, part)), rows((0, part)), local.at[part]).wait()

    first, second = blocks[1 : nd // 2], blocks[nd // 2 + 1 : nd]
    middle = [forward(block) for pair in zip(first, second) for block in pair]
    return [begin] + middle + [end]


def gather_hops(nd):
    return 2 * (nd // 2 - 1) + nd


def gather_semaphores(nd):
    return [
        pltpu.SemaphoreType.DMA((gather_hops(nd),)),
        pltpu.SemaphoreType.DMA((2 * nd,)),
        pltpu.SemaphoreType.DMA((2,)),
    ]


def each_rows(rows, body, unit=16):
    def step(number, carry):
        body(aligned(number * unit, unit))
        return carry

    lax.fori_loop(0, rows // unit, step, 0)


def scatter_steps(nd, me, zed, parts, total, mine, held, landed, core_send, core_recv, send, recv, local):
    half = total.shape[0] // 2
    chain_length = nd // 2

    def piece(ref, number):
        return ref.at[pl.ds(number * half, half)]

    rounds, slot = [], 0
    for part, order in enumerate(bit_orders(nd)):
        length, own_rounds = chain_length, []
        for bit in order[::-1]:
            length = length // 2
            own_rounds.append((bit, length, slot))
            slot = slot + length
        rounds.append(own_rounds)

    def core_copy(number):
        return pltpu.make_async_remote_copy(
            src_ref=piece(parts, nd + number),
            dst_ref=piece(held, number),
            send_sem=core_send.at[number],
            recv_sem=core_recv.at[number],
            device_id=(flip(me, 0), zed),
            device_id_type=MESH,
        )

    def hop(part, bit, number, where):
        return pltpu.make_async_remote_copy(
            src_ref=piece(held, number),
            dst_ref=piece(landed, where),
            send_sem=send.at[where],
            recv_sem=recv.at[where],
            device_id=(flip(me, bit), zed),
            device_id_type=MESH,
        )

    wanted = []
    for number in range(chain_length - 1, -1, -1):
        wanted = wanted + [number, chain_length + number]

    def load(number):
        return pltpu.make_async_copy(piece(parts, number), piece(mine, number), local.at[number])

    def begin():
        for number in wanted:
            core_copy(number).start()
        for number in wanted:
            load(number).start()

    def core_sum(number):
        part, spot = number // chain_length, number % chain_length

        def step():
            load(number).wait()
            core_copy(number).wait_recv()

            def body(rows):
                spot_rows = piece(held, number)
                spot_rows[rows] = spot_rows[rows] + piece(mine, number)[rows]

            each_rows(half, body)
            if rounds[part]:
                bit, length, first = rounds[part][0]
                if spot >= length:
                    hop(part, bit, number, first + spot - length).start()

        return step

    def later_sum(part, turn, spot):
        bit, length, first = rounds[part][turn]
        number = part * chain_length + spot

        def step():
            hop(part, bit, number, first + spot).wait_recv()
            last = turn == len(rounds[part]) - 1

            def body(rows):
                kept, came = piece(held, number)[rows], piece(landed, first + spot)[rows]
                if last:
                    piece(total, part)[rows] = kept.astype(jnp.float32) + came.astype(jnp.float32)
                else:
                    piece(held, number)[rows] = kept + came

            each_rows(half, body)
            if not last:
                next_bit, next_length, next_first = rounds[part][turn + 1]
                if spot >= next_length:
                    hop(part, next_bit, number, next_first + spot - next_length).start()

        return step

    stages = [[core_sum(number) for number in wanted]]
    for turn in range(len(rounds[0])):
        length = rounds[0][turn][1]
        stages.append([later_sum(part, turn, spot) for spot in range(length - 1, -1, -1) for part in range(2)])

    def end():
        for number in range(nd):
            core_copy(number).wait_send()
        for part in range(2):
            for bit, length, first in rounds[part]:
                for spot in range(length):
                    hop(part, bit, part * chain_length + length + spot, first + spot).wait_send()

    return [[begin]] + stages + [[end]]


def staggered(flows):
    steps = [step for flow in flows for step in flow[0]]
    depth = len(flows[0]) - 2
    for turn in range(depth + len(flows) - 1):
        for number in range(len(flows) - 1, -1, -1):
            if 0 <= turn - number < depth:
                steps = steps + flows[number][1 + turn - number]
    return steps + [step for flow in flows for step in flow[-1]]


def scatter_scratch(nd, rows, columns):
    slots = nd - 2
    return [
        pltpu.VMEM((nd * rows // 2, columns), jnp.bfloat16),
        pltpu.VMEM((nd * rows // 2, columns), jnp.bfloat16),
        pltpu.VMEM((slots * rows // 2, columns), jnp.bfloat16),
        pltpu.SemaphoreType.DMA((nd,)),
        pltpu.SemaphoreType.DMA((nd,)),
        pltpu.SemaphoreType.DMA((slots,)),
        pltpu.SemaphoreType.DMA((slots,)),
        pltpu.SemaphoreType.DMA((nd,)),
    ]


def line_gather(nt, me, zed, chunks, own, everything, send, recv):
    size = own.shape[0] // chunks

    def own_rows(chunk):
        return own.at[pl.ds(chunk * size, size)]

    def rows(block, chunk):
        return everything.at[aligned(block * (size * chunks) + chunk * size, size)]

    def copy(source, block, chunk, side):
        return pltpu.make_async_remote_copy(
            src_ref=source,
            dst_ref=rows(block, chunk),
            send_sem=send.at[side, block, chunk],
            recv_sem=recv.at[block, chunk],
            device_id=(me, zed + 1 - 2 * side),
            device_id_type=MESH,
        )

    def keep(chunk):
        return pltpu.make_async_copy(own_rows(chunk), rows(zed, chunk), recv.at[zed, chunk])

    def first(chunk):
        for side, condition in ((0, zed < nt - 1), (1, zed > 0)):

            @pl.when(condition)
            def _(side=side):
                copy(own_rows(chunk), zed, chunk, side).start()

        keep(chunk).start()

    def onward(chunk, distance):
        for side, block in ((0, zed - distance), (1, zed + distance)):
            inside = (block >= 0) if side == 0 else (block < nt)
            open_end = (zed < nt - 1) if side == 0 else (zed > 0)

            @pl.when(inside)
            def _(block=block, side=side):
                copy(rows(block, chunk), block, chunk, side).wait_recv()

            @pl.when(jnp.logical_and(inside, open_end))
            def _(block=block, side=side):
                copy(rows(block, chunk), block, chunk, side).start()

    def end(chunk):
        keep(chunk).wait()
        for side, condition in ((0, zed < nt - 1), (1, zed > 0)):

            @pl.when(condition)
            def _(side=side):
                copy(own_rows(chunk), zed, chunk, side).wait_send()

            for distance in range(1, nt - 1):
                block = zed - distance if side == 0 else zed + distance
                inside = (block >= 0) if side == 0 else (block < nt)

                @pl.when(jnp.logical_and(inside, condition))
                def _(block=block, side=side):
                    copy(rows(block, chunk), block, chunk, side).wait_send()

    return first, onward, end


def line_gather_semaphores(nt, chunks):
    return [pltpu.SemaphoreType.DMA((2, nt, chunks)), pltpu.SemaphoreType.DMA((nt, chunks))]


def line_reduce(nt, me, zed, chunks, parts, rising, falling, send, recv):
    block_rows = parts.shape[0] // nt
    size = block_rows // chunks
    sides = ((0, rising), (1, falling))

    def rows(block, chunk):
        return aligned(block * block_rows + chunk * size, size)

    def copy(source, side, held, block, chunk):
        return pltpu.make_async_remote_copy(
            src_ref=source.at[rows(block, chunk)],
            dst_ref=held.at[rows(block, chunk)],
            send_sem=send.at[side, block, chunk],
            recv_sem=recv.at[side, block, chunk],
            device_id=(me, zed + 1 - 2 * side),
            device_id_type=MESH,
        )

    def role(side, turn):
        away = nt - 1 - turn
        if side == 0:
            return zed + away, zed + away < nt, zed == 0
        return zed - away, zed - away >= 0, zed == nt - 1

    def pass_on(chunk, turn):
        for side, held in sides:
            block, active, source = role(side, turn)

            @pl.when(jnp.logical_and(active, source))
            def _(side=side, held=held, block=block):
                copy(parts, side, held, block, chunk).start()

            @pl.when(jnp.logical_and(active, jnp.logical_not(source)))
            def _(side=side, held=held, block=block):
                copy(held, side, held, block, chunk).wait_recv()

                def body(inner):
                    where = aligned(block * block_rows + chunk * size + inner.start, inner.size)
                    held[where] = parts[where] + held[where]

                each_rows(size, body)
                copy(held, side, held, block, chunk).start()

    def own_sum(chunk, total):
        where = rows(zed, chunk)
        total[...] = parts[where].astype(jnp.float32)
        for side, held in sides:

            @pl.when(zed > 0 if side == 0 else zed < nt - 1)
            def _(side=side, held=held):
                copy(held, side, held, zed, chunk).wait_recv()
                total[...] += held[where].astype(jnp.float32)

    def end(chunk):
        for turn in range(nt - 1):
            for side, held in sides:
                block, active, source = role(side, turn)

                @pl.when(active)
                def _(side=side, held=held, block=block):
                    copy(held, side, held, block, chunk).wait_send()

    return pass_on, own_sum, end


def line_reduce_scratch(nt, block_rows, columns, chunks):
    return [
        pltpu.VMEM((nt * block_rows, columns), jnp.bfloat16),
        pltpu.VMEM((nt * block_rows, columns), jnp.bfloat16),
        pltpu.VMEM((block_rows // chunks, columns), jnp.float32),
        pltpu.SemaphoreType.DMA((2, nt, chunks)),
        pltpu.SemaphoreType.DMA((2, nt, chunks)),
    ]


HBM = pl.BlockSpec(memory_space=pl.ANY)
ONCHIP = pl.BlockSpec(memory_space=pltpu.VMEM)


def near_first(nt, zed, turn):
    block = 0
    for mine in range(nt):
        order = sorted(range(nt), key=lambda other: (abs(other - mine), other))
        block = block + jnp.where(zed == mine, order[turn], 0)
    return block


def first_gathers(nd, nt, rows, grad, small, main_own, out_own, shared_columns):
    chunks = 4
    bits = nd.bit_length() - 1
    blocks = relative_blocks(nd)
    block_rows, width = rows.shape
    lane = width // len(blocks)
    if lane % 128:
        rows, grad = to_relative(rows, 1, nd), to_relative(grad, 1, nd)
    main_columns, small_columns = main_own.shape[1], small.shape[1]
    side_columns = shared_columns + 2 * HEAD_SIZE
    gains_at = shared_columns + 2 * KEY_VALUE_HEADS * HEAD_SIZE
    tile = 256

    def reorder(me, source, target):
        if lane % 128:
            target[...] = source[...]
            return
        for number, (other, part) in enumerate(blocks):
            start = (mixed_with(me, other, bits) * 2 + part) * lane
            target[:, number * lane : (number + 1) * lane] = source[:, pl.ds(pl.multiple_of(start, lane), lane)]

    def kernel(
        rows_in, grad_in, small_ref, main_ref, out_ref,
        rows_ref, grad_ref, gains_ref, normed_all, small_line, main_all, side_all, out_all, main_raw, side_raw,
        row_space, normed, main_space, small_space, side_space, main_stage, side_stage, store_sems, *refs,
    ):
        row_sems, small_sems = refs[:2], refs[2:4]
        main_sems, small_dp, out_sems = refs[4:7], refs[7:10], refs[10:13]
        me, zed = enter(nt, bits)
        small_first, small_onward, small_end = line_gather(nt, me, zed, 1, small_ref, small_line, *small_sems)
        row_first, row_onward, row_end = line_gather(nt, me, zed, chunks, rows_ref, row_space, *row_sems)
        main_flow = gather_steps(nd, me, zed, main_ref, main_space, *main_sems)
        small_flow = gather_steps(nd, me, zed, small_line, small_space, *small_dp)
        out_flow = gather_steps(nd, me, zed, out_ref, out_all, *out_sems)
        head = zed * (QUERY_HEADS // nt) // (QUERY_HEADS // KEY_VALUE_HEADS)

        def columns(turn):
            if turn == 0:
                return small_space.at[:, pl.ds(0, shared_columns)], side_space.at[:, pl.ds(0, shared_columns)]
            start = shared_columns + ((turn - 1) * KEY_VALUE_HEADS + head) * HEAD_SIZE
            target = shared_columns + (turn - 1) * HEAD_SIZE
            return (
                small_space.at[:, pl.ds(pl.multiple_of(start, HEAD_SIZE), HEAD_SIZE)],
                side_space.at[:, pl.ds(target, HEAD_SIZE)],
            )

        def keep(number):
            source, target = ((main_space, main_all), (side_space, side_all), (normed, normed_all))[number]
            return pltpu.make_async_copy(source, target, store_sems.at[number])

        def pick(turn):
            return pltpu.make_async_copy(*columns(turn), store_sems.at[3 + turn])

        def store(turn, number):
            block = near_first(nt, zed, turn)
            stage, target = ((main_stage, main_raw), (side_stage, side_raw))[number]
            return pltpu.make_async_copy(
                stage.at[turn % 2],
                target.at[aligned(block * block_rows, block_rows)],
                store_sems.at[6 + 2 * turn + number],
            )

        def project(turn):
            where = aligned(near_first(nt, zed, turn) * block_rows, block_rows)
            value = (rows_ref[...] if turn == 0 else row_space[where]).astype(jnp.float32)
            scale = lax.rsqrt(jnp.mean(value * value, axis=-1, keepdims=True) + eps)
            mine = (value * scale * gains_ref[0:1]).astype(jnp.bfloat16)
            normed[where] = mine
            if turn >= 2:
                store(turn - 2, 0).wait()
                store(turn - 2, 1).wait()
            for space, stage, number in ((main_space, main_stage, 0), (side_space, side_stage, 1)):
                for start in range(0, space.shape[1], tile):
                    extent = slice(start, min(start + tile, space.shape[1]))
                    stage[turn % 2, :, extent] = jnp.dot(
                        mine, space[:, extent], preferred_element_type=jnp.float32
                    )
                store(turn, number).start()

        small_first(0)
        main_flow[0]()
        reorder(me, rows_in, rows_ref)
        for chunk in range(chunks):
            row_first(chunk)
        for distance in range(1, nt):
            small_onward(0, distance)
        small_end(0)
        small_flow[0]()
        out_flow[0]()
        reorder(me, grad_in, grad_ref)
        near = [
            functools.partial(row_onward, chunk, distance) for distance in range(1, nt - 1) for chunk in range(chunks)
        ]
        together(near, main_flow[1:-1] + small_flow[1:-1])
        small_flow[-1]()
        for turn in range(3):
            pick(turn).start()
        for start in range(0, width, 128):
            turned_block = jnp.transpose(
                small_space[start : start + 128, gains_at : gains_at + 128].astype(jnp.float32)
            )
            gains_ref[:, start : start + 128] = turned_block[:8]
        main_flow[-1]()
        keep(0).start()
        for turn in range(3):
            pick(turn).wait()
        keep(1).start()

        def last_rows():
            for chunk in range(chunks):
                row_onward(chunk, nt - 1)

        compute = [functools.partial(project, turn) for turn in range(nt - 1)] + [last_rows]
        together(compute, out_flow[1:-1])
        project(nt - 1)
        keep(2).start()
        out_flow[-1]()
        for chunk in range(chunks):
            row_end(chunk)
        for turn in range(max(nt - 2, 0), nt):
            store(turn, 0).wait()
            store(turn, 1).wait()
        for number in range(3):
            keep(number).wait()

    def sized(array, times, dtype=None):
        return jax.ShapeDtypeStruct((array.shape[0] * times, array.shape[1]), dtype or array.dtype)

    tokens = block_rows * nt
    return pl.pallas_call(
        kernel,
        out_shape=[
            sized(rows, 1),
            sized(grad, 1),
            jax.ShapeDtypeStruct((8, width), jnp.float32),
            sized(rows, nt),
            sized(small, nt),
            sized(main_own, nd),
            jax.ShapeDtypeStruct((width, side_columns), small.dtype),
            sized(out_own, nd),
            jax.ShapeDtypeStruct((tokens, main_columns), jnp.float32),
            jax.ShapeDtypeStruct((tokens, side_columns), jnp.float32),
        ],
        in_specs=[ONCHIP] * 2 + [HBM] * 3,
        out_specs=[ONCHIP] * 3 + [HBM] * 7,
        scratch_shapes=[
            pltpu.VMEM((tokens, width), jnp.bfloat16),
            pltpu.VMEM((tokens, width), jnp.bfloat16),
            pltpu.VMEM((width, main_columns), jnp.bfloat16),
            pltpu.VMEM((width, small_columns), jnp.bfloat16),
            pltpu.VMEM((width, side_columns), jnp.bfloat16),
            pltpu.VMEM((2, block_rows, main_columns), jnp.float32),
            pltpu.VMEM((2, block_rows, side_columns), jnp.float32),
            pltpu.SemaphoreType.DMA((6 + 2 * nt,)),
        ]
        + line_gather_semaphores(nt, chunks)
        + line_gather_semaphores(nt, 1)
        + gather_semaphores(nd) * 3,
        compiler_params=pltpu.CompilerParams(
            collective_id=0, has_side_effects=True, vmem_limit_bytes=VMEM_LIMIT
        ),
        name="first_gathers",
    )(rows, grad, small, main_own, out_own)


def middle_rows(nd, nt, parts, resid, gain, groups):
    chunks = 4
    bits = nd.bit_length() - 1
    count = len(groups)
    block_rows, width = resid.shape
    size = block_rows // chunks

    def kernel(parts_ref, resid_ref, gain_ref, *refs):
        group_refs, refs = refs[:count], refs[count:]
        middle_ref, rows_all = refs[:2]
        group_all, refs = refs[2 : 2 + count], refs[2 + count :]
        own, rising, falling, total, send, recv = refs[:6]
        gather_sems, refs = refs[6:8], refs[8:]
        me, zed = enter(nt, bits)
        pass_on, own_sum, reduce_end = line_reduce(nt, me, zed, chunks, parts_ref, rising, falling, send, recv)
        first, onward, gather_end = line_gather(nt, me, zed, chunks, own, rows_all, *gather_sems)
        flows = [
            gather_steps(nd, me, zed, group_refs[n], group_all[n], *refs[3 * n : 3 * n + 3]) for n in range(count)
        ]

        def finish(chunk):
            own_sum(chunk, total)
            where = pl.ds(chunk * size, size)
            value = resid_ref[where].astype(jnp.float32) + total[...]
            middle_ref[where] = value
            scale = lax.rsqrt(jnp.mean(value * value, axis=-1, keepdims=True) + eps)
            own[where] = (value * scale * gain_ref[...]).astype(jnp.bfloat16)
            first(chunk)

        line_schedule(nt, chunks, pass_on, finish, onward, [step for flow in flows for step in flow])
        for chunk in range(chunks):
            reduce_end(chunk)
            gather_end(chunk)

    return pl.pallas_call(
        kernel,
        out_shape=[
            jax.ShapeDtypeStruct((block_rows, width), jnp.float32),
            jax.ShapeDtypeStruct((block_rows * nt, width), jnp.bfloat16),
        ]
        + [jax.ShapeDtypeStruct((group.shape[0] * nd, group.shape[1]), group.dtype) for group in groups],
        in_specs=[ONCHIP] * 3 + [HBM] * count,
        out_specs=[ONCHIP] + [HBM] * (1 + count),
        scratch_shapes=[pltpu.VMEM((block_rows, width), jnp.bfloat16)]
        + line_reduce_scratch(nt, block_rows, width, chunks)
        + line_gather_semaphores(nt, chunks)
        + gather_semaphores(nd) * count,
        compiler_params=pltpu.CompilerParams(
            collective_id=1, has_side_effects=True, vmem_limit_bytes=VMEM_LIMIT
        ),
        name="middle_rows",
    )(parts, resid, gain, *groups)


def line_schedule(nt, chunks, pass_on, finish, onward, others):
    steps = []

    def add(function, chunk, *rest):
        if function is not None and 0 <= chunk < chunks:
            steps.append(functools.partial(function, chunk, *rest))

    for chunk in range(chunks + 2):
        add(pass_on, chunk, 0)
        add(finish, chunk - 1)
        add(onward, chunk - 2, nt - 1)
        for turn in range(1, nt - 1):
            add(pass_on, chunk, turn)
            add(onward, chunk - 1, turn)
    together(steps, others)


def absolute_lanes(me, bits, blocks, source, target):
    lane = source.shape[1] // len(blocks)
    for number, (other, part) in enumerate(blocks):
        start = (mixed_with(me, other, bits) * 2 + part) * lane
        target[:, pl.ds(pl.multiple_of(start, lane), lane)] = source[:, number * lane : (number + 1) * lane]


def norm_pull(value, gain, grad):
    scale = lax.rsqrt(jnp.mean(value * value, axis=-1, keepdims=True) + eps)
    scaled = grad * gain
    inner = jnp.mean(scaled * value, axis=-1, keepdims=True)
    return scale * (scaled - value * (inner * scale * scale)), grad * value * scale


def middle_back(nd, nt, parts, middle, cot, gain, groups):
    chunks = 4
    bits = nd.bit_length() - 1
    count = len(groups)
    block_rows, width = middle.shape
    size = block_rows // chunks
    per_group = 8
    blocks = relative_blocks(nd)
    lane = width // len(blocks)

    def kernel(parts_ref, middle_ref, cot_ref, gain_ref, *refs):
        group_refs, refs = refs[:count], refs[count:]
        grad_ref, gain_out, rows_all = refs[:3]
        totals, refs = refs[3 : 3 + count], refs[3 + count :]
        own, gain_grad, rising, falling, total, send, recv = refs[:7]
        gather_sems, refs = refs[7:9], refs[9:]
        me, zed = enter(nt, bits)
        pass_on, own_sum, reduce_end = line_reduce(nt, me, zed, chunks, parts_ref, rising, falling, send, recv)
        first, onward, gather_end = line_gather(nt, me, zed, chunks, own, rows_all, *gather_sems)
        flows = [
            scatter_steps(nd, me, zed, group_refs[n], totals[n], *refs[per_group * n : per_group * (n + 1)])
            for n in range(count)
        ]
        gain_grad[...] = jnp.zeros_like(gain_grad)

        def finish(chunk):
            own_sum(chunk, total)
            where = pl.ds(chunk * size, size)
            through, gained = norm_pull(middle_ref[where], gain_ref[...], total[...])
            value = cot_ref[where].astype(jnp.float32) + through
            gain_grad[...] += jnp.sum(gained, axis=0, keepdims=True)
            grad_ref[where] = value
            own[where] = value.astype(jnp.bfloat16)
            first(chunk)

        line_schedule(nt, chunks, pass_on, finish, onward, staggered(flows))
        if lane % 128:
            gain_out[...] = gain_grad[...]
        else:
            absolute_lanes(me, bits, blocks, gain_grad, gain_out)
        for chunk in range(chunks):
            reduce_end(chunk)
            gather_end(chunk)

    scratch = []
    for group in groups:
        scratch = scratch + scatter_scratch(nd, group.shape[0] // nd, group.shape[1])
    results = pl.pallas_call(
        kernel,
        out_shape=[
            jax.ShapeDtypeStruct((block_rows, width), jnp.float32),
            jax.ShapeDtypeStruct((1, width), jnp.float32),
            jax.ShapeDtypeStruct((block_rows * nt, width), jnp.bfloat16),
        ]
        + [jax.ShapeDtypeStruct((group.shape[0] // nd, group.shape[1]), jnp.float32) for group in groups],
        in_specs=[ONCHIP] * 4 + [HBM] * count,
        out_specs=[ONCHIP, ONCHIP, HBM] + [ONCHIP] * count,
        scratch_shapes=[pltpu.VMEM((block_rows, width), jnp.bfloat16), pltpu.VMEM((1, width), jnp.float32)]
        + line_reduce_scratch(nt, block_rows, width, chunks)
        + line_gather_semaphores(nt, chunks)
        + scratch,
        compiler_params=pltpu.CompilerParams(
            collective_id=2, has_side_effects=True, vmem_limit_bytes=VMEM_LIMIT
        ),
        name="middle_back",
    )(parts, middle, cot, gain, *groups)
    if lane % 128:
        results = (results[0], from_relative(results[1], 1, nd), *results[2:])
    return results


def last_sums(nd, nt, parts, normed, resid, before, gain, small, shared_rows, groups, side):
    chunks = 4
    bits, line_bits = nd.bit_length() - 1, nt.bit_length() - 1
    block_rows, width = resid.shape
    size = block_rows // chunks
    per_group = 8
    blocks = relative_blocks(nd)
    lane = width // len(blocks)
    groups = [*groups, side]
    count = len(groups)
    side_rows, side_columns = side.shape[0] // nd, side.shape[1]
    shared_columns = side_columns - 2 * HEAD_SIZE
    owned = side_rows // nt
    gain_rows = width // 128
    if lane % 128:
        own_gain = jnp.sum(parts.astype(jnp.float32) * normed.astype(jnp.float32), axis=0) / gain[0]
        own_gain = from_relative(own_gain, 0, nd)
        small = jnp.concatenate([own_gain.reshape(gain_rows, 128), small[gain_rows:]])

    def kernel(parts_ref, normed_ref, resid_ref, before_ref, gain_ref, small_ref, *refs):
        group_refs, refs = refs[:count], refs[count:]
        grad_ref, small_out, common_ref = refs[:3]
        totals, refs = refs[3 : 2 + count], refs[2 + count :]
        side_total, rising, falling, total, send, recv = refs[:6]
        sums, landed, small_send, small_recv, gain_grad = refs[6:11]
        side_out, side_in, side_send, side_recv = refs[11:15]
        refs = refs[15:]
        me, zed = enter(nt, bits)
        pass_on, own_sum, reduce_end = line_reduce(nt, me, zed, chunks, parts_ref, rising, falling, send, recv)
        totals = [*totals, side_total]
        flows = [
            scatter_steps(nd, me, zed, group_refs[n], totals[n], *refs[per_group * n : per_group * (n + 1)])
            for n in range(count)
        ]

        def gain_term(number):
            def step():
                if number == 0:
                    gain_grad[...] = jnp.zeros_like(gain_grad)

                def body(inner, carry):
                    where = aligned(number * block_rows + inner * 16, 16)
                    gain_grad[...] += parts_ref[where].astype(jnp.float32) * normed_ref[where].astype(jnp.float32)
                    return carry

                lax.fori_loop(0, block_rows // 16, body, 0)

            return step

        def gain_end():
            sums[0] = small_ref[...]
            if lane % 128 == 0:
                whole = jnp.sum(gain_grad[...], axis=0, keepdims=True) / gain_ref[...]
                for number, (other, part) in enumerate(blocks):
                    spot = mixed_with(me, other, bits) * 2 + part
                    sums[0, pl.ds(spot, 1), :] = whole[:, number * lane : (number + 1) * lane]

        def small_copy(turn):
            if turn < bits:
                device = (flip(me, turn), zed)
            else:
                device = (me, flip(zed, turn - bits))
            extent = slice(None) if turn < bits else pl.ds(0, shared_rows)
            return pltpu.make_async_remote_copy(
                src_ref=sums.at[turn, extent],
                dst_ref=landed.at[turn, extent],
                send_sem=small_send.at[turn],
                recv_sem=small_recv.at[turn],
                device_id=device,
                device_id_type=MESH,
            )

        def small_step(turn):
            def step():
                small_copy(turn).wait_recv()
                if turn < bits:
                    sums[turn + 1] = sums[turn] + landed[turn]
                else:
                    sums[turn + 1] = sums[turn]
                    sums[turn + 1, pl.ds(0, shared_rows)] = (
                        sums[turn, pl.ds(0, shared_rows)] + landed[turn, pl.ds(0, shared_rows)]
                    )
                if turn + 1 < bits + line_bits:
                    small_copy(turn + 1).start()

            return step

        def small_begin():
            gain_end()
            small_copy(0).start()

        def small_end():
            for turn in range(bits + line_bits):
                small_copy(turn).wait_send()
            small_out[...] = sums[bits + line_bits]

        few = [gain_term(number) for number in range(nt if lane % 128 == 0 else 0)]
        few = few + [small_begin] + [small_step(turn) for turn in range(bits + line_bits)] + [small_end]

        def side_copy(source, target):
            return pltpu.make_async_remote_copy(
                src_ref=side_out.at[pl.ds(target * owned, owned)],
                dst_ref=side_in.at[source],
                send_sem=side_send.at[target],
                recv_sem=side_recv.at[source],
                device_id=(me, target),
                device_id_type=MESH,
            )

        def side_begin():
            side_out[...] = side_total[...].astype(jnp.bfloat16)
            for target in range(nt):

                @pl.when(zed != target)
                def _(target=target):
                    side_copy(zed, target).start()

            side_in[zed] = side_out[aligned(zed * owned, owned)]

        def side_end():
            for source in range(nt):

                @pl.when(zed != source)
                def _(source=source):
                    side_copy(source, source).wait_recv()

            common_ref[...] = jnp.zeros_like(common_ref)
            for source in range(nt):
                value = side_in[source].astype(jnp.float32)
                head = source * (QUERY_HEADS // nt) // (QUERY_HEADS // KEY_VALUE_HEADS)
                common_ref[:, :shared_columns] += value[:, :shared_columns]
                for turn in range(2):
                    at = shared_columns + (turn * KEY_VALUE_HEADS + head) * HEAD_SIZE
                    start = shared_columns + turn * HEAD_SIZE
                    common_ref[:, at : at + HEAD_SIZE] += value[:, start : start + HEAD_SIZE]
            for target in range(nt):

                @pl.when(zed != target)
                def _(target=target):
                    side_copy(zed, target).wait_send()

        def finish(chunk):
            own_sum(chunk, total)
            where = pl.ds(chunk * size, size)
            through, _ = norm_pull(resid_ref[where].astype(jnp.float32), gain_ref[...], total[...])
            value = before_ref[where] + through
            if lane % 128:
                grad_ref[where] = value
                return
            for number, (other, part) in enumerate(blocks):
                start = (mixed_with(me, other, bits) * 2 + part) * lane
                grad_ref[where, pl.ds(pl.multiple_of(start, lane), lane)] = value[:, number * lane : (number + 1) * lane]

        over = staggered([flows[-1]] + flows[:-1])
        first = len(flows)
        over = over[:first] + [step for pair in zip(over[first : first + len(few)], few) for step in pair] + over[
            first + len(few) :
        ]
        over = over[: -len(flows)] + [side_begin] + over[-len(flows) :] + [side_end]
        line_schedule(nt, chunks, pass_on, finish, None, over)
        for chunk in range(chunks):
            reduce_end(chunk)

    scratch = []
    for group in groups:
        scratch = scratch + scatter_scratch(nd, group.shape[0] // nd, group.shape[1])
    turns = bits + line_bits
    common_columns = shared_columns + 2 * KEY_VALUE_HEADS * HEAD_SIZE
    results = pl.pallas_call(
        kernel,
        out_shape=[
            jax.ShapeDtypeStruct((block_rows, width), jnp.float32),
            jax.ShapeDtypeStruct(small.shape, jnp.float32),
            jax.ShapeDtypeStruct((owned, common_columns), jnp.float32),
        ]
        + [jax.ShapeDtypeStruct((group.shape[0] // nd, group.shape[1]), jnp.float32) for group in groups[:-1]],
        in_specs=[ONCHIP] * 6 + [HBM] * count,
        out_specs=[ONCHIP] * (2 + count),
        scratch_shapes=[pltpu.VMEM((side_rows, side_columns), jnp.float32)]
        + line_reduce_scratch(nt, block_rows, width, chunks)
        + [
            pltpu.VMEM((turns + 1, *small.shape), jnp.float32),
            pltpu.VMEM((turns, *small.shape), jnp.float32),
            pltpu.SemaphoreType.DMA((turns,)),
            pltpu.SemaphoreType.DMA((turns,)),
            pltpu.VMEM((16, width), jnp.float32),
            pltpu.VMEM((side_rows, side_columns), jnp.bfloat16),
            pltpu.VMEM((nt, owned, side_columns), jnp.bfloat16),
            pltpu.SemaphoreType.DMA((nt,)),
            pltpu.SemaphoreType.DMA((nt,)),
        ]
        + scratch,
        compiler_params=pltpu.CompilerParams(
            collective_id=3, has_side_effects=True, vmem_limit_bytes=VMEM_LIMIT
        ),
        name="last_sums",
    )(parts, normed, resid, before, gain, small, *groups)
    if lane % 128:
        results = (from_relative(results[0], 1, nd), *results[1:])
    return results


def silu_slope(value, sig):
    return sig * (1.0 + value * (1.0 - sig))


def split_dot(value, constant, dims, terms):
    total = None
    for _ in range(terms):
        piece = value.astype(jnp.bfloat16)
        value = value - piece.astype(jnp.float32)
        part = lax.dot_general(*((piece, constant) if dims[0] else (constant, piece)), dims[1], preferred_element_type=jnp.float32)
        total = part if total is None else total + part
    return total


PLAIN = (((1,), (0,)), ((), ()))
LAST = (((1,), (1,)), ((), ()))
FIRST = (((0,), (0,)), ((), ()))


def product(left, right, dims=PLAIN):
    return lax.dot_general(left, right, dims, preferred_element_type=jnp.float32)


def turned(value, cosine, sine):
    return value * cosine + pltpu.roll(value, value.shape[-1] // 2, 1) * sine


class Sizes:
    def __init__(self, channels, state_columns, query_columns, heads, length):
        self.channels, self.states = channels, state_columns // 2
        self.query, self.heads, self.length = query_columns, heads, length
        self.span = SPAN
        self.count = length // SPAN
        self.wide = channels + state_columns
        self.head_width = channels // heads
        self.step_at = 2 * channels + query_columns
        self.main = self.step_at + heads + (-(self.step_at + heads)) % 128
        self.step_lanes = self.main - self.step_at
        self.side = state_columns + 2 * HEAD_SIZE
        self.window = min(length, 3 * SPAN)


def spread_heads(size):
    table = np.zeros((size.step_lanes, size.channels), np.float32)
    for head in range(size.heads):
        table[head, head * size.head_width : (head + 1) * size.head_width] = 1.0
    return table.astype(jnp.bfloat16)


def turn_tables(length):
    half = HEAD_SIZE // 2
    angle = np.arange(length, dtype=np.float64)[:, None] * rope_base ** (-np.arange(half) / half)[None]
    cosine, sine = np.cos(angle), np.sin(angle)
    return (
        np.concatenate([cosine, cosine], 1).astype(np.float32),
        np.concatenate([-sine, sine], 1).astype(np.float32),
    )


def token_flags(segments, taps):
    seg = segments[0]
    length = seg.shape[0]
    columns = [jnp.ones((length,), bool)]
    ahead = []
    for lag in range(1, taps):
        columns.append(jnp.concatenate([jnp.zeros((lag,), bool), seg[lag:] == seg[:-lag]]))
        ahead.append(jnp.concatenate([seg[lag:] == seg[:-lag], jnp.zeros((lag,), bool)]))
    ends = seg.reshape(-1, SPAN)[:, -1]
    before = jnp.concatenate([jnp.full((1,), -1, seg.dtype), ends[:-1]])
    columns.append(seg == jnp.repeat(before, SPAN))
    columns.append(seg == jnp.repeat(ends, SPAN))
    columns = columns + ahead
    return jnp.pad(jnp.stack(columns, 1).astype(jnp.float32), ((0, 0), (0, 16 - len(columns))))


def chunk_values(size, taps, main_ref, wide_ref, flags, spread, taps_ref, heads_ref, segc, segr):
    span = size.span
    pre = wide_ref[pl.ds(8, span), :] * taps_ref[0:1, :]
    for lag in range(1, taps):
        pre = pre + wide_ref[pl.ds(8 - lag, span), :] * (flags[:, lag : lag + 1] * taps_ref[lag : lag + 1, :])
    sig = jax.nn.sigmoid(pre)
    act = pre * sig
    inner = act[:, : size.channels]
    bmat = act[:, size.channels : size.channels + size.states].astype(jnp.bfloat16)
    cmat = act[:, size.channels + size.states :].astype(jnp.bfloat16)
    step_in = main_ref[:, size.step_at :] + heads_ref[0:1, :]
    step = jnp.maximum(step_in, 0.0) + jnp.log1p(jnp.exp(-jnp.abs(step_in)))
    logdec = -step * heads_ref[1:2, :]
    rows = lax.broadcasted_iota(jnp.int32, (span, span), 0)
    columns = lax.broadcasted_iota(jnp.int32, (span, span), 1)
    later = jnp.where(rows >= columns, 1.0, 0.0).astype(jnp.bfloat16)
    cumul = split_dot(logdec, later, (False, PLAIN), 3)
    inside = jnp.logical_and(rows >= columns, segc == segr)
    ending = cumul[span - 1 : span, :]
    reach = jnp.exp(cumul) * flags[:, 4:5]
    tail = jnp.exp(ending - cumul) * flags[:, 5:6]
    step_wide = split_dot(step, spread, (True, PLAIN), 2)
    scaled = inner * step_wide
    return dict(
        pre=pre, sig=sig, inner=inner, bmat=bmat, cmat=cmat, step_in=step_in, step=step, logdec=logdec, later=later,
        cumul=cumul, turned=jnp.transpose(cumul), inside=inside, step_wide=step_wide, scaled=scaled,
        scaled_b=scaled.astype(jnp.bfloat16), meeting=product(cmat, bmat, LAST),
        reach_wide=split_dot(reach, spread, (True, PLAIN), 2), tail_wide=split_dot(tail, spread, (True, PLAIN), 2),
        skip_wide=split_dot(jnp.broadcast_to(heads_ref[2:3, :], (8, size.step_lanes)), spread, (True, PLAIN), 2)[0:1],
    )


def decay_of(values, head):
    spread = values["cumul"][:, head : head + 1] - values["turned"][head : head + 1, :]
    return jnp.exp(jnp.where(values["inside"], spread, -1e30))


def softmax_of(size, query, keys, chunk, start, segc, seg_all):
    scores = product(query, keys, LAST) * (1.0 / math.sqrt(HEAD_SIZE))
    rows = lax.broadcasted_iota(jnp.int32, scores.shape, 0) + chunk * size.span
    columns = lax.broadcasted_iota(jnp.int32, scores.shape, 1) + start
    allowed = jnp.logical_and(rows >= columns, segc == seg_all)
    masked = jnp.where(allowed, scores, -1e30)
    expo = jnp.exp(masked - jnp.max(masked, axis=-1, keepdims=True))
    return expo / jnp.sum(expo, axis=-1, keepdims=True)


def mixers_forward(size, taps, main_raw, side_raw, segments, flags, tap_rows, head_rows):
    span = size.span
    per_head = size.head_width

    def kernel(
        main_ref, side_ref, segc_ref, segr_ref, flags_ref, taps_ref, heads_ref, cos_ref, sin_ref, spread_ref,
        mixed_ref, y_ref, state_ref, keys_ref, values_ref, wide, state,
    ):
        chunk = pl.program_id(0)

        @pl.when(chunk == 0)
        def _():
            wide[0:8, :] = jnp.zeros((8, size.wide), jnp.float32)
            state[...] = jnp.zeros_like(state)
            keys_ref[...] = jnp.zeros_like(keys_ref)
            values_ref[...] = jnp.zeros_like(values_ref)

        wide[pl.ds(8, span), : size.channels] = main_ref[:, size.channels : 2 * size.channels]
        wide[pl.ds(8, span), size.channels :] = side_ref[:, : 2 * size.states]
        flags, spread, segc = flags_ref[...], spread_ref[...], segc_ref[...]
        segr = segr_ref[:, pl.ds(pl.multiple_of(chunk * span, span), span)]
        val = chunk_values(size, taps, main_ref, wide, flags, spread, taps_ref, heads_ref, segc, segr)
        wide[0:8, :] = wide[pl.ds(span, 8), :]
        held = state[...]
        held_b = held.astype(jnp.bfloat16)
        state_ref[...] = held
        across = val["reach_wide"] * product(val["cmat"], held_b)
        lane = lax.broadcasted_iota(jnp.int32, (span, 2 * per_head), 1)
        for pair in range(size.heads // 2):
            where = slice(pair * 2 * per_head, (pair + 1) * 2 * per_head)
            both = []
            for head in (2 * pair, 2 * pair + 1):
                weights = (val["meeting"] * decay_of(val, head)).astype(jnp.bfloat16)
                both.append(product(weights, val["scaled_b"][:, where]))
            result = jnp.where(lane < per_head, both[0], both[1])
            result = result + across[:, where] + val["skip_wide"][:, where] * val["inner"][:, where]
            y_ref[:, where] = result
            gate = main_ref[:, where]
            mixed_ref[:, where] = (result * (gate * jax.nn.sigmoid(gate))).astype(jnp.bfloat16)
        keep = jnp.broadcast_to(val["reach_wide"][span - 1 : span, :], (1, size.channels))
        state[...] = keep * held + product(
            val["bmat"], (val["tail_wide"] * val["scaled"]).astype(jnp.bfloat16), FIRST
        )

        cosine, sine = cos_ref[...], sin_ref[...]
        own = pl.ds(pl.multiple_of(chunk * span, span), span)
        key_at = 2 * size.states
        keys_ref[own, :] = turned(side_ref[:, key_at : key_at + HEAD_SIZE], cosine, sine).astype(jnp.bfloat16)
        values_ref[own, :] = side_ref[:, key_at + HEAD_SIZE :].astype(jnp.bfloat16)
        start = pl.multiple_of(jnp.maximum(chunk + 1 - size.window // span, 0) * span, span)
        seen = pl.ds(start, size.window)
        for head in range(size.query // HEAD_SIZE):
            at = 2 * size.channels + head * HEAD_SIZE
            query = turned(main_ref[:, at : at + HEAD_SIZE], cosine, sine).astype(jnp.bfloat16)
            probs = softmax_of(size, query, keys_ref[seen, :], chunk, start, segc, segr_ref[:, seen])
            result = product(probs.astype(jnp.bfloat16), values_ref[seen, :])
            at = size.channels + head * HEAD_SIZE
            mixed_ref[:, at : at + HEAD_SIZE] = result.astype(jnp.bfloat16)

    def rows(columns):
        return pl.BlockSpec((span, columns), lambda i: (i, 0))

    def whole(array):
        return pl.BlockSpec(array.shape, lambda i: (0, 0))

    cosine, sine = turn_tables(size.length)
    spread = spread_heads(size)
    tokens = size.length
    return pl.pallas_call(
        kernel,
        grid=(size.count,),
        in_specs=[
            rows(size.main), rows(size.side), rows(1), whole(segments), rows(16), whole(tap_rows), whole(head_rows),
            rows(HEAD_SIZE), rows(HEAD_SIZE), whole(spread),
        ],
        out_specs=[
            rows(size.channels + size.query), rows(size.channels),
            pl.BlockSpec((size.states, size.channels), lambda i: (i, 0)),
            pl.BlockSpec((tokens, HEAD_SIZE), lambda i: (0, 0)), pl.BlockSpec((tokens, HEAD_SIZE), lambda i: (0, 0)),
        ],
        out_shape=[
            jax.ShapeDtypeStruct((tokens, size.channels + size.query), jnp.bfloat16),
            jax.ShapeDtypeStruct((tokens, size.channels), jnp.float32),
            jax.ShapeDtypeStruct((size.count * size.states, size.channels), jnp.float32),
            jax.ShapeDtypeStruct((tokens, HEAD_SIZE), jnp.bfloat16),
            jax.ShapeDtypeStruct((tokens, HEAD_SIZE), jnp.bfloat16),
        ],
        scratch_shapes=[
            pltpu.VMEM((span + 8, size.wide), jnp.float32),
            pltpu.VMEM((size.states, size.channels), jnp.float32),
        ],
        compiler_params=pltpu.CompilerParams(
            dimension_semantics=("arbitrary",), vmem_limit_bytes=VMEM_LIMIT
        ),
        name="mixers_forward",
    )(main_raw, side_raw, segments.reshape(tokens, 1), segments, flags, tap_rows, head_rows,
      jnp.asarray(cosine), jnp.asarray(sine), jnp.asarray(spread))


def mixers_backward(
    size, taps, grad_mixed, main_raw, side_raw, segments, flags, tap_rows, head_rows, y_value, states, keys, values
):
    span = size.span
    per_head = size.head_width
    count = size.count

    def kernel(
        grad_ref, main_ref, side_ref, before_ref, side_before_ref, segc_ref, segr_ref, flags_ref, taps_ref, heads_ref,
        cos_ref, sin_ref, spread_ref, y_ref, state_ref, keys_ref, values_ref,
        grad_main, grad_side, tap_sums, head_sums, wide, back, grad_state, grad_keys, grad_values,
    ):
        turn = pl.program_id(0)
        chunk = count - 1 - turn

        @pl.when(turn == 0)
        def _():
            back[pl.ds(span, 8), :] = jnp.zeros((8, size.wide), jnp.float32)
            grad_state[...] = jnp.zeros_like(grad_state)
            grad_keys[...] = jnp.zeros_like(grad_keys)
            grad_values[...] = jnp.zeros_like(grad_values)
            tap_sums[...] = jnp.zeros_like(tap_sums)
            head_sums[...] = jnp.zeros_like(head_sums)

        wide[0:8, : size.channels] = before_ref[...]
        wide[0:8, size.channels :] = side_before_ref[...]
        wide[pl.ds(8, span), : size.channels] = main_ref[:, size.channels : 2 * size.channels]
        wide[pl.ds(8, span), size.channels :] = side_ref[:, : 2 * size.states]
        flags, spread, segc = flags_ref[...], spread_ref[...], segc_ref[...]
        segr = segr_ref[:, pl.ds(pl.multiple_of(chunk * span, span), span)]
        val = chunk_values(size, taps, main_ref, wide, flags, spread, taps_ref, heads_ref, segc, segr)
        inner, scaled = val["inner"], val["scaled"]

        gate = main_ref[:, : size.channels]
        gate_sig = jax.nn.sigmoid(gate)
        grad = grad_ref[:, : size.channels]
        grad_main[:, : size.channels] = (grad * y_ref[...] * silu_slope(gate, gate_sig)).astype(jnp.bfloat16)
        grad_y = grad * (gate * gate_sig)
        grad_y_b = grad_y.astype(jnp.bfloat16)
        tap_sums[4:5, : size.channels] += jnp.sum(grad_y * inner, axis=0, keepdims=True)

        lane = lax.broadcasted_iota(jnp.int32, (span, 2 * per_head), 1)
        head_lane = lax.broadcasted_iota(jnp.int32, (span, size.step_lanes), 1)
        head_row = lax.broadcasted_iota(jnp.int32, (size.step_lanes, span), 0)
        grad_meeting = jnp.zeros((span, span), jnp.float32)
        by_row = jnp.zeros((span, size.step_lanes), jnp.float32)
        by_column = jnp.zeros((size.step_lanes, span), jnp.float32)
        pieces = []
        for pair in range(size.heads // 2):
            where = slice(pair * 2 * per_head, (pair + 1) * 2 * per_head)
            both = []
            for side in range(2):
                head = 2 * pair + side
                decay = decay_of(val, head)
                weights = val["meeting"] * decay
                mine = (lane < per_head) if side == 0 else (lane >= per_head)
                grad_own = jnp.where(mine, grad_y_b[:, where], jnp.zeros((), jnp.bfloat16))
                grad_weights = product(grad_own, val["scaled_b"][:, where], LAST)
                both.append(product(weights.astype(jnp.bfloat16), grad_y_b[:, where], FIRST))
                grad_meeting = grad_meeting + grad_weights * decay
                moved = grad_weights * weights
                by_row = jnp.where(head_lane == head, jnp.sum(moved, axis=1, keepdims=True), by_row)
                by_column = jnp.where(head_row == head, jnp.sum(moved, axis=0, keepdims=True), by_column)
            pieces.append(jnp.where(lane < per_head, both[0], both[1]))
        grad_scaled = jnp.concatenate(pieces, axis=1)
        grad_cumul = by_row - jnp.transpose(by_column)

        held = state_ref[...]
        held_b = held.astype(jnp.bfloat16)
        grad_held = grad_state[...]
        grad_held_b = grad_held.astype(jnp.bfloat16)
        grad_meeting_b = grad_meeting.astype(jnp.bfloat16)
        reached = val["reach_wide"] * grad_y
        reached_b = reached.astype(jnp.bfloat16)
        grad_cumul = grad_cumul + split_dot(reached * product(val["cmat"], held_b), spread, (True, LAST), 2)
        grad_c = product(reached_b, held_b, LAST) + product(grad_meeting_b, val["bmat"])
        from_state = val["tail_wide"] * product(val["bmat"], grad_held_b)
        grad_b = product(grad_meeting_b, val["cmat"], FIRST) + product(
            (val["tail_wide"] * scaled).astype(jnp.bfloat16), grad_held_b, LAST
        )
        grad_scaled = grad_scaled + from_state
        ended = split_dot(scaled * from_state, spread, (True, LAST), 2)
        keep = val["reach_wide"][span - 1 : span, :]
        kept = jnp.sum(grad_held * held, axis=0, keepdims=True) * keep
        kept = split_dot(jnp.broadcast_to(kept, (8, size.channels)), spread, (True, LAST), 2)[0:1]
        at_end = jnp.sum(ended, axis=0, keepdims=True) + kept
        grad_logdec = split_dot(grad_cumul - ended, val["later"], (False, FIRST), 3) + at_end
        grad_state[...] = keep * grad_held + product(val["cmat"], reached_b, FIRST)

        grad_inner = grad_scaled * val["step_wide"] + grad_y * val["skip_wide"]
        grad_step = split_dot(grad_scaled * inner, spread, (True, LAST), 2) - grad_logdec * heads_ref[1:2, :]
        grad_step_raw = grad_step * jax.nn.sigmoid(val["step_in"])
        head_sums[0:1, :] += jnp.sum(grad_step_raw, axis=0, keepdims=True)
        head_sums[1:2, :] += jnp.sum(grad_logdec * val["logdec"], axis=0, keepdims=True)
        grad_main[:, size.step_at :] = grad_step_raw.astype(jnp.bfloat16)

        slope = silu_slope(val["pre"], val["sig"])
        grad_pre = jnp.concatenate([grad_inner, grad_b, grad_c], axis=1) * slope
        back[pl.ds(0, span), :] = grad_pre
        raw = grad_pre * taps_ref[0:1, :]
        tap_sums[0:1, :] += jnp.sum(grad_pre * wide[pl.ds(8, span), :], axis=0, keepdims=True)
        for lag in range(1, taps):
            tap_sums[lag : lag + 1, :] += jnp.sum(
                grad_pre * (wide[pl.ds(8 - lag, span), :] * flags[:, lag : lag + 1]), axis=0, keepdims=True
            )
            raw = raw + back[pl.ds(lag, span), :] * (flags[:, 5 + lag : 6 + lag] * taps_ref[lag : lag + 1, :])
        back[pl.ds(span, 8), :] = back[0:8, :]
        grad_main[:, size.channels : 2 * size.channels] = raw[:, : size.channels].astype(jnp.bfloat16)
        grad_side[:, : 2 * size.states] = raw[:, size.channels :].astype(jnp.bfloat16)

        cosine, sine = cos_ref[...], sin_ref[...]
        start = pl.multiple_of(jnp.maximum(chunk + 1 - size.window // span, 0) * span, span)
        seen = pl.ds(start, size.window)
        seen_keys, seen_values = keys_ref[seen, :], values_ref[seen, :]
        scale = 1.0 / math.sqrt(HEAD_SIZE)
        for head in range(size.query // HEAD_SIZE):
            at = 2 * size.channels + head * HEAD_SIZE
            query = turned(main_ref[:, at : at + HEAD_SIZE], cosine, sine).astype(jnp.bfloat16)
            probs = softmax_of(size, query, seen_keys, chunk, start, segc, segr_ref[:, seen])
            out_at = size.channels + head * HEAD_SIZE
            grad_out = grad_ref[:, out_at : out_at + HEAD_SIZE].astype(jnp.bfloat16)
            grad_probs = product(grad_out, seen_values, LAST)
            delta = jnp.sum(grad_probs * probs, axis=-1, keepdims=True)
            grad_scores = (probs * (grad_probs - delta)).astype(jnp.bfloat16)
            grad_query = product(grad_scores, seen_keys) * scale
            grad_main[:, at : at + HEAD_SIZE] = turned(grad_query, cosine, -sine).astype(jnp.bfloat16)
            grad_keys[seen, :] += product(grad_scores, query, FIRST) * scale
            grad_values[seen, :] += product(probs.astype(jnp.bfloat16), grad_out, FIRST)
        own = pl.ds(pl.multiple_of(chunk * span, span), span)
        key_at = 2 * size.states
        grad_side[:, key_at : key_at + HEAD_SIZE] = turned(grad_keys[own, :], cosine, -sine).astype(jnp.bfloat16)
        grad_side[:, key_at + HEAD_SIZE :] = grad_values[own, :].astype(jnp.bfloat16)

    def rows(columns):
        return pl.BlockSpec((span, columns), lambda i: (count - 1 - i, 0))

    def previous(columns, column):
        return pl.BlockSpec((8, columns), lambda i: (jnp.maximum((count - 1 - i) * (span // 8) - 1, 0), column))

    def whole(array):
        return pl.BlockSpec(array.shape, lambda i: (0, 0))

    cosine, sine = turn_tables(size.length)
    spread = spread_heads(size)
    tokens = size.length
    return pl.pallas_call(
        kernel,
        grid=(count,),
        in_specs=[
            rows(size.channels + size.query), rows(size.main), rows(size.side), previous(size.channels, 1),
            previous(2 * size.states, 0), rows(1), whole(segments), rows(16), whole(tap_rows), whole(head_rows),
            rows(HEAD_SIZE), rows(HEAD_SIZE), whole(spread), rows(size.channels),
            pl.BlockSpec((size.states, size.channels), lambda i: (count - 1 - i, 0)), whole(keys), whole(values),
        ],
        out_specs=[
            rows(size.main), rows(size.side), pl.BlockSpec((8, size.wide), lambda i: (0, 0)),
            pl.BlockSpec((8, size.step_lanes), lambda i: (0, 0)),
        ],
        out_shape=[
            jax.ShapeDtypeStruct((tokens, size.main), jnp.bfloat16),
            jax.ShapeDtypeStruct((tokens, size.side), jnp.bfloat16),
            jax.ShapeDtypeStruct((8, size.wide), jnp.float32),
            jax.ShapeDtypeStruct((8, size.step_lanes), jnp.float32),
        ],
        scratch_shapes=[
            pltpu.VMEM((span + 8, size.wide), jnp.float32),
            pltpu.VMEM((span + 8, size.wide), jnp.float32),
            pltpu.VMEM((size.states, size.channels), jnp.float32),
            pltpu.VMEM((tokens, HEAD_SIZE), jnp.float32),
            pltpu.VMEM((tokens, HEAD_SIZE), jnp.float32),
        ],
        compiler_params=pltpu.CompilerParams(
            dimension_semantics=("arbitrary",), vmem_limit_bytes=VMEM_LIMIT
        ),
        name="mixers_backward",
    )(grad_mixed, main_raw, side_raw, main_raw, side_raw, segments.reshape(tokens, 1), segments, flags, tap_rows,
      head_rows, jnp.asarray(cosine), jnp.asarray(sine), jnp.asarray(spread), y_value, states, keys, values)


def per_device(
    nd,
    nt,
    residual,
    segments,
    mixgain,
    ffngain,
    gateproj,
    innerproj,
    stepproj,
    sharedproj,
    innerconv,
    sharedconv,
    stepbias,
    decaylog,
    skipgain,
    mixerout,
    queryproj,
    keyvalue,
    attnout,
    ffngate,
    upproj,
    downproj,
    cotangent,
):
    bfloat = jnp.bfloat16
    single = jnp.float32
    width = residual.shape[1]
    zed = lax.axis_index("tensor")
    seq_count, length = segments.shape
    token_count = seq_count * length
    channels = innerproj.shape[1]
    state_columns = sharedproj.shape[1]
    heads = stepproj.shape[1]
    query_columns = queryproj.shape[1]
    ffn_columns = ffngate.shape[1]
    small_rows = sharedproj.shape[0]
    conv_rows = sharedconv.shape[0]
    taps = sharedconv.shape[1]

    gains = jnp.concatenate(
        [
            mixgain[:, None],
            ffngain[:, None],
            jnp.pad(sharedconv, ((0, small_rows - conv_rows), (0, 0))),
            jnp.zeros((small_rows, 128 - 2 - taps), bfloat),
        ],
        axis=1,
    )
    main_used = 2 * channels + query_columns + heads
    main_own = jnp.concatenate(
        [
            gateproj,
            innerproj,
            queryproj,
            stepproj,
            jnp.zeros((gateproj.shape[0], -main_used % 128), bfloat),
        ],
        axis=1,
    )
    resid_own, cot_own, gain_rows, normed, _, main, side, out_w, main_raw, side_raw = first_gathers(
        nd,
        nt,
        residual,
        cotangent,
        jnp.concatenate([sharedproj, keyvalue, gains], axis=1),
        main_own,
        jnp.concatenate([mixerout, attnout], axis=1),
        state_columns,
    )
    grad_rows = lax.all_gather(cot_own, "tensor", axis=0, tiled=True)
    gain_one, gain_two = gain_rows[0], gain_rows[1]
    conv_shared = from_relative(gain_rows[2 : 2 + taps], 1, nd)
    conv_shared = conv_shared.reshape(taps, nd * nt, small_rows)[:, :, :conv_rows].reshape(taps, -1)

    size = Sizes(channels, state_columns, query_columns, heads, length)
    flags = token_flags(segments, taps)
    tap_rows = jnp.concatenate([innerconv.astype(single).T, conv_shared], axis=1)
    tap_rows = jnp.pad(tap_rows, ((0, 8 - taps), (0, 0)))
    head_rows = jnp.stack([stepbias.astype(single), jnp.exp(decaylog.astype(single)), skipgain.astype(single)])
    head_rows = jnp.pad(head_rows, ((0, 5), (0, size.step_lanes - heads)))
    mixed_in, y_value, states, keys, values = mixers_forward(
        size, taps, main_raw, side_raw, segments, flags, tap_rows, head_rows
    )
    mix_part = contract_last(mixed_in, out_w).astype(bfloat)
    middle, rows_two, ffn_w = middle_rows(
        nd,
        nt,
        mix_part,
        resid_own,
        gain_two[None],
        [jnp.concatenate([ffngate, upproj, downproj], axis=1)],
    )
    gate_up_w = ffn_w[:, : 2 * ffn_columns]
    down_w = ffn_w[:, 2 * ffn_columns :]
    gate_up = matrix_product(rows_two, gate_up_w)
    gate = gate_up[:, :ffn_columns]
    upper = gate_up[:, ffn_columns:]
    sigma = jax.nn.sigmoid(gate)
    hidden = (gate * sigma * upper).astype(bfloat)
    grad_hidden = matrix_product(grad_rows, down_w)
    grad_gate = (grad_hidden * upper * sigma * (1.0 + gate * (1.0 - sigma))).astype(bfloat)
    grad_upper = (grad_hidden * gate * sigma).astype(bfloat)
    grad_gate_up = jnp.concatenate([grad_gate, grad_upper], axis=1)
    two_part = contract_last(grad_gate_up, gate_up_w).astype(bfloat)
    grad_middle, grad_gain_two, grad_mix_rows, down_g, gate_up_g = middle_back(
        nd,
        nt,
        two_part,
        middle,
        cot_own,
        gain_two[None],
        [
            contract_leading_axis(grad_rows, hidden).astype(bfloat),
            contract_leading_axis(rows_two, grad_gate_up).astype(bfloat),
        ],
    )
    ffn_part = after(contract_last(hidden, down_w).astype(bfloat), grad_mix_rows)
    ffn_out = lax.psum_scatter(ffn_part, "tensor", scatter_dimension=0, tiled=True)
    layer_out = from_relative(middle + ffn_out.astype(single), 1, nd)
    grad_mixed_in = matrix_product(grad_mix_rows, out_w)
    grad_main, grad_side, tap_sums, head_sums = mixers_backward(
        size, taps, grad_mixed_in, main_raw, side_raw, segments, flags, tap_rows, head_rows, y_value, states, keys, values
    )
    one_part = (contract_last(grad_main, main) + contract_last(grad_side, side)).astype(bfloat)
    small = jnp.concatenate(
        [
            jnp.zeros((width,), single),
            grad_gain_two[0],
            tap_sums[:taps, channels:].reshape(-1),
            tap_sums[:taps, :channels].reshape(-1),
            tap_sums[4, :channels],
            head_sums[:2].reshape(-1),
        ]
    )
    shared_length = 2 * width + taps * state_columns
    small = jnp.pad(small, (0, -small.shape[0] % 1024)).reshape(-1, 128)
    grad_residual, small, common_g, main_g, out_g = last_sums(
        nd,
        nt,
        one_part,
        normed,
        resid_own,
        grad_middle,
        gain_one[None],
        small,
        shared_length // 128,
        [
            contract_leading_axis(normed, grad_main).astype(bfloat),
            contract_leading_axis(grad_mix_rows, mixed_in).astype(bfloat),
        ],
        contract_leading_axis(normed, grad_side).astype(bfloat),
    )
    small = small.reshape(-1)
    place = lax.axis_index("dp") * nt + zed
    gain_one_g = lax.dynamic_slice_in_dim(small, place * small_rows, small_rows, 0)
    gain_two_g = lax.dynamic_slice_in_dim(small, width + place * small_rows, small_rows, 0)
    conv_g = lax.dynamic_slice_in_dim(
        small[2 * width : shared_length].reshape(taps, -1), place * conv_rows, conv_rows, 1
    ).T
    local = small[shared_length:]
    skip_at = taps * channels
    head_at = skip_at + channels
    return (
        layer_out,
        grad_residual,
        gain_one_g,
        gain_two_g,
        main_g[:, :channels],
        main_g[:, channels : 2 * channels],
        main_g[:, 2 * channels + query_columns : main_used],
        common_g[:, :state_columns],
        local[:skip_at].reshape(taps, channels).T,
        conv_g,
        local[head_at : head_at + heads],
        local[head_at + size.step_lanes : head_at + size.step_lanes + heads],
        local[skip_at:head_at].reshape(heads, -1).sum(axis=1),
        out_g[:, :channels],
        main_g[:, 2 * channels : 2 * channels + query_columns],
        common_g[:, state_columns:],
        out_g[:, channels:],
        gate_up_g[:, :ffn_columns],
        gate_up_g[:, ffn_columns:],
        down_g,
    )


def solution(mesh):
    return jax.shard_map(
        functools.partial(per_device, mesh.shape["dp"], mesh.shape["tensor"]),
        mesh=mesh,
        in_specs=(
            P(("dp", "tensor"), None),
            P("dp", None),
            P(("dp", "tensor")),
            P(("dp", "tensor")),
            P("dp", "tensor"),
            P("dp", "tensor"),
            P("dp", "tensor"),
            P(("dp", "tensor"), None),
            P("tensor", None),
            P(("dp", "tensor"), None),
            P("tensor"),
            P("tensor"),
            P("tensor"),
            P("dp", "tensor"),
            P("dp", "tensor"),
            P(("dp", "tensor"), None),
            P("dp", "tensor"),
            P("dp", "tensor"),
            P("dp", "tensor"),
            P("dp", "tensor"),
            P(("dp", "tensor"), None),
        ),
        out_specs=(
            P(("dp", "tensor"), None),
            P(("dp", "tensor"), None),
            P(("dp", "tensor")),
            P(("dp", "tensor")),
            P("dp", "tensor"),
            P("dp", "tensor"),
            P("dp", "tensor"),
            P(("dp", "tensor"), None),
            P("tensor", None),
            P(("dp", "tensor"), None),
            P("tensor"),
            P("tensor"),
            P("tensor"),
            P("dp", "tensor"),
            P("dp", "tensor"),
            P(("dp", "tensor"), None),
            P("dp", "tensor"),
            P("dp", "tensor"),
            P("dp", "tensor"),
            P("dp", "tensor"),
        ),
        check_vma=False,
    )
```

```python
import functools
import math

import jax
import jax.numpy as jnp
import numpy as np
from jax import lax
from jax.experimental import pallas as pl
from jax.experimental.pallas import tpu as pltpu
from jax.sharding import PartitionSpec as P

QUERY_HEADS = 8
KEY_VALUE_HEADS = 2
HEAD_SIZE = 128
SPAN = 256


eps = 1e-05
rope_base = 10000.0


def matrix_product(left, right):
    return jnp.dot(left, right, preferred_element_type=jnp.float32)


def contract_leading_axis(left, right):
    return lax.dot_general(
        left, right, (((0,), (0,)), ((), ())), preferred_element_type=jnp.float32
    )


def contract_last(left, right):
    return lax.dot_general(
        left, right, (((1,), (1,)), ((), ())), preferred_element_type=jnp.float32
    )


def bit_orders(size):
    high = list(range(size.bit_length() - 2, 0, -1))
    return high, high[:2][::-1] + high[2:]


def relative_blocks(size):
    both = []
    for half, order in enumerate(bit_orders(size)):
        chain = [0]
        for bit in order:
            chain = chain + [other ^ (1 << bit) for other in chain]
        both = both + [(other, half) for other in chain]
    return both + [(other ^ 1, half) for other, half in both]


def to_relative(value, axis, size):
    me = lax.axis_index("dp")
    width = value.shape[axis] // (2 * size)
    return jnp.concatenate(
        [
            lax.dynamic_slice_in_dim(value, ((me ^ other) * 2 + half) * width, width, axis)
            for other, half in relative_blocks(size)
        ],
        axis,
    )


def from_relative(value, axis, size):
    me = lax.axis_index("dp")
    width = value.shape[axis] // (2 * size)
    blocks = relative_blocks(size)
    place = jnp.asarray([blocks.index((other, half)) for other in range(size) for half in range(2)], jnp.int32)
    return jnp.concatenate(
        [
            lax.dynamic_slice_in_dim(value, place[(me ^ number) * 2 + half] * width, width, axis)
            for number in range(size)
            for half in range(2)
        ],
        axis,
    )


def after(value, *others):
    return lax.optimization_barrier((value,) + others)[0]


MESH = pl.DeviceIdType.MESH
VMEM_LIMIT = 56 * 1024 * 1024
LARGE_LIMIT = 62 * 1024 * 1024


def flip(value, bit):
    unit = 1 << bit
    return value + unit * (1 - 2 * ((value // unit) % 2))


def mixed_with(value, other, bits):
    for bit in range(bits):
        if (other >> bit) & 1:
            value = flip(value, bit)
    return value


def enter(nt, bits):
    me, zed = lax.axis_index("dp"), lax.axis_index("tensor")
    barrier = pltpu.get_barrier_semaphore()
    for other in range(nt):

        @pl.when(zed != other)
        def _(other=other):
            pl.semaphore_signal(barrier, inc=1, device_id=(me, other), device_id_type=MESH)

    for bit in range(bits):
        pl.semaphore_signal(barrier, inc=1, device_id=(flip(me, bit), zed), device_id_type=MESH)
    pl.semaphore_wait(barrier, bits + nt - 1)
    return me, zed


def aligned(start, size):
    return pl.ds(pl.multiple_of(start, 16), size)


def together(*flows):
    flows = [list(flow) for flow in flows]
    order = sorted(
        ((place + 0.5) / len(flow), number, place)
        for number, flow in enumerate(flows)
        for place in range(len(flow))
    )
    for _, number, place in order:
        flows[number][place]()


def gather_steps(nd, me, zed, own, everything, send, recv, local):
    half = own.shape[0] // 2
    blocks = relative_blocks(nd)
    place = {block: number for number, block in enumerate(blocks)}

    def rows(block):
        return everything.at[pl.ds(place[block] * half, half)]

    def source(block):
        return own.at[pl.ds(block[1] * half, half)] if block[0] == 0 else rows(block)

    hops = []
    for part, order in enumerate(bit_orders(nd)):
        chain = [0]
        for bit in order:
            hops = hops + [((other, part), bit) for other in chain]
            chain = chain + [other ^ (1 << bit) for other in chain]
    hops = hops + [(block, 0) for block in blocks[:nd]]

    def copy(number):
        block, bit = hops[number]
        landed = (block[0] ^ (1 << bit), block[1])
        return pltpu.make_async_remote_copy(
            src_ref=source(block),
            dst_ref=rows(landed),
            send_sem=send.at[number],
            recv_sem=recv.at[place[landed]],
            device_id=(flip(me, bit), zed),
            device_id_type=MESH,
        )

    def arrival(block):
        return pltpu.make_async_remote_copy(
            src_ref=rows(block),
            dst_ref=rows(block),
            send_sem=send.at[0],
            recv_sem=recv.at[place[block]],
            device_id=(flip(me, 0), zed),
            device_id_type=MESH,
        )

    def begin():
        for number, (block, bit) in enumerate(hops):
            if block[0] == 0:
                copy(number).start()
        for part in range(2):
            pltpu.make_async_copy(source((0, part)), rows((0, part)), local.at[part]).start()

    def forward(block):
        def step():
            arrival(block).wait_recv()
            for number, (origin, bit) in enumerate(hops):
                if origin == block:
                    copy(number).start()

        return step

    def end():
        for block in blocks[nd:]:
            arrival(block).wait_recv()
        for number in range(len(hops)):
            copy(number).wait_send()
        for part in range(2):
            pltpu.make_async_copy(source((0, part)), rows((0, part)), local.at[part]).wait()

    first, second = blocks[1 : nd // 2], blocks[nd // 2 + 1 : nd]
    middle = [forward(block) for pair in zip(first, second) for block in pair]
    return [begin] + middle + [end]


def gather_hops(nd):
    return 2 * (nd // 2 - 1) + nd


def gather_semaphores(nd):
    return [
        pltpu.SemaphoreType.DMA((gather_hops(nd),)),
        pltpu.SemaphoreType.DMA((2 * nd,)),
        pltpu.SemaphoreType.DMA((2,)),
    ]


def each_rows(rows, body, unit=16):
    def step(number, carry):
        body(aligned(number * unit, unit))
        return carry

    lax.fori_loop(0, rows // unit, step, 0)


def scatter_steps(nd, me, zed, parts, total, mine, held, landed, core_send, core_recv, send, recv, local):
    half = total.shape[0] // 2
    chain_length = nd // 2

    def piece(ref, number):
        return ref.at[pl.ds(number * half, half)]

    rounds, slot = [], 0
    for part, order in enumerate(bit_orders(nd)):
        length, own_rounds = chain_length, []
        for bit in order[::-1]:
            length = length // 2
            own_rounds.append((bit, length, slot))
            slot = slot + length
        rounds.append(own_rounds)

    def core_copy(number):
        return pltpu.make_async_remote_copy(
            src_ref=piece(parts, nd + number),
            dst_ref=piece(held, number),
            send_sem=core_send.at[number],
            recv_sem=core_recv.at[number],
            device_id=(flip(me, 0), zed),
            device_id_type=MESH,
        )

    def hop(part, bit, number, where):
        return pltpu.make_async_remote_copy(
            src_ref=piece(held, number),
            dst_ref=piece(landed, where),
            send_sem=send.at[where],
            recv_sem=recv.at[where],
            device_id=(flip(me, bit), zed),
            device_id_type=MESH,
        )

    wanted = []
    for number in range(chain_length - 1, -1, -1):
        wanted = wanted + [number, chain_length + number]

    def load(number):
        return pltpu.make_async_copy(piece(parts, number), piece(mine, number), local.at[number])

    def begin():
        for number in wanted:
            core_copy(number).start()
        for number in wanted:
            load(number).start()

    def core_sum(number):
        part, spot = number // chain_length, number % chain_length

        def step():
            load(number).wait()
            core_copy(number).wait_recv()

            def body(rows):
                spot_rows = piece(held, number)
                spot_rows[rows] = spot_rows[rows] + piece(mine, number)[rows]

            each_rows(half, body)
            if rounds[part]:
                bit, length, first = rounds[part][0]
                if spot >= length:
                    hop(part, bit, number, first + spot - length).start()

        return step

    def later_sum(part, turn, spot):
        bit, length, first = rounds[part][turn]
        number = part * chain_length + spot

        def step():
            hop(part, bit, number, first + spot).wait_recv()
            last = turn == len(rounds[part]) - 1

            def body(rows):
                kept, came = piece(held, number)[rows], piece(landed, first + spot)[rows]
                if last:
                    piece(total, part)[rows] = kept.astype(jnp.float32) + came.astype(jnp.float32)
                else:
                    piece(held, number)[rows] = kept + came

            each_rows(half, body)
            if not last:
                next_bit, next_length, next_first = rounds[part][turn + 1]
                if spot >= next_length:
                    hop(part, next_bit, number, next_first + spot - next_length).start()

        return step

    stages = [[core_sum(number) for number in wanted]]
    for turn in range(len(rounds[0])):
        length = rounds[0][turn][1]
        stages.append([later_sum(part, turn, spot) for spot in range(length - 1, -1, -1) for part in range(2)])

    def end():
        for number in range(nd):
            core_copy(number).wait_send()
        for part in range(2):
            for bit, length, first in rounds[part]:
                for spot in range(length):
                    hop(part, bit, part * chain_length + length + spot, first + spot).wait_send()

    return [[begin]] + stages + [[end]]


def computed_scatter(nd, me, zed, half, compute, stage, held, landed, totals, core_send, core_recv, send, recv):
    chain_length = nd // 2
    block = 256
    pieces = block // half
    per_part = chain_length // pieces
    turns = [part * per_part + spot for spot in range(per_part - 1, -1, -1) for part in range(2)]

    def piece(ref, number):
        return ref.at[pl.ds(number * half, half)]

    def block_of(ref, number):
        return ref.at[pl.ds(number * block, block)]

    rounds, slot = [], 0
    for part, order in enumerate(bit_orders(nd)):
        length, own_rounds = chain_length, []
        for bit in order[::-1]:
            length = length // 2
            own_rounds.append((bit, length, slot))
            slot = slot + length
        rounds.append(own_rounds)

    def core_copy(number):
        return pltpu.make_async_remote_copy(
            src_ref=block_of(stage, number),
            dst_ref=block_of(held, number),
            send_sem=core_send.at[number],
            recv_sem=core_recv.at[number],
            device_id=(flip(me, 0), zed),
            device_id_type=MESH,
        )

    def hop(bit, number, where):
        return pltpu.make_async_remote_copy(
            src_ref=piece(held, number),
            dst_ref=piece(landed, where),
            send_sem=send.at[where],
            recv_sem=recv.at[where],
            device_id=(flip(me, bit), zed),
            device_id_type=MESH,
        )

    def away(number):
        def step():
            compute(nd * half + number * block, None, block_of(stage, number))
            core_copy(number).start()

        return step

    def near(number):
        def step():
            core_copy(number).wait_recv()
            compute(number * block, block_of(held, number), block_of(held, number))
            for inner in range(pieces):
                place = number * pieces + inner
                part, spot = place // chain_length, place % chain_length
                bit, length, first = rounds[part][0]
                if spot >= length:
                    hop(bit, place, first + spot - length).start()

        return step

    def later_sum(part, turn, spot):
        bit, length, first = rounds[part][turn]
        number = part * chain_length + spot

        def step():
            hop(bit, number, first + spot).wait_recv()
            last = turn == len(rounds[part]) - 1

            def body(rows):
                kept, came = piece(held, number)[rows], piece(landed, first + spot)[rows]
                if last:
                    value = kept.astype(jnp.float32) + came.astype(jnp.float32)
                    for target, start, columns in totals:
                        piece(target, part)[rows] = value[:, start : start + columns]
                else:
                    piece(held, number)[rows] = kept + came

            each_rows(half, body)
            if not last:
                next_bit, next_length, next_first = rounds[part][turn + 1]
                if spot >= next_length:
                    hop(next_bit, number, next_first + spot - next_length).start()

        return step

    def end():
        for number in range(len(turns)):
            core_copy(number).wait_send()
        for part in range(2):
            for bit, length, first in rounds[part]:
                for spot in range(length):
                    hop(bit, part * chain_length + length + spot, first + spot).wait_send()

    later = []
    for turn in range(len(rounds[0])):
        length = rounds[0][turn][1]
        later.append([later_sum(part, turn, spot) for spot in range(length - 1, -1, -1) for part in range(2)])
    return [away(number) for number in turns], [near(number) for number in turns], later, end


def computed_scratch(nd, rows, columns):
    slots = nd - 2
    blocks = nd * rows // 2 // 256
    return [
        pltpu.VMEM((nd * rows // 2, columns), jnp.bfloat16),
        pltpu.VMEM((nd * rows // 2, columns), jnp.bfloat16),
        pltpu.VMEM((slots * rows // 2, columns), jnp.bfloat16),
        pltpu.SemaphoreType.DMA((blocks,)),
        pltpu.SemaphoreType.DMA((blocks,)),
        pltpu.SemaphoreType.DMA((slots,)),
        pltpu.SemaphoreType.DMA((slots,)),
    ]


def products_of(left, rights, tile):
    def compute(start, add, target):
        turned_left = jnp.transpose(left[:, start : start + 256])
        at = 0
        for right, columns in rights:
            for first in range(0, columns, tile):
                extent = slice(first, min(first + tile, columns))
                value = jnp.dot(turned_left, right[:, extent], preferred_element_type=jnp.float32)
                here = slice(at + extent.start, at + extent.stop)
                if add is not None:
                    value = value + add[:, here].astype(jnp.float32)
                target[:, here] = value.astype(jnp.bfloat16)
            at = at + columns

    return compute


def staggered(flows):
    steps = [step for flow in flows for step in flow[0]]
    depth = len(flows[0]) - 2
    for turn in range(depth + len(flows) - 1):
        for number in range(len(flows) - 1, -1, -1):
            if 0 <= turn - number < depth:
                steps = steps + flows[number][1 + turn - number]
    return steps + [step for flow in flows for step in flow[-1]]


def scatter_scratch(nd, rows, columns):
    slots = nd - 2
    return [
        pltpu.VMEM((nd * rows // 2, columns), jnp.bfloat16),
        pltpu.VMEM((nd * rows // 2, columns), jnp.bfloat16),
        pltpu.VMEM((slots * rows // 2, columns), jnp.bfloat16),
        pltpu.SemaphoreType.DMA((nd,)),
        pltpu.SemaphoreType.DMA((nd,)),
        pltpu.SemaphoreType.DMA((slots,)),
        pltpu.SemaphoreType.DMA((slots,)),
        pltpu.SemaphoreType.DMA((nd,)),
    ]


def line_gather(nt, me, zed, chunks, own, everything, send, recv):
    size = own.shape[0] // chunks

    def own_rows(chunk):
        return own.at[pl.ds(chunk * size, size)]

    def rows(block, chunk):
        return everything.at[aligned(block * (size * chunks) + chunk * size, size)]

    def copy(source, block, chunk, side):
        return pltpu.make_async_remote_copy(
            src_ref=source,
            dst_ref=rows(block, chunk),
            send_sem=send.at[side, block, chunk],
            recv_sem=recv.at[block, chunk],
            device_id=(me, zed + 1 - 2 * side),
            device_id_type=MESH,
        )

    def keep(chunk):
        return pltpu.make_async_copy(own_rows(chunk), rows(zed, chunk), recv.at[zed, chunk])

    def first(chunk):
        for side, condition in ((0, zed < nt - 1), (1, zed > 0)):

            @pl.when(condition)
            def _(side=side):
                copy(own_rows(chunk), zed, chunk, side).start()

        keep(chunk).start()

    def onward(chunk, distance):
        for side, block in ((0, zed - distance), (1, zed + distance)):
            inside = (block >= 0) if side == 0 else (block < nt)
            open_end = (zed < nt - 1) if side == 0 else (zed > 0)

            @pl.when(inside)
            def _(block=block, side=side):
                copy(rows(block, chunk), block, chunk, side).wait_recv()

            @pl.when(jnp.logical_and(inside, open_end))
            def _(block=block, side=side):
                copy(rows(block, chunk), block, chunk, side).start()

    def end(chunk):
        keep(chunk).wait()
        for side, condition in ((0, zed < nt - 1), (1, zed > 0)):

            @pl.when(condition)
            def _(side=side):
                copy(own_rows(chunk), zed, chunk, side).wait_send()

            for distance in range(1, nt - 1):
                block = zed - distance if side == 0 else zed + distance
                inside = (block >= 0) if side == 0 else (block < nt)

                @pl.when(jnp.logical_and(inside, condition))
                def _(block=block, side=side):
                    copy(rows(block, chunk), block, chunk, side).wait_send()

    return first, onward, end


def line_gather_semaphores(nt, chunks):
    return [pltpu.SemaphoreType.DMA((2, nt, chunks)), pltpu.SemaphoreType.DMA((nt, chunks))]


def line_reduce(nt, me, zed, chunks, parts, rising, falling, send, recv):
    block_rows = parts.shape[0] // nt
    size = block_rows // chunks
    sides = ((0, rising), (1, falling))

    def rows(block, chunk):
        return aligned(block * block_rows + chunk * size, size)

    def copy(source, side, held, block, chunk):
        return pltpu.make_async_remote_copy(
            src_ref=source.at[rows(block, chunk)],
            dst_ref=held.at[rows(block, chunk)],
            send_sem=send.at[side, block, chunk],
            recv_sem=recv.at[side, block, chunk],
            device_id=(me, zed + 1 - 2 * side),
            device_id_type=MESH,
        )

    def role(side, turn):
        away = nt - 1 - turn
        if side == 0:
            return zed + away, zed + away < nt, zed == 0
        return zed - away, zed - away >= 0, zed == nt - 1

    def pass_on(chunk, turn):
        for side, held in sides:
            block, active, source = role(side, turn)

            @pl.when(jnp.logical_and(active, source))
            def _(side=side, held=held, block=block):
                copy(parts, side, held, block, chunk).start()

            @pl.when(jnp.logical_and(active, jnp.logical_not(source)))
            def _(side=side, held=held, block=block):
                copy(held, side, held, block, chunk).wait_recv()

                def body(inner):
                    where = aligned(block * block_rows + chunk * size + inner.start, inner.size)
                    held[where] = parts[where] + held[where]

                each_rows(size, body)
                copy(held, side, held, block, chunk).start()

    def own_sum(chunk, total):
        where = rows(zed, chunk)
        total[...] = parts[where].astype(jnp.float32)
        for side, held in sides:

            @pl.when(zed > 0 if side == 0 else zed < nt - 1)
            def _(side=side, held=held):
                copy(held, side, held, zed, chunk).wait_recv()
                total[...] += held[where].astype(jnp.float32)

    def end(chunk):
        for turn in range(nt - 1):
            for side, held in sides:
                block, active, source = role(side, turn)

                @pl.when(active)
                def _(side=side, held=held, block=block):
                    copy(held, side, held, block, chunk).wait_send()

    return pass_on, own_sum, end


def line_reduce_scratch(nt, block_rows, columns, chunks):
    return [
        pltpu.VMEM((nt * block_rows, columns), jnp.bfloat16),
        pltpu.VMEM((nt * block_rows, columns), jnp.bfloat16),
        pltpu.VMEM((block_rows // chunks, columns), jnp.float32),
        pltpu.SemaphoreType.DMA((2, nt, chunks)),
        pltpu.SemaphoreType.DMA((2, nt, chunks)),
    ]


HBM = pl.BlockSpec(memory_space=pl.ANY)
ONCHIP = pl.BlockSpec(memory_space=pltpu.VMEM)


def near_first(nt, zed, turn):
    block = 0
    for mine in range(nt):
        order = sorted(range(nt), key=lambda other: (abs(other - mine), other))
        block = block + jnp.where(zed == mine, order[turn], 0)
    return block


def first_gathers(nd, nt, rows, grad, small, main_own, out_own, shared_columns):
    chunks = 4
    bits = nd.bit_length() - 1
    blocks = relative_blocks(nd)
    block_rows, width = rows.shape
    lane = width // len(blocks)
    if lane % 128:
        rows, grad = to_relative(rows, 1, nd), to_relative(grad, 1, nd)
    main_columns, small_columns = main_own.shape[1], small.shape[1]
    side_columns = shared_columns + 2 * HEAD_SIZE
    gains_at = shared_columns + 2 * KEY_VALUE_HEADS * HEAD_SIZE
    tile = 256

    def reorder(me, source, target):
        if lane % 128:
            target[...] = source[...]
            return
        for number, (other, part) in enumerate(blocks):
            start = (mixed_with(me, other, bits) * 2 + part) * lane
            target[:, number * lane : (number + 1) * lane] = source[:, pl.ds(pl.multiple_of(start, lane), lane)]

    def kernel(
        rows_in, grad_in, small_ref, main_ref, out_ref,
        rows_ref, grad_ref, gains_ref, normed_all, small_line, main_all, side_all, out_all, main_raw, side_raw,
        row_space, normed, main_space, small_space, side_space, main_stage, side_stage, store_sems, *refs,
    ):
        row_sems, small_sems = refs[:2], refs[2:4]
        main_sems, small_dp, out_sems = refs[4:7], refs[7:10], refs[10:13]
        me, zed = enter(nt, bits)
        small_first, small_onward, small_end = line_gather(nt, me, zed, 1, small_ref, small_line, *small_sems)
        row_first, row_onward, row_end = line_gather(nt, me, zed, chunks, rows_ref, row_space, *row_sems)
        main_flow = gather_steps(nd, me, zed, main_ref, main_space, *main_sems)
        small_flow = gather_steps(nd, me, zed, small_line, small_space, *small_dp)
        out_flow = gather_steps(nd, me, zed, out_ref, out_all, *out_sems)
        head = zed * (QUERY_HEADS // nt) // (QUERY_HEADS // KEY_VALUE_HEADS)

        def columns(turn):
            if turn == 0:
                return small_space.at[:, pl.ds(0, shared_columns)], side_space.at[:, pl.ds(0, shared_columns)]
            start = shared_columns + ((turn - 1) * KEY_VALUE_HEADS + head) * HEAD_SIZE
            target = shared_columns + (turn - 1) * HEAD_SIZE
            return (
                small_space.at[:, pl.ds(pl.multiple_of(start, HEAD_SIZE), HEAD_SIZE)],
                side_space.at[:, pl.ds(target, HEAD_SIZE)],
            )

        def keep(number):
            source, target = ((main_space, main_all), (side_space, side_all), (normed, normed_all))[number]
            return pltpu.make_async_copy(source, target, store_sems.at[number])

        def pick(turn):
            return pltpu.make_async_copy(*columns(turn), store_sems.at[3 + turn])

        def store(turn, number):
            block = near_first(nt, zed, turn)
            stage, target = ((main_stage, main_raw), (side_stage, side_raw))[number]
            return pltpu.make_async_copy(
                stage.at[turn % 2],
                target.at[aligned(block * block_rows, block_rows)],
                store_sems.at[6 + 2 * turn + number],
            )

        def project(turn):
            where = aligned(near_first(nt, zed, turn) * block_rows, block_rows)
            value = (rows_ref[...] if turn == 0 else row_space[where]).astype(jnp.float32)
            scale = lax.rsqrt(jnp.mean(value * value, axis=-1, keepdims=True) + eps)
            mine = (value * scale * gains_ref[0:1]).astype(jnp.bfloat16)
            normed[where] = mine
            if turn >= 2:
                store(turn - 2, 0).wait()
                store(turn - 2, 1).wait()
            for space, stage, number in ((main_space, main_stage, 0), (side_space, side_stage, 1)):
                for start in range(0, space.shape[1], tile):
                    extent = slice(start, min(start + tile, space.shape[1]))
                    stage[turn % 2, :, extent] = jnp.dot(
                        mine, space[:, extent], preferred_element_type=jnp.float32
                    )
                store(turn, number).start()

        small_first(0)
        main_flow[0]()
        reorder(me, rows_in, rows_ref)
        for chunk in range(chunks):
            row_first(chunk)
        for distance in range(1, nt):
            small_onward(0, distance)
        small_end(0)
        small_flow[0]()
        out_flow[0]()
        reorder(me, grad_in, grad_ref)
        near = [
            functools.partial(row_onward, chunk, distance) for distance in range(1, nt - 1) for chunk in range(chunks)
        ]
        together(near, main_flow[1:-1] + small_flow[1:-1])
        small_flow[-1]()
        for turn in range(3):
            pick(turn).start()
        for start in range(0, width, 128):
            turned_block = jnp.transpose(
                small_space[start : start + 128, gains_at : gains_at + 128].astype(jnp.float32)
            )
            gains_ref[:, start : start + 128] = turned_block[:8]
        main_flow[-1]()
        keep(0).start()
        for turn in range(3):
            pick(turn).wait()
        keep(1).start()

        def last_rows():
            for chunk in range(chunks):
                row_onward(chunk, nt - 1)

        compute = [functools.partial(project, turn) for turn in range(nt - 1)] + [last_rows]
        together(compute, out_flow[1:-1])
        project(nt - 1)
        keep(2).start()
        out_flow[-1]()
        for chunk in range(chunks):
            row_end(chunk)
        for turn in range(max(nt - 2, 0), nt):
            store(turn, 0).wait()
            store(turn, 1).wait()
        for number in range(3):
            keep(number).wait()

    def sized(array, times, dtype=None):
        return jax.ShapeDtypeStruct((array.shape[0] * times, array.shape[1]), dtype or array.dtype)

    tokens = block_rows * nt
    return pl.pallas_call(
        kernel,
        out_shape=[
            sized(rows, 1),
            sized(grad, 1),
            jax.ShapeDtypeStruct((8, width), jnp.float32),
            sized(rows, nt),
            sized(small, nt),
            sized(main_own, nd),
            jax.ShapeDtypeStruct((width, side_columns), small.dtype),
            sized(out_own, nd),
            jax.ShapeDtypeStruct((tokens, main_columns), jnp.float32),
            jax.ShapeDtypeStruct((tokens, side_columns), jnp.float32),
        ],
        in_specs=[ONCHIP] * 2 + [HBM] * 3,
        out_specs=[ONCHIP] * 3 + [HBM] * 7,
        scratch_shapes=[
            pltpu.VMEM((tokens, width), jnp.bfloat16),
            pltpu.VMEM((tokens, width), jnp.bfloat16),
            pltpu.VMEM((width, main_columns), jnp.bfloat16),
            pltpu.VMEM((width, small_columns), jnp.bfloat16),
            pltpu.VMEM((width, side_columns), jnp.bfloat16),
            pltpu.VMEM((2, block_rows, main_columns), jnp.float32),
            pltpu.VMEM((2, block_rows, side_columns), jnp.float32),
            pltpu.SemaphoreType.DMA((6 + 2 * nt,)),
        ]
        + line_gather_semaphores(nt, chunks)
        + line_gather_semaphores(nt, 1)
        + gather_semaphores(nd) * 3,
        compiler_params=pltpu.CompilerParams(
            collective_id=0, has_side_effects=True, vmem_limit_bytes=VMEM_LIMIT
        ),
        name="first_gathers",
    )(rows, grad, small, main_own, out_own)


def middle_rows(nd, nt, parts, resid, gain, groups):
    chunks = 4
    bits = nd.bit_length() - 1
    count = len(groups)
    block_rows, width = resid.shape
    size = block_rows // chunks

    def kernel(parts_ref, resid_ref, gain_ref, *refs):
        group_refs, refs = refs[:count], refs[count:]
        middle_ref, rows_all = refs[:2]
        group_all, refs = refs[2 : 2 + count], refs[2 + count :]
        own, rising, falling, total, send, recv = refs[:6]
        gather_sems, refs = refs[6:8], refs[8:]
        me, zed = enter(nt, bits)
        pass_on, own_sum, reduce_end = line_reduce(nt, me, zed, chunks, parts_ref, rising, falling, send, recv)
        first, onward, gather_end = line_gather(nt, me, zed, chunks, own, rows_all, *gather_sems)
        flows = [
            gather_steps(nd, me, zed, group_refs[n], group_all[n], *refs[3 * n : 3 * n + 3]) for n in range(count)
        ]

        def finish(chunk):
            own_sum(chunk, total)
            where = pl.ds(chunk * size, size)
            value = resid_ref[where].astype(jnp.float32) + total[...]
            middle_ref[where] = value
            scale = lax.rsqrt(jnp.mean(value * value, axis=-1, keepdims=True) + eps)
            own[where] = (value * scale * gain_ref[...]).astype(jnp.bfloat16)
            first(chunk)

        line_schedule(nt, chunks, pass_on, finish, onward, [step for flow in flows for step in flow])
        for chunk in range(chunks):
            reduce_end(chunk)
            gather_end(chunk)

    return pl.pallas_call(
        kernel,
        out_shape=[
            jax.ShapeDtypeStruct((block_rows, width), jnp.float32),
            jax.ShapeDtypeStruct((block_rows * nt, width), jnp.bfloat16),
        ]
        + [jax.ShapeDtypeStruct((group.shape[0] * nd, group.shape[1]), group.dtype) for group in groups],
        in_specs=[ONCHIP] * 3 + [HBM] * count,
        out_specs=[ONCHIP] + [HBM] * (1 + count),
        scratch_shapes=[pltpu.VMEM((block_rows, width), jnp.bfloat16)]
        + line_reduce_scratch(nt, block_rows, width, chunks)
        + line_gather_semaphores(nt, chunks)
        + gather_semaphores(nd) * count,
        compiler_params=pltpu.CompilerParams(
            collective_id=1, has_side_effects=True, vmem_limit_bytes=VMEM_LIMIT
        ),
        name="middle_rows",
    )(parts, resid, gain, *groups)


def line_schedule(nt, chunks, pass_on, finish, onward, others):
    steps = []

    def add(function, chunk, *rest):
        if function is not None and 0 <= chunk < chunks:
            steps.append(functools.partial(function, chunk, *rest))

    for chunk in range(chunks + 2):
        add(pass_on, chunk, 0)
        add(finish, chunk - 1)
        add(onward, chunk - 2, nt - 1)
        for turn in range(1, nt - 1):
            add(pass_on, chunk, turn)
            add(onward, chunk - 1, turn)
    together(steps, others)


def absolute_lanes(me, bits, blocks, source, target):
    lane = source.shape[1] // len(blocks)
    for number, (other, part) in enumerate(blocks):
        start = (mixed_with(me, other, bits) * 2 + part) * lane
        target[:, pl.ds(pl.multiple_of(start, lane), lane)] = source[:, number * lane : (number + 1) * lane]


def norm_pull(value, gain, grad):
    scale = lax.rsqrt(jnp.mean(value * value, axis=-1, keepdims=True) + eps)
    scaled = grad * gain
    inner = jnp.mean(scaled * value, axis=-1, keepdims=True)
    return scale * (scaled - value * (inner * scale * scale)), grad * value * scale


def middle_back(nd, nt, parts, middle, cot, gain, groups):
    chunks = 4
    bits = nd.bit_length() - 1
    count = len(groups)
    block_rows, width = middle.shape
    size = block_rows // chunks
    per_group = 8
    blocks = relative_blocks(nd)
    lane = width // len(blocks)

    def kernel(parts_ref, middle_ref, cot_ref, gain_ref, *refs):
        group_refs, refs = refs[:count], refs[count:]
        grad_ref, gain_out, rows_all = refs[:3]
        totals, refs = refs[3 : 3 + count], refs[3 + count :]
        own, gain_grad, rising, falling, total, send, recv = refs[:7]
        gather_sems, refs = refs[7:9], refs[9:]
        me, zed = enter(nt, bits)
        pass_on, own_sum, reduce_end = line_reduce(nt, me, zed, chunks, parts_ref, rising, falling, send, recv)
        first, onward, gather_end = line_gather(nt, me, zed, chunks, own, rows_all, *gather_sems)
        flows = [
            scatter_steps(nd, me, zed, group_refs[n], totals[n], *refs[per_group * n : per_group * (n + 1)])
            for n in range(count)
        ]
        gain_grad[...] = jnp.zeros_like(gain_grad)

        def finish(chunk):
            own_sum(chunk, total)
            where = pl.ds(chunk * size, size)
            through, gained = norm_pull(middle_ref[where], gain_ref[...], total[...])
            value = cot_ref[where].astype(jnp.float32) + through
            gain_grad[...] += jnp.sum(gained, axis=0, keepdims=True)
            grad_ref[where] = value
            own[where] = value.astype(jnp.bfloat16)
            first(chunk)

        line_schedule(nt, chunks, pass_on, finish, onward, staggered(flows))
        if lane % 128:
            gain_out[...] = gain_grad[...]
        else:
            absolute_lanes(me, bits, blocks, gain_grad, gain_out)
        for chunk in range(chunks):
            reduce_end(chunk)
            gather_end(chunk)

    scratch = []
    for group in groups:
        scratch = scratch + scatter_scratch(nd, group.shape[0] // nd, group.shape[1])
    results = pl.pallas_call(
        kernel,
        out_shape=[
            jax.ShapeDtypeStruct((block_rows, width), jnp.float32),
            jax.ShapeDtypeStruct((1, width), jnp.float32),
            jax.ShapeDtypeStruct((block_rows * nt, width), jnp.bfloat16),
        ]
        + [jax.ShapeDtypeStruct((group.shape[0] // nd, group.shape[1]), jnp.float32) for group in groups],
        in_specs=[ONCHIP] * 4 + [HBM] * count,
        out_specs=[ONCHIP, ONCHIP, HBM] + [ONCHIP] * count,
        scratch_shapes=[pltpu.VMEM((block_rows, width), jnp.bfloat16), pltpu.VMEM((1, width), jnp.float32)]
        + line_reduce_scratch(nt, block_rows, width, chunks)
        + line_gather_semaphores(nt, chunks)
        + scratch,
        compiler_params=pltpu.CompilerParams(
            collective_id=2, has_side_effects=True, vmem_limit_bytes=VMEM_LIMIT
        ),
        name="middle_back",
    )(parts, middle, cot, gain, *groups)
    if lane % 128:
        results = (results[0], from_relative(results[1], 1, nd), *results[2:])
    return results


def last_sums(nd, nt, normed, grad_main, grad_side, main, side, resid, before, gain, small, shared_rows, main_widths):
    chunks = 4
    bits, line_bits = nd.bit_length() - 1, nt.bit_length() - 1
    block_rows, width = resid.shape
    tokens = block_rows * nt
    size = block_rows // chunks
    blocks = relative_blocks(nd)
    lane = width // len(blocks)
    main_columns, side_columns = main.shape[1], side.shape[1]
    shared_columns = side_columns - 2 * HEAD_SIZE
    side_rows = width // nd
    owned = side_rows // nt
    common_columns = shared_columns + 2 * KEY_VALUE_HEADS * HEAD_SIZE
    count = len(main_widths)
    if lane % 128:
        gain_part = jnp.sum(
            (contract_last(grad_main, main) + contract_last(grad_side, side)) * normed.astype(jnp.float32), axis=0
        )
        own_gain = from_relative(gain_part / gain[0], 0, nd)
        small = jnp.concatenate([own_gain.reshape(-1, 128), small[width // 128 :]])

    def kernel(normed_ref, grad_main_ref, grad_side_ref, main_ref, side_ref, resid_ref, before_ref, gain_ref, small_ref, *refs):
        grad_ref, small_out, common_ref = refs[:3]
        totals, refs = refs[3 : 3 + count], refs[3 + count :]
        parts_ref, side_total, rising, falling, total, send, recv = refs[:7]
        sums, landed, small_send, small_recv, gain_grad = refs[7:12]
        side_out, side_in, side_send, side_recv = refs[12:16]
        stage, held, hop_landed, core_send, core_recv, hop_send, hop_recv = refs[16:]
        me, zed = enter(nt, bits)
        pass_on, own_sum, reduce_end = line_reduce(nt, me, zed, chunks, parts_ref, rising, falling, send, recv)
        targets, at = [], 0
        for target, columns in zip(totals, main_widths):
            targets.append((target, at, columns))
            at = at + columns
        targets.append((side_total, main_columns, side_columns))
        away, near, later, scatter_end = computed_scatter(
            nd, me, zed, side_rows // 2,
            products_of(normed_ref, ((grad_main_ref, main_columns), (grad_side_ref, side_columns)), 512),
            stage, held, hop_landed, targets, core_send, core_recv, hop_send, hop_recv,
        )

        def part(turn):
            def step():
                where = aligned(near_first(nt, zed, nt - 1 - turn) * block_rows, block_rows)
                left, right = grad_main_ref[where], grad_side_ref[where]
                for start in range(0, width, 512):
                    extent = slice(start, start + 512)
                    value = product(left, main_ref[extent], LAST) + product(right, side_ref[extent], LAST)
                    parts_ref[where, extent] = value.astype(jnp.bfloat16)

            return step

        def gain_term(number):
            def step():
                if number == 0:
                    gain_grad[...] = jnp.zeros_like(gain_grad)

                def body(inner, carry):
                    where = aligned(number * block_rows + inner * 16, 16)
                    gain_grad[...] += parts_ref[where].astype(jnp.float32) * normed_ref[where].astype(jnp.float32)
                    return carry

                lax.fori_loop(0, block_rows // 16, body, 0)

            return step

        def small_copy(turn):
            if turn < bits:
                device = (flip(me, turn), zed)
            else:
                device = (me, flip(zed, turn - bits))
            extent = slice(None) if turn < bits else pl.ds(0, shared_rows)
            return pltpu.make_async_remote_copy(
                src_ref=sums.at[turn, extent],
                dst_ref=landed.at[turn, extent],
                send_sem=small_send.at[turn],
                recv_sem=small_recv.at[turn],
                device_id=device,
                device_id_type=MESH,
            )

        def small_begin():
            sums[0] = small_ref[...]
            if lane % 128 == 0:
                whole = jnp.sum(gain_grad[...], axis=0, keepdims=True) / gain_ref[...]
                for number, (other, half) in enumerate(blocks):
                    spot = mixed_with(me, other, bits) * 2 + half
                    sums[0, pl.ds(spot, 1), :] = whole[:, number * lane : (number + 1) * lane]
            small_copy(0).start()

        def small_step(turn):
            def step():
                small_copy(turn).wait_recv()
                if turn < bits:
                    sums[turn + 1] = sums[turn] + landed[turn]
                else:
                    sums[turn + 1] = sums[turn]
                    sums[turn + 1, pl.ds(0, shared_rows)] = (
                        sums[turn, pl.ds(0, shared_rows)] + landed[turn, pl.ds(0, shared_rows)]
                    )
                if turn + 1 < bits + line_bits:
                    small_copy(turn + 1).start()

            return step

        def small_end():
            for turn in range(bits + line_bits):
                small_copy(turn).wait_send()
            small_out[...] = sums[bits + line_bits]

        few = [gain_term(number) for number in range(nt if lane % 128 == 0 else 0)]
        few = few + [small_begin] + [small_step(turn) for turn in range(bits + line_bits)]

        def side_copy(source, target):
            return pltpu.make_async_remote_copy(
                src_ref=side_out.at[pl.ds(target * owned, owned)],
                dst_ref=side_in.at[source],
                send_sem=side_send.at[target],
                recv_sem=side_recv.at[source],
                device_id=(me, target),
                device_id_type=MESH,
            )

        def side_begin():
            side_out[...] = side_total[...].astype(jnp.bfloat16)
            for target in range(nt):

                @pl.when(zed != target)
                def _(target=target):
                    side_copy(zed, target).start()

            side_in[zed] = side_out[aligned(zed * owned, owned)]

        def side_end():
            for source in range(nt):

                @pl.when(zed != source)
                def _(source=source):
                    side_copy(source, source).wait_recv()

            common_ref[...] = jnp.zeros_like(common_ref)
            for source in range(nt):
                value = side_in[source].astype(jnp.float32)
                head = source * (QUERY_HEADS // nt) // (QUERY_HEADS // KEY_VALUE_HEADS)
                common_ref[:, :shared_columns] += value[:, :shared_columns]
                for turn in range(2):
                    at = shared_columns + (turn * KEY_VALUE_HEADS + head) * HEAD_SIZE
                    start = shared_columns + turn * HEAD_SIZE
                    common_ref[:, at : at + HEAD_SIZE] += value[:, start : start + HEAD_SIZE]
            for target in range(nt):

                @pl.when(zed != target)
                def _(target=target):
                    side_copy(zed, target).wait_send()

        def finish(chunk):
            own_sum(chunk, total)
            where = pl.ds(chunk * size, size)
            through, _ = norm_pull(resid_ref[where].astype(jnp.float32), gain_ref[...], total[...])
            value = before_ref[where] + through
            if lane % 128:
                grad_ref[where] = value
                return
            for number, (other, half) in enumerate(blocks):
                start = (mixed_with(me, other, bits) * 2 + half) * lane
                grad_ref[where, pl.ds(pl.multiple_of(start, lane), lane)] = value[:, number * lane : (number + 1) * lane]

        def passes(turn):
            return [functools.partial(pass_on, chunk, turn) for chunk in range(chunks)]

        middle = len(away) // 2
        steps = away[:middle] + [part(0)] + passes(0) + away[middle:] + [part(1)] + near[:middle]
        for turn in range(2, nt):
            steps.append(part(turn))
        steps = steps + passes(1) + near[middle:]
        for stage_steps in later[:-1]:
            steps = steps + stage_steps
        for turn in range(2, nt - 1):
            steps = steps + passes(turn)
        steps = steps + few[: -(bits + line_bits)] + later[-1] + [side_begin]
        ends = [functools.partial(finish, chunk) for chunk in range(chunks)]
        rest = few[-(bits + line_bits) :]
        for step in steps:
            step()
        together(ends, rest)
        side_end()
        small_end()
        scatter_end()
        for chunk in range(chunks):
            reduce_end(chunk)

    turns = bits + line_bits
    results = pl.pallas_call(
        kernel,
        out_shape=[
            jax.ShapeDtypeStruct((block_rows, width), jnp.float32),
            jax.ShapeDtypeStruct(small.shape, jnp.float32),
            jax.ShapeDtypeStruct((owned, common_columns), jnp.float32),
        ]
        + [jax.ShapeDtypeStruct((side_rows, columns), jnp.float32) for columns in main_widths],
        in_specs=[ONCHIP] * 9,
        out_specs=[ONCHIP] * (3 + count),
        scratch_shapes=[
            pltpu.VMEM((tokens, width), jnp.bfloat16),
            pltpu.VMEM((side_rows, side_columns), jnp.float32),
        ]
        + line_reduce_scratch(nt, block_rows, width, chunks)
        + [
            pltpu.VMEM((turns + 1, *small.shape), jnp.float32),
            pltpu.VMEM((turns, *small.shape), jnp.float32),
            pltpu.SemaphoreType.DMA((turns,)),
            pltpu.SemaphoreType.DMA((turns,)),
            pltpu.VMEM((16, width), jnp.float32),
            pltpu.VMEM((side_rows, side_columns), jnp.bfloat16),
            pltpu.VMEM((nt, owned, side_columns), jnp.bfloat16),
            pltpu.SemaphoreType.DMA((nt,)),
            pltpu.SemaphoreType.DMA((nt,)),
        ]
        + computed_scratch(nd, side_rows, main_columns + side_columns),
        compiler_params=pltpu.CompilerParams(
            collective_id=3, has_side_effects=True, vmem_limit_bytes=LARGE_LIMIT
        ),
        name="last_sums",
    )(normed, grad_main, grad_side, main, side, resid, before, gain, small)
    if lane % 128:
        results = (from_relative(results[0], 1, nd), *results[1:])
    return results


def silu_slope(value, sig):
    return sig * (1.0 + value * (1.0 - sig))


def split_dot(value, constant, dims, terms):
    total = None
    for _ in range(terms):
        piece = value.astype(jnp.bfloat16)
        value = value - piece.astype(jnp.float32)
        part = lax.dot_general(*((piece, constant) if dims[0] else (constant, piece)), dims[1], preferred_element_type=jnp.float32)
        total = part if total is None else total + part
    return total


PLAIN = (((1,), (0,)), ((), ()))
LAST = (((1,), (1,)), ((), ()))
FIRST = (((0,), (0,)), ((), ()))


def product(left, right, dims=PLAIN):
    return lax.dot_general(left, right, dims, preferred_element_type=jnp.float32)


def turned(value, cosine, sine):
    return value * cosine + pltpu.roll(value, value.shape[-1] // 2, 1) * sine


class Sizes:
    def __init__(self, channels, state_columns, query_columns, heads, length):
        self.channels, self.states = channels, state_columns // 2
        self.query, self.heads, self.length = query_columns, heads, length
        self.span = SPAN
        self.count = length // SPAN
        self.wide = channels + state_columns
        self.head_width = channels // heads
        self.step_at = 2 * channels + query_columns
        self.main = self.step_at + heads + (-(self.step_at + heads)) % 128
        self.step_lanes = self.main - self.step_at
        self.side = state_columns + 2 * HEAD_SIZE
        self.window = min(length, 3 * SPAN)


def spread_heads(size):
    table = np.zeros((size.step_lanes, size.channels), np.float32)
    for head in range(size.heads):
        table[head, head * size.head_width : (head + 1) * size.head_width] = 1.0
    return table.astype(jnp.bfloat16)


def turn_tables(length):
    half = HEAD_SIZE // 2
    angle = np.arange(length, dtype=np.float64)[:, None] * rope_base ** (-np.arange(half) / half)[None]
    cosine, sine = np.cos(angle), np.sin(angle)
    return (
        np.concatenate([cosine, cosine], 1).astype(np.float32),
        np.concatenate([-sine, sine], 1).astype(np.float32),
    )


def token_flags(segments, taps):
    seg = segments[0]
    length = seg.shape[0]
    columns = [jnp.ones((length,), bool)]
    ahead = []
    for lag in range(1, taps):
        columns.append(jnp.concatenate([jnp.zeros((lag,), bool), seg[lag:] == seg[:-lag]]))
        ahead.append(jnp.concatenate([seg[lag:] == seg[:-lag], jnp.zeros((lag,), bool)]))
    ends = seg.reshape(-1, SPAN)[:, -1]
    before = jnp.concatenate([jnp.full((1,), -1, seg.dtype), ends[:-1]])
    columns.append(seg == jnp.repeat(before, SPAN))
    columns.append(seg == jnp.repeat(ends, SPAN))
    columns = columns + ahead
    return jnp.pad(jnp.stack(columns, 1).astype(jnp.float32), ((0, 0), (0, 16 - len(columns))))


def chunk_values(size, taps, main_ref, wide_ref, flags, spread, taps_ref, heads_ref, segc, segr):
    span = size.span
    pre = wide_ref[pl.ds(8, span), :] * taps_ref[0:1, :]
    for lag in range(1, taps):
        pre = pre + wide_ref[pl.ds(8 - lag, span), :] * (flags[:, lag : lag + 1] * taps_ref[lag : lag + 1, :])
    sig = jax.nn.sigmoid(pre)
    act = pre * sig
    inner = act[:, : size.channels]
    bmat = act[:, size.channels : size.channels + size.states].astype(jnp.bfloat16)
    cmat = act[:, size.channels + size.states :].astype(jnp.bfloat16)
    step_in = main_ref[:, size.step_at :] + heads_ref[0:1, :]
    step = jnp.maximum(step_in, 0.0) + jnp.log1p(jnp.exp(-jnp.abs(step_in)))
    logdec = -step * heads_ref[1:2, :]
    rows = lax.broadcasted_iota(jnp.int32, (span, span), 0)
    columns = lax.broadcasted_iota(jnp.int32, (span, span), 1)
    later = jnp.where(rows >= columns, 1.0, 0.0).astype(jnp.bfloat16)
    cumul = split_dot(logdec, later, (False, PLAIN), 3)
    inside = jnp.logical_and(rows >= columns, segc == segr)
    ending = cumul[span - 1 : span, :]
    reach = jnp.exp(cumul) * flags[:, 4:5]
    tail = jnp.exp(ending - cumul) * flags[:, 5:6]
    step_wide = split_dot(step, spread, (True, PLAIN), 2)
    scaled = inner * step_wide
    return dict(
        pre=pre, sig=sig, inner=inner, bmat=bmat, cmat=cmat, step_in=step_in, step=step, logdec=logdec, later=later,
        cumul=cumul, turned=jnp.transpose(cumul), inside=inside, step_wide=step_wide, scaled=scaled,
        scaled_b=scaled.astype(jnp.bfloat16), meeting=product(cmat, bmat, LAST),
        reach_wide=split_dot(reach, spread, (True, PLAIN), 2), tail_wide=split_dot(tail, spread, (True, PLAIN), 2),
        skip_wide=split_dot(jnp.broadcast_to(heads_ref[2:3, :], (8, size.step_lanes)), spread, (True, PLAIN), 2)[0:1],
    )


def decay_of(values, head):
    spread = values["cumul"][:, head : head + 1] - values["turned"][head : head + 1, :]
    return jnp.exp(jnp.where(values["inside"], spread, -1e30))


def softmax_of(size, query, keys, chunk, start, segc, seg_all):
    scores = product(query, keys, LAST) * (1.0 / math.sqrt(HEAD_SIZE))
    rows = lax.broadcasted_iota(jnp.int32, scores.shape, 0) + chunk * size.span
    columns = lax.broadcasted_iota(jnp.int32, scores.shape, 1) + start
    allowed = jnp.logical_and(rows >= columns, segc == seg_all)
    masked = jnp.where(allowed, scores, -1e30)
    expo = jnp.exp(masked - jnp.max(masked, axis=-1, keepdims=True))
    return expo / jnp.sum(expo, axis=-1, keepdims=True)


def mixers_forward(size, taps, main_raw, side_raw, segments, flags, tap_rows, head_rows):
    span = size.span
    per_head = size.head_width

    def kernel(
        main_ref, side_ref, segc_ref, segr_ref, flags_ref, taps_ref, heads_ref, cos_ref, sin_ref, spread_ref,
        mixed_ref, y_ref, state_ref, keys_ref, values_ref, wide, state,
    ):
        chunk = pl.program_id(0)

        @pl.when(chunk == 0)
        def _():
            wide[0:8, :] = jnp.zeros((8, size.wide), jnp.float32)
            state[...] = jnp.zeros_like(state)
            keys_ref[...] = jnp.zeros_like(keys_ref)
            values_ref[...] = jnp.zeros_like(values_ref)

        wide[pl.ds(8, span), : size.channels] = main_ref[:, size.channels : 2 * size.channels]
        wide[pl.ds(8, span), size.channels :] = side_ref[:, : 2 * size.states]
        flags, spread, segc = flags_ref[...], spread_ref[...], segc_ref[...]
        segr = segr_ref[:, pl.ds(pl.multiple_of(chunk * span, span), span)]
        val = chunk_values(size, taps, main_ref, wide, flags, spread, taps_ref, heads_ref, segc, segr)
        wide[0:8, :] = wide[pl.ds(span, 8), :]
        held = state[...]
        held_b = held.astype(jnp.bfloat16)
        state_ref[...] = held
        across = val["reach_wide"] * product(val["cmat"], held_b)
        lane = lax.broadcasted_iota(jnp.int32, (span, 2 * per_head), 1)
        for pair in range(size.heads // 2):
            where = slice(pair * 2 * per_head, (pair + 1) * 2 * per_head)
            both = []
            for head in (2 * pair, 2 * pair + 1):
                weights = (val["meeting"] * decay_of(val, head)).astype(jnp.bfloat16)
                both.append(product(weights, val["scaled_b"][:, where]))
            result = jnp.where(lane < per_head, both[0], both[1])
            result = result + across[:, where] + val["skip_wide"][:, where] * val["inner"][:, where]
            y_ref[:, where] = result
            gate = main_ref[:, where]
            mixed_ref[:, where] = (result * (gate * jax.nn.sigmoid(gate))).astype(jnp.bfloat16)
        keep = jnp.broadcast_to(val["reach_wide"][span - 1 : span, :], (1, size.channels))
        state[...] = keep * held + product(
            val["bmat"], (val["tail_wide"] * val["scaled"]).astype(jnp.bfloat16), FIRST
        )

        cosine, sine = cos_ref[...], sin_ref[...]
        own = pl.ds(pl.multiple_of(chunk * span, span), span)
        key_at = 2 * size.states
        keys_ref[own, :] = turned(side_ref[:, key_at : key_at + HEAD_SIZE], cosine, sine).astype(jnp.bfloat16)
        values_ref[own, :] = side_ref[:, key_at + HEAD_SIZE :].astype(jnp.bfloat16)
        start = pl.multiple_of(jnp.maximum(chunk + 1 - size.window // span, 0) * span, span)
        seen = pl.ds(start, size.window)
        for head in range(size.query // HEAD_SIZE):
            at = 2 * size.channels + head * HEAD_SIZE
            query = turned(main_ref[:, at : at + HEAD_SIZE], cosine, sine).astype(jnp.bfloat16)
            probs = softmax_of(size, query, keys_ref[seen, :], chunk, start, segc, segr_ref[:, seen])
            result = product(probs.astype(jnp.bfloat16), values_ref[seen, :])
            at = size.channels + head * HEAD_SIZE
            mixed_ref[:, at : at + HEAD_SIZE] = result.astype(jnp.bfloat16)

    def rows(columns):
        return pl.BlockSpec((span, columns), lambda i: (i, 0))

    def whole(array):
        return pl.BlockSpec(array.shape, lambda i: (0, 0))

    cosine, sine = turn_tables(size.length)
    spread = spread_heads(size)
    tokens = size.length
    return pl.pallas_call(
        kernel,
        grid=(size.count,),
        in_specs=[
            rows(size.main), rows(size.side), rows(1), whole(segments), rows(16), whole(tap_rows), whole(head_rows),
            rows(HEAD_SIZE), rows(HEAD_SIZE), whole(spread),
        ],
        out_specs=[
            rows(size.channels + size.query), rows(size.channels),
            pl.BlockSpec((size.states, size.channels), lambda i: (i, 0)),
            pl.BlockSpec((tokens, HEAD_SIZE), lambda i: (0, 0)), pl.BlockSpec((tokens, HEAD_SIZE), lambda i: (0, 0)),
        ],
        out_shape=[
            jax.ShapeDtypeStruct((tokens, size.channels + size.query), jnp.bfloat16),
            jax.ShapeDtypeStruct((tokens, size.channels), jnp.float32),
            jax.ShapeDtypeStruct((size.count * size.states, size.channels), jnp.float32),
            jax.ShapeDtypeStruct((tokens, HEAD_SIZE), jnp.bfloat16),
            jax.ShapeDtypeStruct((tokens, HEAD_SIZE), jnp.bfloat16),
        ],
        scratch_shapes=[
            pltpu.VMEM((span + 8, size.wide), jnp.float32),
            pltpu.VMEM((size.states, size.channels), jnp.float32),
        ],
        compiler_params=pltpu.CompilerParams(
            dimension_semantics=("arbitrary",), vmem_limit_bytes=VMEM_LIMIT
        ),
        name="mixers_forward",
    )(main_raw, side_raw, segments.reshape(tokens, 1), segments, flags, tap_rows, head_rows,
      jnp.asarray(cosine), jnp.asarray(sine), jnp.asarray(spread))


def mixers_backward(
    nd, nt, size, taps, grad_mixed, main_raw, side_raw, segments, flags, tap_rows, head_rows, y_value, states, keys, values,
    grad_rows, mixed,
):
    bits = nd.bit_length() - 1
    out_rows, out_columns = grad_rows.shape[1] // nd, mixed.shape[1]
    span = size.span
    per_head = size.head_width
    count = size.count

    def kernel(
        grad_ref, main_ref, side_ref, before_ref, side_before_ref, segc_ref, segr_ref, flags_ref, taps_ref, heads_ref,
        cos_ref, sin_ref, spread_ref, y_ref, state_ref, keys_ref, values_ref, rows_ref, mixed_ref,
        grad_main, grad_side, tap_sums, head_sums, mixer_total, attn_total,
        wide, back, grad_state, grad_keys, grad_values,
        stage, held, landed, core_send, core_recv, hop_send, hop_recv,
    ):
        turn = pl.program_id(0)
        chunk = count - 1 - turn
        me, zed = lax.axis_index("dp"), lax.axis_index("tensor")
        away, near, later, scatter_end = computed_scatter(
            nd, me, zed, out_rows // 2, products_of(rows_ref, ((mixed_ref, out_columns),), 512), stage, held, landed,
            ((mixer_total, 0, size.channels), (attn_total, size.channels, size.query)),
            core_send, core_recv, hop_send, hop_recv,
        )
        stages = [away, near, *later[: count - 3], [step for stage_steps in later[count - 3 :] for step in stage_steps]]
        for number, stage_steps in enumerate(stages):

            @pl.when(turn == number)
            def _(number=number, stage_steps=stage_steps):
                if number == 0:
                    enter(nt, bits)
                for step in stage_steps:
                    step()
                if number == len(stages) - 1:
                    scatter_end()

        @pl.when(turn == 0)
        def _():
            back[pl.ds(span, 8), :] = jnp.zeros((8, size.wide), jnp.float32)
            grad_state[...] = jnp.zeros_like(grad_state)
            grad_keys[...] = jnp.zeros_like(grad_keys)
            grad_values[...] = jnp.zeros_like(grad_values)
            tap_sums[...] = jnp.zeros_like(tap_sums)
            head_sums[...] = jnp.zeros_like(head_sums)

        wide[0:8, : size.channels] = before_ref[...]
        wide[0:8, size.channels :] = side_before_ref[...]
        wide[pl.ds(8, span), : size.channels] = main_ref[:, size.channels : 2 * size.channels]
        wide[pl.ds(8, span), size.channels :] = side_ref[:, : 2 * size.states]
        flags, spread, segc = flags_ref[...], spread_ref[...], segc_ref[...]
        segr = segr_ref[:, pl.ds(pl.multiple_of(chunk * span, span), span)]
        val = chunk_values(size, taps, main_ref, wide, flags, spread, taps_ref, heads_ref, segc, segr)
        inner, scaled = val["inner"], val["scaled"]

        gate = main_ref[:, : size.channels]
        gate_sig = jax.nn.sigmoid(gate)
        grad = grad_ref[:, : size.channels]
        grad_main[:, : size.channels] = (grad * y_ref[...] * silu_slope(gate, gate_sig)).astype(jnp.bfloat16)
        grad_y = grad * (gate * gate_sig)
        grad_y_b = grad_y.astype(jnp.bfloat16)
        tap_sums[4:5, : size.channels] += jnp.sum(grad_y * inner, axis=0, keepdims=True)

        lane = lax.broadcasted_iota(jnp.int32, (span, 2 * per_head), 1)
        head_lane = lax.broadcasted_iota(jnp.int32, (span, size.step_lanes), 1)
        head_row = lax.broadcasted_iota(jnp.int32, (size.step_lanes, span), 0)
        grad_meeting = jnp.zeros((span, span), jnp.float32)
        by_row = jnp.zeros((span, size.step_lanes), jnp.float32)
        by_column = jnp.zeros((size.step_lanes, span), jnp.float32)
        pieces = []
        for pair in range(size.heads // 2):
            where = slice(pair * 2 * per_head, (pair + 1) * 2 * per_head)
            both = []
            for side in range(2):
                head = 2 * pair + side
                decay = decay_of(val, head)
                weights = val["meeting"] * decay
                mine = (lane < per_head) if side == 0 else (lane >= per_head)
                grad_own = jnp.where(mine, grad_y_b[:, where], jnp.zeros((), jnp.bfloat16))
                grad_weights = product(grad_own, val["scaled_b"][:, where], LAST)
                both.append(product(weights.astype(jnp.bfloat16), grad_y_b[:, where], FIRST))
                grad_meeting = grad_meeting + grad_weights * decay
                moved = grad_weights * weights
                by_row = jnp.where(head_lane == head, jnp.sum(moved, axis=1, keepdims=True), by_row)
                by_column = jnp.where(head_row == head, jnp.sum(moved, axis=0, keepdims=True), by_column)
            pieces.append(jnp.where(lane < per_head, both[0], both[1]))
        grad_scaled = jnp.concatenate(pieces, axis=1)
        grad_cumul = by_row - jnp.transpose(by_column)

        held = state_ref[...]
        held_b = held.astype(jnp.bfloat16)
        grad_held = grad_state[...]
        grad_held_b = grad_held.astype(jnp.bfloat16)
        grad_meeting_b = grad_meeting.astype(jnp.bfloat16)
        reached = val["reach_wide"] * grad_y
        reached_b = reached.astype(jnp.bfloat16)
        grad_cumul = grad_cumul + split_dot(reached * product(val["cmat"], held_b), spread, (True, LAST), 2)
        grad_c = product(reached_b, held_b, LAST) + product(grad_meeting_b, val["bmat"])
        from_state = val["tail_wide"] * product(val["bmat"], grad_held_b)
        grad_b = product(grad_meeting_b, val["cmat"], FIRST) + product(
            (val["tail_wide"] * scaled).astype(jnp.bfloat16), grad_held_b, LAST
        )
        grad_scaled = grad_scaled + from_state
        ended = split_dot(scaled * from_state, spread, (True, LAST), 2)
        keep = val["reach_wide"][span - 1 : span, :]
        kept = jnp.sum(grad_held * held, axis=0, keepdims=True) * keep
        kept = split_dot(jnp.broadcast_to(kept, (8, size.channels)), spread, (True, LAST), 2)[0:1]
        at_end = jnp.sum(ended, axis=0, keepdims=True) + kept
        grad_logdec = split_dot(grad_cumul - ended, val["later"], (False, FIRST), 3) + at_end
        grad_state[...] = keep * grad_held + product(val["cmat"], reached_b, FIRST)

        grad_inner = grad_scaled * val["step_wide"] + grad_y * val["skip_wide"]
        grad_step = split_dot(grad_scaled * inner, spread, (True, LAST), 2) - grad_logdec * heads_ref[1:2, :]
        grad_step_raw = grad_step * jax.nn.sigmoid(val["step_in"])
        head_sums[0:1, :] += jnp.sum(grad_step_raw, axis=0, keepdims=True)
        head_sums[1:2, :] += jnp.sum(grad_logdec * val["logdec"], axis=0, keepdims=True)
        grad_main[:, size.step_at :] = grad_step_raw.astype(jnp.bfloat16)

        slope = silu_slope(val["pre"], val["sig"])
        grad_pre = jnp.concatenate([grad_inner, grad_b, grad_c], axis=1) * slope
        back[pl.ds(0, span), :] = grad_pre
        raw = grad_pre * taps_ref[0:1, :]
        tap_sums[0:1, :] += jnp.sum(grad_pre * wide[pl.ds(8, span), :], axis=0, keepdims=True)
        for lag in range(1, taps):
            tap_sums[lag : lag + 1, :] += jnp.sum(
                grad_pre * (wide[pl.ds(8 - lag, span), :] * flags[:, lag : lag + 1]), axis=0, keepdims=True
            )
            raw = raw + back[pl.ds(lag, span), :] * (flags[:, 5 + lag : 6 + lag] * taps_ref[lag : lag + 1, :])
        back[pl.ds(span, 8), :] = back[0:8, :]
        grad_main[:, size.channels : 2 * size.channels] = raw[:, : size.channels].astype(jnp.bfloat16)
        grad_side[:, : 2 * size.states] = raw[:, size.channels :].astype(jnp.bfloat16)

        cosine, sine = cos_ref[...], sin_ref[...]
        start = pl.multiple_of(jnp.maximum(chunk + 1 - size.window // span, 0) * span, span)
        seen = pl.ds(start, size.window)
        seen_keys, seen_values = keys_ref[seen, :], values_ref[seen, :]
        scale = 1.0 / math.sqrt(HEAD_SIZE)
        for head in range(size.query // HEAD_SIZE):
            at = 2 * size.channels + head * HEAD_SIZE
            query = turned(main_ref[:, at : at + HEAD_SIZE], cosine, sine).astype(jnp.bfloat16)
            probs = softmax_of(size, query, seen_keys, chunk, start, segc, segr_ref[:, seen])
            out_at = size.channels + head * HEAD_SIZE
            grad_out = grad_ref[:, out_at : out_at + HEAD_SIZE].astype(jnp.bfloat16)
            grad_probs = product(grad_out, seen_values, LAST)
            delta = jnp.sum(grad_probs * probs, axis=-1, keepdims=True)
            grad_scores = (probs * (grad_probs - delta)).astype(jnp.bfloat16)
            grad_query = product(grad_scores, seen_keys) * scale
            grad_main[:, at : at + HEAD_SIZE] = turned(grad_query, cosine, -sine).astype(jnp.bfloat16)
            grad_keys[seen, :] += product(grad_scores, query, FIRST) * scale
            grad_values[seen, :] += product(probs.astype(jnp.bfloat16), grad_out, FIRST)
        own = pl.ds(pl.multiple_of(chunk * span, span), span)
        key_at = 2 * size.states
        grad_side[:, key_at : key_at + HEAD_SIZE] = turned(grad_keys[own, :], cosine, -sine).astype(jnp.bfloat16)
        grad_side[:, key_at + HEAD_SIZE :] = grad_values[own, :].astype(jnp.bfloat16)

    def rows(columns):
        return pl.BlockSpec((span, columns), lambda i: (count - 1 - i, 0))

    def previous(columns, column):
        return pl.BlockSpec((8, columns), lambda i: (jnp.maximum((count - 1 - i) * (span // 8) - 1, 0), column))

    def whole(array):
        return pl.BlockSpec(array.shape, lambda i: (0, 0))

    cosine, sine = turn_tables(size.length)
    spread = spread_heads(size)
    tokens = size.length
    return pl.pallas_call(
        kernel,
        grid=(count,),
        in_specs=[
            rows(size.channels + size.query), rows(size.main), rows(size.side), previous(size.channels, 1),
            previous(2 * size.states, 0), rows(1), whole(segments), rows(16), whole(tap_rows), whole(head_rows),
            rows(HEAD_SIZE), rows(HEAD_SIZE), whole(spread), rows(size.channels),
            pl.BlockSpec((size.states, size.channels), lambda i: (count - 1 - i, 0)), whole(keys), whole(values),
            whole(grad_rows), whole(mixed),
        ],
        out_specs=[
            rows(size.main), rows(size.side), pl.BlockSpec((8, size.wide), lambda i: (0, 0)),
            pl.BlockSpec((8, size.step_lanes), lambda i: (0, 0)),
            pl.BlockSpec((out_rows, size.channels), lambda i: (0, 0)),
            pl.BlockSpec((out_rows, size.query), lambda i: (0, 0)),
        ],
        out_shape=[
            jax.ShapeDtypeStruct((tokens, size.main), jnp.bfloat16),
            jax.ShapeDtypeStruct((tokens, size.side), jnp.bfloat16),
            jax.ShapeDtypeStruct((8, size.wide), jnp.float32),
            jax.ShapeDtypeStruct((8, size.step_lanes), jnp.float32),
            jax.ShapeDtypeStruct((out_rows, size.channels), jnp.float32),
            jax.ShapeDtypeStruct((out_rows, size.query), jnp.float32),
        ],
        scratch_shapes=[
            pltpu.VMEM((span + 8, size.wide), jnp.float32),
            pltpu.VMEM((span + 8, size.wide), jnp.float32),
            pltpu.VMEM((size.states, size.channels), jnp.float32),
            pltpu.VMEM((tokens, HEAD_SIZE), jnp.float32),
            pltpu.VMEM((tokens, HEAD_SIZE), jnp.float32),
        ]
        + computed_scratch(nd, out_rows, out_columns),
        compiler_params=pltpu.CompilerParams(
            dimension_semantics=("arbitrary",), vmem_limit_bytes=VMEM_LIMIT, collective_id=4, has_side_effects=True
        ),
        cost_estimate=pl.CostEstimate(flops=40 * 10**9, bytes_accessed=60 * 10**6, transcendentals=10**7),
        name="mixers_backward",
    )(grad_mixed, main_raw, side_raw, main_raw, side_raw, segments.reshape(tokens, 1), segments, flags, tap_rows,
      head_rows, jnp.asarray(cosine), jnp.asarray(sine), jnp.asarray(spread), y_value, states, keys, values, grad_rows, mixed)


def per_device(
    nd,
    nt,
    residual,
    segments,
    mixgain,
    ffngain,
    gateproj,
    innerproj,
    stepproj,
    sharedproj,
    innerconv,
    sharedconv,
    stepbias,
    decaylog,
    skipgain,
    mixerout,
    queryproj,
    keyvalue,
    attnout,
    ffngate,
    upproj,
    downproj,
    cotangent,
):
    bfloat = jnp.bfloat16
    single = jnp.float32
    width = residual.shape[1]
    zed = lax.axis_index("tensor")
    seq_count, length = segments.shape
    token_count = seq_count * length
    channels = innerproj.shape[1]
    state_columns = sharedproj.shape[1]
    heads = stepproj.shape[1]
    query_columns = queryproj.shape[1]
    ffn_columns = ffngate.shape[1]
    small_rows = sharedproj.shape[0]
    conv_rows = sharedconv.shape[0]
    taps = sharedconv.shape[1]

    gains = jnp.concatenate(
        [
            mixgain[:, None],
            ffngain[:, None],
            jnp.pad(sharedconv, ((0, small_rows - conv_rows), (0, 0))),
            jnp.zeros((small_rows, 128 - 2 - taps), bfloat),
        ],
        axis=1,
    )
    main_used = 2 * channels + query_columns + heads
    main_own = jnp.concatenate(
        [
            gateproj,
            innerproj,
            queryproj,
            stepproj,
            jnp.zeros((gateproj.shape[0], -main_used % 128), bfloat),
        ],
        axis=1,
    )
    resid_own, cot_own, gain_rows, normed, _, main, side, out_w, main_raw, side_raw = first_gathers(
        nd,
        nt,
        residual,
        cotangent,
        jnp.concatenate([sharedproj, keyvalue, gains], axis=1),
        main_own,
        jnp.concatenate([mixerout, attnout], axis=1),
        state_columns,
    )
    grad_rows = lax.all_gather(cot_own, "tensor", axis=0, tiled=True)
    gain_one, gain_two = gain_rows[0], gain_rows[1]
    conv_shared = from_relative(gain_rows[2 : 2 + taps], 1, nd)
    conv_shared = conv_shared.reshape(taps, nd * nt, small_rows)[:, :, :conv_rows].reshape(taps, -1)

    size = Sizes(channels, state_columns, query_columns, heads, length)
    flags = token_flags(segments, taps)
    tap_rows = jnp.concatenate([innerconv.astype(single).T, conv_shared], axis=1)
    tap_rows = jnp.pad(tap_rows, ((0, 8 - taps), (0, 0)))
    head_rows = jnp.stack([stepbias.astype(single), jnp.exp(decaylog.astype(single)), skipgain.astype(single)])
    head_rows = jnp.pad(head_rows, ((0, 5), (0, size.step_lanes - heads)))
    mixed_in, y_value, states, keys, values = mixers_forward(
        size, taps, main_raw, side_raw, segments, flags, tap_rows, head_rows
    )
    mix_part = contract_last(mixed_in, out_w).astype(bfloat)
    middle, rows_two, ffn_w = middle_rows(
        nd,
        nt,
        mix_part,
        resid_own,
        gain_two[None],
        [jnp.concatenate([ffngate, upproj, downproj], axis=1)],
    )
    gate_up_w = ffn_w[:, : 2 * ffn_columns]
    down_w = ffn_w[:, 2 * ffn_columns :]
    gate_up = matrix_product(rows_two, gate_up_w)
    gate = gate_up[:, :ffn_columns]
    upper = gate_up[:, ffn_columns:]
    sigma = jax.nn.sigmoid(gate)
    hidden = (gate * sigma * upper).astype(bfloat)
    grad_hidden = matrix_product(grad_rows, down_w)
    grad_gate = (grad_hidden * upper * sigma * (1.0 + gate * (1.0 - sigma))).astype(bfloat)
    grad_upper = (grad_hidden * gate * sigma).astype(bfloat)
    grad_gate_up = jnp.concatenate([grad_gate, grad_upper], axis=1)
    two_part = contract_last(grad_gate_up, gate_up_w).astype(bfloat)
    grad_middle, grad_gain_two, grad_mix_rows, down_g, gate_up_g = middle_back(
        nd,
        nt,
        two_part,
        middle,
        cot_own,
        gain_two[None],
        [
            contract_leading_axis(grad_rows, hidden).astype(bfloat),
            contract_leading_axis(rows_two, grad_gate_up).astype(bfloat),
        ],
    )
    ffn_part = after(contract_last(hidden, down_w).astype(bfloat), grad_mix_rows)
    ffn_out = lax.psum_scatter(ffn_part, "tensor", scatter_dimension=0, tiled=True)
    layer_out = from_relative(middle + ffn_out.astype(single), 1, nd)
    grad_mixed_in = matrix_product(grad_mix_rows, out_w)
    grad_main, grad_side, tap_sums, head_sums, mixer_g, attn_g = mixers_backward(
        nd, nt, size, taps, grad_mixed_in, main_raw, side_raw, segments, flags, tap_rows, head_rows, y_value, states,
        keys, values, grad_mix_rows, mixed_in,
    )
    small = jnp.concatenate(
        [
            jnp.zeros((width,), single),
            grad_gain_two[0],
            tap_sums[:taps, channels:].reshape(-1),
            tap_sums[:taps, :channels].reshape(-1),
            tap_sums[4, :channels],
            head_sums[:2].reshape(-1),
        ]
    )
    shared_length = 2 * width + taps * state_columns
    small = jnp.pad(small, (0, -small.shape[0] % 1024)).reshape(-1, 128)
    grad_residual, small, common_g, gate_g, inner_g, query_g, step_g = last_sums(
        nd,
        nt,
        normed,
        grad_main,
        grad_side,
        main,
        side,
        resid_own,
        grad_middle,
        gain_one[None],
        small,
        shared_length // 128,
        (channels, channels, query_columns, heads),
    )
    small = small.reshape(-1)
    place = lax.axis_index("dp") * nt + zed
    gain_one_g = lax.dynamic_slice_in_dim(small, place * small_rows, small_rows, 0)
    gain_two_g = lax.dynamic_slice_in_dim(small, width + place * small_rows, small_rows, 0)
    conv_g = lax.dynamic_slice_in_dim(
        small[2 * width : shared_length].reshape(taps, -1), place * conv_rows, conv_rows, 1
    ).T
    local = small[shared_length:]
    skip_at = taps * channels
    head_at = skip_at + channels
    return (
        layer_out,
        grad_residual,
        gain_one_g,
        gain_two_g,
        gate_g,
        inner_g,
        step_g,
        common_g[:, :state_columns],
        local[:skip_at].reshape(taps, channels).T,
        conv_g,
        local[head_at : head_at + heads],
        local[head_at + size.step_lanes : head_at + size.step_lanes + heads],
        local[skip_at:head_at].reshape(heads, -1).sum(axis=1),
        mixer_g,
        query_g,
        common_g[:, state_columns:],
        attn_g,
        gate_up_g[:, :ffn_columns],
        gate_up_g[:, ffn_columns:],
        down_g,
    )


def solution(mesh):
    return jax.shard_map(
        functools.partial(per_device, mesh.shape["dp"], mesh.shape["tensor"]),
        mesh=mesh,
        in_specs=(
            P(("dp", "tensor"), None),
            P("dp", None),
            P(("dp", "tensor")),
            P(("dp", "tensor")),
            P("dp", "tensor"),
            P("dp", "tensor"),
            P("dp", "tensor"),
            P(("dp", "tensor"), None),
            P("tensor", None),
            P(("dp", "tensor"), None),
            P("tensor"),
            P("tensor"),
            P("tensor"),
            P("dp", "tensor"),
            P("dp", "tensor"),
            P(("dp", "tensor"), None),
            P("dp", "tensor"),
            P("dp", "tensor"),
            P("dp", "tensor"),
            P("dp", "tensor"),
            P(("dp", "tensor"), None),
        ),
        out_specs=(
            P(("dp", "tensor"), None),
            P(("dp", "tensor"), None),
            P(("dp", "tensor")),
            P(("dp", "tensor")),
            P("dp", "tensor"),
            P("dp", "tensor"),
            P("dp", "tensor"),
            P(("dp", "tensor"), None),
            P("tensor", None),
            P(("dp", "tensor"), None),
            P("tensor"),
            P("tensor"),
            P("tensor"),
            P("dp", "tensor"),
            P("dp", "tensor"),
            P(("dp", "tensor"), None),
            P("dp", "tensor"),
            P("dp", "tensor"),
            P("dp", "tensor"),
            P("dp", "tensor"),
        ),
        check_vma=False,
    )
```

```python
import functools
import math

import jax
import jax.numpy as jnp
import numpy as np
from jax import lax
from jax.experimental import pallas as pl
from jax.experimental.pallas import tpu as pltpu
from jax.sharding import PartitionSpec as P

QUERY_HEADS = 8
KEY_VALUE_HEADS = 2
HEAD_SIZE = 128
SPAN = 256


eps = 1e-05
rope_base = 10000.0


def matrix_product(left, right):
    return jnp.dot(left, right, preferred_element_type=jnp.float32)


def contract_leading_axis(left, right):
    return lax.dot_general(
        left, right, (((0,), (0,)), ((), ())), preferred_element_type=jnp.float32
    )


def contract_last(left, right):
    return lax.dot_general(
        left, right, (((1,), (1,)), ((), ())), preferred_element_type=jnp.float32
    )


def bit_orders(size):
    high = list(range(size.bit_length() - 2, 0, -1))
    return high, high[:2][::-1] + high[2:]


def relative_blocks(size):
    both = []
    for half, order in enumerate(bit_orders(size)):
        chain = [0]
        for bit in order:
            chain = chain + [other ^ (1 << bit) for other in chain]
        both = both + [(other, half) for other in chain]
    return both + [(other ^ 1, half) for other, half in both]


def to_relative(value, axis, size):
    me = lax.axis_index("dp")
    width = value.shape[axis] // (2 * size)
    return jnp.concatenate(
        [
            lax.dynamic_slice_in_dim(value, ((me ^ other) * 2 + half) * width, width, axis)
            for other, half in relative_blocks(size)
        ],
        axis,
    )


def from_relative(value, axis, size):
    me = lax.axis_index("dp")
    width = value.shape[axis] // (2 * size)
    blocks = relative_blocks(size)
    place = jnp.asarray([blocks.index((other, half)) for other in range(size) for half in range(2)], jnp.int32)
    return jnp.concatenate(
        [
            lax.dynamic_slice_in_dim(value, place[(me ^ number) * 2 + half] * width, width, axis)
            for number in range(size)
            for half in range(2)
        ],
        axis,
    )


def after(value, *others):
    return lax.optimization_barrier((value,) + others)[0]


MESH = pl.DeviceIdType.MESH
VMEM_LIMIT = 56 * 1024 * 1024
LINE_CHUNKS = 4
LARGE_LIMIT = 62 * 1024 * 1024


def flip(value, bit):
    unit = 1 << bit
    return value + unit * (1 - 2 * ((value // unit) % 2))


def mixed_with(value, other, bits):
    for bit in range(bits):
        if (other >> bit) & 1:
            value = flip(value, bit)
    return value


def enter(nt, bits):
    me, zed = lax.axis_index("dp"), lax.axis_index("tensor")
    barrier = pltpu.get_barrier_semaphore()
    for other in range(nt):

        @pl.when(zed != other)
        def _(other=other):
            pl.semaphore_signal(barrier, inc=1, device_id=(me, other), device_id_type=MESH)

    for bit in range(bits):
        pl.semaphore_signal(barrier, inc=1, device_id=(flip(me, bit), zed), device_id_type=MESH)
    pl.semaphore_wait(barrier, bits + nt - 1)
    return me, zed


def aligned(start, size):
    return pl.ds(pl.multiple_of(start, 16), size)


def together(*flows):
    flows = [list(flow) for flow in flows]
    order = sorted(
        ((place + 0.5) / len(flow), number, place)
        for number, flow in enumerate(flows)
        for place in range(len(flow))
    )
    for _, number, place in order:
        flows[number][place]()


def gather_steps(nd, me, zed, own, everything, send, recv, local):
    half = own.shape[0] // 2
    blocks = relative_blocks(nd)
    place = {block: number for number, block in enumerate(blocks)}

    def rows(block):
        return everything.at[pl.ds(place[block] * half, half)]

    def source(block):
        return own.at[pl.ds(block[1] * half, half)] if block[0] == 0 else rows(block)

    hops = []
    for part, order in enumerate(bit_orders(nd)):
        chain = [0]
        for bit in order:
            hops = hops + [((other, part), bit) for other in chain]
            chain = chain + [other ^ (1 << bit) for other in chain]
    hops = hops + [(block, 0) for block in blocks[:nd]]

    def copy(number):
        block, bit = hops[number]
        landed = (block[0] ^ (1 << bit), block[1])
        return pltpu.make_async_remote_copy(
            src_ref=source(block),
            dst_ref=rows(landed),
            send_sem=send.at[number],
            recv_sem=recv.at[place[landed]],
            device_id=(flip(me, bit), zed),
            device_id_type=MESH,
        )

    def arrival(block):
        return pltpu.make_async_remote_copy(
            src_ref=rows(block),
            dst_ref=rows(block),
            send_sem=send.at[0],
            recv_sem=recv.at[place[block]],
            device_id=(flip(me, 0), zed),
            device_id_type=MESH,
        )

    def begin():
        for number, (block, bit) in enumerate(hops):
            if block[0] == 0:
                copy(number).start()
        for part in range(2):
            pltpu.make_async_copy(source((0, part)), rows((0, part)), local.at[part]).start()

    def forward(block):
        def step():
            arrival(block).wait_recv()
            for number, (origin, bit) in enumerate(hops):
                if origin == block:
                    copy(number).start()

        return step

    def end():
        for block in blocks[nd:]:
            arrival(block).wait_recv()
        for number in range(len(hops)):
            copy(number).wait_send()
        for part in range(2):
            pltpu.make_async_copy(source((0, part)), rows((0, part)), local.at[part]).wait()

    first, second = blocks[1 : nd // 2], blocks[nd // 2 + 1 : nd]
    middle = [forward(block) for pair in zip(first, second) for block in pair]
    return [begin] + middle + [end]


def gather_hops(nd):
    return 2 * (nd // 2 - 1) + nd


def gather_semaphores(nd):
    return [
        pltpu.SemaphoreType.DMA((gather_hops(nd),)),
        pltpu.SemaphoreType.DMA((2 * nd,)),
        pltpu.SemaphoreType.DMA((2,)),
    ]


def each_rows(rows, body, unit=16):
    def step(number, carry):
        body(aligned(number * unit, unit))
        return carry

    lax.fori_loop(0, rows // unit, step, 0)


def scatter_steps(nd, me, zed, parts, total, mine, held, landed, core_send, core_recv, send, recv, local):
    half = total.shape[0] // 2
    chain_length = nd // 2

    def piece(ref, number):
        return ref.at[pl.ds(number * half, half)]

    rounds, slot = [], 0
    for part, order in enumerate(bit_orders(nd)):
        length, own_rounds = chain_length, []
        for bit in order[::-1]:
            length = length // 2
            own_rounds.append((bit, length, slot))
            slot = slot + length
        rounds.append(own_rounds)

    def core_copy(number):
        return pltpu.make_async_remote_copy(
            src_ref=piece(parts, nd + number),
            dst_ref=piece(held, number),
            send_sem=core_send.at[number],
            recv_sem=core_recv.at[number],
            device_id=(flip(me, 0), zed),
            device_id_type=MESH,
        )

    def hop(part, bit, number, where):
        return pltpu.make_async_remote_copy(
            src_ref=piece(held, number),
            dst_ref=piece(landed, where),
            send_sem=send.at[where],
            recv_sem=recv.at[where],
            device_id=(flip(me, bit), zed),
            device_id_type=MESH,
        )

    wanted = []
    for number in range(chain_length - 1, -1, -1):
        wanted = wanted + [number, chain_length + number]

    def load(number):
        return pltpu.make_async_copy(piece(parts, number), piece(mine, number), local.at[number])

    def begin():
        for number in wanted:
            core_copy(number).start()
        for number in wanted:
            load(number).start()

    def core_sum(number):
        part, spot = number // chain_length, number % chain_length

        def step():
            load(number).wait()
            core_copy(number).wait_recv()

            def body(rows):
                spot_rows = piece(held, number)
                spot_rows[rows] = spot_rows[rows] + piece(mine, number)[rows]

            each_rows(half, body)
            if rounds[part]:
                bit, length, first = rounds[part][0]
                if spot >= length:
                    hop(part, bit, number, first + spot - length).start()

        return step

    def later_sum(part, turn, spot):
        bit, length, first = rounds[part][turn]
        number = part * chain_length + spot

        def step():
            hop(part, bit, number, first + spot).wait_recv()
            last = turn == len(rounds[part]) - 1

            def body(rows):
                kept, came = piece(held, number)[rows], piece(landed, first + spot)[rows]
                if last:
                    piece(total, part)[rows] = kept.astype(jnp.float32) + came.astype(jnp.float32)
                else:
                    piece(held, number)[rows] = kept + came

            each_rows(half, body)
            if not last:
                next_bit, next_length, next_first = rounds[part][turn + 1]
                if spot >= next_length:
                    hop(part, next_bit, number, next_first + spot - next_length).start()

        return step

    stages = [[core_sum(number) for number in wanted]]
    for turn in range(len(rounds[0])):
        length = rounds[0][turn][1]
        stages.append([later_sum(part, turn, spot) for spot in range(length - 1, -1, -1) for part in range(2)])

    def end():
        for number in range(nd):
            core_copy(number).wait_send()
        for part in range(2):
            for bit, length, first in rounds[part]:
                for spot in range(length):
                    hop(part, bit, part * chain_length + length + spot, first + spot).wait_send()

    return [[begin]] + stages + [[end]]


def computed_scatter(nd, me, zed, half, compute, stage, held, landed, totals, core_send, core_recv, send, recv):
    chain_length = nd // 2
    block = 256
    pieces = block // half
    per_part = chain_length // pieces
    turns = [part * per_part + spot for spot in range(per_part - 1, -1, -1) for part in range(2)]

    def piece(ref, number):
        return ref.at[pl.ds(number * half, half)]

    def block_of(ref, number):
        return ref.at[pl.ds(number * block, block)]

    rounds, slot = [], 0
    for part, order in enumerate(bit_orders(nd)):
        length, own_rounds = chain_length, []
        for bit in order[::-1]:
            length = length // 2
            own_rounds.append((bit, length, slot))
            slot = slot + length
        rounds.append(own_rounds)

    def core_copy(number):
        return pltpu.make_async_remote_copy(
            src_ref=block_of(stage, number),
            dst_ref=block_of(held, number),
            send_sem=core_send.at[number],
            recv_sem=core_recv.at[number],
            device_id=(flip(me, 0), zed),
            device_id_type=MESH,
        )

    def hop(bit, number, where):
        return pltpu.make_async_remote_copy(
            src_ref=piece(held, number),
            dst_ref=piece(landed, where),
            send_sem=send.at[where],
            recv_sem=recv.at[where],
            device_id=(flip(me, bit), zed),
            device_id_type=MESH,
        )

    def away(number):
        def step():
            compute(nd * half + number * block, None, block_of(stage, number))
            core_copy(number).start()

        return step

    def near(number):
        def step():
            core_copy(number).wait_recv()
            compute(number * block, block_of(held, number), block_of(held, number))
            for inner in range(pieces):
                place = number * pieces + inner
                part, spot = place // chain_length, place % chain_length
                bit, length, first = rounds[part][0]
                if spot >= length:
                    hop(bit, place, first + spot - length).start()

        return step

    def later_sum(part, turn, spot):
        bit, length, first = rounds[part][turn]
        number = part * chain_length + spot

        def step():
            hop(bit, number, first + spot).wait_recv()
            last = turn == len(rounds[part]) - 1

            def body(rows):
                kept, came = piece(held, number)[rows], piece(landed, first + spot)[rows]
                if last:
                    value = kept.astype(jnp.float32) + came.astype(jnp.float32)
                    for target, start, columns in totals:
                        piece(target, part)[rows] = value[:, start : start + columns]
                else:
                    piece(held, number)[rows] = kept + came

            each_rows(half, body)
            if not last:
                next_bit, next_length, next_first = rounds[part][turn + 1]
                if spot >= next_length:
                    hop(next_bit, number, next_first + spot - next_length).start()

        return step

    def end():
        for number in range(len(turns)):
            core_copy(number).wait_send()
        for part in range(2):
            for bit, length, first in rounds[part]:
                for spot in range(length):
                    hop(bit, part * chain_length + length + spot, first + spot).wait_send()

    later = []
    for turn in range(len(rounds[0])):
        length = rounds[0][turn][1]
        later.append([later_sum(part, turn, spot) for spot in range(length - 1, -1, -1) for part in range(2)])
    return [away(number) for number in turns], [near(number) for number in turns], later, end


def computed_scratch(nd, rows, columns):
    slots = nd - 2
    blocks = nd * rows // 2 // 256
    return [
        pltpu.VMEM((nd * rows // 2, columns), jnp.bfloat16),
        pltpu.VMEM((nd * rows // 2, columns), jnp.bfloat16),
        pltpu.VMEM((slots * rows // 2, columns), jnp.bfloat16),
        pltpu.SemaphoreType.DMA((blocks,)),
        pltpu.SemaphoreType.DMA((blocks,)),
        pltpu.SemaphoreType.DMA((slots,)),
        pltpu.SemaphoreType.DMA((slots,)),
    ]


def products_of(left, rights, tile):
    def compute(start, add, target):
        turned_left = jnp.transpose(left[:, start : start + 256])
        at = 0
        for right, columns in rights:
            for first in range(0, columns, tile):
                extent = slice(first, min(first + tile, columns))
                value = jnp.dot(turned_left, right[:, extent], preferred_element_type=jnp.float32)
                here = slice(at + extent.start, at + extent.stop)
                if add is not None:
                    value = value + add[:, here].astype(jnp.float32)
                target[:, here] = value.astype(jnp.bfloat16)
            at = at + columns

    return compute


def staggered(flows):
    steps = [step for flow in flows for step in flow[0]]
    depth = len(flows[0]) - 2
    for turn in range(depth + len(flows) - 1):
        for number in range(len(flows) - 1, -1, -1):
            if 0 <= turn - number < depth:
                steps = steps + flows[number][1 + turn - number]
    return steps + [step for flow in flows for step in flow[-1]]


def scatter_scratch(nd, rows, columns):
    slots = nd - 2
    return [
        pltpu.VMEM((nd * rows // 2, columns), jnp.bfloat16),
        pltpu.VMEM((nd * rows // 2, columns), jnp.bfloat16),
        pltpu.VMEM((slots * rows // 2, columns), jnp.bfloat16),
        pltpu.SemaphoreType.DMA((nd,)),
        pltpu.SemaphoreType.DMA((nd,)),
        pltpu.SemaphoreType.DMA((slots,)),
        pltpu.SemaphoreType.DMA((slots,)),
        pltpu.SemaphoreType.DMA((nd,)),
    ]


def line_gather(nt, me, zed, chunks, own, everything, send, recv, chunked=False, reach=None):
    size = own.shape[0] // chunks
    reach = nt - 1 if reach is None else reach

    def own_rows(chunk):
        return own.at[pl.ds(chunk * size, size)]

    def rows(block, chunk):
        start = (chunk * nt + block) * size if chunked else block * (size * chunks) + chunk * size
        return everything.at[aligned(start, size)]

    def copy(source, block, chunk, side):
        return pltpu.make_async_remote_copy(
            src_ref=source,
            dst_ref=rows(block, chunk),
            send_sem=send.at[side, block, chunk],
            recv_sem=recv.at[block, chunk],
            device_id=(me, zed + 1 - 2 * side),
            device_id_type=MESH,
        )

    def keep(chunk):
        return pltpu.make_async_copy(own_rows(chunk), rows(zed, chunk), recv.at[zed, chunk])

    def first(chunk):
        for side, condition in ((0, zed < nt - 1), (1, zed > 0)):

            @pl.when(condition)
            def _(side=side):
                copy(own_rows(chunk), zed, chunk, side).start()

        keep(chunk).start()

    def onward(chunk, distance):
        for side, block in ((0, zed - distance), (1, zed + distance)):
            inside = (block >= 0) if side == 0 else (block < nt)
            open_end = (zed < nt - 1) if side == 0 else (zed > 0)

            @pl.when(inside)
            def _(block=block, side=side):
                copy(rows(block, chunk), block, chunk, side).wait_recv()

            if distance < reach:

                @pl.when(jnp.logical_and(inside, open_end))
                def _(block=block, side=side):
                    copy(rows(block, chunk), block, chunk, side).start()

    def settle(chunk):
        keep(chunk).wait()

    def end(chunk):
        for side, condition in ((0, zed < nt - 1), (1, zed > 0)):

            @pl.when(condition)
            def _(side=side):
                copy(own_rows(chunk), zed, chunk, side).wait_send()

            for distance in range(1, reach):
                block = zed - distance if side == 0 else zed + distance
                inside = (block >= 0) if side == 0 else (block < nt)

                @pl.when(jnp.logical_and(inside, condition))
                def _(block=block, side=side):
                    copy(rows(block, chunk), block, chunk, side).wait_send()

    return first, onward, settle, end


def line_gather_semaphores(nt, chunks):
    return [pltpu.SemaphoreType.DMA((2, nt, chunks)), pltpu.SemaphoreType.DMA((nt, chunks))]


def line_reduce(nt, me, zed, chunks, parts, held, send, recv, chunked=False):
    block_rows = parts.shape[0] // nt
    size = block_rows // chunks
    def rows(block, chunk):
        if chunked:
            return aligned((chunk * nt + block) * size, size)
        return aligned(block * block_rows + chunk * size, size)

    def held_rows(side, block, chunk):
        return aligned((block + 1 - side) * block_rows + chunk * size, size)

    def copy(own, side, block, chunk):
        place = held_rows(side, block, chunk)
        return pltpu.make_async_remote_copy(
            src_ref=parts.at[rows(block, chunk)] if own else held.at[place],
            dst_ref=held.at[place],
            send_sem=send.at[side, block, chunk],
            recv_sem=recv.at[side, block, chunk],
            device_id=(me, zed + 1 - 2 * side),
            device_id_type=MESH,
        )

    def role(side, turn):
        away = nt - 1 - turn
        if side == 0:
            return zed + away, zed + away < nt, zed == 0
        return zed - away, zed - away >= 0, zed == nt - 1

    def pass_on(chunk, turn):
        for side in range(2):
            block, active, source = role(side, turn)

            @pl.when(jnp.logical_and(active, source))
            def _(side=side, block=block):
                copy(True, side, block, chunk).start()

            @pl.when(jnp.logical_and(active, jnp.logical_not(source)))
            def _(side=side, block=block):
                copy(False, side, block, chunk).wait_recv()
                mine, came = parts.at[rows(block, chunk)], held.at[held_rows(side, block, chunk)]

                def body(inner):
                    came[inner] = mine[inner] + came[inner]

                each_rows(size, body)
                copy(False, side, block, chunk).start()

    def own_sum(chunk, total):
        total[...] = parts[rows(zed, chunk)].astype(jnp.float32)
        for side in range(2):

            @pl.when(zed > 0 if side == 0 else zed < nt - 1)
            def _(side=side):
                copy(False, side, zed, chunk).wait_recv()
                total[...] += held[held_rows(side, zed, chunk)].astype(jnp.float32)

    def end(chunk):
        for turn in range(nt - 1):
            for side in range(2):
                block, active, source = role(side, turn)

                @pl.when(active)
                def _(side=side, block=block):
                    copy(False, side, block, chunk).wait_send()

    return pass_on, own_sum, end


def line_reduce_scratch(nt, block_rows, columns, chunks):
    return [
        pltpu.VMEM(((nt + 1) * block_rows, columns), jnp.bfloat16),
        pltpu.VMEM((block_rows // chunks, columns), jnp.float32),
        pltpu.SemaphoreType.DMA((2, nt, chunks)),
        pltpu.SemaphoreType.DMA((2, nt, chunks)),
    ]


HBM = pl.BlockSpec(memory_space=pl.ANY)
ONCHIP = pl.BlockSpec(memory_space=pltpu.VMEM)


def near_first(nt, zed, turn):
    block = 0
    for mine in range(nt):
        order = sorted(range(nt), key=lambda other: (abs(other - mine), other))
        block = block + jnp.where(zed == mine, order[turn], 0)
    return block


def first_gathers(nd, nt, rows, grad, small, main_own, out_own, shared_columns):
    chunks = LINE_CHUNKS
    bits = nd.bit_length() - 1
    blocks = relative_blocks(nd)
    block_rows, width = rows.shape
    lane = width // len(blocks)
    if lane % 128:
        rows, grad = to_relative(rows, 1, nd), to_relative(grad, 1, nd)
    main_columns, small_columns = main_own.shape[1], small.shape[1]
    side_columns = shared_columns + 2 * HEAD_SIZE
    gains_at = shared_columns + 2 * KEY_VALUE_HEADS * HEAD_SIZE
    tile = 256

    def reorder(me, source, target):
        if lane % 128:
            target[...] = source[...]
            return
        for number, (other, part) in enumerate(blocks):
            start = (mixed_with(me, other, bits) * 2 + part) * lane
            target[:, number * lane : (number + 1) * lane] = source[:, pl.ds(pl.multiple_of(start, lane), lane)]

    def kernel(
        rows_in, grad_in, small_ref, main_ref, out_ref,
        rows_ref, grad_ref, gains_ref, normed_all, grad_all, small_line, main_all, side_all, out_all, main_raw, side_raw,
        row_space, normed, main_space, small_space, side_space, main_stage, side_stage, store_sems, *refs,
    ):
        row_sems, small_sems, grad_sems = refs[:2], refs[2:4], refs[4:6]
        main_sems, small_dp, out_sems = refs[6:9], refs[9:12], refs[12:15]
        me, zed = enter(nt, bits)
        small_first, small_onward, small_settle, small_end = line_gather(
            nt, me, zed, 1, small_ref, small_line, *small_sems
        )
        row_first, row_onward, row_settle, row_end = line_gather(
            nt, me, zed, chunks, rows_ref, row_space, *row_sems
        )
        grad_first, grad_onward, grad_settle, grad_end = line_gather(
            nt, me, zed, chunks, grad_ref, grad_all, *grad_sems, chunked=True, reach=nt - 2
        )
        main_flow = gather_steps(nd, me, zed, main_ref, main_space, *main_sems)
        small_flow = gather_steps(nd, me, zed, small_line, small_space, *small_dp)
        out_flow = gather_steps(nd, me, zed, out_ref, out_all, *out_sems)
        head = zed * (QUERY_HEADS // nt) // (QUERY_HEADS // KEY_VALUE_HEADS)

        def columns(turn):
            if turn == 0:
                return small_space.at[:, pl.ds(0, shared_columns)], side_space.at[:, pl.ds(0, shared_columns)]
            start = shared_columns + ((turn - 1) * KEY_VALUE_HEADS + head) * HEAD_SIZE
            target = shared_columns + (turn - 1) * HEAD_SIZE
            return (
                small_space.at[:, pl.ds(pl.multiple_of(start, HEAD_SIZE), HEAD_SIZE)],
                side_space.at[:, pl.ds(target, HEAD_SIZE)],
            )

        def keep(number):
            source, target = ((main_space, main_all), (side_space, side_all), (normed, normed_all))[number]
            return pltpu.make_async_copy(source, target, store_sems.at[number])

        def pick(turn):
            return pltpu.make_async_copy(*columns(turn), store_sems.at[3 + turn])

        def store(turn, number):
            block = near_first(nt, zed, turn)
            stage, target = ((main_stage, main_raw), (side_stage, side_raw))[number]
            return pltpu.make_async_copy(
                stage.at[turn % 2],
                target.at[aligned(block * block_rows, block_rows)],
                store_sems.at[6 + 2 * turn + number],
            )

        def project(turn):
            where = aligned(near_first(nt, zed, turn) * block_rows, block_rows)
            value = (rows_ref[...] if turn == 0 else row_space[where]).astype(jnp.float32)
            scale = lax.rsqrt(jnp.mean(value * value, axis=-1, keepdims=True) + eps)
            mine = (value * scale * gains_ref[0:1]).astype(jnp.bfloat16)
            normed[where] = mine
            if turn >= 2:
                store(turn - 2, 0).wait()
                store(turn - 2, 1).wait()
            for space, stage, number in ((main_space, main_stage, 0), (side_space, side_stage, 1)):
                for start in range(0, space.shape[1], tile):
                    extent = slice(start, min(start + tile, space.shape[1]))
                    stage[turn % 2, :, extent] = jnp.dot(
                        mine, space[:, extent], preferred_element_type=jnp.float32
                    )
                store(turn, number).start()

        small_first(0)
        main_flow[0]()
        reorder(me, rows_in, rows_ref)
        for chunk in range(chunks):
            row_first(chunk)
        for distance in range(1, nt):
            small_onward(0, distance)
        small_settle(0)
        small_end(0)
        small_flow[0]()
        out_flow[0]()
        reorder(me, grad_in, grad_ref)
        near = [
            functools.partial(row_onward, chunk, distance) for distance in range(1, nt - 1) for chunk in range(chunks)
        ]
        together(near, main_flow[1:-1] + small_flow[1:-1])
        for chunk in range(chunks):
            grad_first(chunk)
        small_flow[-1]()
        for turn in range(3):
            pick(turn).start()
        for start in range(0, width, 128):
            turned_block = jnp.transpose(
                small_space[start : start + 128, gains_at : gains_at + 128].astype(jnp.float32)
            )
            gains_ref[:, start : start + 128] = turned_block[:8]
        main_flow[-1]()
        keep(0).start()
        for turn in range(3):
            pick(turn).wait()
        keep(1).start()

        def last_rows():
            for chunk in range(chunks):
                row_onward(chunk, nt - 1)

        def grads_from(distance):
            for chunk in range(chunks):
                grad_onward(chunk, distance)

        compute = [functools.partial(project, turn) for turn in range(nt - 1)] + [last_rows]
        for distance in range(1, nt - 2):
            compute.append(functools.partial(grads_from, distance))
        together(compute, out_flow[1:-1])
        project(nt - 1)
        keep(2).start()
        if nt > 2:
            grads_from(nt - 2)
        out_flow[-1]()
        for chunk in range(chunks):
            row_settle(chunk)
            row_end(chunk)
            grad_settle(chunk)
            grad_end(chunk)
        for turn in range(max(nt - 2, 0), nt):
            store(turn, 0).wait()
            store(turn, 1).wait()
        for number in range(3):
            keep(number).wait()

    def sized(array, times, dtype=None):
        return jax.ShapeDtypeStruct((array.shape[0] * times, array.shape[1]), dtype or array.dtype)

    tokens = block_rows * nt
    return pl.pallas_call(
        kernel,
        out_shape=[
            sized(rows, 1),
            sized(grad, 1),
            jax.ShapeDtypeStruct((8, width), jnp.float32),
            sized(rows, nt),
            sized(grad, nt),
            sized(small, nt),
            sized(main_own, nd),
            jax.ShapeDtypeStruct((width, side_columns), small.dtype),
            sized(out_own, nd),
            jax.ShapeDtypeStruct((tokens, main_columns), jnp.float32),
            jax.ShapeDtypeStruct((tokens, side_columns), jnp.float32),
        ],
        in_specs=[ONCHIP] * 2 + [HBM] * 3,
        out_specs=[ONCHIP] * 3 + [HBM] * 8,
        scratch_shapes=[
            pltpu.VMEM((tokens, width), jnp.bfloat16),
            pltpu.VMEM((tokens, width), jnp.bfloat16),
            pltpu.VMEM((width, main_columns), jnp.bfloat16),
            pltpu.VMEM((width, small_columns), jnp.bfloat16),
            pltpu.VMEM((width, side_columns), jnp.bfloat16),
            pltpu.VMEM((2, block_rows, main_columns), jnp.float32),
            pltpu.VMEM((2, block_rows, side_columns), jnp.float32),
            pltpu.SemaphoreType.DMA((6 + 2 * nt,)),
        ]
        + line_gather_semaphores(nt, chunks)
        + line_gather_semaphores(nt, 1)
        + line_gather_semaphores(nt, chunks)
        + gather_semaphores(nd) * 3,
        compiler_params=pltpu.CompilerParams(
            collective_id=0, has_side_effects=True, vmem_limit_bytes=VMEM_LIMIT
        ),
        name="first_gathers",
    )(rows, grad, small, main_own, out_own)


def middle_rows(nd, nt, mixed, out_w, resid, gain, grads, ffn_own):
    chunks = LINE_CHUNKS
    bits = nd.bit_length() - 1
    block_rows, width = resid.shape
    tokens = block_rows * nt
    size = block_rows // chunks
    ffn_columns = ffn_own.shape[1] // 3
    tile = 512

    def kernel(
        mixed_ref, out_ref, resid_ref, gain_ref, grads_ref, ffn_ref,
        middle_ref, rows_ref, hidden_ref, slopes_ref, grads_all, ffn_all,
        parts, grad_space, ffn_space, own, held, total, send, recv, gather_send, gather_recv,
        ffn_send, ffn_recv, ffn_local, store_sems, far_send, far_recv, far_space,
    ):
        me, zed = enter(nt, bits)
        load = pltpu.make_async_copy(grads_ref, grad_space, store_sems.at[0])
        load.start()
        pass_on, own_sum, reduce_end = line_reduce(nt, me, zed, chunks, parts, held, send, recv)
        first, onward, settle, gather_end = line_gather(
            nt, me, zed, chunks, own, rows_ref, gather_send, gather_recv, chunked=True
        )
        flow = gather_steps(nd, me, zed, ffn_ref, ffn_space, ffn_send, ffn_recv, ffn_local)
        keeps = [
            pltpu.make_async_copy(grad_space, grads_all, store_sems.at[1]),
            pltpu.make_async_copy(ffn_space, ffn_all, store_sems.at[2]),
        ]

        def part(turn):
            where = aligned(near_first(nt, zed, nt - 1 - turn) * block_rows, block_rows)
            left = mixed_ref[where]
            for start in range(0, width, tile):
                extent = slice(start, start + tile)
                parts[where, extent] = product(left, out_ref[extent], LAST).astype(jnp.bfloat16)

        def far(chunk, up):
            block = 0 if up else nt - 1
            return pltpu.make_async_remote_copy(
                src_ref=grad_space.at[pl.ds((chunk * nt + block) * size, size)],
                dst_ref=far_space.at[pl.ds(chunk * size, size)],
                send_sem=far_send.at[chunk],
                recv_sem=far_recv.at[chunk],
                device_id=(me, nt - 1 if up else 0),
                device_id_type=MESH,
            )

        def far_begin():
            for up, sender in ((True, nt - 2), (False, 1)):

                @pl.when(zed == sender)
                def _(up=up):
                    for chunk in range(chunks):
                        far(chunk, up).start()

        def far_end():
            for up, sender in ((True, nt - 2), (False, 1)):

                @pl.when(zed == sender)
                def _(up=up):
                    for chunk in range(chunks):
                        far(chunk, up).wait_send()

                @pl.when(zed == (nt - 1 if up else 0))
                def _(up=up):
                    for chunk in range(chunks):
                        far(chunk, up).wait_recv()
                        start = (chunk * nt + (0 if up else nt - 1)) * size
                        grad_space[pl.ds(start, size)] = far_space[pl.ds(chunk * size, size)]

        def finish(chunk):
            own_sum(chunk, total)
            where = pl.ds(chunk * size, size)
            value = resid_ref[where].astype(jnp.float32) + total[...]
            middle_ref[where] = value
            scale = lax.rsqrt(jnp.mean(value * value, axis=-1, keepdims=True) + eps)
            own[where] = (value * scale * gain_ref[...]).astype(jnp.bfloat16)
            first(chunk)

        def feed(chunk):
            settle(chunk)
            where = pl.ds(chunk * nt * size, nt * size)
            rows, grads = rows_ref[where], grad_space[where]
            for start in range(0, ffn_columns, tile):
                columns = [slice(turn * ffn_columns + start, turn * ffn_columns + start + tile) for turn in range(3)]
                gate = product(rows, ffn_space[:, columns[0]])
                upper = product(rows, ffn_space[:, columns[1]])
                grad = product(grads, ffn_space[:, columns[2]])
                sigma = jax.nn.sigmoid(gate)
                through = gate * sigma
                hidden_ref[where, columns[0]] = (through * upper).astype(jnp.bfloat16)
                slopes_ref[where, columns[0]] = (grad * upper * silu_slope(gate, sigma)).astype(jnp.bfloat16)
                slopes_ref[where, columns[1]] = (grad * through).astype(jnp.bfloat16)

        flow[0]()
        part(0)
        for chunk in range(chunks):
            pass_on(chunk, 0)
        for turn in range(1, nt):
            part(turn)
        load.wait()
        far_begin()
        ahead = [
            functools.partial(pass_on, 0, turn) for turn in range(1, nt - 1)
        ]
        steps = []

        def add(function, chunk, *rest):
            if 0 <= chunk < chunks:
                steps.append(functools.partial(function, chunk, *rest))

        for chunk in range(1, chunks + 2):
            add(finish, chunk - 1)
            add(onward, chunk - 2, nt - 1)
            for turn in range(1, nt - 1):
                add(pass_on, chunk, turn)
                add(onward, chunk - 1, turn)
            if chunk == 2:
                early = len(steps)
            add(feed, chunk - 2)
        together(ahead + steps[:early], flow[1:] + [far_end])
        for keep in keeps:
            keep.start()
        for step in steps[early:]:
            step()
        for chunk in range(chunks):
            reduce_end(chunk)
            gather_end(chunk)
        for keep in keeps:
            keep.wait()

    return pl.pallas_call(
        kernel,
        out_shape=[
            jax.ShapeDtypeStruct((block_rows, width), jnp.float32),
            jax.ShapeDtypeStruct((tokens, width), jnp.bfloat16),
            jax.ShapeDtypeStruct((tokens, ffn_columns), jnp.bfloat16),
            jax.ShapeDtypeStruct((tokens, 2 * ffn_columns), jnp.bfloat16),
            jax.ShapeDtypeStruct((tokens, width), jnp.bfloat16),
            jax.ShapeDtypeStruct((width, 3 * ffn_columns), jnp.bfloat16),
        ],
        in_specs=[ONCHIP] * 4 + [HBM] * 2,
        out_specs=[ONCHIP] * 4 + [HBM] * 2,
        scratch_shapes=[
            pltpu.VMEM((tokens, width), jnp.bfloat16),
            pltpu.VMEM((tokens, width), jnp.bfloat16),
            pltpu.VMEM((width, 3 * ffn_columns), jnp.bfloat16),
            pltpu.VMEM((block_rows, width), jnp.bfloat16),
        ]
        + line_reduce_scratch(nt, block_rows, width, chunks)
        + line_gather_semaphores(nt, chunks)
        + gather_semaphores(nd)
        + [
            pltpu.SemaphoreType.DMA((3,)),
            pltpu.SemaphoreType.DMA((chunks,)),
            pltpu.SemaphoreType.DMA((chunks,)),
            pltpu.VMEM((block_rows, width), jnp.bfloat16),
        ],
        compiler_params=pltpu.CompilerParams(
            collective_id=1, has_side_effects=True, vmem_limit_bytes=LARGE_LIMIT
        ),
        name="middle_rows",
    )(mixed, out_w, resid, gain, grads, ffn_own)


def line_schedule(nt, chunks, pass_on, finish, onward, others):
    steps = []

    def add(function, chunk, *rest):
        if function is not None and 0 <= chunk < chunks:
            steps.append(functools.partial(function, chunk, *rest))

    for chunk in range(chunks + 2):
        add(pass_on, chunk, 0)
        add(finish, chunk - 1)
        add(onward, chunk - 2, nt - 1)
        for turn in range(1, nt - 1):
            add(pass_on, chunk, turn)
            add(onward, chunk - 1, turn)
    together(steps, others)


def absolute_lanes(me, bits, blocks, source, target):
    lane = source.shape[1] // len(blocks)
    for number, (other, part) in enumerate(blocks):
        start = (mixed_with(me, other, bits) * 2 + part) * lane
        target[:, pl.ds(pl.multiple_of(start, lane), lane)] = source[:, number * lane : (number + 1) * lane]


def norm_pull(value, gain, grad):
    scale = lax.rsqrt(jnp.mean(value * value, axis=-1, keepdims=True) + eps)
    scaled = grad * gain
    inner = jnp.mean(scaled * value, axis=-1, keepdims=True)
    return scale * (scaled - value * (inner * scale * scale)), grad * value * scale


def middle_back(nd, nt, parts, middle, cot, gain, groups):
    chunks = LINE_CHUNKS
    bits = nd.bit_length() - 1
    count = len(groups)
    block_rows, width = middle.shape
    size = block_rows // chunks
    per_group = 8
    blocks = relative_blocks(nd)
    lane = width // len(blocks)

    def kernel(parts_ref, middle_ref, cot_ref, gain_ref, *refs):
        group_refs, refs = refs[:count], refs[count:]
        grad_ref, gain_out, rows_all = refs[:3]
        totals, refs = refs[3 : 3 + count], refs[3 + count :]
        own, gain_grad, held, total, send, recv = refs[:6]
        gather_sems, refs = refs[6:8], refs[8:]
        me, zed = enter(nt, bits)
        pass_on, own_sum, reduce_end = line_reduce(nt, me, zed, chunks, parts_ref, held, send, recv, chunked=True)
        first, onward, settle, gather_end = line_gather(nt, me, zed, chunks, own, rows_all, *gather_sems)
        flows = [
            scatter_steps(nd, me, zed, group_refs[n], totals[n], *refs[per_group * n : per_group * (n + 1)])
            for n in range(count)
        ]
        gain_grad[...] = jnp.zeros_like(gain_grad)

        def finish(chunk):
            own_sum(chunk, total)
            where = pl.ds(chunk * size, size)
            through, gained = norm_pull(middle_ref[where], gain_ref[...], total[...])
            value = cot_ref[where].astype(jnp.float32) + through
            gain_grad[...] += jnp.sum(gained, axis=0, keepdims=True)
            grad_ref[where] = value
            own[where] = value.astype(jnp.bfloat16)
            first(chunk)

        line_schedule(nt, chunks, pass_on, finish, onward, staggered(flows))
        if lane % 128:
            gain_out[...] = gain_grad[...]
        else:
            absolute_lanes(me, bits, blocks, gain_grad, gain_out)
        for chunk in range(chunks):
            reduce_end(chunk)
            settle(chunk)
            gather_end(chunk)

    scratch = []
    for group in groups:
        scratch = scratch + scatter_scratch(nd, group.shape[0] // nd, group.shape[1])
    results = pl.pallas_call(
        kernel,
        out_shape=[
            jax.ShapeDtypeStruct((block_rows, width), jnp.float32),
            jax.ShapeDtypeStruct((1, width), jnp.float32),
            jax.ShapeDtypeStruct((block_rows * nt, width), jnp.bfloat16),
        ]
        + [jax.ShapeDtypeStruct((group.shape[0] // nd, group.shape[1]), jnp.float32) for group in groups],
        in_specs=[ONCHIP] * 4 + [HBM] * count,
        out_specs=[ONCHIP, ONCHIP, HBM] + [ONCHIP] * count,
        scratch_shapes=[pltpu.VMEM((block_rows, width), jnp.bfloat16), pltpu.VMEM((1, width), jnp.float32)]
        + line_reduce_scratch(nt, block_rows, width, chunks)
        + line_gather_semaphores(nt, chunks)
        + scratch,
        compiler_params=pltpu.CompilerParams(
            collective_id=2, has_side_effects=True, vmem_limit_bytes=VMEM_LIMIT
        ),
        name="middle_back",
    )(parts, middle, cot, gain, *groups)
    if lane % 128:
        results = (results[0], from_relative(results[1], 1, nd), *results[2:])
    return results


def last_sums(nd, nt, normed, grad_main, grad_side, main, side, resid, before, gain, small, shared_rows, main_widths):
    chunks = LINE_CHUNKS
    bits, line_bits = nd.bit_length() - 1, nt.bit_length() - 1
    block_rows, width = resid.shape
    tokens = block_rows * nt
    size = block_rows // chunks
    blocks = relative_blocks(nd)
    lane = width // len(blocks)
    main_columns, side_columns = main.shape[1], side.shape[1]
    shared_columns = side_columns - 2 * HEAD_SIZE
    side_rows = width // nd
    owned = side_rows // nt
    common_columns = shared_columns + 2 * KEY_VALUE_HEADS * HEAD_SIZE
    count = len(main_widths)
    if lane % 128:
        gain_part = jnp.sum(
            (contract_last(grad_main, main) + contract_last(grad_side, side)) * normed.astype(jnp.float32), axis=0
        )
        own_gain = from_relative(gain_part / gain[0], 0, nd)
        small = jnp.concatenate([own_gain.reshape(-1, 128), small[width // 128 :]])

    def kernel(normed_ref, grad_main_ref, grad_side_ref, main_ref, side_ref, resid_ref, before_ref, gain_ref, small_ref, *refs):
        grad_ref, small_out, common_ref = refs[:3]
        totals, refs = refs[3 : 3 + count], refs[3 + count :]
        parts_ref, side_total, line_held, total, send, recv = refs[:6]
        sums, landed, small_send, small_recv, gain_grad = refs[6:11]
        side_out, side_in, side_send, side_recv = refs[11:15]
        stage, held, hop_landed, core_send, core_recv, hop_send, hop_recv = refs[15:]
        me, zed = enter(nt, bits)
        pass_on, own_sum, reduce_end = line_reduce(nt, me, zed, chunks, parts_ref, line_held, send, recv)
        targets, at = [], 0
        for target, columns in zip(totals, main_widths):
            targets.append((target, at, columns))
            at = at + columns
        targets.append((side_total, main_columns, side_columns))
        away, near, later, scatter_end = computed_scatter(
            nd, me, zed, side_rows // 2,
            products_of(normed_ref, ((grad_main_ref, main_columns), (grad_side_ref, side_columns)), 512),
            stage, held, hop_landed, targets, core_send, core_recv, hop_send, hop_recv,
        )

        def part(turn):
            def step():
                where = aligned(near_first(nt, zed, nt - 1 - turn) * block_rows, block_rows)
                left, right = grad_main_ref[where], grad_side_ref[where]
                for start in range(0, width, 512):
                    extent = slice(start, start + 512)
                    value = product(left, main_ref[extent], LAST) + product(right, side_ref[extent], LAST)
                    parts_ref[where, extent] = value.astype(jnp.bfloat16)

            return step

        def gain_term(number):
            def step():
                if number == 0:
                    gain_grad[...] = jnp.zeros_like(gain_grad)

                def body(inner, carry):
                    where = aligned(number * block_rows + inner * 16, 16)
                    gain_grad[...] += parts_ref[where].astype(jnp.float32) * normed_ref[where].astype(jnp.float32)
                    return carry

                lax.fori_loop(0, block_rows // 16, body, 0)

            return step

        def small_copy(turn):
            if turn < bits:
                device = (flip(me, turn), zed)
            else:
                device = (me, flip(zed, turn - bits))
            extent = slice(None) if turn < bits else pl.ds(0, shared_rows)
            return pltpu.make_async_remote_copy(
                src_ref=sums.at[turn, extent],
                dst_ref=landed.at[turn, extent],
                send_sem=small_send.at[turn],
                recv_sem=small_recv.at[turn],
                device_id=device,
                device_id_type=MESH,
            )

        def small_begin():
            sums[0] = small_ref[...]
            if lane % 128 == 0:
                whole = jnp.sum(gain_grad[...], axis=0, keepdims=True) / gain_ref[...]
                for number, (other, half) in enumerate(blocks):
                    spot = mixed_with(me, other, bits) * 2 + half
                    sums[0, pl.ds(spot, 1), :] = whole[:, number * lane : (number + 1) * lane]
            small_copy(0).start()

        def small_step(turn):
            def step():
                small_copy(turn).wait_recv()
                if turn < bits:
                    sums[turn + 1] = sums[turn] + landed[turn]
                else:
                    sums[turn + 1] = sums[turn]
                    sums[turn + 1, pl.ds(0, shared_rows)] = (
                        sums[turn, pl.ds(0, shared_rows)] + landed[turn, pl.ds(0, shared_rows)]
                    )
                if turn + 1 < bits + line_bits:
                    small_copy(turn + 1).start()

            return step

        def small_end():
            for turn in range(bits + line_bits):
                small_copy(turn).wait_send()
            small_out[...] = sums[bits + line_bits]

        few = [gain_term(number) for number in range(nt if lane % 128 == 0 else 0)]
        few = few + [small_begin] + [small_step(turn) for turn in range(bits + line_bits)]

        def side_copy(source, target):
            return pltpu.make_async_remote_copy(
                src_ref=side_out.at[pl.ds(target * owned, owned)],
                dst_ref=side_in.at[source],
                send_sem=side_send.at[target],
                recv_sem=side_recv.at[source],
                device_id=(me, target),
                device_id_type=MESH,
            )

        def side_begin():
            side_out[...] = side_total[...].astype(jnp.bfloat16)
            for target in range(nt):

                @pl.when(zed != target)
                def _(target=target):
                    side_copy(zed, target).start()

            side_in[zed] = side_out[aligned(zed * owned, owned)]

        def side_end():
            for source in range(nt):

                @pl.when(zed != source)
                def _(source=source):
                    side_copy(source, source).wait_recv()

            common_ref[...] = jnp.zeros_like(common_ref)
            for source in range(nt):
                value = side_in[source].astype(jnp.float32)
                head = source * (QUERY_HEADS // nt) // (QUERY_HEADS // KEY_VALUE_HEADS)
                common_ref[:, :shared_columns] += value[:, :shared_columns]
                for turn in range(2):
                    at = shared_columns + (turn * KEY_VALUE_HEADS + head) * HEAD_SIZE
                    start = shared_columns + turn * HEAD_SIZE
                    common_ref[:, at : at + HEAD_SIZE] += value[:, start : start + HEAD_SIZE]
            for target in range(nt):

                @pl.when(zed != target)
                def _(target=target):
                    side_copy(zed, target).wait_send()

        def finish(chunk):
            own_sum(chunk, total)
            where = pl.ds(chunk * size, size)
            through, _ = norm_pull(resid_ref[where].astype(jnp.float32), gain_ref[...], total[...])
            value = before_ref[where] + through
            if lane % 128:
                grad_ref[where] = value
                return
            for number, (other, half) in enumerate(blocks):
                start = (mixed_with(me, other, bits) * 2 + half) * lane
                grad_ref[where, pl.ds(pl.multiple_of(start, lane), lane)] = value[:, number * lane : (number + 1) * lane]

        def passes(turn):
            return [functools.partial(pass_on, chunk, turn) for chunk in range(chunks)]

        middle = len(away) // 2
        steps = away[:middle] + [part(0)] + passes(0) + away[middle:] + [part(1)] + near[:middle]
        for turn in range(2, nt):
            steps.append(part(turn))
        steps = steps + passes(1) + near[middle:]
        for stage_steps in later[:-1]:
            steps = steps + stage_steps
        for turn in range(2, nt - 1):
            steps = steps + passes(turn)
        steps = steps + few[: -(bits + line_bits)] + later[-1] + [side_begin]
        ends = [functools.partial(finish, chunk) for chunk in range(chunks)]
        rest = few[-(bits + line_bits) :]
        for step in steps:
            step()
        together(ends, rest)
        side_end()
        small_end()
        scatter_end()
        for chunk in range(chunks):
            reduce_end(chunk)

    turns = bits + line_bits
    results = pl.pallas_call(
        kernel,
        out_shape=[
            jax.ShapeDtypeStruct((block_rows, width), jnp.float32),
            jax.ShapeDtypeStruct(small.shape, jnp.float32),
            jax.ShapeDtypeStruct((owned, common_columns), jnp.float32),
        ]
        + [jax.ShapeDtypeStruct((side_rows, columns), jnp.float32) for columns in main_widths],
        in_specs=[ONCHIP] * 9,
        out_specs=[ONCHIP] * (3 + count),
        scratch_shapes=[
            pltpu.VMEM((tokens, width), jnp.bfloat16),
            pltpu.VMEM((side_rows, side_columns), jnp.float32),
        ]
        + line_reduce_scratch(nt, block_rows, width, chunks)
        + [
            pltpu.VMEM((turns + 1, *small.shape), jnp.float32),
            pltpu.VMEM((turns, *small.shape), jnp.float32),
            pltpu.SemaphoreType.DMA((turns,)),
            pltpu.SemaphoreType.DMA((turns,)),
            pltpu.VMEM((16, width), jnp.float32),
            pltpu.VMEM((side_rows, side_columns), jnp.bfloat16),
            pltpu.VMEM((nt, owned, side_columns), jnp.bfloat16),
            pltpu.SemaphoreType.DMA((nt,)),
            pltpu.SemaphoreType.DMA((nt,)),
        ]
        + computed_scratch(nd, side_rows, main_columns + side_columns),
        compiler_params=pltpu.CompilerParams(
            collective_id=3, has_side_effects=True, vmem_limit_bytes=LARGE_LIMIT
        ),
        name="last_sums",
    )(normed, grad_main, grad_side, main, side, resid, before, gain, small)
    if lane % 128:
        results = (from_relative(results[0], 1, nd), *results[1:])
    return results


def silu_slope(value, sig):
    return sig * (1.0 + value * (1.0 - sig))


def split_dot(value, constant, dims, terms):
    total = None
    for _ in range(terms):
        piece = value.astype(jnp.bfloat16)
        value = value - piece.astype(jnp.float32)
        part = lax.dot_general(*((piece, constant) if dims[0] else (constant, piece)), dims[1], preferred_element_type=jnp.float32)
        total = part if total is None else total + part
    return total


PLAIN = (((1,), (0,)), ((), ()))
LAST = (((1,), (1,)), ((), ()))
FIRST = (((0,), (0,)), ((), ()))


def product(left, right, dims=PLAIN):
    return lax.dot_general(left, right, dims, preferred_element_type=jnp.float32)


def turned(value, cosine, sine):
    return value * cosine + pltpu.roll(value, value.shape[-1] // 2, 1) * sine


class Sizes:
    def __init__(self, channels, state_columns, query_columns, heads, length):
        self.channels, self.states = channels, state_columns // 2
        self.query, self.heads, self.length = query_columns, heads, length
        self.span = SPAN
        self.count = length // SPAN
        self.wide = channels + state_columns
        self.head_width = channels // heads
        self.step_at = 2 * channels + query_columns
        self.main = self.step_at + heads + (-(self.step_at + heads)) % 128
        self.step_lanes = self.main - self.step_at
        self.side = state_columns + 2 * HEAD_SIZE
        self.window = min(length, 3 * SPAN)


def spread_heads(size):
    table = np.zeros((size.step_lanes, size.channels), np.float32)
    for head in range(size.heads):
        table[head, head * size.head_width : (head + 1) * size.head_width] = 1.0
    return table.astype(jnp.bfloat16)


def turn_tables(length):
    half = HEAD_SIZE // 2
    angle = np.arange(length, dtype=np.float64)[:, None] * rope_base ** (-np.arange(half) / half)[None]
    cosine, sine = np.cos(angle), np.sin(angle)
    return (
        np.concatenate([cosine, cosine], 1).astype(np.float32),
        np.concatenate([-sine, sine], 1).astype(np.float32),
    )


def token_flags(segments, taps):
    seg = segments[0]
    length = seg.shape[0]
    columns = [jnp.ones((length,), bool)]
    ahead = []
    for lag in range(1, taps):
        columns.append(jnp.concatenate([jnp.zeros((lag,), bool), seg[lag:] == seg[:-lag]]))
        ahead.append(jnp.concatenate([seg[lag:] == seg[:-lag], jnp.zeros((lag,), bool)]))
    ends = seg.reshape(-1, SPAN)[:, -1]
    before = jnp.concatenate([jnp.full((1,), -1, seg.dtype), ends[:-1]])
    columns.append(seg == jnp.repeat(before, SPAN))
    columns.append(seg == jnp.repeat(ends, SPAN))
    columns = columns + ahead
    return jnp.pad(jnp.stack(columns, 1).astype(jnp.float32), ((0, 0), (0, 16 - len(columns))))


def chunk_values(size, taps, main_ref, wide_ref, flags, spread, taps_ref, heads_ref, segc, segr):
    span = size.span
    pre = wide_ref[pl.ds(8, span), :] * taps_ref[0:1, :]
    for lag in range(1, taps):
        pre = pre + wide_ref[pl.ds(8 - lag, span), :] * (flags[:, lag : lag + 1] * taps_ref[lag : lag + 1, :])
    sig = jax.nn.sigmoid(pre)
    act = pre * sig
    inner = act[:, : size.channels]
    bmat = act[:, size.channels : size.channels + size.states].astype(jnp.bfloat16)
    cmat = act[:, size.channels + size.states :].astype(jnp.bfloat16)
    step_in = main_ref[:, size.step_at :] + heads_ref[0:1, :]
    step = jnp.maximum(step_in, 0.0) + jnp.log1p(jnp.exp(-jnp.abs(step_in)))
    logdec = -step * heads_ref[1:2, :]
    rows = lax.broadcasted_iota(jnp.int32, (span, span), 0)
    columns = lax.broadcasted_iota(jnp.int32, (span, span), 1)
    later = jnp.where(rows >= columns, 1.0, 0.0).astype(jnp.bfloat16)
    cumul = split_dot(logdec, later, (False, PLAIN), 3)
    inside = jnp.logical_and(rows >= columns, segc == segr)
    ending = cumul[span - 1 : span, :]
    reach = jnp.exp(cumul) * flags[:, 4:5]
    tail = jnp.exp(ending - cumul) * flags[:, 5:6]
    step_wide = split_dot(step, spread, (True, PLAIN), 2)
    scaled = inner * step_wide
    return dict(
        pre=pre, sig=sig, inner=inner, bmat=bmat, cmat=cmat, step_in=step_in, step=step, logdec=logdec, later=later,
        cumul=cumul, turned=jnp.transpose(cumul), inside=inside, step_wide=step_wide, scaled=scaled,
        scaled_b=scaled.astype(jnp.bfloat16), meeting=product(cmat, bmat, LAST),
        reach_wide=split_dot(reach, spread, (True, PLAIN), 2), tail_wide=split_dot(tail, spread, (True, PLAIN), 2),
        skip_wide=split_dot(jnp.broadcast_to(heads_ref[2:3, :], (8, size.step_lanes)), spread, (True, PLAIN), 2)[0:1],
    )


def decay_of(values, head):
    spread = values["cumul"][:, head : head + 1] - values["turned"][head : head + 1, :]
    return jnp.exp(jnp.where(values["inside"], spread, -1e30))


def softmax_of(size, query, keys, chunk, start, segc, seg_all):
    scores = product(query, keys, LAST) * (1.0 / math.sqrt(HEAD_SIZE))
    rows = lax.broadcasted_iota(jnp.int32, scores.shape, 0) + chunk * size.span
    columns = lax.broadcasted_iota(jnp.int32, scores.shape, 1) + start
    allowed = jnp.logical_and(rows >= columns, segc == seg_all)
    masked = jnp.where(allowed, scores, -1e30)
    expo = jnp.exp(masked - jnp.max(masked, axis=-1, keepdims=True))
    return expo / jnp.sum(expo, axis=-1, keepdims=True)


def mixers_forward(size, taps, main_raw, side_raw, segments, flags, tap_rows, head_rows):
    span = size.span
    per_head = size.head_width

    def kernel(
        main_ref, side_ref, segc_ref, segr_ref, flags_ref, taps_ref, heads_ref, cos_ref, sin_ref, spread_ref,
        mixed_ref, y_ref, state_ref, keys_ref, values_ref, wide, state,
    ):
        chunk = pl.program_id(0)

        @pl.when(chunk == 0)
        def _():
            wide[0:8, :] = jnp.zeros((8, size.wide), jnp.float32)
            state[...] = jnp.zeros_like(state)
            keys_ref[...] = jnp.zeros_like(keys_ref)
            values_ref[...] = jnp.zeros_like(values_ref)

        wide[pl.ds(8, span), : size.channels] = main_ref[:, size.channels : 2 * size.channels]
        wide[pl.ds(8, span), size.channels :] = side_ref[:, : 2 * size.states]
        flags, spread, segc = flags_ref[...], spread_ref[...], segc_ref[...]
        segr = segr_ref[:, pl.ds(pl.multiple_of(chunk * span, span), span)]
        val = chunk_values(size, taps, main_ref, wide, flags, spread, taps_ref, heads_ref, segc, segr)
        wide[0:8, :] = wide[pl.ds(span, 8), :]
        held = state[...]
        held_b = held.astype(jnp.bfloat16)
        state_ref[...] = held
        across = val["reach_wide"] * product(val["cmat"], held_b)
        lane = lax.broadcasted_iota(jnp.int32, (span, 2 * per_head), 1)
        for pair in range(size.heads // 2):
            where = slice(pair * 2 * per_head, (pair + 1) * 2 * per_head)
            both = []
            for head in (2 * pair, 2 * pair + 1):
                weights = (val["meeting"] * decay_of(val, head)).astype(jnp.bfloat16)
                both.append(product(weights, val["scaled_b"][:, where]))
            result = jnp.where(lane < per_head, both[0], both[1])
            result = result + across[:, where] + val["skip_wide"][:, where] * val["inner"][:, where]
            y_ref[:, where] = result
            gate = main_ref[:, where]
            mixed_ref[:, where] = (result * (gate * jax.nn.sigmoid(gate))).astype(jnp.bfloat16)
        keep = jnp.broadcast_to(val["reach_wide"][span - 1 : span, :], (1, size.channels))
        state[...] = keep * held + product(
            val["bmat"], (val["tail_wide"] * val["scaled"]).astype(jnp.bfloat16), FIRST
        )

        cosine, sine = cos_ref[...], sin_ref[...]
        own = pl.ds(pl.multiple_of(chunk * span, span), span)
        key_at = 2 * size.states
        keys_ref[own, :] = turned(side_ref[:, key_at : key_at + HEAD_SIZE], cosine, sine).astype(jnp.bfloat16)
        values_ref[own, :] = side_ref[:, key_at + HEAD_SIZE :].astype(jnp.bfloat16)
        start = pl.multiple_of(jnp.maximum(chunk + 1 - size.window // span, 0) * span, span)
        seen = pl.ds(start, size.window)
        for head in range(size.query // HEAD_SIZE):
            at = 2 * size.channels + head * HEAD_SIZE
            query = turned(main_ref[:, at : at + HEAD_SIZE], cosine, sine).astype(jnp.bfloat16)
            probs = softmax_of(size, query, keys_ref[seen, :], chunk, start, segc, segr_ref[:, seen])
            result = product(probs.astype(jnp.bfloat16), values_ref[seen, :])
            at = size.channels + head * HEAD_SIZE
            mixed_ref[:, at : at + HEAD_SIZE] = result.astype(jnp.bfloat16)

    def rows(columns):
        return pl.BlockSpec((span, columns), lambda i: (i, 0))

    def whole(array):
        return pl.BlockSpec(array.shape, lambda i: (0, 0))

    cosine, sine = turn_tables(size.length)
    spread = spread_heads(size)
    tokens = size.length
    return pl.pallas_call(
        kernel,
        grid=(size.count,),
        in_specs=[
            rows(size.main), rows(size.side), rows(1), whole(segments), rows(16), whole(tap_rows), whole(head_rows),
            rows(HEAD_SIZE), rows(HEAD_SIZE), whole(spread),
        ],
        out_specs=[
            rows(size.channels + size.query), rows(size.channels),
            pl.BlockSpec((size.states, size.channels), lambda i: (i, 0)),
            pl.BlockSpec((tokens, HEAD_SIZE), lambda i: (0, 0)), pl.BlockSpec((tokens, HEAD_SIZE), lambda i: (0, 0)),
        ],
        out_shape=[
            jax.ShapeDtypeStruct((tokens, size.channels + size.query), jnp.bfloat16),
            jax.ShapeDtypeStruct((tokens, size.channels), jnp.float32),
            jax.ShapeDtypeStruct((size.count * size.states, size.channels), jnp.float32),
            jax.ShapeDtypeStruct((tokens, HEAD_SIZE), jnp.bfloat16),
            jax.ShapeDtypeStruct((tokens, HEAD_SIZE), jnp.bfloat16),
        ],
        scratch_shapes=[
            pltpu.VMEM((span + 8, size.wide), jnp.float32),
            pltpu.VMEM((size.states, size.channels), jnp.float32),
        ],
        compiler_params=pltpu.CompilerParams(
            dimension_semantics=("arbitrary",), vmem_limit_bytes=VMEM_LIMIT
        ),
        name="mixers_forward",
    )(main_raw, side_raw, segments.reshape(tokens, 1), segments, flags, tap_rows, head_rows,
      jnp.asarray(cosine), jnp.asarray(sine), jnp.asarray(spread))


def mixers_backward(
    nd, nt, size, taps, grad_mixed, main_raw, side_raw, segments, flags, tap_rows, head_rows, y_value, states, keys, values,
    grad_rows, mixed,
):
    bits = nd.bit_length() - 1
    out_rows, out_columns = grad_rows.shape[1] // nd, mixed.shape[1]
    span = size.span
    per_head = size.head_width
    count = size.count

    def kernel(
        grad_ref, main_ref, side_ref, before_ref, side_before_ref, segc_ref, segr_ref, flags_ref, taps_ref, heads_ref,
        cos_ref, sin_ref, spread_ref, y_ref, state_ref, keys_ref, values_ref, rows_ref, mixed_ref,
        grad_main, grad_side, tap_sums, head_sums, mixer_total, attn_total,
        wide, back, grad_state, grad_keys, grad_values,
        stage, held, landed, core_send, core_recv, hop_send, hop_recv,
    ):
        turn = pl.program_id(0)
        chunk = count - 1 - turn
        me, zed = lax.axis_index("dp"), lax.axis_index("tensor")
        away, near, later, scatter_end = computed_scatter(
            nd, me, zed, out_rows // 2, products_of(rows_ref, ((mixed_ref, out_columns),), 512), stage, held, landed,
            ((mixer_total, 0, size.channels), (attn_total, size.channels, size.query)),
            core_send, core_recv, hop_send, hop_recv,
        )
        stages = [away, near, *later[: count - 3], [step for stage_steps in later[count - 3 :] for step in stage_steps]]
        for number, stage_steps in enumerate(stages):

            @pl.when(turn == number)
            def _(number=number, stage_steps=stage_steps):
                if number == 0:
                    enter(nt, bits)
                for step in stage_steps:
                    step()
                if number == len(stages) - 1:
                    scatter_end()

        @pl.when(turn == 0)
        def _():
            back[pl.ds(span, 8), :] = jnp.zeros((8, size.wide), jnp.float32)
            grad_state[...] = jnp.zeros_like(grad_state)
            grad_keys[...] = jnp.zeros_like(grad_keys)
            grad_values[...] = jnp.zeros_like(grad_values)
            tap_sums[...] = jnp.zeros_like(tap_sums)
            head_sums[...] = jnp.zeros_like(head_sums)

        wide[0:8, : size.channels] = before_ref[...]
        wide[0:8, size.channels :] = side_before_ref[...]
        wide[pl.ds(8, span), : size.channels] = main_ref[:, size.channels : 2 * size.channels]
        wide[pl.ds(8, span), size.channels :] = side_ref[:, : 2 * size.states]
        flags, spread, segc = flags_ref[...], spread_ref[...], segc_ref[...]
        segr = segr_ref[:, pl.ds(pl.multiple_of(chunk * span, span), span)]
        val = chunk_values(size, taps, main_ref, wide, flags, spread, taps_ref, heads_ref, segc, segr)
        inner, scaled = val["inner"], val["scaled"]

        gate = main_ref[:, : size.channels]
        gate_sig = jax.nn.sigmoid(gate)
        grad = grad_ref[:, : size.channels]
        grad_main[:, : size.channels] = (grad * y_ref[...] * silu_slope(gate, gate_sig)).astype(jnp.bfloat16)
        grad_y = grad * (gate * gate_sig)
        grad_y_b = grad_y.astype(jnp.bfloat16)
        tap_sums[4:5, : size.channels] += jnp.sum(grad_y * inner, axis=0, keepdims=True)

        lane = lax.broadcasted_iota(jnp.int32, (span, 2 * per_head), 1)
        head_lane = lax.broadcasted_iota(jnp.int32, (span, size.step_lanes), 1)
        head_row = lax.broadcasted_iota(jnp.int32, (size.step_lanes, span), 0)
        grad_meeting = jnp.zeros((span, span), jnp.float32)
        by_row = jnp.zeros((span, size.step_lanes), jnp.float32)
        by_column = jnp.zeros((size.step_lanes, span), jnp.float32)
        pieces = []
        for pair in range(size.heads // 2):
            where = slice(pair * 2 * per_head, (pair + 1) * 2 * per_head)
            both = []
            for side in range(2):
                head = 2 * pair + side
                decay = decay_of(val, head)
                weights = val["meeting"] * decay
                mine = (lane < per_head) if side == 0 else (lane >= per_head)
                grad_own = jnp.where(mine, grad_y_b[:, where], jnp.zeros((), jnp.bfloat16))
                grad_weights = product(grad_own, val["scaled_b"][:, where], LAST)
                both.append(product(weights.astype(jnp.bfloat16), grad_y_b[:, where], FIRST))
                grad_meeting = grad_meeting + grad_weights * decay
                moved = grad_weights * weights
                by_row = jnp.where(head_lane == head, jnp.sum(moved, axis=1, keepdims=True), by_row)
                by_column = jnp.where(head_row == head, jnp.sum(moved, axis=0, keepdims=True), by_column)
            pieces.append(jnp.where(lane < per_head, both[0], both[1]))
        grad_scaled = jnp.concatenate(pieces, axis=1)
        grad_cumul = by_row - jnp.transpose(by_column)

        held = state_ref[...]
        held_b = held.astype(jnp.bfloat16)
        grad_held = grad_state[...]
        grad_held_b = grad_held.astype(jnp.bfloat16)
        grad_meeting_b = grad_meeting.astype(jnp.bfloat16)
        reached = val["reach_wide"] * grad_y
        reached_b = reached.astype(jnp.bfloat16)
        grad_cumul = grad_cumul + split_dot(reached * product(val["cmat"], held_b), spread, (True, LAST), 2)
        grad_c = product(reached_b, held_b, LAST) + product(grad_meeting_b, val["bmat"])
        from_state = val["tail_wide"] * product(val["bmat"], grad_held_b)
        grad_b = product(grad_meeting_b, val["cmat"], FIRST) + product(
            (val["tail_wide"] * scaled).astype(jnp.bfloat16), grad_held_b, LAST
        )
        grad_scaled = grad_scaled + from_state
        ended = split_dot(scaled * from_state, spread, (True, LAST), 2)
        keep = val["reach_wide"][span - 1 : span, :]
        kept = jnp.sum(grad_held * held, axis=0, keepdims=True) * keep
        kept = split_dot(jnp.broadcast_to(kept, (8, size.channels)), spread, (True, LAST), 2)[0:1]
        at_end = jnp.sum(ended, axis=0, keepdims=True) + kept
        grad_logdec = split_dot(grad_cumul - ended, val["later"], (False, FIRST), 3) + at_end
        grad_state[...] = keep * grad_held + product(val["cmat"], reached_b, FIRST)

        grad_inner = grad_scaled * val["step_wide"] + grad_y * val["skip_wide"]
        grad_step = split_dot(grad_scaled * inner, spread, (True, LAST), 2) - grad_logdec * heads_ref[1:2, :]
        grad_step_raw = grad_step * jax.nn.sigmoid(val["step_in"])
        head_sums[0:1, :] += jnp.sum(grad_step_raw, axis=0, keepdims=True)
        head_sums[1:2, :] += jnp.sum(grad_logdec * val["logdec"], axis=0, keepdims=True)
        grad_main[:, size.step_at :] = grad_step_raw.astype(jnp.bfloat16)

        slope = silu_slope(val["pre"], val["sig"])
        grad_pre = jnp.concatenate([grad_inner, grad_b, grad_c], axis=1) * slope
        back[pl.ds(0, span), :] = grad_pre
        raw = grad_pre * taps_ref[0:1, :]
        tap_sums[0:1, :] += jnp.sum(grad_pre * wide[pl.ds(8, span), :], axis=0, keepdims=True)
        for lag in range(1, taps):
            tap_sums[lag : lag + 1, :] += jnp.sum(
                grad_pre * (wide[pl.ds(8 - lag, span), :] * flags[:, lag : lag + 1]), axis=0, keepdims=True
            )
            raw = raw + back[pl.ds(lag, span), :] * (flags[:, 5 + lag : 6 + lag] * taps_ref[lag : lag + 1, :])
        back[pl.ds(span, 8), :] = back[0:8, :]
        grad_main[:, size.channels : 2 * size.channels] = raw[:, : size.channels].astype(jnp.bfloat16)
        grad_side[:, : 2 * size.states] = raw[:, size.channels :].astype(jnp.bfloat16)

        cosine, sine = cos_ref[...], sin_ref[...]
        start = pl.multiple_of(jnp.maximum(chunk + 1 - size.window // span, 0) * span, span)
        seen = pl.ds(start, size.window)
        seen_keys, seen_values = keys_ref[seen, :], values_ref[seen, :]
        scale = 1.0 / math.sqrt(HEAD_SIZE)
        for head in range(size.query // HEAD_SIZE):
            at = 2 * size.channels + head * HEAD_SIZE
            query = turned(main_ref[:, at : at + HEAD_SIZE], cosine, sine).astype(jnp.bfloat16)
            probs = softmax_of(size, query, seen_keys, chunk, start, segc, segr_ref[:, seen])
            out_at = size.channels + head * HEAD_SIZE
            grad_out = grad_ref[:, out_at : out_at + HEAD_SIZE].astype(jnp.bfloat16)
            grad_probs = product(grad_out, seen_values, LAST)
            delta = jnp.sum(grad_probs * probs, axis=-1, keepdims=True)
            grad_scores = (probs * (grad_probs - delta)).astype(jnp.bfloat16)
            grad_query = product(grad_scores, seen_keys) * scale
            grad_main[:, at : at + HEAD_SIZE] = turned(grad_query, cosine, -sine).astype(jnp.bfloat16)
            grad_keys[seen, :] += product(grad_scores, query, FIRST) * scale
            grad_values[seen, :] += product(probs.astype(jnp.bfloat16), grad_out, FIRST)
        own = pl.ds(pl.multiple_of(chunk * span, span), span)
        key_at = 2 * size.states
        grad_side[:, key_at : key_at + HEAD_SIZE] = turned(grad_keys[own, :], cosine, -sine).astype(jnp.bfloat16)
        grad_side[:, key_at + HEAD_SIZE :] = grad_values[own, :].astype(jnp.bfloat16)

    def rows(columns):
        return pl.BlockSpec((span, columns), lambda i: (count - 1 - i, 0))

    def previous(columns, column):
        return pl.BlockSpec((8, columns), lambda i: (jnp.maximum((count - 1 - i) * (span // 8) - 1, 0), column))

    def whole(array):
        return pl.BlockSpec(array.shape, lambda i: (0, 0))

    cosine, sine = turn_tables(size.length)
    spread = spread_heads(size)
    tokens = size.length
    return pl.pallas_call(
        kernel,
        grid=(count,),
        in_specs=[
            rows(size.channels + size.query), rows(size.main), rows(size.side), previous(size.channels, 1),
            previous(2 * size.states, 0), rows(1), whole(segments), rows(16), whole(tap_rows), whole(head_rows),
            rows(HEAD_SIZE), rows(HEAD_SIZE), whole(spread), rows(size.channels),
            pl.BlockSpec((size.states, size.channels), lambda i: (count - 1 - i, 0)), whole(keys), whole(values),
            whole(grad_rows), whole(mixed),
        ],
        out_specs=[
            rows(size.main), rows(size.side), pl.BlockSpec((8, size.wide), lambda i: (0, 0)),
            pl.BlockSpec((8, size.step_lanes), lambda i: (0, 0)),
            pl.BlockSpec((out_rows, size.channels), lambda i: (0, 0)),
            pl.BlockSpec((out_rows, size.query), lambda i: (0, 0)),
        ],
        out_shape=[
            jax.ShapeDtypeStruct((tokens, size.main), jnp.bfloat16),
            jax.ShapeDtypeStruct((tokens, size.side), jnp.bfloat16),
            jax.ShapeDtypeStruct((8, size.wide), jnp.float32),
            jax.ShapeDtypeStruct((8, size.step_lanes), jnp.float32),
            jax.ShapeDtypeStruct((out_rows, size.channels), jnp.float32),
            jax.ShapeDtypeStruct((out_rows, size.query), jnp.float32),
        ],
        scratch_shapes=[
            pltpu.VMEM((span + 8, size.wide), jnp.float32),
            pltpu.VMEM((span + 8, size.wide), jnp.float32),
            pltpu.VMEM((size.states, size.channels), jnp.float32),
            pltpu.VMEM((tokens, HEAD_SIZE), jnp.float32),
            pltpu.VMEM((tokens, HEAD_SIZE), jnp.float32),
        ]
        + computed_scratch(nd, out_rows, out_columns),
        compiler_params=pltpu.CompilerParams(
            dimension_semantics=("arbitrary",), vmem_limit_bytes=VMEM_LIMIT, collective_id=4, has_side_effects=True
        ),
        cost_estimate=pl.CostEstimate(flops=40 * 10**9, bytes_accessed=60 * 10**6, transcendentals=10**7),
        name="mixers_backward",
    )(grad_mixed, main_raw, side_raw, main_raw, side_raw, segments.reshape(tokens, 1), segments, flags, tap_rows,
      head_rows, jnp.asarray(cosine), jnp.asarray(sine), jnp.asarray(spread), y_value, states, keys, values, grad_rows, mixed)


def per_device(
    nd,
    nt,
    residual,
    segments,
    mixgain,
    ffngain,
    gateproj,
    innerproj,
    stepproj,
    sharedproj,
    innerconv,
    sharedconv,
    stepbias,
    decaylog,
    skipgain,
    mixerout,
    queryproj,
    keyvalue,
    attnout,
    ffngate,
    upproj,
    downproj,
    cotangent,
):
    bfloat = jnp.bfloat16
    single = jnp.float32
    width = residual.shape[1]
    zed = lax.axis_index("tensor")
    seq_count, length = segments.shape
    token_count = seq_count * length
    channels = innerproj.shape[1]
    state_columns = sharedproj.shape[1]
    heads = stepproj.shape[1]
    query_columns = queryproj.shape[1]
    ffn_columns = ffngate.shape[1]
    small_rows = sharedproj.shape[0]
    conv_rows = sharedconv.shape[0]
    taps = sharedconv.shape[1]

    gains = jnp.concatenate(
        [
            mixgain[:, None],
            ffngain[:, None],
            jnp.pad(sharedconv, ((0, small_rows - conv_rows), (0, 0))),
            jnp.zeros((small_rows, 128 - 2 - taps), bfloat),
        ],
        axis=1,
    )
    main_used = 2 * channels + query_columns + heads
    main_own = jnp.concatenate(
        [
            gateproj,
            innerproj,
            queryproj,
            stepproj,
            jnp.zeros((gateproj.shape[0], -main_used % 128), bfloat),
        ],
        axis=1,
    )
    resid_own, cot_own, gain_rows, normed, grad_rows, _, main, side, out_w, main_raw, side_raw = first_gathers(
        nd,
        nt,
        residual,
        cotangent,
        jnp.concatenate([sharedproj, keyvalue, gains], axis=1),
        main_own,
        jnp.concatenate([mixerout, attnout], axis=1),
        state_columns,
    )
    gain_one, gain_two = gain_rows[0], gain_rows[1]
    conv_shared = from_relative(gain_rows[2 : 2 + taps], 1, nd)
    conv_shared = conv_shared.reshape(taps, nd * nt, small_rows)[:, :, :conv_rows].reshape(taps, -1)

    size = Sizes(channels, state_columns, query_columns, heads, length)
    flags = token_flags(segments, taps)
    tap_rows = jnp.concatenate([innerconv.astype(single).T, conv_shared], axis=1)
    tap_rows = jnp.pad(tap_rows, ((0, 8 - taps), (0, 0)))
    head_rows = jnp.stack([stepbias.astype(single), jnp.exp(decaylog.astype(single)), skipgain.astype(single)])
    head_rows = jnp.pad(head_rows, ((0, 5), (0, size.step_lanes - heads)))
    mixed_in, y_value, states, keys, values = mixers_forward(
        size, taps, main_raw, side_raw, segments, flags, tap_rows, head_rows
    )
    middle, rows_two, hidden, grad_gate_up, grad_rows, ffn_w = middle_rows(
        nd,
        nt,
        mixed_in,
        out_w,
        resid_own,
        gain_two[None],
        grad_rows,
        jnp.concatenate([ffngate, upproj, downproj], axis=1),
    )
    gate_up_w = ffn_w[:, : 2 * ffn_columns]
    down_w = ffn_w[:, 2 * ffn_columns :]
    two_part = contract_last(grad_gate_up, gate_up_w).astype(bfloat)
    grad_middle, grad_gain_two, grad_mix_rows, down_g, gate_up_g = middle_back(
        nd,
        nt,
        two_part,
        middle,
        cot_own,
        gain_two[None],
        [
            contract_leading_axis(grad_rows, hidden).astype(bfloat),
            contract_leading_axis(rows_two, grad_gate_up).astype(bfloat),
        ],
    )
    ffn_part = contract_last(hidden, down_w).astype(bfloat)
    ffn_part = ffn_part.reshape(-1, nt, middle.shape[0] // LINE_CHUNKS, width).swapaxes(0, 1).reshape(token_count, width)
    ffn_part = after(ffn_part, grad_mix_rows)
    ffn_out = lax.psum_scatter(ffn_part, "tensor", scatter_dimension=0, tiled=True)
    layer_out = from_relative(middle + ffn_out.astype(single), 1, nd)
    grad_mixed_in = matrix_product(grad_mix_rows, out_w)
    grad_main, grad_side, tap_sums, head_sums, mixer_g, attn_g = mixers_backward(
        nd, nt, size, taps, grad_mixed_in, main_raw, side_raw, segments, flags, tap_rows, head_rows, y_value, states,
        keys, values, grad_mix_rows, mixed_in,
    )
    small = jnp.concatenate(
        [
            jnp.zeros((width,), single),
            grad_gain_two[0],
            tap_sums[:taps, channels:].reshape(-1),
            tap_sums[:taps, :channels].reshape(-1),
            tap_sums[4, :channels],
            head_sums[:2].reshape(-1),
        ]
    )
    shared_length = 2 * width + taps * state_columns
    small = jnp.pad(small, (0, -small.shape[0] % 1024)).reshape(-1, 128)
    grad_residual, small, common_g, gate_g, inner_g, query_g, step_g = last_sums(
        nd,
        nt,
        normed,
        grad_main,
        grad_side,
        main,
        side,
        resid_own,
        grad_middle,
        gain_one[None],
        small,
        shared_length // 128,
        (channels, channels, query_columns, heads),
    )
    small = small.reshape(-1)
    place = lax.axis_index("dp") * nt + zed
    gain_one_g = lax.dynamic_slice_in_dim(small, place * small_rows, small_rows, 0)
    gain_two_g = lax.dynamic_slice_in_dim(small, width + place * small_rows, small_rows, 0)
    conv_g = lax.dynamic_slice_in_dim(
        small[2 * width : shared_length].reshape(taps, -1), place * conv_rows, conv_rows, 1
    ).T
    local = small[shared_length:]
    skip_at = taps * channels
    head_at = skip_at + channels
    return (
        layer_out,
        grad_residual,
        gain_one_g,
        gain_two_g,
        gate_g,
        inner_g,
        step_g,
        common_g[:, :state_columns],
        local[:skip_at].reshape(taps, channels).T,
        conv_g,
        local[head_at : head_at + heads],
        local[head_at + size.step_lanes : head_at + size.step_lanes + heads],
        local[skip_at:head_at].reshape(heads, -1).sum(axis=1),
        mixer_g,
        query_g,
        common_g[:, state_columns:],
        attn_g,
        gate_up_g[:, :ffn_columns],
        gate_up_g[:, ffn_columns:],
        down_g,
    )


def solution(mesh):
    return jax.shard_map(
        functools.partial(per_device, mesh.shape["dp"], mesh.shape["tensor"]),
        mesh=mesh,
        in_specs=(
            P(("dp", "tensor"), None),
            P("dp", None),
            P(("dp", "tensor")),
            P(("dp", "tensor")),
            P("dp", "tensor"),
            P("dp", "tensor"),
            P("dp", "tensor"),
            P(("dp", "tensor"), None),
            P("tensor", None),
            P(("dp", "tensor"), None),
            P("tensor"),
            P("tensor"),
            P("tensor"),
            P("dp", "tensor"),
            P("dp", "tensor"),
            P(("dp", "tensor"), None),
            P("dp", "tensor"),
            P("dp", "tensor"),
            P("dp", "tensor"),
            P("dp", "tensor"),
            P(("dp", "tensor"), None),
        ),
        out_specs=(
            P(("dp", "tensor"), None),
            P(("dp", "tensor"), None),
            P(("dp", "tensor")),
            P(("dp", "tensor")),
            P("dp", "tensor"),
            P("dp", "tensor"),
            P("dp", "tensor"),
            P(("dp", "tensor"), None),
            P("tensor", None),
            P(("dp", "tensor"), None),
            P("tensor"),
            P("tensor"),
            P("tensor"),
            P("dp", "tensor"),
            P("dp", "tensor"),
            P(("dp", "tensor"), None),
            P("dp", "tensor"),
            P("dp", "tensor"),
            P("dp", "tensor"),
            P("dp", "tensor"),
        ),
        check_vma=False,
    )
```

```python
import functools
import math

import jax
import jax.numpy as jnp
import numpy as np
from jax import lax
from jax.experimental import pallas as pl
from jax.experimental.pallas import tpu as pltpu
from jax.sharding import PartitionSpec as P

QUERY_HEADS = 8
KEY_VALUE_HEADS = 2
HEAD_SIZE = 128
SPAN = 256


eps = 1e-05
rope_base = 10000.0


def matrix_product(left, right):
    return jnp.dot(left, right, preferred_element_type=jnp.float32)


def contract_leading_axis(left, right):
    return lax.dot_general(
        left, right, (((0,), (0,)), ((), ())), preferred_element_type=jnp.float32
    )


def contract_last(left, right):
    return lax.dot_general(
        left, right, (((1,), (1,)), ((), ())), preferred_element_type=jnp.float32
    )


def bit_orders(size):
    high = list(range(size.bit_length() - 2, 0, -1))
    return high, high[:2][::-1] + high[2:]


def relative_blocks(size):
    both = []
    for half, order in enumerate(bit_orders(size)):
        chain = [0]
        for bit in order:
            chain = chain + [other ^ (1 << bit) for other in chain]
        both = both + [(other, half) for other in chain]
    return both + [(other ^ 1, half) for other, half in both]


def to_relative(value, axis, size):
    me = lax.axis_index("dp")
    width = value.shape[axis] // (2 * size)
    return jnp.concatenate(
        [
            lax.dynamic_slice_in_dim(value, ((me ^ other) * 2 + half) * width, width, axis)
            for other, half in relative_blocks(size)
        ],
        axis,
    )


def from_relative(value, axis, size):
    me = lax.axis_index("dp")
    width = value.shape[axis] // (2 * size)
    blocks = relative_blocks(size)
    place = jnp.asarray([blocks.index((other, half)) for other in range(size) for half in range(2)], jnp.int32)
    return jnp.concatenate(
        [
            lax.dynamic_slice_in_dim(value, place[(me ^ number) * 2 + half] * width, width, axis)
            for number in range(size)
            for half in range(2)
        ],
        axis,
    )


def after(value, *others):
    return lax.optimization_barrier((value,) + others)[0]


MESH = pl.DeviceIdType.MESH
VMEM_LIMIT = 56 * 1024 * 1024
LINE_CHUNKS = 4
LARGE_LIMIT = 62 * 1024 * 1024


def flip(value, bit):
    unit = 1 << bit
    return value + unit * (1 - 2 * ((value // unit) % 2))


def mixed_with(value, other, bits):
    for bit in range(bits):
        if (other >> bit) & 1:
            value = flip(value, bit)
    return value


def enter(nt, bits):
    me, zed = lax.axis_index("dp"), lax.axis_index("tensor")
    barrier = pltpu.get_barrier_semaphore()
    for other in range(nt):

        @pl.when(zed != other)
        def _(other=other):
            pl.semaphore_signal(barrier, inc=1, device_id=(me, other), device_id_type=MESH)

    for bit in range(bits):
        pl.semaphore_signal(barrier, inc=1, device_id=(flip(me, bit), zed), device_id_type=MESH)
    pl.semaphore_wait(barrier, bits + nt - 1)
    return me, zed


def aligned(start, size):
    return pl.ds(pl.multiple_of(start, 16), size)


def together(*flows):
    flows = [list(flow) for flow in flows]
    order = sorted(
        ((place + 0.5) / len(flow), number, place)
        for number, flow in enumerate(flows)
        for place in range(len(flow))
    )
    for _, number, place in order:
        flows[number][place]()


def gather_steps(nd, me, zed, own, everything, send, recv, local):
    half = own.shape[0] // 2
    blocks = relative_blocks(nd)
    place = {block: number for number, block in enumerate(blocks)}

    def rows(block):
        return everything.at[pl.ds(place[block] * half, half)]

    def source(block):
        return own.at[pl.ds(block[1] * half, half)] if block[0] == 0 else rows(block)

    hops = []
    for part, order in enumerate(bit_orders(nd)):
        chain = [0]
        for bit in order:
            hops = hops + [((other, part), bit) for other in chain]
            chain = chain + [other ^ (1 << bit) for other in chain]
    hops = hops + [(block, 0) for block in blocks[:nd]]

    def copy(number):
        block, bit = hops[number]
        landed = (block[0] ^ (1 << bit), block[1])
        return pltpu.make_async_remote_copy(
            src_ref=source(block),
            dst_ref=rows(landed),
            send_sem=send.at[number],
            recv_sem=recv.at[place[landed]],
            device_id=(flip(me, bit), zed),
            device_id_type=MESH,
        )

    def arrival(block):
        return pltpu.make_async_remote_copy(
            src_ref=rows(block),
            dst_ref=rows(block),
            send_sem=send.at[0],
            recv_sem=recv.at[place[block]],
            device_id=(flip(me, 0), zed),
            device_id_type=MESH,
        )

    def begin():
        for number, (block, bit) in enumerate(hops):
            if block[0] == 0:
                copy(number).start()
        for part in range(2):
            pltpu.make_async_copy(source((0, part)), rows((0, part)), local.at[part]).start()

    def forward(block):
        def step():
            arrival(block).wait_recv()
            for number, (origin, bit) in enumerate(hops):
                if origin == block:
                    copy(number).start()

        return step

    def end():
        for block in blocks[nd:]:
            arrival(block).wait_recv()
        for number in range(len(hops)):
            copy(number).wait_send()
        for part in range(2):
            pltpu.make_async_copy(source((0, part)), rows((0, part)), local.at[part]).wait()

    first, second = blocks[1 : nd // 2], blocks[nd // 2 + 1 : nd]
    middle = [forward(block) for pair in zip(first, second) for block in pair]
    return [begin] + middle + [end]


def gather_hops(nd):
    return 2 * (nd // 2 - 1) + nd


def gather_semaphores(nd):
    return [
        pltpu.SemaphoreType.DMA((gather_hops(nd),)),
        pltpu.SemaphoreType.DMA((2 * nd,)),
        pltpu.SemaphoreType.DMA((2,)),
    ]


def each_rows(rows, body, unit=16):
    def step(number, carry):
        body(aligned(number * unit, unit))
        return carry

    lax.fori_loop(0, rows // unit, step, 0)


def computed_scatter(nd, me, zed, half, compute, stage, held, landed, totals, core_send, core_recv, send, recv):
    chain_length = nd // 2
    block = 256
    pieces = block // half
    per_part = chain_length // pieces
    turns = [part * per_part + spot for spot in range(per_part - 1, -1, -1) for part in range(2)]

    def piece(ref, number):
        return ref.at[pl.ds(number * half, half)]

    def block_of(ref, number):
        return ref.at[pl.ds(number * block, block)]

    rounds, slot = [], 0
    for part, order in enumerate(bit_orders(nd)):
        length, own_rounds = chain_length, []
        for bit in order[::-1]:
            length = length // 2
            own_rounds.append((bit, length, slot))
            slot = slot + length
        rounds.append(own_rounds)

    def core_copy(number):
        return pltpu.make_async_remote_copy(
            src_ref=block_of(stage, number),
            dst_ref=block_of(held, number),
            send_sem=core_send.at[number],
            recv_sem=core_recv.at[number],
            device_id=(flip(me, 0), zed),
            device_id_type=MESH,
        )

    def hop(bit, number, where):
        return pltpu.make_async_remote_copy(
            src_ref=piece(held, number),
            dst_ref=piece(landed, where),
            send_sem=send.at[where],
            recv_sem=recv.at[where],
            device_id=(flip(me, bit), zed),
            device_id_type=MESH,
        )

    def away(number):
        def step():
            compute(nd * half + number * block, None, block_of(stage, number))
            core_copy(number).start()

        return step

    def near(number):
        def step():
            core_copy(number).wait_recv()
            compute(number * block, block_of(held, number), block_of(held, number))
            for inner in range(pieces):
                place = number * pieces + inner
                part, spot = place // chain_length, place % chain_length
                bit, length, first = rounds[part][0]
                if spot >= length:
                    hop(bit, place, first + spot - length).start()

        return step

    def later_sum(part, turn, spot):
        bit, length, first = rounds[part][turn]
        number = part * chain_length + spot

        def step():
            hop(bit, number, first + spot).wait_recv()
            last = turn == len(rounds[part]) - 1

            def body(rows):
                kept, came = piece(held, number)[rows], piece(landed, first + spot)[rows]
                if last:
                    value = kept.astype(jnp.float32) + came.astype(jnp.float32)
                    for target, start, columns in totals:
                        piece(target, part)[rows] = value[:, start : start + columns]
                else:
                    piece(held, number)[rows] = kept + came

            each_rows(half, body)
            if not last:
                next_bit, next_length, next_first = rounds[part][turn + 1]
                if spot >= next_length:
                    hop(next_bit, number, next_first + spot - next_length).start()

        return step

    def end():
        for number in range(len(turns)):
            core_copy(number).wait_send()
        for part in range(2):
            for bit, length, first in rounds[part]:
                for spot in range(length):
                    hop(bit, part * chain_length + length + spot, first + spot).wait_send()

    later = []
    for turn in range(len(rounds[0])):
        length = rounds[0][turn][1]
        later.append([later_sum(part, turn, spot) for spot in range(length - 1, -1, -1) for part in range(2)])
    return [away(number) for number in turns], [near(number) for number in turns], later, end


def computed_scratch(nd, rows, columns):
    slots = nd - 2
    blocks = nd * rows // 2 // 256
    return [
        pltpu.VMEM((nd * rows // 2, columns), jnp.bfloat16),
        pltpu.VMEM((nd * rows // 2, columns), jnp.bfloat16),
        pltpu.VMEM((slots * rows // 2, columns), jnp.bfloat16),
        pltpu.SemaphoreType.DMA((blocks,)),
        pltpu.SemaphoreType.DMA((blocks,)),
        pltpu.SemaphoreType.DMA((slots,)),
        pltpu.SemaphoreType.DMA((slots,)),
    ]


def products_of(left, rights, tile):
    def compute(start, add, target):
        turned_left = jnp.transpose(left[:, start : start + 256])
        at = 0
        for right, columns in rights:
            for first in range(0, columns, tile):
                extent = slice(first, min(first + tile, columns))
                value = jnp.dot(turned_left, right[:, extent], preferred_element_type=jnp.float32)
                here = slice(at + extent.start, at + extent.stop)
                if add is not None:
                    value = value + add[:, here].astype(jnp.float32)
                target[:, here] = value.astype(jnp.bfloat16)
            at = at + columns

    return compute


def line_gather(nt, me, zed, chunks, own, everything, send, recv, chunked=False, reach=None):
    size = own.shape[0] // chunks
    reach = nt - 1 if reach is None else reach

    def own_rows(chunk):
        return own.at[pl.ds(chunk * size, size)]

    def rows(block, chunk):
        start = (chunk * nt + block) * size if chunked else block * (size * chunks) + chunk * size
        return everything.at[aligned(start, size)]

    def copy(source, block, chunk, side, away=1):
        return pltpu.make_async_remote_copy(
            src_ref=source,
            dst_ref=rows(block, chunk),
            send_sem=send.at[side + 2 * (away - 1), block, chunk],
            recv_sem=recv.at[block, chunk],
            device_id=(me, zed + away * (1 - 2 * side)),
            device_id_type=MESH,
        )

    def keep(chunk):
        return pltpu.make_async_copy(own_rows(chunk), rows(zed, chunk), recv.at[zed, chunk])

    def straight(action):
        for away in range(1, min(2, reach) + 1):
            for side in range(2):

                @pl.when(zed < nt - away if side == 0 else zed >= away)
                def _(side=side, away=away):
                    action(side, away)

    def first(chunk):
        straight(lambda side, away: copy(own_rows(chunk), zed, chunk, side, away).start())
        keep(chunk).start()

    def passed(distance, action):
        for side in range(2):
            block = zed - distance if side == 0 else zed + distance
            inside = (block >= 0) if side == 0 else (block < nt)
            open_end = (zed < nt - 1) if side == 0 else (zed > 0)

            @pl.when(jnp.logical_and(inside, open_end))
            def _(block=block, side=side):
                action(block, side)

    def onward(chunk, distance):
        for side in range(2):
            block = zed - distance if side == 0 else zed + distance

            @pl.when((block >= 0) if side == 0 else (block < nt))
            def _(block=block, side=side):
                copy(rows(block, chunk), block, chunk, side).wait_recv()

        if 2 <= distance < reach:
            passed(distance, lambda block, side: copy(rows(block, chunk), block, chunk, side).start())

    def settle(chunk):
        keep(chunk).wait()

    def end(chunk):
        straight(lambda side, away: copy(own_rows(chunk), zed, chunk, side, away).wait_send())
        for distance in range(2, reach):
            passed(distance, lambda block, side: copy(rows(block, chunk), block, chunk, side).wait_send())

    return first, onward, settle, end


def line_gather_semaphores(nt, chunks):
    return [pltpu.SemaphoreType.DMA((4, nt, chunks)), pltpu.SemaphoreType.DMA((nt, chunks))]


def line_reduce(nt, me, zed, chunks, parts, held, send, recv, chunked=False):
    block_rows = parts.shape[0] // nt
    size = block_rows // chunks
    def rows(block, chunk):
        if chunked:
            return aligned((chunk * nt + block) * size, size)
        return aligned(block * block_rows + chunk * size, size)

    def held_rows(side, block, chunk):
        return aligned((block + 1 - side) * block_rows + chunk * size, size)

    def copy(own, side, block, chunk):
        place = held_rows(side, block, chunk)
        return pltpu.make_async_remote_copy(
            src_ref=parts.at[rows(block, chunk)] if own else held.at[place],
            dst_ref=held.at[place],
            send_sem=send.at[side, block, chunk],
            recv_sem=recv.at[side, block, chunk],
            device_id=(me, zed + 1 - 2 * side),
            device_id_type=MESH,
        )

    def role(side, turn):
        away = nt - 1 - turn
        if side == 0:
            return zed + away, zed + away < nt, zed == 0
        return zed - away, zed - away >= 0, zed == nt - 1

    def pass_on(chunk, turn):
        for side in range(2):
            block, active, source = role(side, turn)

            @pl.when(jnp.logical_and(active, source))
            def _(side=side, block=block):
                copy(True, side, block, chunk).start()

            @pl.when(jnp.logical_and(active, jnp.logical_not(source)))
            def _(side=side, block=block):
                copy(False, side, block, chunk).wait_recv()
                mine, came = parts.at[rows(block, chunk)], held.at[held_rows(side, block, chunk)]

                def body(inner):
                    came[inner] = mine[inner] + came[inner]

                each_rows(size, body)
                copy(False, side, block, chunk).start()

    def own_sum(chunk, total):
        total[...] = parts[rows(zed, chunk)].astype(jnp.float32)
        for side in range(2):

            @pl.when(zed > 0 if side == 0 else zed < nt - 1)
            def _(side=side):
                copy(False, side, zed, chunk).wait_recv()
                total[...] += held[held_rows(side, zed, chunk)].astype(jnp.float32)

    def end(chunk):
        for turn in range(nt - 1):
            for side in range(2):
                block, active, source = role(side, turn)

                @pl.when(active)
                def _(side=side, block=block):
                    copy(False, side, block, chunk).wait_send()

    return pass_on, own_sum, end


def line_reduce_scratch(nt, block_rows, columns, chunks):
    return [
        pltpu.VMEM(((nt + 1) * block_rows, columns), jnp.bfloat16),
        pltpu.VMEM((block_rows // chunks, columns), jnp.float32),
        pltpu.SemaphoreType.DMA((2, nt, chunks)),
        pltpu.SemaphoreType.DMA((2, nt, chunks)),
    ]


HBM = pl.BlockSpec(memory_space=pl.ANY)
ONCHIP = pl.BlockSpec(memory_space=pltpu.VMEM)


def near_first(nt, zed, turn):
    block = 0
    for mine in range(nt):
        order = sorted(range(nt), key=lambda other: (abs(other - mine), other))
        block = block + jnp.where(zed == mine, order[turn], 0)
    return block


def first_gathers(nd, nt, rows, grad, small, main_own, out_own, shared_columns):
    chunks = LINE_CHUNKS
    bits = nd.bit_length() - 1
    blocks = relative_blocks(nd)
    block_rows, width = rows.shape
    lane = width // len(blocks)
    if lane % 128:
        rows, grad = to_relative(rows, 1, nd), to_relative(grad, 1, nd)
    main_columns, small_columns = main_own.shape[1], small.shape[1]
    side_columns = shared_columns + 2 * HEAD_SIZE
    gains_at = shared_columns + 2 * KEY_VALUE_HEADS * HEAD_SIZE
    tile = 256

    def reorder(me, source, target):
        if lane % 128:
            target[...] = source[...]
            return
        for number, (other, part) in enumerate(blocks):
            start = (mixed_with(me, other, bits) * 2 + part) * lane
            target[:, number * lane : (number + 1) * lane] = source[:, pl.ds(pl.multiple_of(start, lane), lane)]

    def kernel(
        rows_in, grad_in, small_ref, main_ref, out_ref,
        rows_ref, grad_ref, gains_ref, normed_all, grad_all, small_line, main_all, side_all, out_all, main_raw, side_raw,
        row_space, normed, main_space, small_space, side_space, main_stage, side_stage, store_sems, *refs,
    ):
        row_sems, small_sems, grad_sems = refs[:2], refs[2:4], refs[4:6]
        main_sems, small_dp, out_sems = refs[6:9], refs[9:12], refs[12:15]
        me, zed = enter(nt, bits)
        small_first, small_onward, small_settle, small_end = line_gather(
            nt, me, zed, 1, small_ref, small_line, *small_sems
        )
        row_first, row_onward, row_settle, row_end = line_gather(
            nt, me, zed, chunks, rows_ref, row_space, *row_sems
        )
        grad_first, grad_onward, grad_settle, grad_end = line_gather(
            nt, me, zed, chunks, grad_ref, grad_all, *grad_sems, chunked=True, reach=nt - 2
        )
        main_flow = gather_steps(nd, me, zed, main_ref, main_space, *main_sems)
        small_flow = gather_steps(nd, me, zed, small_line, small_space, *small_dp)
        out_flow = gather_steps(nd, me, zed, out_ref, out_all, *out_sems)
        head = zed * (QUERY_HEADS // nt) // (QUERY_HEADS // KEY_VALUE_HEADS)

        def columns(turn):
            if turn == 0:
                return small_space.at[:, pl.ds(0, shared_columns)], side_space.at[:, pl.ds(0, shared_columns)]
            start = shared_columns + ((turn - 1) * KEY_VALUE_HEADS + head) * HEAD_SIZE
            target = shared_columns + (turn - 1) * HEAD_SIZE
            return (
                small_space.at[:, pl.ds(pl.multiple_of(start, HEAD_SIZE), HEAD_SIZE)],
                side_space.at[:, pl.ds(target, HEAD_SIZE)],
            )

        def keep(number):
            source, target = ((main_space, main_all), (side_space, side_all), (normed, normed_all))[number]
            return pltpu.make_async_copy(source, target, store_sems.at[number])

        def pick(turn):
            return pltpu.make_async_copy(*columns(turn), store_sems.at[3 + turn])

        def store(turn, number):
            block = near_first(nt, zed, turn)
            stage, target = ((main_stage, main_raw), (side_stage, side_raw))[number]
            return pltpu.make_async_copy(
                stage.at[turn % 2],
                target.at[aligned(block * block_rows, block_rows)],
                store_sems.at[6 + 2 * turn + number],
            )

        def project(turn):
            where = aligned(near_first(nt, zed, turn) * block_rows, block_rows)
            value = (rows_ref[...] if turn == 0 else row_space[where]).astype(jnp.float32)
            scale = lax.rsqrt(jnp.mean(value * value, axis=-1, keepdims=True) + eps)
            mine = (value * scale * gains_ref[0:1]).astype(jnp.bfloat16)
            normed[where] = mine
            if turn >= 2:
                store(turn - 2, 0).wait()
                store(turn - 2, 1).wait()
            for space, stage, number in ((main_space, main_stage, 0), (side_space, side_stage, 1)):
                for start in range(0, space.shape[1], tile):
                    extent = slice(start, min(start + tile, space.shape[1]))
                    stage[turn % 2, :, extent] = jnp.dot(
                        mine, space[:, extent], preferred_element_type=jnp.float32
                    )
                store(turn, number).start()

        small_first(0)
        main_flow[0]()
        reorder(me, rows_in, rows_ref)
        for chunk in range(chunks):
            row_first(chunk)
        for distance in range(1, nt):
            small_onward(0, distance)
        small_settle(0)
        small_end(0)
        small_flow[0]()
        out_flow[0]()
        reorder(me, grad_in, grad_ref)
        for step in main_flow[1:-1]:
            step()
        near = [
            functools.partial(row_onward, chunk, distance) for distance in range(1, nt - 1) for chunk in range(chunks)
        ]
        together(small_flow[1:-1], near)
        for chunk in range(chunks):
            grad_first(chunk)
        small_flow[-1]()
        for turn in range(3):
            pick(turn).start()
        for start in range(0, width, 128):
            turned_block = jnp.transpose(
                small_space[start : start + 128, gains_at : gains_at + 128].astype(jnp.float32)
            )
            gains_ref[:, start : start + 128] = turned_block[:8]
        main_flow[-1]()
        keep(0).start()
        for turn in range(3):
            pick(turn).wait()
        keep(1).start()

        def last_rows():
            for chunk in range(chunks):
                row_onward(chunk, nt - 1)

        def grads_from(distance):
            for chunk in range(chunks):
                grad_onward(chunk, distance)

        compute = [functools.partial(project, turn) for turn in range(nt - 1)] + [last_rows]
        together(compute, out_flow[1:-1])
        project(nt - 1)
        keep(2).start()
        for distance in range(1, nt - 1):
            grads_from(distance)
        out_flow[-1]()
        for chunk in range(chunks):
            row_settle(chunk)
            row_end(chunk)
            grad_settle(chunk)
            grad_end(chunk)
        for turn in range(max(nt - 2, 0), nt):
            store(turn, 0).wait()
            store(turn, 1).wait()
        for number in range(3):
            keep(number).wait()

    def sized(array, times, dtype=None):
        return jax.ShapeDtypeStruct((array.shape[0] * times, array.shape[1]), dtype or array.dtype)

    tokens = block_rows * nt
    return pl.pallas_call(
        kernel,
        out_shape=[
            sized(rows, 1),
            sized(grad, 1),
            jax.ShapeDtypeStruct((8, width), jnp.float32),
            sized(rows, nt),
            sized(grad, nt),
            sized(small, nt),
            sized(main_own, nd),
            jax.ShapeDtypeStruct((width, side_columns), small.dtype),
            sized(out_own, nd),
            jax.ShapeDtypeStruct((tokens, main_columns), jnp.float32),
            jax.ShapeDtypeStruct((tokens, side_columns), jnp.float32),
        ],
        in_specs=[ONCHIP] * 2 + [HBM] * 3,
        out_specs=[ONCHIP] * 3 + [HBM] * 8,
        scratch_shapes=[
            pltpu.VMEM((tokens, width), jnp.bfloat16),
            pltpu.VMEM((tokens, width), jnp.bfloat16),
            pltpu.VMEM((width, main_columns), jnp.bfloat16),
            pltpu.VMEM((width, small_columns), jnp.bfloat16),
            pltpu.VMEM((width, side_columns), jnp.bfloat16),
            pltpu.VMEM((2, block_rows, main_columns), jnp.float32),
            pltpu.VMEM((2, block_rows, side_columns), jnp.float32),
            pltpu.SemaphoreType.DMA((6 + 2 * nt,)),
        ]
        + line_gather_semaphores(nt, chunks)
        + line_gather_semaphores(nt, 1)
        + line_gather_semaphores(nt, chunks)
        + gather_semaphores(nd) * 3,
        compiler_params=pltpu.CompilerParams(
            collective_id=0, has_side_effects=True, vmem_limit_bytes=VMEM_LIMIT
        ),
        name="first_gathers",
    )(rows, grad, small, main_own, out_own)


def middle_rows(nd, nt, mixed, out_w, resid, gain, grads, ffn_own):
    chunks = LINE_CHUNKS
    bits = nd.bit_length() - 1
    block_rows, width = resid.shape
    tokens = block_rows * nt
    size = block_rows // chunks
    ffn_columns = ffn_own.shape[1] // 3
    tile = 512

    def kernel(
        mixed_ref, out_ref, resid_ref, gain_ref, grads_ref, ffn_ref,
        middle_ref, rows_ref, hidden_ref, slopes_ref, grads_all, ffn_all,
        parts, grad_space, ffn_space, own, held, total, send, recv, gather_send, gather_recv,
        ffn_send, ffn_recv, ffn_local, store_sems, far_send, far_recv, far_space,
    ):
        me, zed = enter(nt, bits)
        load = pltpu.make_async_copy(grads_ref, grad_space, store_sems.at[0])
        load.start()
        pass_on, own_sum, reduce_end = line_reduce(nt, me, zed, chunks, parts, held, send, recv)
        first, onward, settle, gather_end = line_gather(
            nt, me, zed, chunks, own, rows_ref, gather_send, gather_recv, chunked=True
        )
        flow = gather_steps(nd, me, zed, ffn_ref, ffn_space, ffn_send, ffn_recv, ffn_local)
        keeps = [
            pltpu.make_async_copy(grad_space, grads_all, store_sems.at[1]),
            pltpu.make_async_copy(ffn_space, ffn_all, store_sems.at[2]),
        ]

        def part(turn):
            where = aligned(near_first(nt, zed, nt - 1 - turn) * block_rows, block_rows)
            left = mixed_ref[where]
            for start in range(0, width, tile):
                extent = slice(start, start + tile)
                parts[where, extent] = product(left, out_ref[extent], LAST).astype(jnp.bfloat16)

        def far(chunk, up):
            block = 0 if up else nt - 1
            return pltpu.make_async_remote_copy(
                src_ref=grad_space.at[pl.ds((chunk * nt + block) * size, size)],
                dst_ref=far_space.at[pl.ds(chunk * size, size)],
                send_sem=far_send.at[chunk],
                recv_sem=far_recv.at[chunk],
                device_id=(me, nt - 1 if up else 0),
                device_id_type=MESH,
            )

        def far_begin():
            for up, sender in ((True, nt - 2), (False, 1)):

                @pl.when(zed == sender)
                def _(up=up):
                    for chunk in range(chunks):
                        far(chunk, up).start()

        def far_end():
            for up, sender in ((True, nt - 2), (False, 1)):

                @pl.when(zed == sender)
                def _(up=up):
                    for chunk in range(chunks):
                        far(chunk, up).wait_send()

                @pl.when(zed == (nt - 1 if up else 0))
                def _(up=up):
                    for chunk in range(chunks):
                        far(chunk, up).wait_recv()
                        start = (chunk * nt + (0 if up else nt - 1)) * size
                        grad_space[pl.ds(start, size)] = far_space[pl.ds(chunk * size, size)]

        def finish(chunk):
            own_sum(chunk, total)
            where = pl.ds(chunk * size, size)
            value = resid_ref[where].astype(jnp.float32) + total[...]
            middle_ref[where] = value
            scale = lax.rsqrt(jnp.mean(value * value, axis=-1, keepdims=True) + eps)
            own[where] = (value * scale * gain_ref[...]).astype(jnp.bfloat16)
            first(chunk)

        def feed(chunk):
            settle(chunk)
            where = pl.ds(chunk * nt * size, nt * size)
            rows, grads = rows_ref[where], grad_space[where]
            for start in range(0, ffn_columns, tile):
                columns = [slice(turn * ffn_columns + start, turn * ffn_columns + start + tile) for turn in range(3)]
                gate = product(rows, ffn_space[:, columns[0]])
                upper = product(rows, ffn_space[:, columns[1]])
                grad = product(grads, ffn_space[:, columns[2]])
                sigma = jax.nn.sigmoid(gate)
                through = gate * sigma
                hidden_ref[where, columns[0]] = (through * upper).astype(jnp.bfloat16)
                slopes_ref[where, columns[0]] = (grad * upper * silu_slope(gate, sigma)).astype(jnp.bfloat16)
                slopes_ref[where, columns[1]] = (grad * through).astype(jnp.bfloat16)

        flow[0]()
        part(0)
        for chunk in range(chunks):
            pass_on(chunk, 0)
        for turn in range(1, nt):
            part(turn)
        load.wait()
        far_begin()
        ahead = [
            functools.partial(pass_on, 0, turn) for turn in range(1, nt - 1)
        ]
        steps = []

        def add(function, chunk, *rest):
            if 0 <= chunk < chunks:
                steps.append(functools.partial(function, chunk, *rest))

        for chunk in range(1, chunks + 2):
            add(finish, chunk - 1)
            add(onward, chunk - 2, nt - 1)
            for turn in range(1, nt - 1):
                add(pass_on, chunk, turn)
                add(onward, chunk - 1, turn)
            if chunk == 2:
                early = len(steps)
            add(feed, chunk - 2)
        together(ahead + steps[:early], flow[1:] + [far_end])
        for keep in keeps:
            keep.start()
        for step in steps[early:]:
            step()
        for chunk in range(chunks):
            reduce_end(chunk)
            gather_end(chunk)
        for keep in keeps:
            keep.wait()

    return pl.pallas_call(
        kernel,
        out_shape=[
            jax.ShapeDtypeStruct((block_rows, width), jnp.float32),
            jax.ShapeDtypeStruct((tokens, width), jnp.bfloat16),
            jax.ShapeDtypeStruct((tokens, ffn_columns), jnp.bfloat16),
            jax.ShapeDtypeStruct((tokens, 2 * ffn_columns), jnp.bfloat16),
            jax.ShapeDtypeStruct((tokens, width), jnp.bfloat16),
            jax.ShapeDtypeStruct((width, 3 * ffn_columns), jnp.bfloat16),
        ],
        in_specs=[ONCHIP] * 4 + [HBM] * 2,
        out_specs=[ONCHIP] * 4 + [HBM] * 2,
        scratch_shapes=[
            pltpu.VMEM((tokens, width), jnp.bfloat16),
            pltpu.VMEM((tokens, width), jnp.bfloat16),
            pltpu.VMEM((width, 3 * ffn_columns), jnp.bfloat16),
            pltpu.VMEM((block_rows, width), jnp.bfloat16),
        ]
        + line_reduce_scratch(nt, block_rows, width, chunks)
        + line_gather_semaphores(nt, chunks)
        + gather_semaphores(nd)
        + [
            pltpu.SemaphoreType.DMA((3,)),
            pltpu.SemaphoreType.DMA((chunks,)),
            pltpu.SemaphoreType.DMA((chunks,)),
            pltpu.VMEM((block_rows, width), jnp.bfloat16),
        ],
        compiler_params=pltpu.CompilerParams(
            collective_id=1, has_side_effects=True, vmem_limit_bytes=LARGE_LIMIT
        ),
        name="middle_rows",
    )(mixed, out_w, resid, gain, grads, ffn_own)


def absolute_lanes(me, bits, blocks, source, target):
    lane = source.shape[1] // len(blocks)
    for number, (other, part) in enumerate(blocks):
        start = (mixed_with(me, other, bits) * 2 + part) * lane
        target[:, pl.ds(pl.multiple_of(start, lane), lane)] = source[:, number * lane : (number + 1) * lane]


def norm_pull(value, gain, grad):
    scale = lax.rsqrt(jnp.mean(value * value, axis=-1, keepdims=True) + eps)
    scaled = grad * gain
    inner = jnp.mean(scaled * value, axis=-1, keepdims=True)
    return scale * (scaled - value * (inner * scale * scale)), grad * value * scale


def line_steps(nt, chunks, pass_on, finish, onward, settle=None):
    steps = []

    def add(function, chunk, *rest):
        if 0 <= chunk < chunks:
            steps.append(functools.partial(function, chunk, *rest))

    for chunk in range(chunks + 2):
        add(finish, chunk - 1)
        add(onward, chunk - 2, nt - 1)
        for turn in range(1, nt - 1):
            add(pass_on, chunk, turn)
            add(onward, chunk - 1, turn)
    return steps


def middle_back(nd, nt, slopes, hidden, rows, grads, ffn_w, middle, cot, gain):
    chunks = LINE_CHUNKS
    bits = nd.bit_length() - 1
    block_rows, width = middle.shape
    tokens = block_rows * nt
    size = block_rows // chunks
    blocks = relative_blocks(nd)
    lane = width // len(blocks)
    ffn_columns = hidden.shape[1]
    out_rows = width // nd
    tile = 512

    def kernel(
        slopes_in, hidden_in, rows_in, grads_in, ffn_ref, middle_ref, cot_ref, gain_ref,
        grad_ref, gain_out, rows_all, gate_total, up_total, down_total,
        slopes_ref, hidden_ref, rows_ref, grads_ref, weights, load_sems, parts, own, gain_grad,
        line_held, total, send, recv, gather_send, gather_recv, *refs,
    ):
        loads = [
            pltpu.make_async_copy(source, target, load_sems.at[number])
            for number, (source, target) in enumerate(
                (
                    (ffn_ref.at[:, pl.ds(0, 2 * ffn_columns)], weights),
                    (slopes_in, slopes_ref),
                    (rows_in, rows_ref),
                    (hidden_in, hidden_ref),
                    (grads_in, grads_ref),
                )
            )
        ]
        for load in loads:
            load.start()
        me, zed = enter(nt, bits)
        pass_on, own_sum, reduce_end = line_reduce(nt, me, zed, chunks, parts, line_held, send, recv, chunked=True)
        first, onward, settle, gather_end = line_gather(nt, me, zed, chunks, own, rows_all, gather_send, gather_recv)
        half = nd * out_rows // 2
        scatters = [
            computed_scatter(
                nd, me, zed, out_rows // 2, products_of(rows_ref, ((slopes_ref, 2 * ffn_columns),), tile),
                weights.at[pl.ds(0, half)], *refs[:2],
                ((gate_total, 0, ffn_columns), (up_total, ffn_columns, ffn_columns)), *refs[2:6],
            ),
            computed_scatter(
                nd, me, zed, out_rows // 2, products_of(grads_ref, ((hidden_ref, ffn_columns),), tile),
                weights.at[pl.ds(half, half), pl.ds(0, ffn_columns)], *refs[6:8],
                ((down_total, 0, ffn_columns),), *refs[8:12],
            ),
        ]
        gain_grad[...] = jnp.zeros_like(gain_grad)

        def part(chunk):
            where = pl.ds(chunk * nt * size, nt * size)
            left = slopes_ref[where]
            for start in range(0, width, tile):
                extent = slice(start, start + tile)
                parts[where, extent] = product(left, weights[extent], LAST).astype(jnp.bfloat16)

        def finish(chunk):
            own_sum(chunk, total)
            where = pl.ds(chunk * size, size)
            through, gained = norm_pull(middle_ref[where], gain_ref[...], total[...])
            value = cot_ref[where].astype(jnp.float32) + through
            gain_grad[...] += jnp.sum(gained, axis=0, keepdims=True)
            grad_ref[where] = value
            own[where] = value.astype(jnp.bfloat16)
            first(chunk)

        loads[0].wait()
        loads[1].wait()
        for chunk in range(chunks):
            part(chunk)
            pass_on(chunk, 0)
        for load in loads[2:]:
            load.wait()
        over = []
        for number in range(2):
            over = over + [step for pair in zip(scatters[0][number], scatters[1][number]) for step in pair]
        for number in range(len(scatters[0][2])):
            over = over + scatters[0][2][number] + scatters[1][2][number]
        together(line_steps(nt, chunks, pass_on, finish, onward), over)
        for scatter in scatters:
            scatter[3]()
        for chunk in range(chunks):
            reduce_end(chunk)
            settle(chunk)
            gather_end(chunk)
        if lane % 128:
            gain_out[...] = gain_grad[...]
        else:
            absolute_lanes(me, bits, blocks, gain_grad, gain_out)

    results = pl.pallas_call(
        kernel,
        out_shape=[
            jax.ShapeDtypeStruct((block_rows, width), jnp.float32),
            jax.ShapeDtypeStruct((1, width), jnp.float32),
            jax.ShapeDtypeStruct((tokens, width), jnp.bfloat16),
        ]
        + [jax.ShapeDtypeStruct((out_rows, ffn_columns), jnp.float32)] * 3,
        in_specs=[HBM] * 5 + [ONCHIP] * 3,
        out_specs=[ONCHIP, ONCHIP, HBM] + [ONCHIP] * 3,
        scratch_shapes=[
            pltpu.VMEM(slopes.shape, jnp.bfloat16),
            pltpu.VMEM(hidden.shape, jnp.bfloat16),
            pltpu.VMEM(rows.shape, jnp.bfloat16),
            pltpu.VMEM(grads.shape, jnp.bfloat16),
            pltpu.VMEM((width, 2 * ffn_columns), jnp.bfloat16),
            pltpu.SemaphoreType.DMA((5,)),
            pltpu.VMEM((tokens, width), jnp.bfloat16),
            pltpu.VMEM((block_rows, width), jnp.bfloat16),
            pltpu.VMEM((1, width), jnp.float32),
        ]
        + line_reduce_scratch(nt, block_rows, width, chunks)
        + line_gather_semaphores(nt, chunks)
        + computed_scratch(nd, out_rows, 2 * ffn_columns)[1:]
        + computed_scratch(nd, out_rows, ffn_columns)[1:],
        compiler_params=pltpu.CompilerParams(
            collective_id=2, has_side_effects=True, vmem_limit_bytes=LARGE_LIMIT
        ),
        name="middle_back",
    )(slopes, hidden, rows, grads, ffn_w, middle, cot, gain)
    if lane % 128:
        results = (results[0], from_relative(results[1], 1, nd), *results[2:])
    return results


def last_sums(nd, nt, normed, grad_main, grad_side, main, side, resid, before, gain, small, shared_rows, main_widths):
    chunks = LINE_CHUNKS
    bits, line_bits = nd.bit_length() - 1, nt.bit_length() - 1
    block_rows, width = resid.shape
    tokens = block_rows * nt
    size = block_rows // chunks
    blocks = relative_blocks(nd)
    lane = width // len(blocks)
    main_columns, side_columns = main.shape[1], side.shape[1]
    shared_columns = side_columns - 2 * HEAD_SIZE
    side_rows = width // nd
    owned = side_rows // nt
    common_columns = shared_columns + 2 * KEY_VALUE_HEADS * HEAD_SIZE
    count = len(main_widths)
    if lane % 128:
        gain_part = jnp.sum(
            (contract_last(grad_main, main) + contract_last(grad_side, side)) * normed.astype(jnp.float32), axis=0
        )
        own_gain = from_relative(gain_part / gain[0], 0, nd)
        small = jnp.concatenate([own_gain.reshape(-1, 128), small[width // 128 :]])

    def kernel(normed_ref, grad_main_ref, grad_side_ref, main_ref, side_ref, resid_ref, before_ref, gain_ref, small_ref, *refs):
        grad_ref, small_out, common_ref = refs[:3]
        totals, refs = refs[3 : 3 + count], refs[3 + count :]
        parts_ref, side_total, line_held, total, send, recv = refs[:6]
        sums, landed, small_send, small_recv, gain_grad = refs[6:11]
        side_out, side_in, side_send, side_recv = refs[11:15]
        stage, held, hop_landed, core_send, core_recv, hop_send, hop_recv = refs[15:]
        me, zed = enter(nt, bits)
        pass_on, own_sum, reduce_end = line_reduce(nt, me, zed, chunks, parts_ref, line_held, send, recv)
        targets, at = [], 0
        for target, columns in zip(totals, main_widths):
            targets.append((target, at, columns))
            at = at + columns
        targets.append((side_total, main_columns, side_columns))
        away, near, later, scatter_end = computed_scatter(
            nd, me, zed, side_rows // 2,
            products_of(normed_ref, ((grad_main_ref, main_columns), (grad_side_ref, side_columns)), 512),
            stage, held, hop_landed, targets, core_send, core_recv, hop_send, hop_recv,
        )

        def part(turn):
            def step():
                where = aligned(near_first(nt, zed, nt - 1 - turn) * block_rows, block_rows)
                left, right = grad_main_ref[where], grad_side_ref[where]
                for start in range(0, width, 512):
                    extent = slice(start, start + 512)
                    value = product(left, main_ref[extent], LAST) + product(right, side_ref[extent], LAST)
                    parts_ref[where, extent] = value.astype(jnp.bfloat16)

            return step

        def gain_term(number):
            def step():
                if number == 0:
                    gain_grad[...] = jnp.zeros_like(gain_grad)

                def body(inner, carry):
                    where = aligned(number * block_rows + inner * 16, 16)
                    gain_grad[...] += parts_ref[where].astype(jnp.float32) * normed_ref[where].astype(jnp.float32)
                    return carry

                lax.fori_loop(0, block_rows // 16, body, 0)

            return step

        def small_copy(turn):
            if turn < bits:
                device = (flip(me, turn), zed)
            else:
                device = (me, flip(zed, turn - bits))
            extent = slice(None) if turn < bits else pl.ds(0, shared_rows)
            return pltpu.make_async_remote_copy(
                src_ref=sums.at[turn, extent],
                dst_ref=landed.at[turn, extent],
                send_sem=small_send.at[turn],
                recv_sem=small_recv.at[turn],
                device_id=device,
                device_id_type=MESH,
            )

        def small_begin():
            sums[0] = small_ref[...]
            if lane % 128 == 0:
                whole = jnp.sum(gain_grad[...], axis=0, keepdims=True) / gain_ref[...]
                for number, (other, half) in enumerate(blocks):
                    spot = mixed_with(me, other, bits) * 2 + half
                    sums[0, pl.ds(spot, 1), :] = whole[:, number * lane : (number + 1) * lane]
            small_copy(0).start()

        def small_step(turn):
            def step():
                small_copy(turn).wait_recv()
                if turn < bits:
                    sums[turn + 1] = sums[turn] + landed[turn]
                else:
                    sums[turn + 1] = sums[turn]
                    sums[turn + 1, pl.ds(0, shared_rows)] = (
                        sums[turn, pl.ds(0, shared_rows)] + landed[turn, pl.ds(0, shared_rows)]
                    )
                if turn + 1 < bits + line_bits:
                    small_copy(turn + 1).start()

            return step

        def small_end():
            for turn in range(bits + line_bits):
                small_copy(turn).wait_send()
            small_out[...] = sums[bits + line_bits]

        few = [gain_term(number) for number in range(nt if lane % 128 == 0 else 0)]
        few = few + [small_begin] + [small_step(turn) for turn in range(bits + line_bits)]

        def side_copy(source, target):
            return pltpu.make_async_remote_copy(
                src_ref=side_out.at[pl.ds(target * owned, owned)],
                dst_ref=side_in.at[source],
                send_sem=side_send.at[target],
                recv_sem=side_recv.at[source],
                device_id=(me, target),
                device_id_type=MESH,
            )

        def side_begin():
            side_out[...] = side_total[...].astype(jnp.bfloat16)
            for target in range(nt):

                @pl.when(zed != target)
                def _(target=target):
                    side_copy(zed, target).start()

            side_in[zed] = side_out[aligned(zed * owned, owned)]

        def side_end():
            for source in range(nt):

                @pl.when(zed != source)
                def _(source=source):
                    side_copy(source, source).wait_recv()

            common_ref[...] = jnp.zeros_like(common_ref)
            for source in range(nt):
                value = side_in[source].astype(jnp.float32)
                head = source * (QUERY_HEADS // nt) // (QUERY_HEADS // KEY_VALUE_HEADS)
                common_ref[:, :shared_columns] += value[:, :shared_columns]
                for turn in range(2):
                    at = shared_columns + (turn * KEY_VALUE_HEADS + head) * HEAD_SIZE
                    start = shared_columns + turn * HEAD_SIZE
                    common_ref[:, at : at + HEAD_SIZE] += value[:, start : start + HEAD_SIZE]
            for target in range(nt):

                @pl.when(zed != target)
                def _(target=target):
                    side_copy(zed, target).wait_send()

        def finish(chunk):
            own_sum(chunk, total)
            where = pl.ds(chunk * size, size)
            through, _ = norm_pull(resid_ref[where].astype(jnp.float32), gain_ref[...], total[...])
            value = before_ref[where] + through
            if lane % 128:
                grad_ref[where] = value
                return
            for number, (other, half) in enumerate(blocks):
                start = (mixed_with(me, other, bits) * 2 + half) * lane
                grad_ref[where, pl.ds(pl.multiple_of(start, lane), lane)] = value[:, number * lane : (number + 1) * lane]

        def passes(turn):
            return [functools.partial(pass_on, chunk, turn) for chunk in range(chunks)]

        middle = len(away) // 2
        steps = away[:middle] + [part(0)] + passes(0) + away[middle:] + [part(1)] + near[:middle]
        for turn in range(2, nt):
            steps.append(part(turn))
        steps = steps + passes(1) + near[middle:]
        for stage_steps in later[:-1]:
            steps = steps + stage_steps
        for turn in range(2, nt - 1):
            steps = steps + passes(turn)
        steps = steps + few[: -(bits + line_bits)] + later[-1] + [side_begin]
        ends = [functools.partial(finish, chunk) for chunk in range(chunks)]
        rest = few[-(bits + line_bits) :]
        for step in steps:
            step()
        together(ends, rest)
        side_end()
        small_end()
        scatter_end()
        for chunk in range(chunks):
            reduce_end(chunk)

    turns = bits + line_bits
    results = pl.pallas_call(
        kernel,
        out_shape=[
            jax.ShapeDtypeStruct((block_rows, width), jnp.float32),
            jax.ShapeDtypeStruct(small.shape, jnp.float32),
            jax.ShapeDtypeStruct((owned, common_columns), jnp.float32),
        ]
        + [jax.ShapeDtypeStruct((side_rows, columns), jnp.float32) for columns in main_widths],
        in_specs=[ONCHIP] * 9,
        out_specs=[ONCHIP] * (3 + count),
        scratch_shapes=[
            pltpu.VMEM((tokens, width), jnp.bfloat16),
            pltpu.VMEM((side_rows, side_columns), jnp.float32),
        ]
        + line_reduce_scratch(nt, block_rows, width, chunks)
        + [
            pltpu.VMEM((turns + 1, *small.shape), jnp.float32),
            pltpu.VMEM((turns, *small.shape), jnp.float32),
            pltpu.SemaphoreType.DMA((turns,)),
            pltpu.SemaphoreType.DMA((turns,)),
            pltpu.VMEM((16, width), jnp.float32),
            pltpu.VMEM((side_rows, side_columns), jnp.bfloat16),
            pltpu.VMEM((nt, owned, side_columns), jnp.bfloat16),
            pltpu.SemaphoreType.DMA((nt,)),
            pltpu.SemaphoreType.DMA((nt,)),
        ]
        + computed_scratch(nd, side_rows, main_columns + side_columns),
        compiler_params=pltpu.CompilerParams(
            collective_id=3, has_side_effects=True, vmem_limit_bytes=LARGE_LIMIT
        ),
        name="last_sums",
    )(normed, grad_main, grad_side, main, side, resid, before, gain, small)
    if lane % 128:
        results = (from_relative(results[0], 1, nd), *results[1:])
    return results


def silu_slope(value, sig):
    return sig * (1.0 + value * (1.0 - sig))


def split_dot(value, constant, dims, terms):
    total = None
    for _ in range(terms):
        piece = value.astype(jnp.bfloat16)
        value = value - piece.astype(jnp.float32)
        part = lax.dot_general(*((piece, constant) if dims[0] else (constant, piece)), dims[1], preferred_element_type=jnp.float32)
        total = part if total is None else total + part
    return total


PLAIN = (((1,), (0,)), ((), ()))
LAST = (((1,), (1,)), ((), ()))
FIRST = (((0,), (0,)), ((), ()))


def product(left, right, dims=PLAIN):
    return lax.dot_general(left, right, dims, preferred_element_type=jnp.float32)


def turned(value, cosine, sine):
    return value * cosine + pltpu.roll(value, value.shape[-1] // 2, 1) * sine


class Sizes:
    def __init__(self, channels, state_columns, query_columns, heads, length):
        self.channels, self.states = channels, state_columns // 2
        self.query, self.heads, self.length = query_columns, heads, length
        self.span = SPAN
        self.count = length // SPAN
        self.wide = channels + state_columns
        self.head_width = channels // heads
        self.step_at = 2 * channels + query_columns
        self.main = self.step_at + heads + (-(self.step_at + heads)) % 128
        self.step_lanes = self.main - self.step_at
        self.side = state_columns + 2 * HEAD_SIZE
        self.window = min(length, 3 * SPAN)


def spread_heads(size):
    table = np.zeros((size.step_lanes, size.channels), np.float32)
    for head in range(size.heads):
        table[head, head * size.head_width : (head + 1) * size.head_width] = 1.0
    return table.astype(jnp.bfloat16)


def turn_tables(length):
    half = HEAD_SIZE // 2
    angle = np.arange(length, dtype=np.float64)[:, None] * rope_base ** (-np.arange(half) / half)[None]
    cosine, sine = np.cos(angle), np.sin(angle)
    return (
        np.concatenate([cosine, cosine], 1).astype(np.float32),
        np.concatenate([-sine, sine], 1).astype(np.float32),
    )


def token_flags(segments, taps):
    seg = segments[0]
    length = seg.shape[0]
    columns = [jnp.ones((length,), bool)]
    ahead = []
    for lag in range(1, taps):
        columns.append(jnp.concatenate([jnp.zeros((lag,), bool), seg[lag:] == seg[:-lag]]))
        ahead.append(jnp.concatenate([seg[lag:] == seg[:-lag], jnp.zeros((lag,), bool)]))
    ends = seg.reshape(-1, SPAN)[:, -1]
    before = jnp.concatenate([jnp.full((1,), -1, seg.dtype), ends[:-1]])
    columns.append(seg == jnp.repeat(before, SPAN))
    columns.append(seg == jnp.repeat(ends, SPAN))
    columns = columns + ahead
    return jnp.pad(jnp.stack(columns, 1).astype(jnp.float32), ((0, 0), (0, 16 - len(columns))))


def chunk_values(size, taps, main_ref, wide_ref, flags, spread, taps_ref, heads_ref, segc, segr):
    span = size.span
    pre = wide_ref[pl.ds(8, span), :] * taps_ref[0:1, :]
    for lag in range(1, taps):
        pre = pre + wide_ref[pl.ds(8 - lag, span), :] * (flags[:, lag : lag + 1] * taps_ref[lag : lag + 1, :])
    sig = jax.nn.sigmoid(pre)
    act = pre * sig
    inner = act[:, : size.channels]
    bmat = act[:, size.channels : size.channels + size.states].astype(jnp.bfloat16)
    cmat = act[:, size.channels + size.states :].astype(jnp.bfloat16)
    step_in = main_ref[:, size.step_at :] + heads_ref[0:1, :]
    step = jnp.maximum(step_in, 0.0) + jnp.log1p(jnp.exp(-jnp.abs(step_in)))
    logdec = -step * heads_ref[1:2, :]
    rows = lax.broadcasted_iota(jnp.int32, (span, span), 0)
    columns = lax.broadcasted_iota(jnp.int32, (span, span), 1)
    later = jnp.where(rows >= columns, 1.0, 0.0).astype(jnp.bfloat16)
    cumul = split_dot(logdec, later, (False, PLAIN), 3)
    inside = jnp.logical_and(rows >= columns, segc == segr)
    ending = cumul[span - 1 : span, :]
    reach = jnp.exp(cumul) * flags[:, 4:5]
    tail = jnp.exp(ending - cumul) * flags[:, 5:6]
    step_wide = split_dot(step, spread, (True, PLAIN), 2)
    scaled = inner * step_wide
    return dict(
        pre=pre, sig=sig, inner=inner, bmat=bmat, cmat=cmat, step_in=step_in, step=step, logdec=logdec, later=later,
        cumul=cumul, turned=jnp.transpose(cumul), inside=inside, step_wide=step_wide, scaled=scaled,
        scaled_b=scaled.astype(jnp.bfloat16), meeting=product(cmat, bmat, LAST),
        reach_wide=split_dot(reach, spread, (True, PLAIN), 2), tail_wide=split_dot(tail, spread, (True, PLAIN), 2),
        skip_wide=split_dot(jnp.broadcast_to(heads_ref[2:3, :], (8, size.step_lanes)), spread, (True, PLAIN), 2)[0:1],
    )


def decay_of(values, head):
    spread = values["cumul"][:, head : head + 1] - values["turned"][head : head + 1, :]
    return jnp.exp(jnp.where(values["inside"], spread, -1e30))


def softmax_of(size, query, keys, chunk, start, segc, seg_all):
    scores = product(query, keys, LAST) * (1.0 / math.sqrt(HEAD_SIZE))
    rows = lax.broadcasted_iota(jnp.int32, scores.shape, 0) + chunk * size.span
    columns = lax.broadcasted_iota(jnp.int32, scores.shape, 1) + start
    allowed = jnp.logical_and(rows >= columns, segc == seg_all)
    masked = jnp.where(allowed, scores, -1e30)
    expo = jnp.exp(masked - jnp.max(masked, axis=-1, keepdims=True))
    return expo / jnp.sum(expo, axis=-1, keepdims=True)


def mixers_forward(size, taps, main_raw, side_raw, segments, flags, tap_rows, head_rows):
    span = size.span
    per_head = size.head_width

    def kernel(
        main_ref, side_ref, segc_ref, segr_ref, flags_ref, taps_ref, heads_ref, cos_ref, sin_ref, spread_ref,
        mixed_ref, y_ref, state_ref, keys_ref, values_ref, wide, state,
    ):
        chunk = pl.program_id(0)

        @pl.when(chunk == 0)
        def _():
            wide[0:8, :] = jnp.zeros((8, size.wide), jnp.float32)
            state[...] = jnp.zeros_like(state)
            keys_ref[...] = jnp.zeros_like(keys_ref)
            values_ref[...] = jnp.zeros_like(values_ref)

        wide[pl.ds(8, span), : size.channels] = main_ref[:, size.channels : 2 * size.channels]
        wide[pl.ds(8, span), size.channels :] = side_ref[:, : 2 * size.states]
        flags, spread, segc = flags_ref[...], spread_ref[...], segc_ref[...]
        segr = segr_ref[:, pl.ds(pl.multiple_of(chunk * span, span), span)]
        val = chunk_values(size, taps, main_ref, wide, flags, spread, taps_ref, heads_ref, segc, segr)
        wide[0:8, :] = wide[pl.ds(span, 8), :]
        held = state[...]
        held_b = held.astype(jnp.bfloat16)
        state_ref[...] = held
        across = val["reach_wide"] * product(val["cmat"], held_b)
        lane = lax.broadcasted_iota(jnp.int32, (span, 2 * per_head), 1)
        for pair in range(size.heads // 2):
            where = slice(pair * 2 * per_head, (pair + 1) * 2 * per_head)
            both = []
            for head in (2 * pair, 2 * pair + 1):
                weights = (val["meeting"] * decay_of(val, head)).astype(jnp.bfloat16)
                both.append(product(weights, val["scaled_b"][:, where]))
            result = jnp.where(lane < per_head, both[0], both[1])
            result = result + across[:, where] + val["skip_wide"][:, where] * val["inner"][:, where]
            y_ref[:, where] = result
            gate = main_ref[:, where]
            mixed_ref[:, where] = (result * (gate * jax.nn.sigmoid(gate))).astype(jnp.bfloat16)
        keep = jnp.broadcast_to(val["reach_wide"][span - 1 : span, :], (1, size.channels))
        state[...] = keep * held + product(
            val["bmat"], (val["tail_wide"] * val["scaled"]).astype(jnp.bfloat16), FIRST
        )

        cosine, sine = cos_ref[...], sin_ref[...]
        own = pl.ds(pl.multiple_of(chunk * span, span), span)
        key_at = 2 * size.states
        keys_ref[own, :] = turned(side_ref[:, key_at : key_at + HEAD_SIZE], cosine, sine).astype(jnp.bfloat16)
        values_ref[own, :] = side_ref[:, key_at + HEAD_SIZE :].astype(jnp.bfloat16)
        start = pl.multiple_of(jnp.maximum(chunk + 1 - size.window // span, 0) * span, span)
        seen = pl.ds(start, size.window)
        for head in range(size.query // HEAD_SIZE):
            at = 2 * size.channels + head * HEAD_SIZE
            query = turned(main_ref[:, at : at + HEAD_SIZE], cosine, sine).astype(jnp.bfloat16)
            probs = softmax_of(size, query, keys_ref[seen, :], chunk, start, segc, segr_ref[:, seen])
            result = product(probs.astype(jnp.bfloat16), values_ref[seen, :])
            at = size.channels + head * HEAD_SIZE
            mixed_ref[:, at : at + HEAD_SIZE] = result.astype(jnp.bfloat16)

    def rows(columns):
        return pl.BlockSpec((span, columns), lambda i: (i, 0))

    def whole(array):
        return pl.BlockSpec(array.shape, lambda i: (0, 0))

    cosine, sine = turn_tables(size.length)
    spread = spread_heads(size)
    tokens = size.length
    return pl.pallas_call(
        kernel,
        grid=(size.count,),
        in_specs=[
            rows(size.main), rows(size.side), rows(1), whole(segments), rows(16), whole(tap_rows), whole(head_rows),
            rows(HEAD_SIZE), rows(HEAD_SIZE), whole(spread),
        ],
        out_specs=[
            rows(size.channels + size.query), rows(size.channels),
            pl.BlockSpec((size.states, size.channels), lambda i: (i, 0)),
            pl.BlockSpec((tokens, HEAD_SIZE), lambda i: (0, 0)), pl.BlockSpec((tokens, HEAD_SIZE), lambda i: (0, 0)),
        ],
        out_shape=[
            jax.ShapeDtypeStruct((tokens, size.channels + size.query), jnp.bfloat16),
            jax.ShapeDtypeStruct((tokens, size.channels), jnp.float32),
            jax.ShapeDtypeStruct((size.count * size.states, size.channels), jnp.float32),
            jax.ShapeDtypeStruct((tokens, HEAD_SIZE), jnp.bfloat16),
            jax.ShapeDtypeStruct((tokens, HEAD_SIZE), jnp.bfloat16),
        ],
        scratch_shapes=[
            pltpu.VMEM((span + 8, size.wide), jnp.float32),
            pltpu.VMEM((size.states, size.channels), jnp.float32),
        ],
        compiler_params=pltpu.CompilerParams(
            dimension_semantics=("arbitrary",), vmem_limit_bytes=VMEM_LIMIT
        ),
        name="mixers_forward",
    )(main_raw, side_raw, segments.reshape(tokens, 1), segments, flags, tap_rows, head_rows,
      jnp.asarray(cosine), jnp.asarray(sine), jnp.asarray(spread))


def mixers_backward(
    nd, nt, size, taps, grad_mixed, main_raw, side_raw, segments, flags, tap_rows, head_rows, y_value, states, keys, values,
    grad_rows, mixed,
):
    bits = nd.bit_length() - 1
    out_rows, out_columns = grad_rows.shape[1] // nd, mixed.shape[1]
    span = size.span
    per_head = size.head_width
    count = size.count

    def kernel(
        grad_ref, main_ref, side_ref, before_ref, side_before_ref, segc_ref, segr_ref, flags_ref, taps_ref, heads_ref,
        cos_ref, sin_ref, spread_ref, y_ref, state_ref, keys_ref, values_ref, rows_ref, mixed_ref,
        grad_main, grad_side, tap_sums, head_sums, mixer_total, attn_total,
        wide, back, grad_state, grad_keys, grad_values,
        stage, held, landed, core_send, core_recv, hop_send, hop_recv,
    ):
        turn = pl.program_id(0)
        chunk = count - 1 - turn
        me, zed = lax.axis_index("dp"), lax.axis_index("tensor")
        away, near, later, scatter_end = computed_scatter(
            nd, me, zed, out_rows // 2, products_of(rows_ref, ((mixed_ref, out_columns),), 512), stage, held, landed,
            ((mixer_total, 0, size.channels), (attn_total, size.channels, size.query)),
            core_send, core_recv, hop_send, hop_recv,
        )
        stages = [away, near, *later[: count - 3], [step for stage_steps in later[count - 3 :] for step in stage_steps]]
        for number, stage_steps in enumerate(stages):

            @pl.when(turn == number)
            def _(number=number, stage_steps=stage_steps):
                if number == 0:
                    enter(nt, bits)
                for step in stage_steps:
                    step()
                if number == len(stages) - 1:
                    scatter_end()

        @pl.when(turn == 0)
        def _():
            back[pl.ds(span, 8), :] = jnp.zeros((8, size.wide), jnp.float32)
            grad_state[...] = jnp.zeros_like(grad_state)
            grad_keys[...] = jnp.zeros_like(grad_keys)
            grad_values[...] = jnp.zeros_like(grad_values)
            tap_sums[...] = jnp.zeros_like(tap_sums)
            head_sums[...] = jnp.zeros_like(head_sums)

        wide[0:8, : size.channels] = before_ref[...]
        wide[0:8, size.channels :] = side_before_ref[...]
        wide[pl.ds(8, span), : size.channels] = main_ref[:, size.channels : 2 * size.channels]
        wide[pl.ds(8, span), size.channels :] = side_ref[:, : 2 * size.states]
        flags, spread, segc = flags_ref[...], spread_ref[...], segc_ref[...]
        segr = segr_ref[:, pl.ds(pl.multiple_of(chunk * span, span), span)]
        val = chunk_values(size, taps, main_ref, wide, flags, spread, taps_ref, heads_ref, segc, segr)
        inner, scaled = val["inner"], val["scaled"]

        gate = main_ref[:, : size.channels]
        gate_sig = jax.nn.sigmoid(gate)
        grad = grad_ref[:, : size.channels]
        grad_main[:, : size.channels] = (grad * y_ref[...] * silu_slope(gate, gate_sig)).astype(jnp.bfloat16)
        grad_y = grad * (gate * gate_sig)
        grad_y_b = grad_y.astype(jnp.bfloat16)
        tap_sums[4:5, : size.channels] += jnp.sum(grad_y * inner, axis=0, keepdims=True)

        lane = lax.broadcasted_iota(jnp.int32, (span, 2 * per_head), 1)
        head_lane = lax.broadcasted_iota(jnp.int32, (span, size.step_lanes), 1)
        head_row = lax.broadcasted_iota(jnp.int32, (size.step_lanes, span), 0)
        grad_meeting = jnp.zeros((span, span), jnp.float32)
        by_row = jnp.zeros((span, size.step_lanes), jnp.float32)
        by_column = jnp.zeros((size.step_lanes, span), jnp.float32)
        pieces = []
        for pair in range(size.heads // 2):
            where = slice(pair * 2 * per_head, (pair + 1) * 2 * per_head)
            both = []
            for side in range(2):
                head = 2 * pair + side
                decay = decay_of(val, head)
                weights = val["meeting"] * decay
                mine = (lane < per_head) if side == 0 else (lane >= per_head)
                grad_own = jnp.where(mine, grad_y_b[:, where], jnp.zeros((), jnp.bfloat16))
                grad_weights = product(grad_own, val["scaled_b"][:, where], LAST)
                both.append(product(weights.astype(jnp.bfloat16), grad_y_b[:, where], FIRST))
                grad_meeting = grad_meeting + grad_weights * decay
                moved = grad_weights * weights
                by_row = jnp.where(head_lane == head, jnp.sum(moved, axis=1, keepdims=True), by_row)
                by_column = jnp.where(head_row == head, jnp.sum(moved, axis=0, keepdims=True), by_column)
            pieces.append(jnp.where(lane < per_head, both[0], both[1]))
        grad_scaled = jnp.concatenate(pieces, axis=1)
        grad_cumul = by_row - jnp.transpose(by_column)

        held = state_ref[...]
        held_b = held.astype(jnp.bfloat16)
        grad_held = grad_state[...]
        grad_held_b = grad_held.astype(jnp.bfloat16)
        grad_meeting_b = grad_meeting.astype(jnp.bfloat16)
        reached = val["reach_wide"] * grad_y
        reached_b = reached.astype(jnp.bfloat16)
        grad_cumul = grad_cumul + split_dot(reached * product(val["cmat"], held_b), spread, (True, LAST), 2)
        grad_c = product(reached_b, held_b, LAST) + product(grad_meeting_b, val["bmat"])
        from_state = val["tail_wide"] * product(val["bmat"], grad_held_b)
        grad_b = product(grad_meeting_b, val["cmat"], FIRST) + product(
            (val["tail_wide"] * scaled).astype(jnp.bfloat16), grad_held_b, LAST
        )
        grad_scaled = grad_scaled + from_state
        ended = split_dot(scaled * from_state, spread, (True, LAST), 2)
        keep = val["reach_wide"][span - 1 : span, :]
        kept = jnp.sum(grad_held * held, axis=0, keepdims=True) * keep
        kept = split_dot(jnp.broadcast_to(kept, (8, size.channels)), spread, (True, LAST), 2)[0:1]
        at_end = jnp.sum(ended, axis=0, keepdims=True) + kept
        grad_logdec = split_dot(grad_cumul - ended, val["later"], (False, FIRST), 3) + at_end
        grad_state[...] = keep * grad_held + product(val["cmat"], reached_b, FIRST)

        grad_inner = grad_scaled * val["step_wide"] + grad_y * val["skip_wide"]
        grad_step = split_dot(grad_scaled * inner, spread, (True, LAST), 2) - grad_logdec * heads_ref[1:2, :]
        grad_step_raw = grad_step * jax.nn.sigmoid(val["step_in"])
        head_sums[0:1, :] += jnp.sum(grad_step_raw, axis=0, keepdims=True)
        head_sums[1:2, :] += jnp.sum(grad_logdec * val["logdec"], axis=0, keepdims=True)
        grad_main[:, size.step_at :] = grad_step_raw.astype(jnp.bfloat16)

        slope = silu_slope(val["pre"], val["sig"])
        grad_pre = jnp.concatenate([grad_inner, grad_b, grad_c], axis=1) * slope
        back[pl.ds(0, span), :] = grad_pre
        raw = grad_pre * taps_ref[0:1, :]
        tap_sums[0:1, :] += jnp.sum(grad_pre * wide[pl.ds(8, span), :], axis=0, keepdims=True)
        for lag in range(1, taps):
            tap_sums[lag : lag + 1, :] += jnp.sum(
                grad_pre * (wide[pl.ds(8 - lag, span), :] * flags[:, lag : lag + 1]), axis=0, keepdims=True
            )
            raw = raw + back[pl.ds(lag, span), :] * (flags[:, 5 + lag : 6 + lag] * taps_ref[lag : lag + 1, :])
        back[pl.ds(span, 8), :] = back[0:8, :]
        grad_main[:, size.channels : 2 * size.channels] = raw[:, : size.channels].astype(jnp.bfloat16)
        grad_side[:, : 2 * size.states] = raw[:, size.channels :].astype(jnp.bfloat16)

        cosine, sine = cos_ref[...], sin_ref[...]
        start = pl.multiple_of(jnp.maximum(chunk + 1 - size.window // span, 0) * span, span)
        seen = pl.ds(start, size.window)
        seen_keys, seen_values = keys_ref[seen, :], values_ref[seen, :]
        scale = 1.0 / math.sqrt(HEAD_SIZE)
        for head in range(size.query // HEAD_SIZE):
            at = 2 * size.channels + head * HEAD_SIZE
            query = turned(main_ref[:, at : at + HEAD_SIZE], cosine, sine).astype(jnp.bfloat16)
            probs = softmax_of(size, query, seen_keys, chunk, start, segc, segr_ref[:, seen])
            out_at = size.channels + head * HEAD_SIZE
            grad_out = grad_ref[:, out_at : out_at + HEAD_SIZE].astype(jnp.bfloat16)
            grad_probs = product(grad_out, seen_values, LAST)
            delta = jnp.sum(grad_probs * probs, axis=-1, keepdims=True)
            grad_scores = (probs * (grad_probs - delta)).astype(jnp.bfloat16)
            grad_query = product(grad_scores, seen_keys) * scale
            grad_main[:, at : at + HEAD_SIZE] = turned(grad_query, cosine, -sine).astype(jnp.bfloat16)
            grad_keys[seen, :] += product(grad_scores, query, FIRST) * scale
            grad_values[seen, :] += product(probs.astype(jnp.bfloat16), grad_out, FIRST)
        own = pl.ds(pl.multiple_of(chunk * span, span), span)
        key_at = 2 * size.states
        grad_side[:, key_at : key_at + HEAD_SIZE] = turned(grad_keys[own, :], cosine, -sine).astype(jnp.bfloat16)
        grad_side[:, key_at + HEAD_SIZE :] = grad_values[own, :].astype(jnp.bfloat16)

    def rows(columns):
        return pl.BlockSpec((span, columns), lambda i: (count - 1 - i, 0))

    def previous(columns, column):
        return pl.BlockSpec((8, columns), lambda i: (jnp.maximum((count - 1 - i) * (span // 8) - 1, 0), column))

    def whole(array):
        return pl.BlockSpec(array.shape, lambda i: (0, 0))

    cosine, sine = turn_tables(size.length)
    spread = spread_heads(size)
    tokens = size.length
    return pl.pallas_call(
        kernel,
        grid=(count,),
        in_specs=[
            rows(size.channels + size.query), rows(size.main), rows(size.side), previous(size.channels, 1),
            previous(2 * size.states, 0), rows(1), whole(segments), rows(16), whole(tap_rows), whole(head_rows),
            rows(HEAD_SIZE), rows(HEAD_SIZE), whole(spread), rows(size.channels),
            pl.BlockSpec((size.states, size.channels), lambda i: (count - 1 - i, 0)), whole(keys), whole(values),
            whole(grad_rows), whole(mixed),
        ],
        out_specs=[
            rows(size.main), rows(size.side), pl.BlockSpec((8, size.wide), lambda i: (0, 0)),
            pl.BlockSpec((8, size.step_lanes), lambda i: (0, 0)),
            pl.BlockSpec((out_rows, size.channels), lambda i: (0, 0)),
            pl.BlockSpec((out_rows, size.query), lambda i: (0, 0)),
        ],
        out_shape=[
            jax.ShapeDtypeStruct((tokens, size.main), jnp.bfloat16),
            jax.ShapeDtypeStruct((tokens, size.side), jnp.bfloat16),
            jax.ShapeDtypeStruct((8, size.wide), jnp.float32),
            jax.ShapeDtypeStruct((8, size.step_lanes), jnp.float32),
            jax.ShapeDtypeStruct((out_rows, size.channels), jnp.float32),
            jax.ShapeDtypeStruct((out_rows, size.query), jnp.float32),
        ],
        scratch_shapes=[
            pltpu.VMEM((span + 8, size.wide), jnp.float32),
            pltpu.VMEM((span + 8, size.wide), jnp.float32),
            pltpu.VMEM((size.states, size.channels), jnp.float32),
            pltpu.VMEM((tokens, HEAD_SIZE), jnp.float32),
            pltpu.VMEM((tokens, HEAD_SIZE), jnp.float32),
        ]
        + computed_scratch(nd, out_rows, out_columns),
        compiler_params=pltpu.CompilerParams(
            dimension_semantics=("arbitrary",), vmem_limit_bytes=VMEM_LIMIT, collective_id=4, has_side_effects=True
        ),
        cost_estimate=pl.CostEstimate(flops=40 * 10**9, bytes_accessed=60 * 10**6, transcendentals=10**7),
        name="mixers_backward",
    )(grad_mixed, main_raw, side_raw, main_raw, side_raw, segments.reshape(tokens, 1), segments, flags, tap_rows,
      head_rows, jnp.asarray(cosine), jnp.asarray(sine), jnp.asarray(spread), y_value, states, keys, values, grad_rows, mixed)


def per_device(
    nd,
    nt,
    residual,
    segments,
    mixgain,
    ffngain,
    gateproj,
    innerproj,
    stepproj,
    sharedproj,
    innerconv,
    sharedconv,
    stepbias,
    decaylog,
    skipgain,
    mixerout,
    queryproj,
    keyvalue,
    attnout,
    ffngate,
    upproj,
    downproj,
    cotangent,
):
    bfloat = jnp.bfloat16
    single = jnp.float32
    width = residual.shape[1]
    zed = lax.axis_index("tensor")
    seq_count, length = segments.shape
    token_count = seq_count * length
    channels = innerproj.shape[1]
    state_columns = sharedproj.shape[1]
    heads = stepproj.shape[1]
    query_columns = queryproj.shape[1]
    ffn_columns = ffngate.shape[1]
    small_rows = sharedproj.shape[0]
    conv_rows = sharedconv.shape[0]
    taps = sharedconv.shape[1]

    gains = jnp.concatenate(
        [
            mixgain[:, None],
            ffngain[:, None],
            jnp.pad(sharedconv, ((0, small_rows - conv_rows), (0, 0))),
            jnp.zeros((small_rows, 128 - 2 - taps), bfloat),
        ],
        axis=1,
    )
    main_used = 2 * channels + query_columns + heads
    main_own = jnp.concatenate(
        [
            gateproj,
            innerproj,
            queryproj,
            stepproj,
            jnp.zeros((gateproj.shape[0], -main_used % 128), bfloat),
        ],
        axis=1,
    )
    resid_own, cot_own, gain_rows, normed, grad_rows, _, main, side, out_w, main_raw, side_raw = first_gathers(
        nd,
        nt,
        residual,
        cotangent,
        jnp.concatenate([sharedproj, keyvalue, gains], axis=1),
        main_own,
        jnp.concatenate([mixerout, attnout], axis=1),
        state_columns,
    )
    gain_one, gain_two = gain_rows[0], gain_rows[1]
    conv_shared = from_relative(gain_rows[2 : 2 + taps], 1, nd)
    conv_shared = conv_shared.reshape(taps, nd * nt, small_rows)[:, :, :conv_rows].reshape(taps, -1)

    size = Sizes(channels, state_columns, query_columns, heads, length)
    flags = token_flags(segments, taps)
    tap_rows = jnp.concatenate([innerconv.astype(single).T, conv_shared], axis=1)
    tap_rows = jnp.pad(tap_rows, ((0, 8 - taps), (0, 0)))
    head_rows = jnp.stack([stepbias.astype(single), jnp.exp(decaylog.astype(single)), skipgain.astype(single)])
    head_rows = jnp.pad(head_rows, ((0, 5), (0, size.step_lanes - heads)))
    mixed_in, y_value, states, keys, values = mixers_forward(
        size, taps, main_raw, side_raw, segments, flags, tap_rows, head_rows
    )
    middle, rows_two, hidden, grad_gate_up, grad_rows, ffn_w = middle_rows(
        nd,
        nt,
        mixed_in,
        out_w,
        resid_own,
        gain_two[None],
        grad_rows,
        jnp.concatenate([ffngate, upproj, downproj], axis=1),
    )
    down_w = ffn_w[:, 2 * ffn_columns :]
    grad_middle, grad_gain_two, grad_mix_rows, gate_g, up_g, down_g = middle_back(
        nd, nt, grad_gate_up, hidden, rows_two, grad_rows, ffn_w, middle, cot_own, gain_two[None]
    )
    ffn_part = contract_last(hidden, down_w).astype(bfloat)
    ffn_part = ffn_part.reshape(-1, nt, middle.shape[0] // LINE_CHUNKS, width).swapaxes(0, 1).reshape(token_count, width)
    ffn_part = after(ffn_part, grad_mix_rows)
    ffn_out = lax.psum_scatter(ffn_part, "tensor", scatter_dimension=0, tiled=True)
    layer_out = from_relative(middle + ffn_out.astype(single), 1, nd)
    grad_mixed_in = matrix_product(grad_mix_rows, out_w)
    grad_main, grad_side, tap_sums, head_sums, mixer_g, attn_g = mixers_backward(
        nd, nt, size, taps, grad_mixed_in, main_raw, side_raw, segments, flags, tap_rows, head_rows, y_value, states,
        keys, values, grad_mix_rows, mixed_in,
    )
    small = jnp.concatenate(
        [
            jnp.zeros((width,), single),
            grad_gain_two[0],
            tap_sums[:taps, channels:].reshape(-1),
            tap_sums[:taps, :channels].reshape(-1),
            tap_sums[4, :channels],
            head_sums[:2].reshape(-1),
        ]
    )
    shared_length = 2 * width + taps * state_columns
    small = jnp.pad(small, (0, -small.shape[0] % 1024)).reshape(-1, 128)
    grad_residual, small, common_g, gateproj_g, inner_g, query_g, step_g = last_sums(
        nd,
        nt,
        normed,
        grad_main,
        grad_side,
        main,
        side,
        resid_own,
        grad_middle,
        gain_one[None],
        small,
        shared_length // 128,
        (channels, channels, query_columns, heads),
    )
    small = small.reshape(-1)
    place = lax.axis_index("dp") * nt + zed
    gain_one_g = lax.dynamic_slice_in_dim(small, place * small_rows, small_rows, 0)
    gain_two_g = lax.dynamic_slice_in_dim(small, width + place * small_rows, small_rows, 0)
    conv_g = lax.dynamic_slice_in_dim(
        small[2 * width : shared_length].reshape(taps, -1), place * conv_rows, conv_rows, 1
    ).T
    local = small[shared_length:]
    skip_at = taps * channels
    head_at = skip_at + channels
    return (
        layer_out,
        grad_residual,
        gain_one_g,
        gain_two_g,
        gateproj_g,
        inner_g,
        step_g,
        common_g[:, :state_columns],
        local[:skip_at].reshape(taps, channels).T,
        conv_g,
        local[head_at : head_at + heads],
        local[head_at + size.step_lanes : head_at + size.step_lanes + heads],
        local[skip_at:head_at].reshape(heads, -1).sum(axis=1),
        mixer_g,
        query_g,
        common_g[:, state_columns:],
        attn_g,
        gate_g,
        up_g,
        down_g,
    )


def solution(mesh):
    return jax.shard_map(
        functools.partial(per_device, mesh.shape["dp"], mesh.shape["tensor"]),
        mesh=mesh,
        in_specs=(
            P(("dp", "tensor"), None),
            P("dp", None),
            P(("dp", "tensor")),
            P(("dp", "tensor")),
            P("dp", "tensor"),
            P("dp", "tensor"),
            P("dp", "tensor"),
            P(("dp", "tensor"), None),
            P("tensor", None),
            P(("dp", "tensor"), None),
            P("tensor"),
            P("tensor"),
            P("tensor"),
            P("dp", "tensor"),
            P("dp", "tensor"),
            P(("dp", "tensor"), None),
            P("dp", "tensor"),
            P("dp", "tensor"),
            P("dp", "tensor"),
            P("dp", "tensor"),
            P(("dp", "tensor"), None),
        ),
        out_specs=(
            P(("dp", "tensor"), None),
            P(("dp", "tensor"), None),
            P(("dp", "tensor")),
            P(("dp", "tensor")),
            P("dp", "tensor"),
            P("dp", "tensor"),
            P("dp", "tensor"),
            P(("dp", "tensor"), None),
            P("tensor", None),
            P(("dp", "tensor"), None),
            P("tensor"),
            P("tensor"),
            P("tensor"),
            P("dp", "tensor"),
            P("dp", "tensor"),
            P(("dp", "tensor"), None),
            P("dp", "tensor"),
            P("dp", "tensor"),
            P("dp", "tensor"),
            P("dp", "tensor"),
        ),
        check_vma=False,
    )
```

```python
import functools
import math

import jax
import jax.numpy as jnp
import numpy as np
from jax import lax
from jax.experimental import pallas as pl
from jax.experimental.pallas import tpu as pltpu
from jax.sharding import PartitionSpec as P

QUERY_HEADS = 8
KEY_VALUE_HEADS = 2
HEAD_SIZE = 128
SPAN = 256


eps = 1e-05
rope_base = 10000.0


def matrix_product(left, right):
    return jnp.dot(left, right, preferred_element_type=jnp.float32)


def contract_leading_axis(left, right):
    return lax.dot_general(
        left, right, (((0,), (0,)), ((), ())), preferred_element_type=jnp.float32
    )


def contract_last(left, right):
    return lax.dot_general(
        left, right, (((1,), (1,)), ((), ())), preferred_element_type=jnp.float32
    )


def bit_orders(size):
    high = list(range(size.bit_length() - 2, 0, -1))
    return high, high[:2][::-1] + high[2:]


def relative_blocks(size):
    both = []
    for half, order in enumerate(bit_orders(size)):
        chain = [0]
        for bit in order:
            chain = chain + [other ^ (1 << bit) for other in chain]
        both = both + [(other, half) for other in chain]
    return both + [(other ^ 1, half) for other, half in both]


def to_relative(value, axis, size):
    me = lax.axis_index("dp")
    width = value.shape[axis] // (2 * size)
    return jnp.concatenate(
        [
            lax.dynamic_slice_in_dim(value, ((me ^ other) * 2 + half) * width, width, axis)
            for other, half in relative_blocks(size)
        ],
        axis,
    )


def from_relative(value, axis, size):
    me = lax.axis_index("dp")
    width = value.shape[axis] // (2 * size)
    blocks = relative_blocks(size)
    place = jnp.asarray([blocks.index((other, half)) for other in range(size) for half in range(2)], jnp.int32)
    return jnp.concatenate(
        [
            lax.dynamic_slice_in_dim(value, place[(me ^ number) * 2 + half] * width, width, axis)
            for number in range(size)
            for half in range(2)
        ],
        axis,
    )


def after(value, *others):
    return lax.optimization_barrier((value,) + others)[0]


MESH = pl.DeviceIdType.MESH
VMEM_LIMIT = 56 * 1024 * 1024
LINE_CHUNKS = 4
LARGE_LIMIT = 62 * 1024 * 1024


def flip(value, bit):
    unit = 1 << bit
    return value + unit * (1 - 2 * ((value // unit) % 2))


def mixed_with(value, other, bits):
    for bit in range(bits):
        if (other >> bit) & 1:
            value = flip(value, bit)
    return value


def enter(nt, bits):
    me, zed = lax.axis_index("dp"), lax.axis_index("tensor")
    barrier = pltpu.get_barrier_semaphore()
    for other in range(nt):

        @pl.when(zed != other)
        def _(other=other):
            pl.semaphore_signal(barrier, inc=1, device_id=(me, other), device_id_type=MESH)

    for bit in range(bits):
        pl.semaphore_signal(barrier, inc=1, device_id=(flip(me, bit), zed), device_id_type=MESH)
    pl.semaphore_wait(barrier, bits + nt - 1)
    return me, zed


def aligned(start, size):
    return pl.ds(pl.multiple_of(start, 16), size)


def together(*flows):
    flows = [list(flow) for flow in flows]
    order = sorted(
        ((place + 0.5) / len(flow), number, place)
        for number, flow in enumerate(flows)
        for place in range(len(flow))
    )
    for _, number, place in order:
        flows[number][place]()


def gather_steps(nd, me, zed, own, everything, send, recv, local):
    half = own.shape[0] // 2
    blocks = relative_blocks(nd)
    place = {block: number for number, block in enumerate(blocks)}

    def rows(block):
        return everything.at[pl.ds(place[block] * half, half)]

    def source(block):
        return own.at[pl.ds(block[1] * half, half)] if block[0] == 0 else rows(block)

    hops = []
    for part, order in enumerate(bit_orders(nd)):
        chain = [0]
        for bit in order:
            hops = hops + [((other, part), bit) for other in chain]
            chain = chain + [other ^ (1 << bit) for other in chain]
    hops = hops + [(block, 0) for block in blocks[:nd]]

    def copy(number):
        block, bit = hops[number]
        landed = (block[0] ^ (1 << bit), block[1])
        return pltpu.make_async_remote_copy(
            src_ref=source(block),
            dst_ref=rows(landed),
            send_sem=send.at[number],
            recv_sem=recv.at[place[landed]],
            device_id=(flip(me, bit), zed),
            device_id_type=MESH,
        )

    def arrival(block):
        return pltpu.make_async_remote_copy(
            src_ref=rows(block),
            dst_ref=rows(block),
            send_sem=send.at[0],
            recv_sem=recv.at[place[block]],
            device_id=(flip(me, 0), zed),
            device_id_type=MESH,
        )

    def begin():
        for number, (block, bit) in enumerate(hops):
            if block[0] == 0:
                copy(number).start()
        for part in range(2):
            pltpu.make_async_copy(source((0, part)), rows((0, part)), local.at[part]).start()

    def forward(block):
        def step():
            arrival(block).wait_recv()
            for number, (origin, bit) in enumerate(hops):
                if origin == block:
                    copy(number).start()

        return step

    def end():
        for block in blocks[nd:]:
            arrival(block).wait_recv()
        for number in range(len(hops)):
            copy(number).wait_send()
        for part in range(2):
            pltpu.make_async_copy(source((0, part)), rows((0, part)), local.at[part]).wait()

    first, second = blocks[1 : nd // 2], blocks[nd // 2 + 1 : nd]
    middle = [forward(block) for pair in zip(first, second) for block in pair]
    return [begin] + middle + [end]


def gather_hops(nd):
    return 2 * (nd // 2 - 1) + nd


def gather_semaphores(nd):
    return [
        pltpu.SemaphoreType.DMA((gather_hops(nd),)),
        pltpu.SemaphoreType.DMA((2 * nd,)),
        pltpu.SemaphoreType.DMA((2,)),
    ]


def each_rows(rows, body, unit=16):
    def step(number, carry):
        body(aligned(number * unit, unit))
        return carry

    lax.fori_loop(0, rows // unit, step, 0)


def computed_scatter(nd, me, zed, half, compute, stage, held, landed, totals, core_send, core_recv, send, recv):
    chain_length = nd // 2
    block = 256
    pieces = block // half
    per_part = chain_length // pieces
    turns = [part * per_part + spot for spot in range(per_part - 1, -1, -1) for part in range(2)]

    def piece(ref, number):
        return ref.at[pl.ds(number * half, half)]

    def block_of(ref, number):
        return ref.at[pl.ds(number * block, block)]

    rounds, slot = [], 0
    for part, order in enumerate(bit_orders(nd)):
        length, own_rounds = chain_length, []
        for bit in order[::-1]:
            length = length // 2
            own_rounds.append((bit, length, slot))
            slot = slot + length
        rounds.append(own_rounds)

    def core_copy(number):
        return pltpu.make_async_remote_copy(
            src_ref=block_of(stage, number),
            dst_ref=block_of(held, number),
            send_sem=core_send.at[number],
            recv_sem=core_recv.at[number],
            device_id=(flip(me, 0), zed),
            device_id_type=MESH,
        )

    def hop(bit, number, where):
        return pltpu.make_async_remote_copy(
            src_ref=piece(held, number),
            dst_ref=piece(landed, where),
            send_sem=send.at[where],
            recv_sem=recv.at[where],
            device_id=(flip(me, bit), zed),
            device_id_type=MESH,
        )

    def away(number):
        def step():
            compute(nd * half + number * block, None, block_of(stage, number))
            core_copy(number).start()

        return step

    def near(number):
        def step():
            core_copy(number).wait_recv()
            compute(number * block, block_of(held, number), block_of(held, number))
            for inner in range(pieces):
                place = number * pieces + inner
                part, spot = place // chain_length, place % chain_length
                bit, length, first = rounds[part][0]
                if spot >= length:
                    hop(bit, place, first + spot - length).start()

        return step

    def later_sum(part, turn, spot):
        bit, length, first = rounds[part][turn]
        number = part * chain_length + spot

        def step():
            hop(bit, number, first + spot).wait_recv()
            last = turn == len(rounds[part]) - 1

            def body(rows):
                kept, came = piece(held, number)[rows], piece(landed, first + spot)[rows]
                if last:
                    value = kept.astype(jnp.float32) + came.astype(jnp.float32)
                    for target, start, columns in totals:
                        piece(target, part)[rows] = value[:, start : start + columns]
                else:
                    piece(held, number)[rows] = kept + came

            each_rows(half, body)
            if not last:
                next_bit, next_length, next_first = rounds[part][turn + 1]
                if spot >= next_length:
                    hop(next_bit, number, next_first + spot - next_length).start()

        return step

    def end():
        for number in range(len(turns)):
            core_copy(number).wait_send()
        for part in range(2):
            for bit, length, first in rounds[part]:
                for spot in range(length):
                    hop(bit, part * chain_length + length + spot, first + spot).wait_send()

    later = []
    for turn in range(len(rounds[0])):
        length = rounds[0][turn][1]
        later.append([later_sum(part, turn, spot) for spot in range(length - 1, -1, -1) for part in range(2)])
    return [away(number) for number in turns], [near(number) for number in turns], later, end


def computed_scratch(nd, rows, columns):
    slots = nd - 2
    blocks = nd * rows // 2 // 256
    return [
        pltpu.VMEM((nd * rows // 2, columns), jnp.bfloat16),
        pltpu.VMEM((nd * rows // 2, columns), jnp.bfloat16),
        pltpu.VMEM((slots * rows // 2, columns), jnp.bfloat16),
        pltpu.SemaphoreType.DMA((blocks,)),
        pltpu.SemaphoreType.DMA((blocks,)),
        pltpu.SemaphoreType.DMA((slots,)),
        pltpu.SemaphoreType.DMA((slots,)),
    ]


def products_of(left, rights, tile):
    def compute(start, add, target):
        turned_left = jnp.transpose(left[:, start : start + 256])
        at = 0
        for right, columns in rights:
            for first in range(0, columns, tile):
                extent = slice(first, min(first + tile, columns))
                value = jnp.dot(turned_left, right[:, extent], preferred_element_type=jnp.float32)
                here = slice(at + extent.start, at + extent.stop)
                if add is not None:
                    value = value + add[:, here].astype(jnp.float32)
                target[:, here] = value.astype(jnp.bfloat16)
            at = at + columns

    return compute


def line_gather(nt, me, zed, chunks, own, everything, send, recv, chunked=False, reach=None):
    size = own.shape[0] // chunks
    reach = nt - 1 if reach is None else reach

    def own_rows(chunk):
        return own.at[pl.ds(chunk * size, size)]

    def rows(block, chunk):
        start = (chunk * nt + block) * size if chunked else block * (size * chunks) + chunk * size
        return everything.at[aligned(start, size)]

    def copy(source, block, chunk, side):
        return pltpu.make_async_remote_copy(
            src_ref=source,
            dst_ref=rows(block, chunk),
            send_sem=send.at[side, block, chunk],
            recv_sem=recv.at[block, chunk],
            device_id=(me, zed + 1 - 2 * side),
            device_id_type=MESH,
        )

    def keep(chunk):
        return pltpu.make_async_copy(own_rows(chunk), rows(zed, chunk), recv.at[zed, chunk])

    def first(chunk):
        for side, condition in ((0, zed < nt - 1), (1, zed > 0)):

            @pl.when(condition)
            def _(side=side):
                copy(own_rows(chunk), zed, chunk, side).start()

        keep(chunk).start()

    def onward(chunk, distance):
        for side, block in ((0, zed - distance), (1, zed + distance)):
            inside = (block >= 0) if side == 0 else (block < nt)
            open_end = (zed < nt - 1) if side == 0 else (zed > 0)

            @pl.when(inside)
            def _(block=block, side=side):
                copy(rows(block, chunk), block, chunk, side).wait_recv()

            if distance < reach:

                @pl.when(jnp.logical_and(inside, open_end))
                def _(block=block, side=side):
                    copy(rows(block, chunk), block, chunk, side).start()

    def settle(chunk):
        keep(chunk).wait()

    def end(chunk):
        for side, condition in ((0, zed < nt - 1), (1, zed > 0)):

            @pl.when(condition)
            def _(side=side):
                copy(own_rows(chunk), zed, chunk, side).wait_send()

            for distance in range(1, reach):
                block = zed - distance if side == 0 else zed + distance
                inside = (block >= 0) if side == 0 else (block < nt)

                @pl.when(jnp.logical_and(inside, condition))
                def _(block=block, side=side):
                    copy(rows(block, chunk), block, chunk, side).wait_send()

    return first, onward, settle, end


def line_gather_semaphores(nt, chunks):
    return [pltpu.SemaphoreType.DMA((2, nt, chunks)), pltpu.SemaphoreType.DMA((nt, chunks))]


def line_reduce(nt, me, zed, chunks, parts, held, send, recv, chunked=False):
    block_rows = parts.shape[0] // nt
    size = block_rows // chunks
    def rows(block, chunk):
        if chunked:
            return aligned((chunk * nt + block) * size, size)
        return aligned(block * block_rows + chunk * size, size)

    def held_rows(side, block, chunk):
        return aligned((block + 1 - side) * block_rows + chunk * size, size)

    def copy(own, side, block, chunk):
        place = held_rows(side, block, chunk)
        return pltpu.make_async_remote_copy(
            src_ref=parts.at[rows(block, chunk)] if own else held.at[place],
            dst_ref=held.at[place],
            send_sem=send.at[side, block, chunk],
            recv_sem=recv.at[side, block, chunk],
            device_id=(me, zed + 1 - 2 * side),
            device_id_type=MESH,
        )

    def role(side, turn):
        away = nt - 1 - turn
        if side == 0:
            return zed + away, zed + away < nt, zed == 0
        return zed - away, zed - away >= 0, zed == nt - 1

    def pass_on(chunk, turn):
        for side in range(2):
            block, active, source = role(side, turn)

            @pl.when(jnp.logical_and(active, source))
            def _(side=side, block=block):
                copy(True, side, block, chunk).start()

            @pl.when(jnp.logical_and(active, jnp.logical_not(source)))
            def _(side=side, block=block):
                copy(False, side, block, chunk).wait_recv()
                mine, came = parts.at[rows(block, chunk)], held.at[held_rows(side, block, chunk)]

                def body(inner):
                    came[inner] = mine[inner] + came[inner]

                each_rows(size, body)
                copy(False, side, block, chunk).start()

    def own_sum(chunk, total):
        total[...] = parts[rows(zed, chunk)].astype(jnp.float32)
        for side in range(2):

            @pl.when(zed > 0 if side == 0 else zed < nt - 1)
            def _(side=side):
                copy(False, side, zed, chunk).wait_recv()
                total[...] += held[held_rows(side, zed, chunk)].astype(jnp.float32)

    def end(chunk):
        for turn in range(nt - 1):
            for side in range(2):
                block, active, source = role(side, turn)

                @pl.when(active)
                def _(side=side, block=block):
                    copy(False, side, block, chunk).wait_send()

    return pass_on, own_sum, end


def line_reduce_scratch(nt, block_rows, columns, chunks):
    return [
        pltpu.VMEM(((nt + 1) * block_rows, columns), jnp.bfloat16),
        pltpu.VMEM((block_rows // chunks, columns), jnp.float32),
        pltpu.SemaphoreType.DMA((2, nt, chunks)),
        pltpu.SemaphoreType.DMA((2, nt, chunks)),
    ]


HBM = pl.BlockSpec(memory_space=pl.ANY)
ONCHIP = pl.BlockSpec(memory_space=pltpu.VMEM)


def near_first(nt, zed, turn):
    block = 0
    for mine in range(nt):
        order = sorted(range(nt), key=lambda other: (abs(other - mine), other))
        block = block + jnp.where(zed == mine, order[turn], 0)
    return block


def first_gathers(nd, nt, rows, grad, small, main_own, out_own, shared_columns):
    chunks = LINE_CHUNKS
    bits = nd.bit_length() - 1
    blocks = relative_blocks(nd)
    block_rows, width = rows.shape
    lane = width // len(blocks)
    if lane % 128:
        rows, grad = to_relative(rows, 1, nd), to_relative(grad, 1, nd)
    main_columns, small_columns = main_own.shape[1], small.shape[1]
    side_columns = shared_columns + 2 * HEAD_SIZE
    gains_at = shared_columns + 2 * KEY_VALUE_HEADS * HEAD_SIZE
    tile = 256

    def reorder(me, source, target):
        if lane % 128:
            target[...] = source[...]
            return
        for number, (other, part) in enumerate(blocks):
            start = (mixed_with(me, other, bits) * 2 + part) * lane
            target[:, number * lane : (number + 1) * lane] = source[:, pl.ds(pl.multiple_of(start, lane), lane)]

    def kernel(
        rows_in, grad_in, small_ref, main_ref, out_ref,
        rows_ref, grad_ref, gains_ref, normed_all, grad_all, small_line, main_all, side_all, out_all, main_raw, side_raw,
        row_space, normed, main_space, small_space, side_space, main_stage, side_stage, store_sems, *refs,
    ):
        row_sems, small_sems, grad_sems = refs[:2], refs[2:4], refs[4:6]
        main_sems, small_dp, out_sems = refs[6:9], refs[9:12], refs[12:15]
        me, zed = enter(nt, bits)
        small_first, small_onward, small_settle, small_end = line_gather(
            nt, me, zed, 1, small_ref, small_line, *small_sems
        )
        row_first, row_onward, row_settle, row_end = line_gather(
            nt, me, zed, chunks, rows_ref, row_space, *row_sems
        )
        grad_first, grad_onward, grad_settle, grad_end = line_gather(
            nt, me, zed, chunks, grad_ref, grad_all, *grad_sems, chunked=True, reach=1
        )
        main_flow = gather_steps(nd, me, zed, main_ref, main_space, *main_sems)
        small_flow = gather_steps(nd, me, zed, small_line, small_space, *small_dp)
        out_flow = gather_steps(nd, me, zed, out_ref, out_all, *out_sems)
        head = zed * (QUERY_HEADS // nt) // (QUERY_HEADS // KEY_VALUE_HEADS)

        def columns(turn):
            if turn == 0:
                return small_space.at[:, pl.ds(0, shared_columns)], side_space.at[:, pl.ds(0, shared_columns)]
            start = shared_columns + ((turn - 1) * KEY_VALUE_HEADS + head) * HEAD_SIZE
            target = shared_columns + (turn - 1) * HEAD_SIZE
            return (
                small_space.at[:, pl.ds(pl.multiple_of(start, HEAD_SIZE), HEAD_SIZE)],
                side_space.at[:, pl.ds(target, HEAD_SIZE)],
            )

        def keep(number):
            source, target = ((main_space, main_all), (side_space, side_all), (normed, normed_all))[number]
            return pltpu.make_async_copy(source, target, store_sems.at[number])

        def pick(turn):
            return pltpu.make_async_copy(*columns(turn), store_sems.at[3 + turn])

        def store(turn, number):
            block = near_first(nt, zed, turn)
            stage, target = ((main_stage, main_raw), (side_stage, side_raw))[number]
            return pltpu.make_async_copy(
                stage.at[turn % 2],
                target.at[aligned(block * block_rows, block_rows)],
                store_sems.at[6 + 2 * turn + number],
            )

        def project(turn):
            where = aligned(near_first(nt, zed, turn) * block_rows, block_rows)
            value = (rows_ref[...] if turn == 0 else row_space[where]).astype(jnp.float32)
            scale = lax.rsqrt(jnp.mean(value * value, axis=-1, keepdims=True) + eps)
            mine = (value * scale * gains_ref[0:1]).astype(jnp.bfloat16)
            normed[where] = mine
            if turn >= 2:
                store(turn - 2, 0).wait()
                store(turn - 2, 1).wait()
            for space, stage, number in ((main_space, main_stage, 0), (side_space, side_stage, 1)):
                for start in range(0, space.shape[1], tile):
                    extent = slice(start, min(start + tile, space.shape[1]))
                    stage[turn % 2, :, extent] = jnp.dot(
                        mine, space[:, extent], preferred_element_type=jnp.float32
                    )
                store(turn, number).start()

        small_first(0)
        main_flow[0]()
        reorder(me, rows_in, rows_ref)
        for chunk in range(chunks):
            row_first(chunk)
        for distance in range(1, nt):
            small_onward(0, distance)
        small_settle(0)
        small_end(0)
        small_flow[0]()
        out_flow[0]()
        reorder(me, grad_in, grad_ref)
        near = [
            functools.partial(row_onward, chunk, distance) for distance in range(1, nt - 1) for chunk in range(chunks)
        ]
        together(near, main_flow[1:-1] + small_flow[1:-1])
        for chunk in range(chunks):
            grad_first(chunk)
        small_flow[-1]()
        for turn in range(3):
            pick(turn).start()
        for start in range(0, width, 128):
            turned_block = jnp.transpose(
                small_space[start : start + 128, gains_at : gains_at + 128].astype(jnp.float32)
            )
            gains_ref[:, start : start + 128] = turned_block[:8]
        main_flow[-1]()
        keep(0).start()
        for turn in range(3):
            pick(turn).wait()
        keep(1).start()

        def last_rows():
            for chunk in range(chunks):
                row_onward(chunk, nt - 1)

        def grads_from(distance):
            for chunk in range(chunks):
                grad_onward(chunk, distance)

        compute = [functools.partial(project, turn) for turn in range(nt - 1)] + [last_rows]
        together(compute, out_flow[1:-1])
        project(nt - 1)
        keep(2).start()
        grads_from(1)
        out_flow[-1]()
        for chunk in range(chunks):
            row_settle(chunk)
            row_end(chunk)
            grad_settle(chunk)
            grad_end(chunk)
        for turn in range(max(nt - 2, 0), nt):
            store(turn, 0).wait()
            store(turn, 1).wait()
        for number in range(3):
            keep(number).wait()

    def sized(array, times, dtype=None):
        return jax.ShapeDtypeStruct((array.shape[0] * times, array.shape[1]), dtype or array.dtype)

    tokens = block_rows * nt
    return pl.pallas_call(
        kernel,
        out_shape=[
            sized(rows, 1),
            sized(grad, 1),
            jax.ShapeDtypeStruct((8, width), jnp.float32),
            sized(rows, nt),
            sized(grad, nt),
            sized(small, nt),
            sized(main_own, nd),
            jax.ShapeDtypeStruct((width, side_columns), small.dtype),
            sized(out_own, nd),
            jax.ShapeDtypeStruct((tokens, main_columns), jnp.float32),
            jax.ShapeDtypeStruct((tokens, side_columns), jnp.float32),
        ],
        in_specs=[ONCHIP] * 2 + [HBM] * 3,
        out_specs=[ONCHIP] * 3 + [HBM] * 8,
        scratch_shapes=[
            pltpu.VMEM((tokens, width), jnp.bfloat16),
            pltpu.VMEM((tokens, width), jnp.bfloat16),
            pltpu.VMEM((width, main_columns), jnp.bfloat16),
            pltpu.VMEM((width, small_columns), jnp.bfloat16),
            pltpu.VMEM((width, side_columns), jnp.bfloat16),
            pltpu.VMEM((2, block_rows, main_columns), jnp.float32),
            pltpu.VMEM((2, block_rows, side_columns), jnp.float32),
            pltpu.SemaphoreType.DMA((6 + 2 * nt,)),
        ]
        + line_gather_semaphores(nt, chunks)
        + line_gather_semaphores(nt, 1)
        + line_gather_semaphores(nt, chunks)
        + gather_semaphores(nd) * 3,
        compiler_params=pltpu.CompilerParams(
            collective_id=0, has_side_effects=True, vmem_limit_bytes=VMEM_LIMIT
        ),
        name="first_gathers",
    )(rows, grad, small, main_own, out_own)


def second_neighbours(nt, grads):
    zed = lax.axis_index("tensor")
    width = grads.shape[1]
    blocks = grads.reshape(LINE_CHUNKS, nt, -1, width)
    below = lax.dynamic_slice_in_dim(blocks, jnp.maximum(zed - 1, 0), 1, 1).reshape(-1, width)
    above = lax.dynamic_slice_in_dim(blocks, jnp.minimum(zed + 1, nt - 1), 1, 1).reshape(-1, width)
    return (
        lax.ppermute(below, "tensor", [(i, i + 1) for i in range(1, nt - 1)]),
        lax.ppermute(above, "tensor", [(i, i - 1) for i in range(1, nt - 1)]),
    )


def middle_rows(nd, nt, mixed, out_w, resid, gain, grads, grads_below, grads_above, ffn_own):
    chunks = LINE_CHUNKS
    bits = nd.bit_length() - 1
    block_rows, width = resid.shape
    tokens = block_rows * nt
    size = block_rows // chunks
    ffn_columns = ffn_own.shape[1] // 3
    tile = 512

    def kernel(
        mixed_ref, out_ref, resid_ref, gain_ref, grads_ref, below_ref, above_ref, ffn_ref,
        middle_ref, rows_ref, hidden_ref, slopes_ref, grads_all, ffn_all,
        parts, grad_space, ffn_space, own, held, total, send, recv, gather_send, gather_recv,
        ffn_send, ffn_recv, ffn_local, store_sems, far_send, far_recv, far_space, second_sems,
    ):
        me, zed = enter(nt, bits)
        load = pltpu.make_async_copy(grads_ref, grad_space, store_sems.at[0])
        load.start()
        pass_on, own_sum, reduce_end = line_reduce(nt, me, zed, chunks, parts, held, send, recv)
        first, onward, settle, gather_end = line_gather(
            nt, me, zed, chunks, own, rows_ref, gather_send, gather_recv, chunked=True
        )
        flow = gather_steps(nd, me, zed, ffn_ref, ffn_space, ffn_send, ffn_recv, ffn_local)
        keeps = [
            pltpu.make_async_copy(grad_space, grads_all, store_sems.at[1]),
            pltpu.make_async_copy(ffn_space, ffn_all, store_sems.at[2]),
        ]

        def part(turn):
            where = aligned(near_first(nt, zed, nt - 1 - turn) * block_rows, block_rows)
            left = mixed_ref[where]
            for start in range(0, width, tile):
                extent = slice(start, start + tile)
                parts[where, extent] = product(left, out_ref[extent], LAST).astype(jnp.bfloat16)

        def second(action):
            for side, source in ((0, below_ref), (1, above_ref)):

                @pl.when(zed >= 2 if side == 0 else zed < nt - 2)
                def _(side=side, source=source):
                    block = zed - 2 if side == 0 else zed + 2
                    for chunk in range(chunks):
                        place = aligned((chunk * nt + block) * size, size)
                        action(
                            pltpu.make_async_copy(
                                source.at[pl.ds(chunk * size, size)], grad_space.at[place], second_sems.at[side, chunk]
                            )
                        )

        def far(chunk, up):
            block = 0 if up else nt - 1
            return pltpu.make_async_remote_copy(
                src_ref=grad_space.at[pl.ds((chunk * nt + block) * size, size)],
                dst_ref=far_space.at[pl.ds(chunk * size, size)],
                send_sem=far_send.at[chunk],
                recv_sem=far_recv.at[chunk],
                device_id=(me, nt - 1 if up else 0),
                device_id_type=MESH,
            )

        def far_begin():
            for up, sender in ((True, nt - 2), (False, 1)):

                @pl.when(zed == sender)
                def _(up=up):
                    for chunk in range(chunks):
                        far(chunk, up).start()

        def far_end():
            for up, sender in ((True, nt - 2), (False, 1)):

                @pl.when(zed == sender)
                def _(up=up):
                    for chunk in range(chunks):
                        far(chunk, up).wait_send()

                @pl.when(zed == (nt - 1 if up else 0))
                def _(up=up):
                    for chunk in range(chunks):
                        far(chunk, up).wait_recv()
                        start = (chunk * nt + (0 if up else nt - 1)) * size
                        grad_space[pl.ds(start, size)] = far_space[pl.ds(chunk * size, size)]

        def finish(chunk):
            own_sum(chunk, total)
            where = pl.ds(chunk * size, size)
            value = resid_ref[where].astype(jnp.float32) + total[...]
            middle_ref[where] = value
            scale = lax.rsqrt(jnp.mean(value * value, axis=-1, keepdims=True) + eps)
            own[where] = (value * scale * gain_ref[...]).astype(jnp.bfloat16)
            first(chunk)

        def feed(chunk):
            settle(chunk)
            where = pl.ds(chunk * nt * size, nt * size)
            rows, grads = rows_ref[where], grad_space[where]
            for start in range(0, ffn_columns, tile):
                columns = [slice(turn * ffn_columns + start, turn * ffn_columns + start + tile) for turn in range(3)]
                gate = product(rows, ffn_space[:, columns[0]])
                upper = product(rows, ffn_space[:, columns[1]])
                grad = product(grads, ffn_space[:, columns[2]])
                sigma = jax.nn.sigmoid(gate)
                through = gate * sigma
                hidden_ref[where, columns[0]] = (through * upper).astype(jnp.bfloat16)
                slopes_ref[where, columns[0]] = (grad * upper * silu_slope(gate, sigma)).astype(jnp.bfloat16)
                slopes_ref[where, columns[1]] = (grad * through).astype(jnp.bfloat16)

        flow[0]()
        part(0)
        for chunk in range(chunks):
            pass_on(chunk, 0)
        load.wait()
        second(lambda copy: copy.start())
        for turn in range(1, nt):
            part(turn)
        second(lambda copy: copy.wait())
        far_begin()
        ahead = [
            functools.partial(pass_on, 0, turn) for turn in range(1, nt - 1)
        ]
        steps = []

        def add(function, chunk, *rest):
            if 0 <= chunk < chunks:
                steps.append(functools.partial(function, chunk, *rest))

        for chunk in range(1, chunks + 2):
            add(finish, chunk - 1)
            add(onward, chunk - 2, nt - 1)
            for turn in range(1, nt - 1):
                add(pass_on, chunk, turn)
                add(onward, chunk - 1, turn)
            if chunk == 2:
                early = len(steps)
            add(feed, chunk - 2)
        together(ahead + steps[:early], flow[1:] + [far_end])
        for keep in keeps:
            keep.start()
        for step in steps[early:]:
            step()
        for chunk in range(chunks):
            reduce_end(chunk)
            gather_end(chunk)
        for keep in keeps:
            keep.wait()

    return pl.pallas_call(
        kernel,
        out_shape=[
            jax.ShapeDtypeStruct((block_rows, width), jnp.float32),
            jax.ShapeDtypeStruct((tokens, width), jnp.bfloat16),
            jax.ShapeDtypeStruct((tokens, ffn_columns), jnp.bfloat16),
            jax.ShapeDtypeStruct((tokens, 2 * ffn_columns), jnp.bfloat16),
            jax.ShapeDtypeStruct((tokens, width), jnp.bfloat16),
            jax.ShapeDtypeStruct((width, 3 * ffn_columns), jnp.bfloat16),
        ],
        in_specs=[ONCHIP] * 4 + [HBM] * 4,
        out_specs=[ONCHIP] * 4 + [HBM] * 2,
        scratch_shapes=[
            pltpu.VMEM((tokens, width), jnp.bfloat16),
            pltpu.VMEM((tokens, width), jnp.bfloat16),
            pltpu.VMEM((width, 3 * ffn_columns), jnp.bfloat16),
            pltpu.VMEM((block_rows, width), jnp.bfloat16),
        ]
        + line_reduce_scratch(nt, block_rows, width, chunks)
        + line_gather_semaphores(nt, chunks)
        + gather_semaphores(nd)
        + [
            pltpu.SemaphoreType.DMA((3,)),
            pltpu.SemaphoreType.DMA((chunks,)),
            pltpu.SemaphoreType.DMA((chunks,)),
            pltpu.VMEM((block_rows, width), jnp.bfloat16),
            pltpu.SemaphoreType.DMA((2, chunks)),
        ],
        compiler_params=pltpu.CompilerParams(
            collective_id=1, has_side_effects=True, vmem_limit_bytes=LARGE_LIMIT
        ),
        name="middle_rows",
    )(mixed, out_w, resid, gain, grads, grads_below, grads_above, ffn_own)


def absolute_lanes(me, bits, blocks, source, target):
    lane = source.shape[1] // len(blocks)
    for number, (other, part) in enumerate(blocks):
        start = (mixed_with(me, other, bits) * 2 + part) * lane
        target[:, pl.ds(pl.multiple_of(start, lane), lane)] = source[:, number * lane : (number + 1) * lane]


def norm_pull(value, gain, grad):
    scale = lax.rsqrt(jnp.mean(value * value, axis=-1, keepdims=True) + eps)
    scaled = grad * gain
    inner = jnp.mean(scaled * value, axis=-1, keepdims=True)
    return scale * (scaled - value * (inner * scale * scale)), grad * value * scale


def line_steps(nt, chunks, pass_on, finish, onward, settle=None):
    steps = []

    def add(function, chunk, *rest):
        if 0 <= chunk < chunks:
            steps.append(functools.partial(function, chunk, *rest))

    for chunk in range(chunks + 2):
        add(finish, chunk - 1)
        add(onward, chunk - 2, nt - 1)
        for turn in range(1, nt - 1):
            add(pass_on, chunk, turn)
            add(onward, chunk - 1, turn)
    return steps


def middle_back(nd, nt, slopes, hidden, rows, grads, ffn_w, middle, cot, gain):
    chunks = LINE_CHUNKS
    bits = nd.bit_length() - 1
    block_rows, width = middle.shape
    tokens = block_rows * nt
    size = block_rows // chunks
    blocks = relative_blocks(nd)
    lane = width // len(blocks)
    ffn_columns = hidden.shape[1]
    out_rows = width // nd
    tile = 512

    def kernel(
        slopes_in, hidden_in, rows_in, grads_in, ffn_ref, middle_ref, cot_ref, gain_ref,
        grad_ref, gain_out, rows_all, gate_total, up_total, down_total,
        slopes_ref, hidden_ref, rows_ref, grads_ref, weights, load_sems, parts, own, gain_grad,
        line_held, total, send, recv, gather_send, gather_recv, *refs,
    ):
        loads = [
            pltpu.make_async_copy(source, target, load_sems.at[number])
            for number, (source, target) in enumerate(
                (
                    (ffn_ref.at[:, pl.ds(0, 2 * ffn_columns)], weights),
                    (slopes_in, slopes_ref),
                    (rows_in, rows_ref),
                    (hidden_in, hidden_ref),
                    (grads_in, grads_ref),
                )
            )
        ]
        for load in loads:
            load.start()
        me, zed = enter(nt, bits)
        pass_on, own_sum, reduce_end = line_reduce(nt, me, zed, chunks, parts, line_held, send, recv, chunked=True)
        first, onward, settle, gather_end = line_gather(nt, me, zed, chunks, own, rows_all, gather_send, gather_recv)
        half = nd * out_rows // 2
        scatters = [
            computed_scatter(
                nd, me, zed, out_rows // 2, products_of(rows_ref, ((slopes_ref, 2 * ffn_columns),), tile),
                weights.at[pl.ds(0, half)], *refs[:2],
                ((gate_total, 0, ffn_columns), (up_total, ffn_columns, ffn_columns)), *refs[2:6],
            ),
            computed_scatter(
                nd, me, zed, out_rows // 2, products_of(grads_ref, ((hidden_ref, ffn_columns),), tile),
                weights.at[pl.ds(half, half), pl.ds(0, ffn_columns)], *refs[6:8],
                ((down_total, 0, ffn_columns),), *refs[8:12],
            ),
        ]
        gain_grad[...] = jnp.zeros_like(gain_grad)

        def part(chunk):
            where = pl.ds(chunk * nt * size, nt * size)
            left = slopes_ref[where]
            for start in range(0, width, tile):
                extent = slice(start, start + tile)
                parts[where, extent] = product(left, weights[extent], LAST).astype(jnp.bfloat16)

        def finish(chunk):
            own_sum(chunk, total)
            where = pl.ds(chunk * size, size)
            through, gained = norm_pull(middle_ref[where], gain_ref[...], total[...])
            value = cot_ref[where].astype(jnp.float32) + through
            gain_grad[...] += jnp.sum(gained, axis=0, keepdims=True)
            grad_ref[where] = value
            own[where] = value.astype(jnp.bfloat16)
            first(chunk)

        loads[0].wait()
        loads[1].wait()
        for chunk in range(chunks):
            part(chunk)
            pass_on(chunk, 0)
        for load in loads[2:]:
            load.wait()
        over = []
        for number in range(2):
            over = over + [step for pair in zip(scatters[0][number], scatters[1][number]) for step in pair]
        for number in range(len(scatters[0][2])):
            over = over + scatters[0][2][number] + scatters[1][2][number]
        together(line_steps(nt, chunks, pass_on, finish, onward), over)
        for scatter in scatters:
            scatter[3]()
        for chunk in range(chunks):
            reduce_end(chunk)
            settle(chunk)
            gather_end(chunk)
        if lane % 128:
            gain_out[...] = gain_grad[...]
        else:
            absolute_lanes(me, bits, blocks, gain_grad, gain_out)

    results = pl.pallas_call(
        kernel,
        out_shape=[
            jax.ShapeDtypeStruct((block_rows, width), jnp.float32),
            jax.ShapeDtypeStruct((1, width), jnp.float32),
            jax.ShapeDtypeStruct((tokens, width), jnp.bfloat16),
        ]
        + [jax.ShapeDtypeStruct((out_rows, ffn_columns), jnp.float32)] * 3,
        in_specs=[HBM] * 5 + [ONCHIP] * 3,
        out_specs=[ONCHIP, ONCHIP, HBM] + [ONCHIP] * 3,
        scratch_shapes=[
            pltpu.VMEM(slopes.shape, jnp.bfloat16),
            pltpu.VMEM(hidden.shape, jnp.bfloat16),
            pltpu.VMEM(rows.shape, jnp.bfloat16),
            pltpu.VMEM(grads.shape, jnp.bfloat16),
            pltpu.VMEM((width, 2 * ffn_columns), jnp.bfloat16),
            pltpu.SemaphoreType.DMA((5,)),
            pltpu.VMEM((tokens, width), jnp.bfloat16),
            pltpu.VMEM((block_rows, width), jnp.bfloat16),
            pltpu.VMEM((1, width), jnp.float32),
        ]
        + line_reduce_scratch(nt, block_rows, width, chunks)
        + line_gather_semaphores(nt, chunks)
        + computed_scratch(nd, out_rows, 2 * ffn_columns)[1:]
        + computed_scratch(nd, out_rows, ffn_columns)[1:],
        compiler_params=pltpu.CompilerParams(
            collective_id=2, has_side_effects=True, vmem_limit_bytes=LARGE_LIMIT
        ),
        name="middle_back",
    )(slopes, hidden, rows, grads, ffn_w, middle, cot, gain)
    if lane % 128:
        results = (results[0], from_relative(results[1], 1, nd), *results[2:])
    return results


def last_sums(nd, nt, normed, grad_main, grad_side, main, side, resid, before, gain, small, shared_rows, main_widths):
    chunks = LINE_CHUNKS
    bits, line_bits = nd.bit_length() - 1, nt.bit_length() - 1
    block_rows, width = resid.shape
    tokens = block_rows * nt
    size = block_rows // chunks
    blocks = relative_blocks(nd)
    lane = width // len(blocks)
    main_columns, side_columns = main.shape[1], side.shape[1]
    shared_columns = side_columns - 2 * HEAD_SIZE
    side_rows = width // nd
    owned = side_rows // nt
    common_columns = shared_columns + 2 * KEY_VALUE_HEADS * HEAD_SIZE
    count = len(main_widths)
    if lane % 128:
        gain_part = jnp.sum(
            (contract_last(grad_main, main) + contract_last(grad_side, side)) * normed.astype(jnp.float32), axis=0
        )
        own_gain = from_relative(gain_part / gain[0], 0, nd)
        small = jnp.concatenate([own_gain.reshape(-1, 128), small[width // 128 :]])

    def kernel(normed_ref, grad_main_ref, grad_side_ref, main_ref, side_ref, resid_ref, before_ref, gain_ref, small_ref, *refs):
        grad_ref, small_out, common_ref = refs[:3]
        totals, refs = refs[3 : 3 + count], refs[3 + count :]
        parts_ref, side_total, line_held, total, send, recv = refs[:6]
        sums, landed, small_send, small_recv, gain_grad = refs[6:11]
        side_out, side_in, side_send, side_recv = refs[11:15]
        stage, held, hop_landed, core_send, core_recv, hop_send, hop_recv = refs[15:]
        me, zed = enter(nt, bits)
        pass_on, own_sum, reduce_end = line_reduce(nt, me, zed, chunks, parts_ref, line_held, send, recv)
        targets, at = [], 0
        for target, columns in zip(totals, main_widths):
            targets.append((target, at, columns))
            at = at + columns
        targets.append((side_total, main_columns, side_columns))
        away, near, later, scatter_end = computed_scatter(
            nd, me, zed, side_rows // 2,
            products_of(normed_ref, ((grad_main_ref, main_columns), (grad_side_ref, side_columns)), 512),
            stage, held, hop_landed, targets, core_send, core_recv, hop_send, hop_recv,
        )

        def part(turn):
            def step():
                where = aligned(near_first(nt, zed, nt - 1 - turn) * block_rows, block_rows)
                left, right = grad_main_ref[where], grad_side_ref[where]
                for start in range(0, width, 512):
                    extent = slice(start, start + 512)
                    value = product(left, main_ref[extent], LAST) + product(right, side_ref[extent], LAST)
                    parts_ref[where, extent] = value.astype(jnp.bfloat16)

            return step

        def gain_term(number):
            def step():
                if number == 0:
                    gain_grad[...] = jnp.zeros_like(gain_grad)

                def body(inner, carry):
                    where = aligned(number * block_rows + inner * 16, 16)
                    gain_grad[...] += parts_ref[where].astype(jnp.float32) * normed_ref[where].astype(jnp.float32)
                    return carry

                lax.fori_loop(0, block_rows // 16, body, 0)

            return step

        def small_copy(turn):
            if turn < bits:
                device = (flip(me, turn), zed)
            else:
                device = (me, flip(zed, turn - bits))
            extent = slice(None) if turn < bits else pl.ds(0, shared_rows)
            return pltpu.make_async_remote_copy(
                src_ref=sums.at[turn, extent],
                dst_ref=landed.at[turn, extent],
                send_sem=small_send.at[turn],
                recv_sem=small_recv.at[turn],
                device_id=device,
                device_id_type=MESH,
            )

        def small_begin():
            sums[0] = small_ref[...]
            if lane % 128 == 0:
                whole = jnp.sum(gain_grad[...], axis=0, keepdims=True) / gain_ref[...]
                for number, (other, half) in enumerate(blocks):
                    spot = mixed_with(me, other, bits) * 2 + half
                    sums[0, pl.ds(spot, 1), :] = whole[:, number * lane : (number + 1) * lane]
            small_copy(0).start()

        def small_step(turn):
            def step():
                small_copy(turn).wait_recv()
                if turn < bits:
                    sums[turn + 1] = sums[turn] + landed[turn]
                else:
                    sums[turn + 1] = sums[turn]
                    sums[turn + 1, pl.ds(0, shared_rows)] = (
                        sums[turn, pl.ds(0, shared_rows)] + landed[turn, pl.ds(0, shared_rows)]
                    )
                if turn + 1 < bits + line_bits:
                    small_copy(turn + 1).start()

            return step

        def small_end():
            for turn in range(bits + line_bits):
                small_copy(turn).wait_send()
            small_out[...] = sums[bits + line_bits]

        few = [gain_term(number) for number in range(nt if lane % 128 == 0 else 0)]
        few = few + [small_begin] + [small_step(turn) for turn in range(bits + line_bits)]

        def side_copy(source, target):
            return pltpu.make_async_remote_copy(
                src_ref=side_out.at[pl.ds(target * owned, owned)],
                dst_ref=side_in.at[source],
                send_sem=side_send.at[target],
                recv_sem=side_recv.at[source],
                device_id=(me, target),
                device_id_type=MESH,
            )

        def side_begin():
            side_out[...] = side_total[...].astype(jnp.bfloat16)
            for target in range(nt):

                @pl.when(zed != target)
                def _(target=target):
                    side_copy(zed, target).start()

            side_in[zed] = side_out[aligned(zed * owned, owned)]

        def side_end():
            for source in range(nt):

                @pl.when(zed != source)
                def _(source=source):
                    side_copy(source, source).wait_recv()

            common_ref[...] = jnp.zeros_like(common_ref)
            for source in range(nt):
                value = side_in[source].astype(jnp.float32)
                head = source * (QUERY_HEADS // nt) // (QUERY_HEADS // KEY_VALUE_HEADS)
                common_ref[:, :shared_columns] += value[:, :shared_columns]
                for turn in range(2):
                    at = shared_columns + (turn * KEY_VALUE_HEADS + head) * HEAD_SIZE
                    start = shared_columns + turn * HEAD_SIZE
                    common_ref[:, at : at + HEAD_SIZE] += value[:, start : start + HEAD_SIZE]
            for target in range(nt):

                @pl.when(zed != target)
                def _(target=target):
                    side_copy(zed, target).wait_send()

        def finish(chunk):
            own_sum(chunk, total)
            where = pl.ds(chunk * size, size)
            through, _ = norm_pull(resid_ref[where].astype(jnp.float32), gain_ref[...], total[...])
            value = before_ref[where] + through
            if lane % 128:
                grad_ref[where] = value
                return
            for number, (other, half) in enumerate(blocks):
                start = (mixed_with(me, other, bits) * 2 + half) * lane
                grad_ref[where, pl.ds(pl.multiple_of(start, lane), lane)] = value[:, number * lane : (number + 1) * lane]

        def passes(turn):
            return [functools.partial(pass_on, chunk, turn) for chunk in range(chunks)]

        middle = len(away) // 2
        steps = away[:middle] + [part(0)] + passes(0) + away[middle:] + [part(1)] + near[:middle]
        for turn in range(2, nt):
            steps.append(part(turn))
        steps = steps + passes(1) + near[middle:]
        for stage_steps in later[:-1]:
            steps = steps + stage_steps
        for turn in range(2, nt - 1):
            steps = steps + passes(turn)
        steps = steps + few[: -(bits + line_bits)] + later[-1] + [side_begin]
        ends = [functools.partial(finish, chunk) for chunk in range(chunks)]
        rest = few[-(bits + line_bits) :]
        for step in steps:
            step()
        together(ends, rest)
        side_end()
        small_end()
        scatter_end()
        for chunk in range(chunks):
            reduce_end(chunk)

    turns = bits + line_bits
    results = pl.pallas_call(
        kernel,
        out_shape=[
            jax.ShapeDtypeStruct((block_rows, width), jnp.float32),
            jax.ShapeDtypeStruct(small.shape, jnp.float32),
            jax.ShapeDtypeStruct((owned, common_columns), jnp.float32),
        ]
        + [jax.ShapeDtypeStruct((side_rows, columns), jnp.float32) for columns in main_widths],
        in_specs=[ONCHIP] * 9,
        out_specs=[ONCHIP] * (3 + count),
        scratch_shapes=[
            pltpu.VMEM((tokens, width), jnp.bfloat16),
            pltpu.VMEM((side_rows, side_columns), jnp.float32),
        ]
        + line_reduce_scratch(nt, block_rows, width, chunks)
        + [
            pltpu.VMEM((turns + 1, *small.shape), jnp.float32),
            pltpu.VMEM((turns, *small.shape), jnp.float32),
            pltpu.SemaphoreType.DMA((turns,)),
            pltpu.SemaphoreType.DMA((turns,)),
            pltpu.VMEM((16, width), jnp.float32),
            pltpu.VMEM((side_rows, side_columns), jnp.bfloat16),
            pltpu.VMEM((nt, owned, side_columns), jnp.bfloat16),
            pltpu.SemaphoreType.DMA((nt,)),
            pltpu.SemaphoreType.DMA((nt,)),
        ]
        + computed_scratch(nd, side_rows, main_columns + side_columns),
        compiler_params=pltpu.CompilerParams(
            collective_id=3, has_side_effects=True, vmem_limit_bytes=LARGE_LIMIT
        ),
        name="last_sums",
    )(normed, grad_main, grad_side, main, side, resid, before, gain, small)
    if lane % 128:
        results = (from_relative(results[0], 1, nd), *results[1:])
    return results


def silu_slope(value, sig):
    return sig * (1.0 + value * (1.0 - sig))


def split_dot(value, constant, dims, terms):
    total = None
    for _ in range(terms):
        piece = value.astype(jnp.bfloat16)
        value = value - piece.astype(jnp.float32)
        part = lax.dot_general(*((piece, constant) if dims[0] else (constant, piece)), dims[1], preferred_element_type=jnp.float32)
        total = part if total is None else total + part
    return total


PLAIN = (((1,), (0,)), ((), ()))
LAST = (((1,), (1,)), ((), ()))
FIRST = (((0,), (0,)), ((), ()))


def product(left, right, dims=PLAIN):
    return lax.dot_general(left, right, dims, preferred_element_type=jnp.float32)


def turned(value, cosine, sine):
    return value * cosine + pltpu.roll(value, value.shape[-1] // 2, 1) * sine


class Sizes:
    def __init__(self, channels, state_columns, query_columns, heads, length):
        self.channels, self.states = channels, state_columns // 2
        self.query, self.heads, self.length = query_columns, heads, length
        self.span = SPAN
        self.count = length // SPAN
        self.wide = channels + state_columns
        self.head_width = channels // heads
        self.step_at = 2 * channels + query_columns
        self.main = self.step_at + heads + (-(self.step_at + heads)) % 128
        self.step_lanes = self.main - self.step_at
        self.side = state_columns + 2 * HEAD_SIZE
        self.window = min(length, 3 * SPAN)


def spread_heads(size):
    table = np.zeros((size.step_lanes, size.channels), np.float32)
    for head in range(size.heads):
        table[head, head * size.head_width : (head + 1) * size.head_width] = 1.0
    return table.astype(jnp.bfloat16)


def turn_tables(length):
    half = HEAD_SIZE // 2
    angle = np.arange(length, dtype=np.float64)[:, None] * rope_base ** (-np.arange(half) / half)[None]
    cosine, sine = np.cos(angle), np.sin(angle)
    return (
        np.concatenate([cosine, cosine], 1).astype(np.float32),
        np.concatenate([-sine, sine], 1).astype(np.float32),
    )


def token_flags(segments, taps):
    seg = segments[0]
    length = seg.shape[0]
    ends = jnp.broadcast_to(seg.reshape(-1, SPAN)[:, -1:], (length // SPAN, SPAN)).reshape(-1)
    before = jnp.pad(ends, (SPAN, 0), constant_values=-1)[:length]
    lines = [seg == seg]
    lines = lines + [jnp.pad(seg, (lag, 0), constant_values=-1)[:length] == seg for lag in range(1, taps)]
    lines = lines + [before == seg, ends == seg]
    lines = lines + [jnp.pad(seg, (0, lag), constant_values=-1)[lag:] == seg for lag in range(1, taps)]
    lines = lines + [jnp.zeros((length,), bool)] * (16 - len(lines))
    return jnp.stack(lines).astype(jnp.float32).T


def chunk_values(size, taps, main_ref, wide_ref, flags, spread, taps_ref, heads_ref, segc, segr):
    span = size.span
    pre = wide_ref[pl.ds(8, span), :] * taps_ref[0:1, :]
    for lag in range(1, taps):
        pre = pre + wide_ref[pl.ds(8 - lag, span), :] * (flags[:, lag : lag + 1] * taps_ref[lag : lag + 1, :])
    sig = jax.nn.sigmoid(pre)
    act = pre * sig
    inner = act[:, : size.channels]
    bmat = act[:, size.channels : size.channels + size.states].astype(jnp.bfloat16)
    cmat = act[:, size.channels + size.states :].astype(jnp.bfloat16)
    step_in = main_ref[:, size.step_at :] + heads_ref[0:1, :]
    step = jnp.maximum(step_in, 0.0) + jnp.log1p(jnp.exp(-jnp.abs(step_in)))
    logdec = -step * heads_ref[1:2, :]
    rows = lax.broadcasted_iota(jnp.int32, (span, span), 0)
    columns = lax.broadcasted_iota(jnp.int32, (span, span), 1)
    later = jnp.where(rows >= columns, 1.0, 0.0).astype(jnp.bfloat16)
    cumul = split_dot(logdec, later, (False, PLAIN), 3)
    inside = jnp.logical_and(rows >= columns, segc == segr)
    ending = cumul[span - 1 : span, :]
    reach = jnp.exp(cumul) * flags[:, 4:5]
    tail = jnp.exp(ending - cumul) * flags[:, 5:6]
    step_wide = split_dot(step, spread, (True, PLAIN), 2)
    scaled = inner * step_wide
    return dict(
        pre=pre, sig=sig, inner=inner, bmat=bmat, cmat=cmat, step_in=step_in, step=step, logdec=logdec, later=later,
        cumul=cumul, turned=jnp.transpose(cumul), inside=inside, step_wide=step_wide, scaled=scaled,
        scaled_b=scaled.astype(jnp.bfloat16), meeting=product(cmat, bmat, LAST),
        reach_wide=split_dot(reach, spread, (True, PLAIN), 2), tail_wide=split_dot(tail, spread, (True, PLAIN), 2),
        skip_wide=split_dot(jnp.broadcast_to(heads_ref[2:3, :], (8, size.step_lanes)), spread, (True, PLAIN), 2)[0:1],
    )


def decay_of(values, head):
    spread = values["cumul"][:, head : head + 1] - values["turned"][head : head + 1, :]
    return jnp.exp(jnp.where(values["inside"], spread, -1e30))


def softmax_of(size, query, keys, chunk, start, segc, seg_all):
    scores = product(query, keys, LAST) * (1.0 / math.sqrt(HEAD_SIZE))
    rows = lax.broadcasted_iota(jnp.int32, scores.shape, 0) + chunk * size.span
    columns = lax.broadcasted_iota(jnp.int32, scores.shape, 1) + start
    allowed = jnp.logical_and(rows >= columns, segc == seg_all)
    masked = jnp.where(allowed, scores, -1e30)
    expo = jnp.exp(masked - jnp.max(masked, axis=-1, keepdims=True))
    return expo / jnp.sum(expo, axis=-1, keepdims=True)


def mixers_forward(size, taps, main_raw, side_raw, segments, flags, tap_rows, head_rows):
    span = size.span
    per_head = size.head_width

    def kernel(
        main_ref, side_ref, segc_ref, segr_ref, flags_ref, taps_ref, heads_ref, cos_ref, sin_ref, spread_ref,
        mixed_ref, y_ref, state_ref, keys_ref, values_ref, wide, state,
    ):
        chunk = pl.program_id(0)

        @pl.when(chunk == 0)
        def _():
            wide[0:8, :] = jnp.zeros((8, size.wide), jnp.float32)
            state[...] = jnp.zeros_like(state)
            keys_ref[...] = jnp.zeros_like(keys_ref)
            values_ref[...] = jnp.zeros_like(values_ref)

        wide[pl.ds(8, span), : size.channels] = main_ref[:, size.channels : 2 * size.channels]
        wide[pl.ds(8, span), size.channels :] = side_ref[:, : 2 * size.states]
        flags, spread, segc = flags_ref[...], spread_ref[...], segc_ref[...]
        segr = segr_ref[:, pl.ds(pl.multiple_of(chunk * span, span), span)]
        val = chunk_values(size, taps, main_ref, wide, flags, spread, taps_ref, heads_ref, segc, segr)
        wide[0:8, :] = wide[pl.ds(span, 8), :]
        held = state[...]
        held_b = held.astype(jnp.bfloat16)
        state_ref[...] = held
        across = val["reach_wide"] * product(val["cmat"], held_b)
        lane = lax.broadcasted_iota(jnp.int32, (span, 2 * per_head), 1)
        for pair in range(size.heads // 2):
            where = slice(pair * 2 * per_head, (pair + 1) * 2 * per_head)
            both = []
            for head in (2 * pair, 2 * pair + 1):
                weights = (val["meeting"] * decay_of(val, head)).astype(jnp.bfloat16)
                both.append(product(weights, val["scaled_b"][:, where]))
            result = jnp.where(lane < per_head, both[0], both[1])
            result = result + across[:, where] + val["skip_wide"][:, where] * val["inner"][:, where]
            y_ref[:, where] = result
            gate = main_ref[:, where]
            mixed_ref[:, where] = (result * (gate * jax.nn.sigmoid(gate))).astype(jnp.bfloat16)
        keep = jnp.broadcast_to(val["reach_wide"][span - 1 : span, :], (1, size.channels))
        state[...] = keep * held + product(
            val["bmat"], (val["tail_wide"] * val["scaled"]).astype(jnp.bfloat16), FIRST
        )

        cosine, sine = cos_ref[...], sin_ref[...]
        own = pl.ds(pl.multiple_of(chunk * span, span), span)
        key_at = 2 * size.states
        keys_ref[own, :] = turned(side_ref[:, key_at : key_at + HEAD_SIZE], cosine, sine).astype(jnp.bfloat16)
        values_ref[own, :] = side_ref[:, key_at + HEAD_SIZE :].astype(jnp.bfloat16)
        start = pl.multiple_of(jnp.maximum(chunk + 1 - size.window // span, 0) * span, span)
        seen = pl.ds(start, size.window)
        for head in range(size.query // HEAD_SIZE):
            at = 2 * size.channels + head * HEAD_SIZE
            query = turned(main_ref[:, at : at + HEAD_SIZE], cosine, sine).astype(jnp.bfloat16)
            probs = softmax_of(size, query, keys_ref[seen, :], chunk, start, segc, segr_ref[:, seen])
            result = product(probs.astype(jnp.bfloat16), values_ref[seen, :])
            at = size.channels + head * HEAD_SIZE
            mixed_ref[:, at : at + HEAD_SIZE] = result.astype(jnp.bfloat16)

    def rows(columns):
        return pl.BlockSpec((span, columns), lambda i: (i, 0))

    def whole(array):
        return pl.BlockSpec(array.shape, lambda i: (0, 0))

    cosine, sine = turn_tables(size.length)
    spread = spread_heads(size)
    tokens = size.length
    return pl.pallas_call(
        kernel,
        grid=(size.count,),
        in_specs=[
            rows(size.main), rows(size.side), rows(1), whole(segments), rows(16), whole(tap_rows), whole(head_rows),
            rows(HEAD_SIZE), rows(HEAD_SIZE), whole(spread),
        ],
        out_specs=[
            rows(size.channels + size.query), rows(size.channels),
            pl.BlockSpec((size.states, size.channels), lambda i: (i, 0)),
            pl.BlockSpec((tokens, HEAD_SIZE), lambda i: (0, 0)), pl.BlockSpec((tokens, HEAD_SIZE), lambda i: (0, 0)),
        ],
        out_shape=[
            jax.ShapeDtypeStruct((tokens, size.channels + size.query), jnp.bfloat16),
            jax.ShapeDtypeStruct((tokens, size.channels), jnp.float32),
            jax.ShapeDtypeStruct((size.count * size.states, size.channels), jnp.float32),
            jax.ShapeDtypeStruct((tokens, HEAD_SIZE), jnp.bfloat16),
            jax.ShapeDtypeStruct((tokens, HEAD_SIZE), jnp.bfloat16),
        ],
        scratch_shapes=[
            pltpu.VMEM((span + 8, size.wide), jnp.float32),
            pltpu.VMEM((size.states, size.channels), jnp.float32),
        ],
        compiler_params=pltpu.CompilerParams(
            dimension_semantics=("arbitrary",), vmem_limit_bytes=VMEM_LIMIT
        ),
        cost_estimate=pl.CostEstimate(flops=20 * 10**9, bytes_accessed=25 * 10**6, transcendentals=5 * 10**6),
        name="mixers_forward",
    )(main_raw, side_raw, segments.reshape(tokens, 1), segments, flags, tap_rows, head_rows,
      jnp.asarray(cosine), jnp.asarray(sine), jnp.asarray(spread))


def mixers_backward(
    nd, nt, size, taps, grad_mixed, main_raw, side_raw, segments, flags, tap_rows, head_rows, y_value, states, keys, values,
    grad_rows, mixed,
):
    bits = nd.bit_length() - 1
    out_rows, out_columns = grad_rows.shape[1] // nd, mixed.shape[1]
    span = size.span
    per_head = size.head_width
    count = size.count

    def kernel(
        grad_ref, main_ref, side_ref, before_ref, side_before_ref, segc_ref, segr_ref, flags_ref, taps_ref, heads_ref,
        cos_ref, sin_ref, spread_ref, y_ref, state_ref, keys_ref, values_ref, rows_ref, mixed_ref,
        grad_main, grad_side, tap_sums, head_sums, mixer_total, attn_total,
        wide, back, grad_state, grad_keys, grad_values,
        stage, held, landed, core_send, core_recv, hop_send, hop_recv,
    ):
        turn = pl.program_id(0)
        chunk = count - 1 - turn
        me, zed = lax.axis_index("dp"), lax.axis_index("tensor")
        away, near, later, scatter_end = computed_scatter(
            nd, me, zed, out_rows // 2, products_of(rows_ref, ((mixed_ref, out_columns),), 512), stage, held, landed,
            ((mixer_total, 0, size.channels), (attn_total, size.channels, size.query)),
            core_send, core_recv, hop_send, hop_recv,
        )
        stages = [away, near, *later[: count - 3], [step for stage_steps in later[count - 3 :] for step in stage_steps]]
        for number, stage_steps in enumerate(stages):

            @pl.when(turn == number)
            def _(number=number, stage_steps=stage_steps):
                if number == 0:
                    enter(nt, bits)
                for step in stage_steps:
                    step()
                if number == len(stages) - 1:
                    scatter_end()

        @pl.when(turn == 0)
        def _():
            back[pl.ds(span, 8), :] = jnp.zeros((8, size.wide), jnp.float32)
            grad_state[...] = jnp.zeros_like(grad_state)
            grad_keys[...] = jnp.zeros_like(grad_keys)
            grad_values[...] = jnp.zeros_like(grad_values)
            tap_sums[...] = jnp.zeros_like(tap_sums)
            head_sums[...] = jnp.zeros_like(head_sums)

        wide[0:8, : size.channels] = before_ref[...]
        wide[0:8, size.channels :] = side_before_ref[...]
        wide[pl.ds(8, span), : size.channels] = main_ref[:, size.channels : 2 * size.channels]
        wide[pl.ds(8, span), size.channels :] = side_ref[:, : 2 * size.states]
        flags, spread, segc = flags_ref[...], spread_ref[...], segc_ref[...]
        segr = segr_ref[:, pl.ds(pl.multiple_of(chunk * span, span), span)]
        val = chunk_values(size, taps, main_ref, wide, flags, spread, taps_ref, heads_ref, segc, segr)
        inner, scaled = val["inner"], val["scaled"]

        gate = main_ref[:, : size.channels]
        gate_sig = jax.nn.sigmoid(gate)
        grad = grad_ref[:, : size.channels]
        grad_main[:, : size.channels] = (grad * y_ref[...] * silu_slope(gate, gate_sig)).astype(jnp.bfloat16)
        grad_y = grad * (gate * gate_sig)
        grad_y_b = grad_y.astype(jnp.bfloat16)
        tap_sums[4:5, : size.channels] += jnp.sum(grad_y * inner, axis=0, keepdims=True)

        lane = lax.broadcasted_iota(jnp.int32, (span, 2 * per_head), 1)
        head_lane = lax.broadcasted_iota(jnp.int32, (span, size.step_lanes), 1)
        head_row = lax.broadcasted_iota(jnp.int32, (size.step_lanes, span), 0)
        grad_meeting = jnp.zeros((span, span), jnp.float32)
        by_row = jnp.zeros((span, size.step_lanes), jnp.float32)
        by_column = jnp.zeros((size.step_lanes, span), jnp.float32)
        pieces = []
        for pair in range(size.heads // 2):
            where = slice(pair * 2 * per_head, (pair + 1) * 2 * per_head)
            both = []
            for side in range(2):
                head = 2 * pair + side
                decay = decay_of(val, head)
                weights = val["meeting"] * decay
                mine = (lane < per_head) if side == 0 else (lane >= per_head)
                grad_own = jnp.where(mine, grad_y_b[:, where], jnp.zeros((), jnp.bfloat16))
                grad_weights = product(grad_own, val["scaled_b"][:, where], LAST)
                both.append(product(weights.astype(jnp.bfloat16), grad_y_b[:, where], FIRST))
                grad_meeting = grad_meeting + grad_weights * decay
                moved = grad_weights * weights
                by_row = jnp.where(head_lane == head, jnp.sum(moved, axis=1, keepdims=True), by_row)
                by_column = jnp.where(head_row == head, jnp.sum(moved, axis=0, keepdims=True), by_column)
            pieces.append(jnp.where(lane < per_head, both[0], both[1]))
        grad_scaled = jnp.concatenate(pieces, axis=1)
        grad_cumul = by_row - jnp.transpose(by_column)

        held = state_ref[...]
        held_b = held.astype(jnp.bfloat16)
        grad_held = grad_state[...]
        grad_held_b = grad_held.astype(jnp.bfloat16)
        grad_meeting_b = grad_meeting.astype(jnp.bfloat16)
        reached = val["reach_wide"] * grad_y
        reached_b = reached.astype(jnp.bfloat16)
        grad_cumul = grad_cumul + split_dot(reached * product(val["cmat"], held_b), spread, (True, LAST), 2)
        grad_c = product(reached_b, held_b, LAST) + product(grad_meeting_b, val["bmat"])
        from_state = val["tail_wide"] * product(val["bmat"], grad_held_b)
        grad_b = product(grad_meeting_b, val["cmat"], FIRST) + product(
            (val["tail_wide"] * scaled).astype(jnp.bfloat16), grad_held_b, LAST
        )
        grad_scaled = grad_scaled + from_state
        ended = split_dot(scaled * from_state, spread, (True, LAST), 2)
        keep = val["reach_wide"][span - 1 : span, :]
        kept = jnp.sum(grad_held * held, axis=0, keepdims=True) * keep
        kept = split_dot(jnp.broadcast_to(kept, (8, size.channels)), spread, (True, LAST), 2)[0:1]
        at_end = jnp.sum(ended, axis=0, keepdims=True) + kept
        grad_logdec = split_dot(grad_cumul - ended, val["later"], (False, FIRST), 3) + at_end
        grad_state[...] = keep * grad_held + product(val["cmat"], reached_b, FIRST)

        grad_inner = grad_scaled * val["step_wide"] + grad_y * val["skip_wide"]
        grad_step = split_dot(grad_scaled * inner, spread, (True, LAST), 2) - grad_logdec * heads_ref[1:2, :]
        grad_step_raw = grad_step * jax.nn.sigmoid(val["step_in"])
        head_sums[0:1, :] += jnp.sum(grad_step_raw, axis=0, keepdims=True)
        head_sums[1:2, :] += jnp.sum(grad_logdec * val["logdec"], axis=0, keepdims=True)
        grad_main[:, size.step_at :] = grad_step_raw.astype(jnp.bfloat16)

        slope = silu_slope(val["pre"], val["sig"])
        grad_pre = jnp.concatenate([grad_inner, grad_b, grad_c], axis=1) * slope
        back[pl.ds(0, span), :] = grad_pre
        raw = grad_pre * taps_ref[0:1, :]
        tap_sums[0:1, :] += jnp.sum(grad_pre * wide[pl.ds(8, span), :], axis=0, keepdims=True)
        for lag in range(1, taps):
            tap_sums[lag : lag + 1, :] += jnp.sum(
                grad_pre * (wide[pl.ds(8 - lag, span), :] * flags[:, lag : lag + 1]), axis=0, keepdims=True
            )
            raw = raw + back[pl.ds(lag, span), :] * (flags[:, 5 + lag : 6 + lag] * taps_ref[lag : lag + 1, :])
        back[pl.ds(span, 8), :] = back[0:8, :]
        grad_main[:, size.channels : 2 * size.channels] = raw[:, : size.channels].astype(jnp.bfloat16)
        grad_side[:, : 2 * size.states] = raw[:, size.channels :].astype(jnp.bfloat16)

        cosine, sine = cos_ref[...], sin_ref[...]
        start = pl.multiple_of(jnp.maximum(chunk + 1 - size.window // span, 0) * span, span)
        seen = pl.ds(start, size.window)
        seen_keys, seen_values = keys_ref[seen, :], values_ref[seen, :]
        scale = 1.0 / math.sqrt(HEAD_SIZE)
        for head in range(size.query // HEAD_SIZE):
            at = 2 * size.channels + head * HEAD_SIZE
            query = turned(main_ref[:, at : at + HEAD_SIZE], cosine, sine).astype(jnp.bfloat16)
            probs = softmax_of(size, query, seen_keys, chunk, start, segc, segr_ref[:, seen])
            out_at = size.channels + head * HEAD_SIZE
            grad_out = grad_ref[:, out_at : out_at + HEAD_SIZE].astype(jnp.bfloat16)
            grad_probs = product(grad_out, seen_values, LAST)
            delta = jnp.sum(grad_probs * probs, axis=-1, keepdims=True)
            grad_scores = (probs * (grad_probs - delta)).astype(jnp.bfloat16)
            grad_query = product(grad_scores, seen_keys) * scale
            grad_main[:, at : at + HEAD_SIZE] = turned(grad_query, cosine, -sine).astype(jnp.bfloat16)
            grad_keys[seen, :] += product(grad_scores, query, FIRST) * scale
            grad_values[seen, :] += product(probs.astype(jnp.bfloat16), grad_out, FIRST)
        own = pl.ds(pl.multiple_of(chunk * span, span), span)
        key_at = 2 * size.states
        grad_side[:, key_at : key_at + HEAD_SIZE] = turned(grad_keys[own, :], cosine, -sine).astype(jnp.bfloat16)
        grad_side[:, key_at + HEAD_SIZE :] = grad_values[own, :].astype(jnp.bfloat16)

    def rows(columns):
        return pl.BlockSpec((span, columns), lambda i: (count - 1 - i, 0))

    def previous(columns, column):
        return pl.BlockSpec((8, columns), lambda i: (jnp.maximum((count - 1 - i) * (span // 8) - 1, 0), column))

    def whole(array):
        return pl.BlockSpec(array.shape, lambda i: (0, 0))

    cosine, sine = turn_tables(size.length)
    spread = spread_heads(size)
    tokens = size.length
    return pl.pallas_call(
        kernel,
        grid=(count,),
        in_specs=[
            rows(size.channels + size.query), rows(size.main), rows(size.side), previous(size.channels, 1),
            previous(2 * size.states, 0), rows(1), whole(segments), rows(16), whole(tap_rows), whole(head_rows),
            rows(HEAD_SIZE), rows(HEAD_SIZE), whole(spread), rows(size.channels),
            pl.BlockSpec((size.states, size.channels), lambda i: (count - 1 - i, 0)), whole(keys), whole(values),
            whole(grad_rows), whole(mixed),
        ],
        out_specs=[
            rows(size.main), rows(size.side), pl.BlockSpec((8, size.wide), lambda i: (0, 0)),
            pl.BlockSpec((8, size.step_lanes), lambda i: (0, 0)),
            pl.BlockSpec((out_rows, size.channels), lambda i: (0, 0)),
            pl.BlockSpec((out_rows, size.query), lambda i: (0, 0)),
        ],
        out_shape=[
            jax.ShapeDtypeStruct((tokens, size.main), jnp.bfloat16),
            jax.ShapeDtypeStruct((tokens, size.side), jnp.bfloat16),
            jax.ShapeDtypeStruct((8, size.wide), jnp.float32),
            jax.ShapeDtypeStruct((8, size.step_lanes), jnp.float32),
            jax.ShapeDtypeStruct((out_rows, size.channels), jnp.float32),
            jax.ShapeDtypeStruct((out_rows, size.query), jnp.float32),
        ],
        scratch_shapes=[
            pltpu.VMEM((span + 8, size.wide), jnp.float32),
            pltpu.VMEM((span + 8, size.wide), jnp.float32),
            pltpu.VMEM((size.states, size.channels), jnp.float32),
            pltpu.VMEM((tokens, HEAD_SIZE), jnp.float32),
            pltpu.VMEM((tokens, HEAD_SIZE), jnp.float32),
        ]
        + computed_scratch(nd, out_rows, out_columns),
        compiler_params=pltpu.CompilerParams(
            dimension_semantics=("arbitrary",), vmem_limit_bytes=VMEM_LIMIT, collective_id=4, has_side_effects=True
        ),
        cost_estimate=pl.CostEstimate(flops=40 * 10**9, bytes_accessed=60 * 10**6, transcendentals=10**7),
        name="mixers_backward",
    )(grad_mixed, main_raw, side_raw, main_raw, side_raw, segments.reshape(tokens, 1), segments, flags, tap_rows,
      head_rows, jnp.asarray(cosine), jnp.asarray(sine), jnp.asarray(spread), y_value, states, keys, values, grad_rows, mixed)


def per_device(
    nd,
    nt,
    residual,
    segments,
    mixgain,
    ffngain,
    gateproj,
    innerproj,
    stepproj,
    sharedproj,
    innerconv,
    sharedconv,
    stepbias,
    decaylog,
    skipgain,
    mixerout,
    queryproj,
    keyvalue,
    attnout,
    ffngate,
    upproj,
    downproj,
    cotangent,
):
    bfloat = jnp.bfloat16
    single = jnp.float32
    width = residual.shape[1]
    zed = lax.axis_index("tensor")
    seq_count, length = segments.shape
    token_count = seq_count * length
    channels = innerproj.shape[1]
    state_columns = sharedproj.shape[1]
    heads = stepproj.shape[1]
    query_columns = queryproj.shape[1]
    ffn_columns = ffngate.shape[1]
    small_rows = sharedproj.shape[0]
    conv_rows = sharedconv.shape[0]
    taps = sharedconv.shape[1]

    gains = jnp.concatenate(
        [
            mixgain[:, None],
            ffngain[:, None],
            jnp.pad(sharedconv, ((0, small_rows - conv_rows), (0, 0))),
            jnp.zeros((small_rows, 128 - 2 - taps), bfloat),
        ],
        axis=1,
    )
    main_used = 2 * channels + query_columns + heads
    main_own = jnp.concatenate(
        [
            gateproj,
            innerproj,
            queryproj,
            stepproj,
            jnp.zeros((gateproj.shape[0], -main_used % 128), bfloat),
        ],
        axis=1,
    )
    resid_own, cot_own, gain_rows, normed, grad_rows, _, main, side, out_w, main_raw, side_raw = first_gathers(
        nd,
        nt,
        residual,
        cotangent,
        jnp.concatenate([sharedproj, keyvalue, gains], axis=1),
        main_own,
        jnp.concatenate([mixerout, attnout], axis=1),
        state_columns,
    )
    gain_one, gain_two = gain_rows[0], gain_rows[1]
    conv_shared = from_relative(gain_rows[2 : 2 + taps], 1, nd)
    conv_shared = conv_shared.reshape(taps, nd * nt, small_rows)[:, :, :conv_rows].reshape(taps, -1)

    size = Sizes(channels, state_columns, query_columns, heads, length)
    flags = token_flags(segments, taps)
    tap_rows = jnp.concatenate([innerconv.astype(single).T, conv_shared], axis=1)
    tap_rows = jnp.pad(tap_rows, ((0, 8 - taps), (0, 0)))
    head_rows = jnp.stack([stepbias.astype(single), jnp.exp(decaylog.astype(single)), skipgain.astype(single)])
    head_rows = jnp.pad(head_rows, ((0, 5), (0, size.step_lanes - heads)))
    mixed_in, y_value, states, keys, values = mixers_forward(
        size, taps, main_raw, side_raw, segments, flags, tap_rows, head_rows
    )
    middle, rows_two, hidden, grad_gate_up, grad_rows, ffn_w = middle_rows(
        nd,
        nt,
        mixed_in,
        out_w,
        resid_own,
        gain_two[None],
        grad_rows,
        *second_neighbours(nt, grad_rows),
        jnp.concatenate([ffngate, upproj, downproj], axis=1),
    )
    down_w = ffn_w[:, 2 * ffn_columns :]
    grad_middle, grad_gain_two, grad_mix_rows, gate_g, up_g, down_g = middle_back(
        nd, nt, grad_gate_up, hidden, rows_two, grad_rows, ffn_w, middle, cot_own, gain_two[None]
    )
    ffn_part = contract_last(hidden, down_w).astype(bfloat)
    ffn_part = ffn_part.reshape(-1, nt, middle.shape[0] // LINE_CHUNKS, width).swapaxes(0, 1).reshape(token_count, width)
    ffn_part = after(ffn_part, grad_mix_rows)
    ffn_out = lax.psum_scatter(ffn_part, "tensor", scatter_dimension=0, tiled=True)
    layer_out = from_relative(middle + ffn_out.astype(single), 1, nd)
    grad_mixed_in = matrix_product(grad_mix_rows, out_w)
    grad_main, grad_side, tap_sums, head_sums, mixer_g, attn_g = mixers_backward(
        nd, nt, size, taps, grad_mixed_in, main_raw, side_raw, segments, flags, tap_rows, head_rows, y_value, states,
        keys, values, grad_mix_rows, mixed_in,
    )
    small = jnp.concatenate(
        [
            jnp.zeros((width,), single),
            grad_gain_two[0],
            tap_sums[:taps, channels:].reshape(-1),
            tap_sums[:taps, :channels].reshape(-1),
            tap_sums[4, :channels],
            head_sums[:2].reshape(-1),
        ]
    )
    shared_length = 2 * width + taps * state_columns
    small = jnp.pad(small, (0, -small.shape[0] % 1024)).reshape(-1, 128)
    grad_residual, small, common_g, gateproj_g, inner_g, query_g, step_g = last_sums(
        nd,
        nt,
        normed,
        grad_main,
        grad_side,
        main,
        side,
        resid_own,
        grad_middle,
        gain_one[None],
        small,
        shared_length // 128,
        (channels, channels, query_columns, heads),
    )
    small = small.reshape(-1)
    place = lax.axis_index("dp") * nt + zed
    gain_one_g = lax.dynamic_slice_in_dim(small, place * small_rows, small_rows, 0)
    gain_two_g = lax.dynamic_slice_in_dim(small, width + place * small_rows, small_rows, 0)
    conv_g = lax.dynamic_slice_in_dim(
        small[2 * width : shared_length].reshape(taps, -1), place * conv_rows, conv_rows, 1
    ).T
    local = small[shared_length:]
    skip_at = taps * channels
    head_at = skip_at + channels
    return (
        layer_out,
        grad_residual,
        gain_one_g,
        gain_two_g,
        gateproj_g,
        inner_g,
        step_g,
        common_g[:, :state_columns],
        local[:skip_at].reshape(taps, channels).T,
        conv_g,
        local[head_at : head_at + heads],
        local[head_at + size.step_lanes : head_at + size.step_lanes + heads],
        local[skip_at:head_at].reshape(heads, -1).sum(axis=1),
        mixer_g,
        query_g,
        common_g[:, state_columns:],
        attn_g,
        gate_g,
        up_g,
        down_g,
    )


def solution(mesh):
    return jax.shard_map(
        functools.partial(per_device, mesh.shape["dp"], mesh.shape["tensor"]),
        mesh=mesh,
        in_specs=(
            P(("dp", "tensor"), None),
            P("dp", None),
            P(("dp", "tensor")),
            P(("dp", "tensor")),
            P("dp", "tensor"),
            P("dp", "tensor"),
            P("dp", "tensor"),
            P(("dp", "tensor"), None),
            P("tensor", None),
            P(("dp", "tensor"), None),
            P("tensor"),
            P("tensor"),
            P("tensor"),
            P("dp", "tensor"),
            P("dp", "tensor"),
            P(("dp", "tensor"), None),
            P("dp", "tensor"),
            P("dp", "tensor"),
            P("dp", "tensor"),
            P("dp", "tensor"),
            P(("dp", "tensor"), None),
        ),
        out_specs=(
            P(("dp", "tensor"), None),
            P(("dp", "tensor"), None),
            P(("dp", "tensor")),
            P(("dp", "tensor")),
            P("dp", "tensor"),
            P("dp", "tensor"),
            P("dp", "tensor"),
            P(("dp", "tensor"), None),
            P("tensor", None),
            P(("dp", "tensor"), None),
            P("tensor"),
            P("tensor"),
            P("tensor"),
            P("dp", "tensor"),
            P("dp", "tensor"),
            P(("dp", "tensor"), None),
            P("dp", "tensor"),
            P("dp", "tensor"),
            P("dp", "tensor"),
            P("dp", "tensor"),
        ),
        check_vma=False,
    )
```

```python
import functools
import math

import jax
import jax.numpy as jnp
import numpy as np
from jax import lax
from jax.experimental import pallas as pl
from jax.experimental.pallas import tpu as pltpu
from jax.sharding import PartitionSpec as P

QUERY_HEADS = 8
KEY_VALUE_HEADS = 2
HEAD_SIZE = 128
SPAN = 256


eps = 1e-05
rope_base = 10000.0


def contract_last(left, right):
    return lax.dot_general(
        left, right, (((1,), (1,)), ((), ())), preferred_element_type=jnp.float32
    )


def bit_orders(size):
    high = list(range(size.bit_length() - 2, 0, -1))
    return high, high[:2][::-1] + high[2:]


def relative_blocks(size):
    both = []
    for half, order in enumerate(bit_orders(size)):
        chain = [0]
        for bit in order:
            chain = chain + [other ^ (1 << bit) for other in chain]
        both = both + [(other, half) for other in chain]
    return both + [(other ^ 1, half) for other, half in both]


def relative_place(other, half, size):
    place = half * (size // 2) + (other & 1) * size
    for digit, bit in enumerate(bit_orders(size)[half]):
        place = place + (((other >> bit) & 1) << digit)
    return place


def to_relative(value, axis, size):
    me = lax.axis_index("dp")
    width = value.shape[axis] // (2 * size)
    return jnp.concatenate(
        [
            lax.dynamic_slice_in_dim(value, ((me ^ other) * 2 + half) * width, width, axis)
            for other, half in relative_blocks(size)
        ],
        axis,
    )


def from_relative(value, axis, size):
    me = lax.axis_index("dp")
    width = value.shape[axis] // (2 * size)
    return jnp.concatenate(
        [
            lax.dynamic_slice_in_dim(value, relative_place(me ^ number, half, size) * width, width, axis)
            for number in range(size)
            for half in range(2)
        ],
        axis,
    )


MESH = pl.DeviceIdType.MESH
VMEM_LIMIT = 56 * 1024 * 1024
LINE_CHUNKS = 4
LARGE_LIMIT = 62 * 1024 * 1024


def flip(value, bit):
    unit = 1 << bit
    return value + unit * (1 - 2 * ((value // unit) % 2))


def mixed_with(value, other, bits):
    for bit in range(bits):
        if (other >> bit) & 1:
            value = flip(value, bit)
    return value


def enter(nt, bits):
    me, zed = lax.axis_index("dp"), lax.axis_index("tensor")
    barrier = pltpu.get_barrier_semaphore()
    for other in range(nt):

        @pl.when(zed != other)
        def _(other=other):
            pl.semaphore_signal(barrier, inc=1, device_id=(me, other), device_id_type=MESH)

    for bit in range(bits):
        pl.semaphore_signal(barrier, inc=1, device_id=(flip(me, bit), zed), device_id_type=MESH)
    pl.semaphore_wait(barrier, bits + nt - 1)
    return me, zed


def aligned(start, size):
    return pl.ds(pl.multiple_of(start, 16), size)


def together(*flows):
    flows = [list(flow) for flow in flows]
    order = sorted(
        ((place + 0.5) / len(flow), number, place)
        for number, flow in enumerate(flows)
        for place in range(len(flow))
    )
    for _, number, place in order:
        flows[number][place]()


def gather_steps(nd, me, zed, own, everything, send, recv, local):
    half = own.shape[0] // 2
    blocks = relative_blocks(nd)
    place = {block: number for number, block in enumerate(blocks)}

    def rows(block):
        return everything.at[pl.ds(place[block] * half, half)]

    def source(block):
        return own.at[pl.ds(block[1] * half, half)] if block[0] == 0 else rows(block)

    hops = []
    for part, order in enumerate(bit_orders(nd)):
        chain = [0]
        for bit in order:
            hops = hops + [((other, part), bit) for other in chain]
            chain = chain + [other ^ (1 << bit) for other in chain]
    hops = hops + [(block, 0) for block in blocks[:nd]]

    def copy(number):
        block, bit = hops[number]
        landed = (block[0] ^ (1 << bit), block[1])
        return pltpu.make_async_remote_copy(
            src_ref=source(block),
            dst_ref=rows(landed),
            send_sem=send.at[number],
            recv_sem=recv.at[place[landed]],
            device_id=(flip(me, bit), zed),
            device_id_type=MESH,
        )

    def arrival(block):
        return pltpu.make_async_remote_copy(
            src_ref=rows(block),
            dst_ref=rows(block),
            send_sem=send.at[0],
            recv_sem=recv.at[place[block]],
            device_id=(flip(me, 0), zed),
            device_id_type=MESH,
        )

    def begin():
        for number, (block, bit) in enumerate(hops):
            if block[0] == 0:
                copy(number).start()
        for part in range(2):
            pltpu.make_async_copy(source((0, part)), rows((0, part)), local.at[part]).start()

    def forward(block):
        def step():
            arrival(block).wait_recv()
            for number, (origin, bit) in enumerate(hops):
                if origin == block:
                    copy(number).start()

        return step

    def end():
        for block in blocks[nd:]:
            arrival(block).wait_recv()
        for number in range(len(hops)):
            copy(number).wait_send()
        for part in range(2):
            pltpu.make_async_copy(source((0, part)), rows((0, part)), local.at[part]).wait()

    first, second = blocks[1 : nd // 2], blocks[nd // 2 + 1 : nd]
    middle = [forward(block) for pair in zip(first, second) for block in pair]
    return [begin] + middle + [end]


def gather_hops(nd):
    return 2 * (nd // 2 - 1) + nd


def gather_semaphores(nd):
    return [
        pltpu.SemaphoreType.DMA((gather_hops(nd),)),
        pltpu.SemaphoreType.DMA((2 * nd,)),
        pltpu.SemaphoreType.DMA((2,)),
    ]


def each_rows(rows, body, unit=16):
    def step(number, carry):
        body(aligned(number * unit, unit))
        return carry

    lax.fori_loop(0, rows // unit, step, 0)


def computed_scatter(nd, me, zed, half, compute, stage, held, landed, totals, core_send, core_recv, send, recv):
    chain_length = nd // 2
    block = 256
    pieces = block // half
    per_part = chain_length // pieces
    turns = [part * per_part + spot for spot in range(per_part - 1, -1, -1) for part in range(2)]

    def piece(ref, number):
        return ref.at[pl.ds(number * half, half)]

    def block_of(ref, number):
        return ref.at[pl.ds(number * block, block)]

    rounds, slot = [], 0
    for part, order in enumerate(bit_orders(nd)):
        length, own_rounds = chain_length, []
        for bit in order[::-1]:
            length = length // 2
            own_rounds.append((bit, length, slot))
            slot = slot + length
        rounds.append(own_rounds)

    def core_copy(number):
        return pltpu.make_async_remote_copy(
            src_ref=block_of(stage, number),
            dst_ref=block_of(held, number),
            send_sem=core_send.at[number],
            recv_sem=core_recv.at[number],
            device_id=(flip(me, 0), zed),
            device_id_type=MESH,
        )

    def hop(bit, number, where):
        return pltpu.make_async_remote_copy(
            src_ref=piece(held, number),
            dst_ref=piece(landed, where),
            send_sem=send.at[where],
            recv_sem=recv.at[where],
            device_id=(flip(me, bit), zed),
            device_id_type=MESH,
        )

    def away(number):
        def step():
            compute(nd * half + number * block, None, block_of(stage, number))
            core_copy(number).start()

        return step

    def near(number):
        def step():
            core_copy(number).wait_recv()
            compute(number * block, block_of(held, number), block_of(held, number))
            for inner in range(pieces):
                place = number * pieces + inner
                part, spot = place // chain_length, place % chain_length
                bit, length, first = rounds[part][0]
                if spot >= length:
                    hop(bit, place, first + spot - length).start()

        return step

    def later_sum(part, turn, spot):
        bit, length, first = rounds[part][turn]
        number = part * chain_length + spot

        def step():
            hop(bit, number, first + spot).wait_recv()
            last = turn == len(rounds[part]) - 1

            def body(rows):
                kept, came = piece(held, number)[rows], piece(landed, first + spot)[rows]
                if last:
                    value = kept.astype(jnp.float32) + came.astype(jnp.float32)
                    for target, start, columns in totals:
                        piece(target, part)[rows] = value[:, start : start + columns]
                else:
                    piece(held, number)[rows] = kept + came

            each_rows(half, body)
            if not last:
                next_bit, next_length, next_first = rounds[part][turn + 1]
                if spot >= next_length:
                    hop(next_bit, number, next_first + spot - next_length).start()

        return step

    def end():
        for number in range(len(turns)):
            core_copy(number).wait_send()
        for part in range(2):
            for bit, length, first in rounds[part]:
                for spot in range(length):
                    hop(bit, part * chain_length + length + spot, first + spot).wait_send()

    later = []
    for turn in range(len(rounds[0])):
        length = rounds[0][turn][1]
        later.append([later_sum(part, turn, spot) for spot in range(length - 1, -1, -1) for part in range(2)])
    return [away(number) for number in turns], [near(number) for number in turns], later, end


def computed_scratch(nd, rows, columns):
    slots = nd - 2
    blocks = nd * rows // 2 // 256
    return [
        pltpu.VMEM((nd * rows // 2, columns), jnp.bfloat16),
        pltpu.VMEM((nd * rows // 2, columns), jnp.bfloat16),
        pltpu.VMEM((slots * rows // 2, columns), jnp.bfloat16),
        pltpu.SemaphoreType.DMA((blocks,)),
        pltpu.SemaphoreType.DMA((blocks,)),
        pltpu.SemaphoreType.DMA((slots,)),
        pltpu.SemaphoreType.DMA((slots,)),
    ]


def products_of(left, rights, tile):
    def compute(start, add, target):
        turned_left = jnp.transpose(left[:, start : start + 256])
        at = 0
        for right, columns in rights:
            for first in range(0, columns, tile):
                extent = slice(first, min(first + tile, columns))
                value = jnp.dot(turned_left, right[:, extent], preferred_element_type=jnp.float32)
                here = slice(at + extent.start, at + extent.stop)
                if add is not None:
                    value = value + add[:, here].astype(jnp.float32)
                target[:, here] = value.astype(jnp.bfloat16)
            at = at + columns

    return compute


def line_gather(nt, me, zed, chunks, own, everything, send, recv, chunked=False, reach=None):
    size = own.shape[0] // chunks
    reach = nt - 1 if reach is None else reach

    def own_rows(chunk):
        return own.at[pl.ds(chunk * size, size)]

    def rows(block, chunk):
        start = (chunk * nt + block) * size if chunked else block * (size * chunks) + chunk * size
        return everything.at[aligned(start, size)]

    def copy(source, block, chunk, side):
        return pltpu.make_async_remote_copy(
            src_ref=source,
            dst_ref=rows(block, chunk),
            send_sem=send.at[side, block, chunk],
            recv_sem=recv.at[block, chunk],
            device_id=(me, zed + 1 - 2 * side),
            device_id_type=MESH,
        )

    def keep(chunk):
        return pltpu.make_async_copy(own_rows(chunk), rows(zed, chunk), recv.at[zed, chunk])

    def first(chunk):
        for side, condition in ((0, zed < nt - 1), (1, zed > 0)):

            @pl.when(condition)
            def _(side=side):
                copy(own_rows(chunk), zed, chunk, side).start()

        keep(chunk).start()

    def onward(chunk, distance):
        for side, block in ((0, zed - distance), (1, zed + distance)):
            inside = (block >= 0) if side == 0 else (block < nt)
            open_end = (zed < nt - 1) if side == 0 else (zed > 0)

            @pl.when(inside)
            def _(block=block, side=side):
                copy(rows(block, chunk), block, chunk, side).wait_recv()

            if distance < reach:

                @pl.when(jnp.logical_and(inside, open_end))
                def _(block=block, side=side):
                    copy(rows(block, chunk), block, chunk, side).start()

    def settle(chunk):
        keep(chunk).wait()

    def end(chunk):
        for side, condition in ((0, zed < nt - 1), (1, zed > 0)):

            @pl.when(condition)
            def _(side=side):
                copy(own_rows(chunk), zed, chunk, side).wait_send()

            for distance in range(1, reach):
                block = zed - distance if side == 0 else zed + distance
                inside = (block >= 0) if side == 0 else (block < nt)

                @pl.when(jnp.logical_and(inside, condition))
                def _(block=block, side=side):
                    copy(rows(block, chunk), block, chunk, side).wait_send()

    return first, onward, settle, end


def line_gather_semaphores(nt, chunks):
    return [pltpu.SemaphoreType.DMA((2, nt, chunks)), pltpu.SemaphoreType.DMA((nt, chunks))]


def line_reduce(nt, me, zed, chunks, parts, held, send, recv, chunked=False):
    block_rows = parts.shape[0] // nt
    size = block_rows // chunks
    def rows(block, chunk):
        if chunked:
            return aligned((chunk * nt + block) * size, size)
        return aligned(block * block_rows + chunk * size, size)

    def held_rows(side, block, chunk):
        return aligned((block + 1 - side) * block_rows + chunk * size, size)

    def copy(own, side, block, chunk):
        place = held_rows(side, block, chunk)
        return pltpu.make_async_remote_copy(
            src_ref=parts.at[rows(block, chunk)] if own else held.at[place],
            dst_ref=held.at[place],
            send_sem=send.at[side, block, chunk],
            recv_sem=recv.at[side, block, chunk],
            device_id=(me, zed + 1 - 2 * side),
            device_id_type=MESH,
        )

    def role(side, turn):
        away = nt - 1 - turn
        if side == 0:
            return zed + away, zed + away < nt, zed == 0
        return zed - away, zed - away >= 0, zed == nt - 1

    def pass_on(chunk, turn):
        for side in range(2):
            block, active, source = role(side, turn)

            @pl.when(jnp.logical_and(active, source))
            def _(side=side, block=block):
                copy(True, side, block, chunk).start()

            @pl.when(jnp.logical_and(active, jnp.logical_not(source)))
            def _(side=side, block=block):
                copy(False, side, block, chunk).wait_recv()
                mine, came = parts.at[rows(block, chunk)], held.at[held_rows(side, block, chunk)]

                def body(inner):
                    came[inner] = mine[inner] + came[inner]

                each_rows(size, body)
                copy(False, side, block, chunk).start()

    def own_sum(chunk, total):
        total[...] = parts[rows(zed, chunk)].astype(jnp.float32)
        for side in range(2):

            @pl.when(zed > 0 if side == 0 else zed < nt - 1)
            def _(side=side):
                copy(False, side, zed, chunk).wait_recv()
                total[...] += held[held_rows(side, zed, chunk)].astype(jnp.float32)

    def end(chunk):
        for turn in range(nt - 1):
            for side in range(2):
                block, active, source = role(side, turn)

                @pl.when(active)
                def _(side=side, block=block):
                    copy(False, side, block, chunk).wait_send()

    return pass_on, own_sum, end


def line_reduce_scratch(nt, block_rows, columns, chunks):
    return [
        pltpu.VMEM(((nt + 1) * block_rows, columns), jnp.bfloat16),
        pltpu.VMEM((block_rows // chunks, columns), jnp.float32),
        pltpu.SemaphoreType.DMA((2, nt, chunks)),
        pltpu.SemaphoreType.DMA((2, nt, chunks)),
    ]


HBM = pl.BlockSpec(memory_space=pl.ANY)
ONCHIP = pl.BlockSpec(memory_space=pltpu.VMEM)


def near_first(nt, zed, turn):
    block = 0
    for mine in range(nt):
        order = sorted(range(nt), key=lambda other: (abs(other - mine), other))
        block = block + jnp.where(zed == mine, order[turn], 0)
    return block


def first_gathers(nd, nt, rows, grad, small, main_own, out_own, shared_columns):
    chunks = LINE_CHUNKS
    bits = nd.bit_length() - 1
    blocks = relative_blocks(nd)
    block_rows, width = rows.shape
    lane = width // len(blocks)
    if lane % 128:
        rows, grad = to_relative(rows, 1, nd), to_relative(grad, 1, nd)
    main_columns, small_columns = main_own.shape[1], small.shape[1]
    side_columns = shared_columns + 2 * HEAD_SIZE
    gains_at = shared_columns + 2 * KEY_VALUE_HEADS * HEAD_SIZE
    tile = 256

    def reorder(me, source, target):
        if lane % 128:
            target[...] = source[...]
            return
        for number, (other, part) in enumerate(blocks):
            start = (mixed_with(me, other, bits) * 2 + part) * lane
            target[:, number * lane : (number + 1) * lane] = source[:, pl.ds(pl.multiple_of(start, lane), lane)]

    def kernel(
        rows_in, grad_in, small_ref, main_ref, out_ref,
        rows_ref, grad_ref, gains_ref, normed_all, grad_all, small_line, main_all, side_all, out_all, main_raw, side_raw,
        row_space, normed, main_space, small_space, side_space, main_stage, side_stage, store_sems, *refs,
    ):
        row_sems, small_sems, grad_sems = refs[:2], refs[2:4], refs[4:6]
        main_sems, small_dp, out_sems = refs[6:9], refs[9:12], refs[12:15]
        me, zed = enter(nt, bits)
        small_first, small_onward, small_settle, small_end = line_gather(
            nt, me, zed, 1, small_ref, small_line, *small_sems
        )
        row_first, row_onward, row_settle, row_end = line_gather(
            nt, me, zed, chunks, rows_ref, row_space, *row_sems
        )
        grad_first, grad_onward, grad_settle, grad_end = line_gather(
            nt, me, zed, chunks, grad_ref, grad_all, *grad_sems, chunked=True, reach=1
        )
        main_flow = gather_steps(nd, me, zed, main_ref, main_space, *main_sems)
        small_flow = gather_steps(nd, me, zed, small_line, small_space, *small_dp)
        out_flow = gather_steps(nd, me, zed, out_ref, out_all, *out_sems)
        head = zed * (QUERY_HEADS // nt) // (QUERY_HEADS // KEY_VALUE_HEADS)

        def columns(turn):
            if turn == 0:
                return small_space.at[:, pl.ds(0, shared_columns)], side_space.at[:, pl.ds(0, shared_columns)]
            start = shared_columns + ((turn - 1) * KEY_VALUE_HEADS + head) * HEAD_SIZE
            target = shared_columns + (turn - 1) * HEAD_SIZE
            return (
                small_space.at[:, pl.ds(pl.multiple_of(start, HEAD_SIZE), HEAD_SIZE)],
                side_space.at[:, pl.ds(target, HEAD_SIZE)],
            )

        def keep(number):
            source, target = ((main_space, main_all), (side_space, side_all), (normed, normed_all))[number]
            return pltpu.make_async_copy(source, target, store_sems.at[number])

        def pick(turn):
            return pltpu.make_async_copy(*columns(turn), store_sems.at[3 + turn])

        def store(turn, number):
            block = near_first(nt, zed, turn)
            stage, target = ((main_stage, main_raw), (side_stage, side_raw))[number]
            return pltpu.make_async_copy(
                stage.at[turn % 2],
                target.at[aligned(block * block_rows, block_rows)],
                store_sems.at[6 + 2 * turn + number],
            )

        def project(turn):
            where = aligned(near_first(nt, zed, turn) * block_rows, block_rows)
            value = (rows_ref[...] if turn == 0 else row_space[where]).astype(jnp.float32)
            scale = lax.rsqrt(jnp.mean(value * value, axis=-1, keepdims=True) + eps)
            mine = (value * scale * gains_ref[0:1]).astype(jnp.bfloat16)
            normed[where] = mine
            if turn >= 2:
                store(turn - 2, 0).wait()
                store(turn - 2, 1).wait()
            for space, stage, number in ((main_space, main_stage, 0), (side_space, side_stage, 1)):
                for start in range(0, space.shape[1], tile):
                    extent = slice(start, min(start + tile, space.shape[1]))
                    stage[turn % 2, :, extent] = jnp.dot(
                        mine, space[:, extent], preferred_element_type=jnp.float32
                    )
                store(turn, number).start()

        small_first(0)
        main_flow[0]()
        reorder(me, rows_in, rows_ref)
        for chunk in range(chunks):
            row_first(chunk)
        for distance in range(1, nt):
            small_onward(0, distance)
        small_settle(0)
        small_end(0)
        small_flow[0]()
        out_flow[0]()
        reorder(me, grad_in, grad_ref)
        near = [
            functools.partial(row_onward, chunk, distance) for distance in range(1, nt - 1) for chunk in range(chunks)
        ]
        together(near, main_flow[1:-1] + small_flow[1:-1])
        for chunk in range(chunks):
            grad_first(chunk)
        small_flow[-1]()
        for turn in range(3):
            pick(turn).start()
        for start in range(0, width, 128):
            turned_block = jnp.transpose(
                small_space[start : start + 128, gains_at : gains_at + 128].astype(jnp.float32)
            )
            gains_ref[:, start : start + 128] = turned_block[:8]
        main_flow[-1]()
        keep(0).start()
        for turn in range(3):
            pick(turn).wait()
        keep(1).start()

        def last_rows():
            for chunk in range(chunks):
                row_onward(chunk, nt - 1)

        def grads_from(distance):
            for chunk in range(chunks):
                grad_onward(chunk, distance)

        compute = [functools.partial(project, turn) for turn in range(nt - 1)] + [last_rows]
        together(compute, out_flow[1:-1])
        project(nt - 1)
        keep(2).start()
        grads_from(1)
        out_flow[-1]()
        for chunk in range(chunks):
            row_settle(chunk)
            row_end(chunk)
            grad_settle(chunk)
            grad_end(chunk)
        for turn in range(max(nt - 2, 0), nt):
            store(turn, 0).wait()
            store(turn, 1).wait()
        for number in range(3):
            keep(number).wait()

    def sized(array, times, dtype=None):
        return jax.ShapeDtypeStruct((array.shape[0] * times, array.shape[1]), dtype or array.dtype)

    tokens = block_rows * nt
    return pl.pallas_call(
        kernel,
        out_shape=[
            sized(rows, 1),
            sized(grad, 1),
            jax.ShapeDtypeStruct((8, width), jnp.float32),
            sized(rows, nt),
            sized(grad, nt),
            sized(small, nt),
            sized(main_own, nd),
            jax.ShapeDtypeStruct((width, side_columns), small.dtype),
            sized(out_own, nd),
            jax.ShapeDtypeStruct((tokens, main_columns), jnp.float32),
            jax.ShapeDtypeStruct((tokens, side_columns), jnp.float32),
        ],
        in_specs=[ONCHIP] * 2 + [HBM] * 3,
        out_specs=[ONCHIP] * 3 + [HBM] * 8,
        scratch_shapes=[
            pltpu.VMEM((tokens, width), jnp.bfloat16),
            pltpu.VMEM((tokens, width), jnp.bfloat16),
            pltpu.VMEM((width, main_columns), jnp.bfloat16),
            pltpu.VMEM((width, small_columns), jnp.bfloat16),
            pltpu.VMEM((width, side_columns), jnp.bfloat16),
            pltpu.VMEM((2, block_rows, main_columns), jnp.float32),
            pltpu.VMEM((2, block_rows, side_columns), jnp.float32),
            pltpu.SemaphoreType.DMA((6 + 2 * nt,)),
        ]
        + line_gather_semaphores(nt, chunks)
        + line_gather_semaphores(nt, 1)
        + line_gather_semaphores(nt, chunks)
        + gather_semaphores(nd) * 3,
        compiler_params=pltpu.CompilerParams(
            collective_id=0, has_side_effects=True, vmem_limit_bytes=VMEM_LIMIT
        ),
        name="first_gathers",
    )(rows, grad, small, main_own, out_own)


def second_neighbours(nt, grads):
    zed = lax.axis_index("tensor")
    width = grads.shape[1]
    blocks = grads.reshape(LINE_CHUNKS, nt, -1, width)
    below = lax.dynamic_slice_in_dim(blocks, jnp.maximum(zed - 1, 0), 1, 1).reshape(-1, width)
    above = lax.dynamic_slice_in_dim(blocks, jnp.minimum(zed + 1, nt - 1), 1, 1).reshape(-1, width)
    return (
        lax.ppermute(below, "tensor", [(i, i + 1) for i in range(1, nt - 1)]),
        lax.ppermute(above, "tensor", [(i, i - 1) for i in range(1, nt - 1)]),
    )


def middle_rows(nd, nt, mixed, out_w, resid, gain, grads, grads_below, grads_above, ffn_own):
    chunks = LINE_CHUNKS
    bits = nd.bit_length() - 1
    block_rows, width = resid.shape
    tokens = block_rows * nt
    size = block_rows // chunks
    ffn_columns = ffn_own.shape[1] // 3
    tile = 512

    def kernel(
        mixed_ref, out_ref, resid_ref, gain_ref, grads_ref, below_ref, above_ref, ffn_ref,
        middle_ref, rows_ref, hidden_ref, slopes_ref, grads_all, ffn_all,
        parts, grad_space, ffn_space, own, held, total, send, recv, gather_send, gather_recv,
        ffn_send, ffn_recv, ffn_local, store_sems, far_send, far_recv, far_space, second_sems,
    ):
        me, zed = enter(nt, bits)
        load = pltpu.make_async_copy(grads_ref, grad_space, store_sems.at[0])
        load.start()
        pass_on, own_sum, reduce_end = line_reduce(nt, me, zed, chunks, parts, held, send, recv)
        first, onward, settle, gather_end = line_gather(
            nt, me, zed, chunks, own, rows_ref, gather_send, gather_recv, chunked=True
        )
        flow = gather_steps(nd, me, zed, ffn_ref, ffn_space, ffn_send, ffn_recv, ffn_local)
        keeps = [
            pltpu.make_async_copy(grad_space, grads_all, store_sems.at[1]),
            pltpu.make_async_copy(ffn_space, ffn_all, store_sems.at[2]),
        ]

        def part(turn):
            where = aligned(near_first(nt, zed, nt - 1 - turn) * block_rows, block_rows)
            left = mixed_ref[where]
            for start in range(0, width, tile):
                extent = slice(start, start + tile)
                parts[where, extent] = product(left, out_ref[extent], LAST).astype(jnp.bfloat16)

        def second(action):
            for side, source in ((0, below_ref), (1, above_ref)):

                @pl.when(zed >= 2 if side == 0 else zed < nt - 2)
                def _(side=side, source=source):
                    block = zed - 2 if side == 0 else zed + 2
                    for chunk in range(chunks):
                        place = aligned((chunk * nt + block) * size, size)
                        action(
                            pltpu.make_async_copy(
                                source.at[pl.ds(chunk * size, size)], grad_space.at[place], second_sems.at[side, chunk]
                            )
                        )

        def far(chunk, up):
            block = 0 if up else nt - 1
            return pltpu.make_async_remote_copy(
                src_ref=grad_space.at[pl.ds((chunk * nt + block) * size, size)],
                dst_ref=far_space.at[pl.ds(chunk * size, size)],
                send_sem=far_send.at[chunk],
                recv_sem=far_recv.at[chunk],
                device_id=(me, nt - 1 if up else 0),
                device_id_type=MESH,
            )

        def far_begin():
            for up, sender in ((True, nt - 2), (False, 1)):

                @pl.when(zed == sender)
                def _(up=up):
                    for chunk in range(chunks):
                        far(chunk, up).start()

        def far_end():
            for up, sender in ((True, nt - 2), (False, 1)):

                @pl.when(zed == sender)
                def _(up=up):
                    for chunk in range(chunks):
                        far(chunk, up).wait_send()

                @pl.when(zed == (nt - 1 if up else 0))
                def _(up=up):
                    for chunk in range(chunks):
                        far(chunk, up).wait_recv()
                        start = (chunk * nt + (0 if up else nt - 1)) * size
                        grad_space[pl.ds(start, size)] = far_space[pl.ds(chunk * size, size)]

        def finish(chunk):
            own_sum(chunk, total)
            where = pl.ds(chunk * size, size)
            value = resid_ref[where].astype(jnp.float32) + total[...]
            middle_ref[where] = value
            scale = lax.rsqrt(jnp.mean(value * value, axis=-1, keepdims=True) + eps)
            own[where] = (value * scale * gain_ref[...]).astype(jnp.bfloat16)
            first(chunk)

        def feed(chunk):
            settle(chunk)
            where = pl.ds(chunk * nt * size, nt * size)
            rows, grads = rows_ref[where], grad_space[where]
            for start in range(0, ffn_columns, tile):
                columns = [slice(turn * ffn_columns + start, turn * ffn_columns + start + tile) for turn in range(3)]
                gate = product(rows, ffn_space[:, columns[0]])
                upper = product(rows, ffn_space[:, columns[1]])
                grad = product(grads, ffn_space[:, columns[2]])
                sigma = jax.nn.sigmoid(gate)
                through = gate * sigma
                hidden_ref[where, columns[0]] = (through * upper).astype(jnp.bfloat16)
                slopes_ref[where, columns[0]] = (grad * upper * silu_slope(gate, sigma)).astype(jnp.bfloat16)
                slopes_ref[where, columns[1]] = (grad * through).astype(jnp.bfloat16)

        flow[0]()
        part(0)
        for chunk in range(chunks):
            pass_on(chunk, 0)
        load.wait()
        second(lambda copy: copy.start())
        for turn in range(1, nt):
            part(turn)
        second(lambda copy: copy.wait())
        far_begin()
        steps = line_steps(nt, chunks, pass_on, finish, onward)
        drain = nt
        together(steps[:-drain], flow[1:] + [far_end])
        for keep in keeps:
            keep.start()
        feeds = [functools.partial(feed, chunk) for chunk in range(chunks)]
        for number, step in enumerate(steps[-drain:]):
            if 0 < number < drain and feeds and number - 1 < chunks - 1:
                feeds.pop(0)()
            step()
        for step in feeds:
            step()
        for chunk in range(chunks):
            reduce_end(chunk)
            gather_end(chunk)
        for keep in keeps:
            keep.wait()

    return pl.pallas_call(
        kernel,
        out_shape=[
            jax.ShapeDtypeStruct((block_rows, width), jnp.float32),
            jax.ShapeDtypeStruct((tokens, width), jnp.bfloat16),
            jax.ShapeDtypeStruct((tokens, ffn_columns), jnp.bfloat16),
            jax.ShapeDtypeStruct((tokens, 2 * ffn_columns), jnp.bfloat16),
            jax.ShapeDtypeStruct((tokens, width), jnp.bfloat16),
            jax.ShapeDtypeStruct((width, 3 * ffn_columns), jnp.bfloat16),
        ],
        in_specs=[ONCHIP] * 4 + [HBM] * 4,
        out_specs=[ONCHIP] * 4 + [HBM] * 2,
        scratch_shapes=[
            pltpu.VMEM((tokens, width), jnp.bfloat16),
            pltpu.VMEM((tokens, width), jnp.bfloat16),
            pltpu.VMEM((width, 3 * ffn_columns), jnp.bfloat16),
            pltpu.VMEM((block_rows, width), jnp.bfloat16),
        ]
        + line_reduce_scratch(nt, block_rows, width, chunks)
        + line_gather_semaphores(nt, chunks)
        + gather_semaphores(nd)
        + [
            pltpu.SemaphoreType.DMA((3,)),
            pltpu.SemaphoreType.DMA((chunks,)),
            pltpu.SemaphoreType.DMA((chunks,)),
            pltpu.VMEM((block_rows, width), jnp.bfloat16),
            pltpu.SemaphoreType.DMA((2, chunks)),
        ],
        compiler_params=pltpu.CompilerParams(
            collective_id=1, has_side_effects=True, vmem_limit_bytes=LARGE_LIMIT
        ),
        name="middle_rows",
    )(mixed, out_w, resid, gain, grads, grads_below, grads_above, ffn_own)


def absolute_lanes(me, bits, blocks, source, target):
    lane = source.shape[1] // len(blocks)
    for number, (other, part) in enumerate(blocks):
        start = (mixed_with(me, other, bits) * 2 + part) * lane
        target[:, pl.ds(pl.multiple_of(start, lane), lane)] = source[:, number * lane : (number + 1) * lane]


def norm_pull(value, gain, grad):
    scale = lax.rsqrt(jnp.mean(value * value, axis=-1, keepdims=True) + eps)
    scaled = grad * gain
    inner = jnp.mean(scaled * value, axis=-1, keepdims=True)
    return scale * (scaled - value * (inner * scale * scale)), grad * value * scale


def line_steps(nt, chunks, pass_on, finish, onward, settle=None):
    steps = []

    def add(function, chunk, *rest):
        if 0 <= chunk < chunks:
            steps.append(functools.partial(function, chunk, *rest))

    for chunk in range(chunks + 2):
        add(finish, chunk - 1)
        add(onward, chunk - 2, nt - 1)
        for turn in range(1, nt - 1):
            add(pass_on, chunk, turn)
            add(onward, chunk - 1, turn)
    return steps


def middle_back(nd, nt, slopes, hidden, rows, grads, ffn_w, middle, cot, gain):
    chunks = LINE_CHUNKS
    bits = nd.bit_length() - 1
    block_rows, width = middle.shape
    tokens = block_rows * nt
    size = block_rows // chunks
    blocks = relative_blocks(nd)
    lane = width // len(blocks)
    ffn_columns = hidden.shape[1]
    out_rows = width // nd
    tile = 512

    def kernel(
        slopes_in, hidden_in, rows_in, grads_in, ffn_ref, middle_ref, cot_ref, gain_ref,
        grad_ref, gain_out, rows_all, out_all, gate_total, up_total, down_total,
        slopes_ref, hidden_ref, rows_ref, grads_ref, weights, down_weights, load_sems, parts, own, gain_grad,
        out_stage, out_sems,
        line_held, total, send, recv, gather_send, gather_recv, *refs,
    ):
        loads = [
            pltpu.make_async_copy(source, target, load_sems.at[number])
            for number, (source, target) in enumerate(
                (
                    (ffn_ref.at[:, pl.ds(0, 2 * ffn_columns)], weights),
                    (slopes_in, slopes_ref),
                    (rows_in, rows_ref),
                    (hidden_in, hidden_ref),
                    (grads_in, grads_ref),
                    (ffn_ref.at[:, pl.ds(2 * ffn_columns, ffn_columns)], down_weights),
                )
            )
        ]
        for load in loads:
            load.start()
        me, zed = enter(nt, bits)
        pass_on, own_sum, reduce_end = line_reduce(nt, me, zed, chunks, parts, line_held, send, recv, chunked=True)
        first, onward, settle, gather_end = line_gather(nt, me, zed, chunks, own, rows_all, gather_send, gather_recv)
        half = nd * out_rows // 2
        scatters = [
            computed_scatter(
                nd, me, zed, out_rows // 2, products_of(rows_ref, ((slopes_ref, 2 * ffn_columns),), tile),
                weights.at[pl.ds(0, half)], *refs[:2],
                ((gate_total, 0, ffn_columns), (up_total, ffn_columns, ffn_columns)), *refs[2:6],
            ),
            computed_scatter(
                nd, me, zed, out_rows // 2, products_of(grads_ref, ((hidden_ref, ffn_columns),), tile),
                weights.at[pl.ds(half, half), pl.ds(0, ffn_columns)], *refs[6:8],
                ((down_total, 0, ffn_columns),), *refs[8:12],
            ),
        ]
        gain_grad[...] = jnp.zeros_like(gain_grad)

        def out_copy(chunk, block):
            return pltpu.make_async_copy(
                out_stage.at[pl.ds(block * size, size)],
                out_all.at[pl.ds(block * block_rows + chunk * size, size)],
                out_sems.at[chunk, block],
            )

        def feed_out(chunk):
            if chunk > 0:
                for block in range(nt):
                    out_copy(chunk - 1, block).wait()
            left = hidden_ref[pl.ds(chunk * nt * size, nt * size)]
            for start in range(0, width, tile):
                extent = slice(start, start + tile)
                out_stage[:, extent] = product(left, down_weights[extent], LAST).astype(jnp.bfloat16)
            for block in range(nt):
                out_copy(chunk, block).start()

        def part(chunk):
            where = pl.ds(chunk * nt * size, nt * size)
            left = slopes_ref[where]
            for start in range(0, width, tile):
                extent = slice(start, start + tile)
                parts[where, extent] = product(left, weights[extent], LAST).astype(jnp.bfloat16)

        def finish(chunk):
            own_sum(chunk, total)
            where = pl.ds(chunk * size, size)
            through, gained = norm_pull(middle_ref[where], gain_ref[...], total[...])
            value = cot_ref[where].astype(jnp.float32) + through
            gain_grad[...] += jnp.sum(gained, axis=0, keepdims=True)
            grad_ref[where] = value
            own[where] = value.astype(jnp.bfloat16)
            first(chunk)

        loads[0].wait()
        loads[1].wait()
        for chunk in range(chunks):
            part(chunk)
            pass_on(chunk, 0)
        for load in loads[2:]:
            load.wait()
        over = []
        for number in range(2):
            over = over + [step for pair in zip(scatters[0][number], scatters[1][number]) for step in pair]
        for number in range(len(scatters[0][2])):
            over = over + scatters[0][2][number] + scatters[1][2][number]
            if number == 0:
                over = over + [functools.partial(feed_out, chunk) for chunk in range(chunks)]
        together(line_steps(nt, chunks, pass_on, finish, onward), over)
        for scatter in scatters:
            scatter[3]()
        for block in range(nt):
            out_copy(chunks - 1, block).wait()
        for chunk in range(chunks):
            reduce_end(chunk)
            settle(chunk)
            gather_end(chunk)
        if lane % 128:
            gain_out[...] = gain_grad[...]
        else:
            absolute_lanes(me, bits, blocks, gain_grad, gain_out)

    results = pl.pallas_call(
        kernel,
        out_shape=[
            jax.ShapeDtypeStruct((block_rows, width), jnp.float32),
            jax.ShapeDtypeStruct((1, width), jnp.float32),
            jax.ShapeDtypeStruct((tokens, width), jnp.bfloat16),
            jax.ShapeDtypeStruct((tokens, width), jnp.bfloat16),
        ]
        + [jax.ShapeDtypeStruct((out_rows, ffn_columns), jnp.float32)] * 3,
        in_specs=[HBM] * 5 + [ONCHIP] * 3,
        out_specs=[ONCHIP, ONCHIP, HBM, HBM] + [ONCHIP] * 3,
        scratch_shapes=[
            pltpu.VMEM(slopes.shape, jnp.bfloat16),
            pltpu.VMEM(hidden.shape, jnp.bfloat16),
            pltpu.VMEM(rows.shape, jnp.bfloat16),
            pltpu.VMEM(grads.shape, jnp.bfloat16),
            pltpu.VMEM((width, 2 * ffn_columns), jnp.bfloat16),
            pltpu.VMEM((width, ffn_columns), jnp.bfloat16),
            pltpu.SemaphoreType.DMA((6,)),
            pltpu.VMEM((tokens, width), jnp.bfloat16),
            pltpu.VMEM((block_rows, width), jnp.bfloat16),
            pltpu.VMEM((1, width), jnp.float32),
            pltpu.VMEM((nt * size, width), jnp.bfloat16),
            pltpu.SemaphoreType.DMA((chunks, nt)),
        ]
        + line_reduce_scratch(nt, block_rows, width, chunks)
        + line_gather_semaphores(nt, chunks)
        + computed_scratch(nd, out_rows, 2 * ffn_columns)[1:]
        + computed_scratch(nd, out_rows, ffn_columns)[1:],
        compiler_params=pltpu.CompilerParams(
            collective_id=2, has_side_effects=True, vmem_limit_bytes=LARGE_LIMIT
        ),
        name="middle_back",
    )(slopes, hidden, rows, grads, ffn_w, middle, cot, gain)
    if lane % 128:
        results = (results[0], from_relative(results[1], 1, nd), *results[2:])
    return results


def last_sums(nd, nt, normed, grad_main, grad_side, main, side, resid, before, gain, small, shared_rows, main_widths):
    chunks = LINE_CHUNKS
    bits, line_bits = nd.bit_length() - 1, nt.bit_length() - 1
    block_rows, width = resid.shape
    tokens = block_rows * nt
    size = block_rows // chunks
    blocks = relative_blocks(nd)
    lane = width // len(blocks)
    main_columns, side_columns = main.shape[1], side.shape[1]
    shared_columns = side_columns - 2 * HEAD_SIZE
    side_rows = width // nd
    owned = side_rows // nt
    common_columns = shared_columns + 2 * KEY_VALUE_HEADS * HEAD_SIZE
    count = len(main_widths)
    if lane % 128:
        gain_part = jnp.sum(
            (contract_last(grad_main, main) + contract_last(grad_side, side)) * normed.astype(jnp.float32), axis=0
        )
        own_gain = from_relative(gain_part / gain[0], 0, nd)
        small = jnp.concatenate([own_gain.reshape(-1, 128), small[width // 128 :]])

    def kernel(normed_ref, grad_main_ref, grad_side_ref, main_ref, side_ref, resid_ref, before_ref, gain_ref, small_ref, *refs):
        grad_ref, small_out, common_ref = refs[:3]
        totals, refs = refs[3 : 3 + count], refs[3 + count :]
        parts_ref, side_total, line_held, total, send, recv = refs[:6]
        sums, landed, small_send, small_recv, gain_grad = refs[6:11]
        side_out, side_in, side_send, side_recv = refs[11:15]
        stage, held, hop_landed, core_send, core_recv, hop_send, hop_recv = refs[15:]
        me, zed = enter(nt, bits)
        pass_on, own_sum, reduce_end = line_reduce(nt, me, zed, chunks, parts_ref, line_held, send, recv)
        targets, at = [], 0
        for target, columns in zip(totals, main_widths):
            targets.append((target, at, columns))
            at = at + columns
        targets.append((side_total, main_columns, side_columns))
        away, near, later, scatter_end = computed_scatter(
            nd, me, zed, side_rows // 2,
            products_of(normed_ref, ((grad_main_ref, main_columns), (grad_side_ref, side_columns)), 512),
            stage, held, hop_landed, targets, core_send, core_recv, hop_send, hop_recv,
        )

        def part(turn):
            def step():
                where = aligned(near_first(nt, zed, nt - 1 - turn) * block_rows, block_rows)
                left, right = grad_main_ref[where], grad_side_ref[where]
                for start in range(0, width, 512):
                    extent = slice(start, start + 512)
                    value = product(left, main_ref[extent], LAST) + product(right, side_ref[extent], LAST)
                    parts_ref[where, extent] = value.astype(jnp.bfloat16)

            return step

        def gain_term(number):
            def step():
                if number == 0:
                    gain_grad[...] = jnp.zeros_like(gain_grad)

                def body(inner, carry):
                    where = aligned(number * block_rows + inner * 16, 16)
                    gain_grad[...] += parts_ref[where].astype(jnp.float32) * normed_ref[where].astype(jnp.float32)
                    return carry

                lax.fori_loop(0, block_rows // 16, body, 0)

            return step

        def small_copy(turn):
            if turn < bits:
                device = (flip(me, turn), zed)
            else:
                device = (me, flip(zed, turn - bits))
            extent = slice(None) if turn < bits else pl.ds(0, shared_rows)
            return pltpu.make_async_remote_copy(
                src_ref=sums.at[turn, extent],
                dst_ref=landed.at[turn, extent],
                send_sem=small_send.at[turn],
                recv_sem=small_recv.at[turn],
                device_id=device,
                device_id_type=MESH,
            )

        def small_begin():
            sums[0] = small_ref[...]
            if lane % 128 == 0:
                whole = jnp.sum(gain_grad[...], axis=0, keepdims=True) / gain_ref[...]
                for number, (other, half) in enumerate(blocks):
                    spot = mixed_with(me, other, bits) * 2 + half
                    sums[0, pl.ds(spot, 1), :] = whole[:, number * lane : (number + 1) * lane]
            small_copy(0).start()

        def small_step(turn):
            def step():
                small_copy(turn).wait_recv()
                if turn < bits:
                    sums[turn + 1] = sums[turn] + landed[turn]
                else:
                    sums[turn + 1] = sums[turn]
                    sums[turn + 1, pl.ds(0, shared_rows)] = (
                        sums[turn, pl.ds(0, shared_rows)] + landed[turn, pl.ds(0, shared_rows)]
                    )
                if turn + 1 < bits + line_bits:
                    small_copy(turn + 1).start()

            return step

        def small_end():
            for turn in range(bits + line_bits):
                small_copy(turn).wait_send()
            small_out[...] = sums[bits + line_bits]

        few = [gain_term(number) for number in range(nt if lane % 128 == 0 else 0)]
        few = few + [small_begin] + [small_step(turn) for turn in range(bits + line_bits)]

        def side_copy(source, target):
            return pltpu.make_async_remote_copy(
                src_ref=side_out.at[pl.ds(target * owned, owned)],
                dst_ref=side_in.at[source],
                send_sem=side_send.at[target],
                recv_sem=side_recv.at[source],
                device_id=(me, target),
                device_id_type=MESH,
            )

        def side_begin():
            side_out[...] = side_total[...].astype(jnp.bfloat16)
            for target in range(nt):

                @pl.when(zed != target)
                def _(target=target):
                    side_copy(zed, target).start()

            side_in[zed] = side_out[aligned(zed * owned, owned)]

        def side_end():
            for source in range(nt):

                @pl.when(zed != source)
                def _(source=source):
                    side_copy(source, source).wait_recv()

            common_ref[...] = jnp.zeros_like(common_ref)
            for source in range(nt):
                value = side_in[source].astype(jnp.float32)
                head = source * (QUERY_HEADS // nt) // (QUERY_HEADS // KEY_VALUE_HEADS)
                common_ref[:, :shared_columns] += value[:, :shared_columns]
                for turn in range(2):
                    at = shared_columns + (turn * KEY_VALUE_HEADS + head) * HEAD_SIZE
                    start = shared_columns + turn * HEAD_SIZE
                    common_ref[:, at : at + HEAD_SIZE] += value[:, start : start + HEAD_SIZE]
            for target in range(nt):

                @pl.when(zed != target)
                def _(target=target):
                    side_copy(zed, target).wait_send()

        def finish(chunk):
            own_sum(chunk, total)
            where = pl.ds(chunk * size, size)
            through, _ = norm_pull(resid_ref[where].astype(jnp.float32), gain_ref[...], total[...])
            value = before_ref[where] + through
            if lane % 128:
                grad_ref[where] = value
                return
            for number, (other, half) in enumerate(blocks):
                start = (mixed_with(me, other, bits) * 2 + half) * lane
                grad_ref[where, pl.ds(pl.multiple_of(start, lane), lane)] = value[:, number * lane : (number + 1) * lane]

        def passes(turn):
            return [functools.partial(pass_on, chunk, turn) for chunk in range(chunks)]

        middle = len(away) // 2
        steps = away[:middle] + [part(0)] + passes(0) + away[middle:] + [part(1)] + near[:middle]
        for turn in range(2, nt):
            steps.append(part(turn))
        steps = steps + passes(1) + near[middle:]
        for stage_steps in later[:-1]:
            steps = steps + stage_steps
        for turn in range(2, nt - 1):
            steps = steps + passes(turn)
        steps = steps + few[: -(bits + line_bits)] + later[-1] + [side_begin]
        ends = [functools.partial(finish, chunk) for chunk in range(chunks)]
        rest = few[-(bits + line_bits) :]
        for step in steps:
            step()
        together(ends, rest)
        side_end()
        small_end()
        scatter_end()
        for chunk in range(chunks):
            reduce_end(chunk)

    turns = bits + line_bits
    results = pl.pallas_call(
        kernel,
        out_shape=[
            jax.ShapeDtypeStruct((block_rows, width), jnp.float32),
            jax.ShapeDtypeStruct(small.shape, jnp.float32),
            jax.ShapeDtypeStruct((owned, common_columns), jnp.float32),
        ]
        + [jax.ShapeDtypeStruct((side_rows, columns), jnp.float32) for columns in main_widths],
        in_specs=[ONCHIP] * 9,
        out_specs=[ONCHIP] * (3 + count),
        scratch_shapes=[
            pltpu.VMEM((tokens, width), jnp.bfloat16),
            pltpu.VMEM((side_rows, side_columns), jnp.float32),
        ]
        + line_reduce_scratch(nt, block_rows, width, chunks)
        + [
            pltpu.VMEM((turns + 1, *small.shape), jnp.float32),
            pltpu.VMEM((turns, *small.shape), jnp.float32),
            pltpu.SemaphoreType.DMA((turns,)),
            pltpu.SemaphoreType.DMA((turns,)),
            pltpu.VMEM((16, width), jnp.float32),
            pltpu.VMEM((side_rows, side_columns), jnp.bfloat16),
            pltpu.VMEM((nt, owned, side_columns), jnp.bfloat16),
            pltpu.SemaphoreType.DMA((nt,)),
            pltpu.SemaphoreType.DMA((nt,)),
        ]
        + computed_scratch(nd, side_rows, main_columns + side_columns),
        compiler_params=pltpu.CompilerParams(
            collective_id=3, has_side_effects=True, vmem_limit_bytes=LARGE_LIMIT
        ),
        name="last_sums",
    )(normed, grad_main, grad_side, main, side, resid, before, gain, small)
    if lane % 128:
        results = (from_relative(results[0], 1, nd), *results[1:])
    return results


def silu_slope(value, sig):
    return sig * (1.0 + value * (1.0 - sig))


def split_dot(value, constant, dims, terms):
    total = None
    for _ in range(terms):
        piece = value.astype(jnp.bfloat16)
        value = value - piece.astype(jnp.float32)
        part = lax.dot_general(*((piece, constant) if dims[0] else (constant, piece)), dims[1], preferred_element_type=jnp.float32)
        total = part if total is None else total + part
    return total


PLAIN = (((1,), (0,)), ((), ()))
LAST = (((1,), (1,)), ((), ()))
FIRST = (((0,), (0,)), ((), ()))


def product(left, right, dims=PLAIN):
    return lax.dot_general(left, right, dims, preferred_element_type=jnp.float32)


def turned(value, cosine, sine):
    return value * cosine + pltpu.roll(value, value.shape[-1] // 2, 1) * sine


class Sizes:
    def __init__(self, channels, state_columns, query_columns, heads, length):
        self.channels, self.states = channels, state_columns // 2
        self.query, self.heads, self.length = query_columns, heads, length
        self.span = SPAN
        self.count = length // SPAN
        self.wide = channels + state_columns
        self.head_width = channels // heads
        self.step_at = 2 * channels + query_columns
        self.main = self.step_at + heads + (-(self.step_at + heads)) % 128
        self.step_lanes = self.main - self.step_at
        self.side = state_columns + 2 * HEAD_SIZE
        self.window = min(length, 3 * SPAN)


def spread_heads(size):
    table = np.zeros((size.step_lanes, size.channels), np.float32)
    for head in range(size.heads):
        table[head, head * size.head_width : (head + 1) * size.head_width] = 1.0
    return table.astype(jnp.bfloat16)


def turn_tables(length):
    half = HEAD_SIZE // 2
    angle = np.arange(length, dtype=np.float64)[:, None] * rope_base ** (-np.arange(half) / half)[None]
    cosine, sine = np.cos(angle), np.sin(angle)
    return (
        np.concatenate([cosine, cosine], 1).astype(np.float32),
        np.concatenate([-sine, sine], 1).astype(np.float32),
    )


def token_flags(segments, taps):
    seg = segments[0]
    length = seg.shape[0]
    ends = jnp.broadcast_to(seg.reshape(-1, SPAN)[:, -1:], (length // SPAN, SPAN)).reshape(-1)
    before = jnp.pad(ends, (SPAN, 0), constant_values=-1)[:length]
    lines = [seg == seg]
    lines = lines + [jnp.pad(seg, (lag, 0), constant_values=-1)[:length] == seg for lag in range(1, taps)]
    lines = lines + [before == seg, ends == seg]
    lines = lines + [jnp.pad(seg, (0, lag), constant_values=-1)[lag:] == seg for lag in range(1, taps)]
    lines = lines + [jnp.zeros((length,), bool)] * (16 - len(lines))
    return jnp.stack(lines).astype(jnp.float32).T


def chunk_values(size, taps, main_ref, wide_ref, flags, spread, taps_ref, heads_ref, segc, segr):
    span = size.span
    pre = wide_ref[pl.ds(8, span), :] * taps_ref[0:1, :]
    for lag in range(1, taps):
        pre = pre + wide_ref[pl.ds(8 - lag, span), :] * (flags[:, lag : lag + 1] * taps_ref[lag : lag + 1, :])
    sig = jax.nn.sigmoid(pre)
    act = pre * sig
    inner = act[:, : size.channels]
    bmat = act[:, size.channels : size.channels + size.states].astype(jnp.bfloat16)
    cmat = act[:, size.channels + size.states :].astype(jnp.bfloat16)
    step_in = main_ref[:, size.step_at :] + heads_ref[0:1, :]
    step = jnp.maximum(step_in, 0.0) + jnp.log1p(jnp.exp(-jnp.abs(step_in)))
    logdec = -step * heads_ref[1:2, :]
    rows = lax.broadcasted_iota(jnp.int32, (span, span), 0)
    columns = lax.broadcasted_iota(jnp.int32, (span, span), 1)
    later = jnp.where(rows >= columns, 1.0, 0.0).astype(jnp.bfloat16)
    cumul = split_dot(logdec, later, (False, PLAIN), 3)
    inside = jnp.logical_and(rows >= columns, segc == segr)
    ending = cumul[span - 1 : span, :]
    reach = jnp.exp(cumul) * flags[:, 4:5]
    tail = jnp.exp(ending - cumul) * flags[:, 5:6]
    step_wide = split_dot(step, spread, (True, PLAIN), 2)
    scaled = inner * step_wide
    return dict(
        pre=pre, sig=sig, inner=inner, bmat=bmat, cmat=cmat, step_in=step_in, step=step, logdec=logdec, later=later,
        cumul=cumul, turned=jnp.transpose(cumul), inside=inside, step_wide=step_wide, scaled=scaled,
        scaled_b=scaled.astype(jnp.bfloat16), meeting=product(cmat, bmat, LAST),
        reach_wide=split_dot(reach, spread, (True, PLAIN), 2), tail_wide=split_dot(tail, spread, (True, PLAIN), 2),
        skip_wide=split_dot(jnp.broadcast_to(heads_ref[2:3, :], (8, size.step_lanes)), spread, (True, PLAIN), 2)[0:1],
    )


def decay_of(values, head):
    spread = values["cumul"][:, head : head + 1] - values["turned"][head : head + 1, :]
    return jnp.exp(jnp.where(values["inside"], spread, -1e30))


def softmax_of(size, query, keys, chunk, start, segc, seg_all):
    scores = product(query, keys, LAST) * (1.0 / math.sqrt(HEAD_SIZE))
    rows = lax.broadcasted_iota(jnp.int32, scores.shape, 0) + chunk * size.span
    columns = lax.broadcasted_iota(jnp.int32, scores.shape, 1) + start
    allowed = jnp.logical_and(rows >= columns, segc == seg_all)
    masked = jnp.where(allowed, scores, -1e30)
    expo = jnp.exp(masked - jnp.max(masked, axis=-1, keepdims=True))
    return expo / jnp.sum(expo, axis=-1, keepdims=True)


def mixers_forward(size, taps, main_raw, side_raw, segments, flags, tap_rows, head_rows):
    span = size.span
    per_head = size.head_width

    def kernel(
        main_ref, side_ref, segc_ref, segr_ref, flags_ref, taps_ref, heads_ref, cos_ref, sin_ref, spread_ref,
        mixed_ref, y_ref, state_ref, keys_ref, values_ref, wide, state,
    ):
        chunk = pl.program_id(0)

        @pl.when(chunk == 0)
        def _():
            wide[0:8, :] = jnp.zeros((8, size.wide), jnp.float32)
            state[...] = jnp.zeros_like(state)
            keys_ref[...] = jnp.zeros_like(keys_ref)
            values_ref[...] = jnp.zeros_like(values_ref)

        wide[pl.ds(8, span), : size.channels] = main_ref[:, size.channels : 2 * size.channels]
        wide[pl.ds(8, span), size.channels :] = side_ref[:, : 2 * size.states]
        flags, spread, segc = flags_ref[...], spread_ref[...], segc_ref[...]
        segr = segr_ref[:, pl.ds(pl.multiple_of(chunk * span, span), span)]
        val = chunk_values(size, taps, main_ref, wide, flags, spread, taps_ref, heads_ref, segc, segr)
        wide[0:8, :] = wide[pl.ds(span, 8), :]
        held = state[...]
        held_b = held.astype(jnp.bfloat16)
        state_ref[...] = held
        across = val["reach_wide"] * product(val["cmat"], held_b)
        lane = lax.broadcasted_iota(jnp.int32, (span, 2 * per_head), 1)
        for pair in range(size.heads // 2):
            where = slice(pair * 2 * per_head, (pair + 1) * 2 * per_head)
            both = []
            for head in (2 * pair, 2 * pair + 1):
                weights = (val["meeting"] * decay_of(val, head)).astype(jnp.bfloat16)
                both.append(product(weights, val["scaled_b"][:, where]))
            result = jnp.where(lane < per_head, both[0], both[1])
            result = result + across[:, where] + val["skip_wide"][:, where] * val["inner"][:, where]
            y_ref[:, where] = result
            gate = main_ref[:, where]
            mixed_ref[:, where] = (result * (gate * jax.nn.sigmoid(gate))).astype(jnp.bfloat16)
        keep = jnp.broadcast_to(val["reach_wide"][span - 1 : span, :], (1, size.channels))
        state[...] = keep * held + product(
            val["bmat"], (val["tail_wide"] * val["scaled"]).astype(jnp.bfloat16), FIRST
        )

        cosine, sine = cos_ref[...], sin_ref[...]
        own = pl.ds(pl.multiple_of(chunk * span, span), span)
        key_at = 2 * size.states
        keys_ref[own, :] = turned(side_ref[:, key_at : key_at + HEAD_SIZE], cosine, sine).astype(jnp.bfloat16)
        values_ref[own, :] = side_ref[:, key_at + HEAD_SIZE :].astype(jnp.bfloat16)
        start = pl.multiple_of(jnp.maximum(chunk + 1 - size.window // span, 0) * span, span)
        seen = pl.ds(start, size.window)
        for head in range(size.query // HEAD_SIZE):
            at = 2 * size.channels + head * HEAD_SIZE
            query = turned(main_ref[:, at : at + HEAD_SIZE], cosine, sine).astype(jnp.bfloat16)
            probs = softmax_of(size, query, keys_ref[seen, :], chunk, start, segc, segr_ref[:, seen])
            result = product(probs.astype(jnp.bfloat16), values_ref[seen, :])
            at = size.channels + head * HEAD_SIZE
            mixed_ref[:, at : at + HEAD_SIZE] = result.astype(jnp.bfloat16)

    def rows(columns):
        return pl.BlockSpec((span, columns), lambda i: (i, 0))

    def whole(array):
        return pl.BlockSpec(array.shape, lambda i: (0, 0))

    cosine, sine = turn_tables(size.length)
    spread = spread_heads(size)
    tokens = size.length
    return pl.pallas_call(
        kernel,
        grid=(size.count,),
        in_specs=[
            rows(size.main), rows(size.side), rows(1), whole(segments), rows(16), whole(tap_rows), whole(head_rows),
            rows(HEAD_SIZE), rows(HEAD_SIZE), whole(spread),
        ],
        out_specs=[
            rows(size.channels + size.query), rows(size.channels),
            pl.BlockSpec((size.states, size.channels), lambda i: (i, 0)),
            pl.BlockSpec((tokens, HEAD_SIZE), lambda i: (0, 0)), pl.BlockSpec((tokens, HEAD_SIZE), lambda i: (0, 0)),
        ],
        out_shape=[
            jax.ShapeDtypeStruct((tokens, size.channels + size.query), jnp.bfloat16),
            jax.ShapeDtypeStruct((tokens, size.channels), jnp.float32),
            jax.ShapeDtypeStruct((size.count * size.states, size.channels), jnp.float32),
            jax.ShapeDtypeStruct((tokens, HEAD_SIZE), jnp.bfloat16),
            jax.ShapeDtypeStruct((tokens, HEAD_SIZE), jnp.bfloat16),
        ],
        scratch_shapes=[
            pltpu.VMEM((span + 8, size.wide), jnp.float32),
            pltpu.VMEM((size.states, size.channels), jnp.float32),
        ],
        compiler_params=pltpu.CompilerParams(
            dimension_semantics=("arbitrary",), vmem_limit_bytes=VMEM_LIMIT
        ),
        cost_estimate=pl.CostEstimate(flops=20 * 10**9, bytes_accessed=25 * 10**6, transcendentals=5 * 10**6),
        name="mixers_forward",
    )(main_raw, side_raw, segments.reshape(tokens, 1), segments, flags, tap_rows, head_rows,
      jnp.asarray(cosine), jnp.asarray(sine), jnp.asarray(spread))


def mixers_backward(
    nd, nt, size, taps, out_w, main_raw, side_raw, segments, flags, tap_rows, head_rows, y_value, states, keys, values,
    grad_rows, mixed,
):
    bits = nd.bit_length() - 1
    out_rows, out_columns = grad_rows.shape[1] // nd, mixed.shape[1]
    span = size.span
    per_head = size.head_width
    count = size.count

    def kernel(
        out_ref, main_ref, side_ref, before_ref, side_before_ref, segc_ref, segr_ref, flags_ref, taps_ref, heads_ref,
        cos_ref, sin_ref, spread_ref, y_ref, state_ref, keys_ref, values_ref, rows_ref, mixed_ref,
        grad_main, grad_side, tap_sums, head_sums, mixer_total, attn_total,
        wide, back, grad_state, grad_keys, grad_values, grad_ref,
        stage, held, landed, core_send, core_recv, hop_send, hop_recv,
    ):
        turn = pl.program_id(0)
        chunk = count - 1 - turn
        me, zed = lax.axis_index("dp"), lax.axis_index("tensor")
        away, near, later, scatter_end = computed_scatter(
            nd, me, zed, out_rows // 2, products_of(rows_ref, ((mixed_ref, out_columns),), 512), stage, held, landed,
            ((mixer_total, 0, size.channels), (attn_total, size.channels, size.query)),
            core_send, core_recv, hop_send, hop_recv,
        )
        stages = [away, near, *later[: count - 3], [step for stage_steps in later[count - 3 :] for step in stage_steps]]
        for number, stage_steps in enumerate(stages):

            @pl.when(turn == number)
            def _(number=number, stage_steps=stage_steps):
                if number == 0:
                    enter(nt, bits)
                for step in stage_steps:
                    step()
                if number == len(stages) - 1:
                    scatter_end()

        @pl.when(turn == 0)
        def _():
            back[pl.ds(span, 8), :] = jnp.zeros((8, size.wide), jnp.float32)
            grad_state[...] = jnp.zeros_like(grad_state)
            grad_keys[...] = jnp.zeros_like(grad_keys)
            grad_values[...] = jnp.zeros_like(grad_values)
            tap_sums[...] = jnp.zeros_like(tap_sums)
            head_sums[...] = jnp.zeros_like(head_sums)

        own_rows = rows_ref[pl.ds(pl.multiple_of(chunk * span, span), span), :]
        for start in range(0, out_columns, 512):
            extent = slice(start, start + 512)
            grad_ref[:, extent] = product(own_rows, out_ref[:, extent])
        wide[0:8, : size.channels] = before_ref[...]
        wide[0:8, size.channels :] = side_before_ref[...]
        wide[pl.ds(8, span), : size.channels] = main_ref[:, size.channels : 2 * size.channels]
        wide[pl.ds(8, span), size.channels :] = side_ref[:, : 2 * size.states]
        flags, spread, segc = flags_ref[...], spread_ref[...], segc_ref[...]
        segr = segr_ref[:, pl.ds(pl.multiple_of(chunk * span, span), span)]
        val = chunk_values(size, taps, main_ref, wide, flags, spread, taps_ref, heads_ref, segc, segr)
        inner, scaled = val["inner"], val["scaled"]

        gate = main_ref[:, : size.channels]
        gate_sig = jax.nn.sigmoid(gate)
        grad = grad_ref[:, : size.channels]
        grad_main[:, : size.channels] = (grad * y_ref[...] * silu_slope(gate, gate_sig)).astype(jnp.bfloat16)
        grad_y = grad * (gate * gate_sig)
        grad_y_b = grad_y.astype(jnp.bfloat16)
        tap_sums[4:5, : size.channels] += jnp.sum(grad_y * inner, axis=0, keepdims=True)

        lane = lax.broadcasted_iota(jnp.int32, (span, 2 * per_head), 1)
        head_lane = lax.broadcasted_iota(jnp.int32, (span, size.step_lanes), 1)
        head_row = lax.broadcasted_iota(jnp.int32, (size.step_lanes, span), 0)
        grad_meeting = jnp.zeros((span, span), jnp.float32)
        by_row = jnp.zeros((span, size.step_lanes), jnp.float32)
        by_column = jnp.zeros((size.step_lanes, span), jnp.float32)
        pieces = []
        for pair in range(size.heads // 2):
            where = slice(pair * 2 * per_head, (pair + 1) * 2 * per_head)
            both = []
            for side in range(2):
                head = 2 * pair + side
                decay = decay_of(val, head)
                weights = val["meeting"] * decay
                mine = (lane < per_head) if side == 0 else (lane >= per_head)
                grad_own = jnp.where(mine, grad_y_b[:, where], jnp.zeros((), jnp.bfloat16))
                grad_weights = product(grad_own, val["scaled_b"][:, where], LAST)
                both.append(product(weights.astype(jnp.bfloat16), grad_y_b[:, where], FIRST))
                grad_meeting = grad_meeting + grad_weights * decay
                moved = grad_weights * weights
                by_row = jnp.where(head_lane == head, jnp.sum(moved, axis=1, keepdims=True), by_row)
                by_column = jnp.where(head_row == head, jnp.sum(moved, axis=0, keepdims=True), by_column)
            pieces.append(jnp.where(lane < per_head, both[0], both[1]))
        grad_scaled = jnp.concatenate(pieces, axis=1)
        grad_cumul = by_row - jnp.transpose(by_column)

        held = state_ref[...]
        held_b = held.astype(jnp.bfloat16)
        grad_held = grad_state[...]
        grad_held_b = grad_held.astype(jnp.bfloat16)
        grad_meeting_b = grad_meeting.astype(jnp.bfloat16)
        reached = val["reach_wide"] * grad_y
        reached_b = reached.astype(jnp.bfloat16)
        grad_cumul = grad_cumul + split_dot(reached * product(val["cmat"], held_b), spread, (True, LAST), 2)
        grad_c = product(reached_b, held_b, LAST) + product(grad_meeting_b, val["bmat"])
        from_state = val["tail_wide"] * product(val["bmat"], grad_held_b)
        grad_b = product(grad_meeting_b, val["cmat"], FIRST) + product(
            (val["tail_wide"] * scaled).astype(jnp.bfloat16), grad_held_b, LAST
        )
        grad_scaled = grad_scaled + from_state
        ended = split_dot(scaled * from_state, spread, (True, LAST), 2)
        keep = val["reach_wide"][span - 1 : span, :]
        kept = jnp.sum(grad_held * held, axis=0, keepdims=True) * keep
        kept = split_dot(jnp.broadcast_to(kept, (8, size.channels)), spread, (True, LAST), 2)[0:1]
        at_end = jnp.sum(ended, axis=0, keepdims=True) + kept
        grad_logdec = split_dot(grad_cumul - ended, val["later"], (False, FIRST), 3) + at_end
        grad_state[...] = keep * grad_held + product(val["cmat"], reached_b, FIRST)

        grad_inner = grad_scaled * val["step_wide"] + grad_y * val["skip_wide"]
        grad_step = split_dot(grad_scaled * inner, spread, (True, LAST), 2) - grad_logdec * heads_ref[1:2, :]
        grad_step_raw = grad_step * jax.nn.sigmoid(val["step_in"])
        head_sums[0:1, :] += jnp.sum(grad_step_raw, axis=0, keepdims=True)
        head_sums[1:2, :] += jnp.sum(grad_logdec * val["logdec"], axis=0, keepdims=True)
        grad_main[:, size.step_at :] = grad_step_raw.astype(jnp.bfloat16)

        slope = silu_slope(val["pre"], val["sig"])
        grad_pre = jnp.concatenate([grad_inner, grad_b, grad_c], axis=1) * slope
        back[pl.ds(0, span), :] = grad_pre
        raw = grad_pre * taps_ref[0:1, :]
        tap_sums[0:1, :] += jnp.sum(grad_pre * wide[pl.ds(8, span), :], axis=0, keepdims=True)
        for lag in range(1, taps):
            tap_sums[lag : lag + 1, :] += jnp.sum(
                grad_pre * (wide[pl.ds(8 - lag, span), :] * flags[:, lag : lag + 1]), axis=0, keepdims=True
            )
            raw = raw + back[pl.ds(lag, span), :] * (flags[:, 5 + lag : 6 + lag] * taps_ref[lag : lag + 1, :])
        back[pl.ds(span, 8), :] = back[0:8, :]
        grad_main[:, size.channels : 2 * size.channels] = raw[:, : size.channels].astype(jnp.bfloat16)
        grad_side[:, : 2 * size.states] = raw[:, size.channels :].astype(jnp.bfloat16)

        cosine, sine = cos_ref[...], sin_ref[...]
        start = pl.multiple_of(jnp.maximum(chunk + 1 - size.window // span, 0) * span, span)
        seen = pl.ds(start, size.window)
        seen_keys, seen_values = keys_ref[seen, :], values_ref[seen, :]
        scale = 1.0 / math.sqrt(HEAD_SIZE)
        for head in range(size.query // HEAD_SIZE):
            at = 2 * size.channels + head * HEAD_SIZE
            query = turned(main_ref[:, at : at + HEAD_SIZE], cosine, sine).astype(jnp.bfloat16)
            probs = softmax_of(size, query, seen_keys, chunk, start, segc, segr_ref[:, seen])
            out_at = size.channels + head * HEAD_SIZE
            grad_out = grad_ref[:, out_at : out_at + HEAD_SIZE].astype(jnp.bfloat16)
            grad_probs = product(grad_out, seen_values, LAST)
            delta = jnp.sum(grad_probs * probs, axis=-1, keepdims=True)
            grad_scores = (probs * (grad_probs - delta)).astype(jnp.bfloat16)
            grad_query = product(grad_scores, seen_keys) * scale
            grad_main[:, at : at + HEAD_SIZE] = turned(grad_query, cosine, -sine).astype(jnp.bfloat16)
            grad_keys[seen, :] += product(grad_scores, query, FIRST) * scale
            grad_values[seen, :] += product(probs.astype(jnp.bfloat16), grad_out, FIRST)
        own = pl.ds(pl.multiple_of(chunk * span, span), span)
        key_at = 2 * size.states
        grad_side[:, key_at : key_at + HEAD_SIZE] = turned(grad_keys[own, :], cosine, -sine).astype(jnp.bfloat16)
        grad_side[:, key_at + HEAD_SIZE :] = grad_values[own, :].astype(jnp.bfloat16)

    def rows(columns):
        return pl.BlockSpec((span, columns), lambda i: (count - 1 - i, 0))

    def previous(columns, column):
        return pl.BlockSpec((8, columns), lambda i: (jnp.maximum((count - 1 - i) * (span // 8) - 1, 0), column))

    def whole(array):
        return pl.BlockSpec(array.shape, lambda i: (0, 0))

    cosine, sine = turn_tables(size.length)
    spread = spread_heads(size)
    tokens = size.length
    return pl.pallas_call(
        kernel,
        grid=(count,),
        in_specs=[
            whole(out_w), rows(size.main), rows(size.side), previous(size.channels, 1),
            previous(2 * size.states, 0), rows(1), whole(segments), rows(16), whole(tap_rows), whole(head_rows),
            rows(HEAD_SIZE), rows(HEAD_SIZE), whole(spread), rows(size.channels),
            pl.BlockSpec((size.states, size.channels), lambda i: (count - 1 - i, 0)), whole(keys), whole(values),
            whole(grad_rows), whole(mixed),
        ],
        out_specs=[
            rows(size.main), rows(size.side), pl.BlockSpec((8, size.wide), lambda i: (0, 0)),
            pl.BlockSpec((8, size.step_lanes), lambda i: (0, 0)),
            pl.BlockSpec((out_rows, size.channels), lambda i: (0, 0)),
            pl.BlockSpec((out_rows, size.query), lambda i: (0, 0)),
        ],
        out_shape=[
            jax.ShapeDtypeStruct((tokens, size.main), jnp.bfloat16),
            jax.ShapeDtypeStruct((tokens, size.side), jnp.bfloat16),
            jax.ShapeDtypeStruct((8, size.wide), jnp.float32),
            jax.ShapeDtypeStruct((8, size.step_lanes), jnp.float32),
            jax.ShapeDtypeStruct((out_rows, size.channels), jnp.float32),
            jax.ShapeDtypeStruct((out_rows, size.query), jnp.float32),
        ],
        scratch_shapes=[
            pltpu.VMEM((span + 8, size.wide), jnp.float32),
            pltpu.VMEM((span + 8, size.wide), jnp.float32),
            pltpu.VMEM((size.states, size.channels), jnp.float32),
            pltpu.VMEM((tokens, HEAD_SIZE), jnp.float32),
            pltpu.VMEM((tokens, HEAD_SIZE), jnp.float32),
            pltpu.VMEM((span, out_columns), jnp.float32),
        ]
        + computed_scratch(nd, out_rows, out_columns),
        compiler_params=pltpu.CompilerParams(
            dimension_semantics=("arbitrary",), vmem_limit_bytes=VMEM_LIMIT, collective_id=4, has_side_effects=True
        ),
        cost_estimate=pl.CostEstimate(flops=40 * 10**9, bytes_accessed=60 * 10**6, transcendentals=10**7),
        name="mixers_backward",
    )(out_w, main_raw, side_raw, main_raw, side_raw, segments.reshape(tokens, 1), segments, flags, tap_rows,
      head_rows, jnp.asarray(cosine), jnp.asarray(sine), jnp.asarray(spread), y_value, states, keys, values, grad_rows, mixed)


def per_device(
    nd,
    nt,
    residual,
    segments,
    mixgain,
    ffngain,
    gateproj,
    innerproj,
    stepproj,
    sharedproj,
    innerconv,
    sharedconv,
    stepbias,
    decaylog,
    skipgain,
    mixerout,
    queryproj,
    keyvalue,
    attnout,
    ffngate,
    upproj,
    downproj,
    cotangent,
):
    bfloat = jnp.bfloat16
    single = jnp.float32
    width = residual.shape[1]
    zed = lax.axis_index("tensor")
    seq_count, length = segments.shape
    token_count = seq_count * length
    channels = innerproj.shape[1]
    state_columns = sharedproj.shape[1]
    heads = stepproj.shape[1]
    query_columns = queryproj.shape[1]
    ffn_columns = ffngate.shape[1]
    small_rows = sharedproj.shape[0]
    conv_rows = sharedconv.shape[0]
    taps = sharedconv.shape[1]

    gains = jnp.concatenate(
        [
            mixgain[:, None],
            ffngain[:, None],
            jnp.pad(sharedconv, ((0, small_rows - conv_rows), (0, 0))),
            jnp.zeros((small_rows, 128 - 2 - taps), bfloat),
        ],
        axis=1,
    )
    main_used = 2 * channels + query_columns + heads
    main_own = jnp.concatenate(
        [
            gateproj,
            innerproj,
            queryproj,
            stepproj,
            jnp.zeros((gateproj.shape[0], -main_used % 128), bfloat),
        ],
        axis=1,
    )
    resid_own, cot_own, gain_rows, normed, grad_rows, _, main, side, out_w, main_raw, side_raw = first_gathers(
        nd,
        nt,
        residual,
        cotangent,
        jnp.concatenate([sharedproj, keyvalue, gains], axis=1),
        main_own,
        jnp.concatenate([mixerout, attnout], axis=1),
        state_columns,
    )
    gain_one, gain_two = gain_rows[0], gain_rows[1]
    conv_shared = from_relative(gain_rows[2 : 2 + taps], 1, nd)
    conv_shared = conv_shared.reshape(taps, nd * nt, small_rows)[:, :, :conv_rows].reshape(taps, -1)

    size = Sizes(channels, state_columns, query_columns, heads, length)
    flags = token_flags(segments, taps)
    tap_rows = jnp.concatenate([innerconv.astype(single).T, conv_shared], axis=1)
    tap_rows = jnp.pad(tap_rows, ((0, 8 - taps), (0, 0)))
    head_rows = jnp.stack([stepbias.astype(single), jnp.exp(decaylog.astype(single)), skipgain.astype(single)])
    head_rows = jnp.pad(head_rows, ((0, 5), (0, size.step_lanes - heads)))
    mixed_in, y_value, states, keys, values = mixers_forward(
        size, taps, main_raw, side_raw, segments, flags, tap_rows, head_rows
    )
    middle, rows_two, hidden, grad_gate_up, grad_rows, ffn_w = middle_rows(
        nd,
        nt,
        mixed_in,
        out_w,
        resid_own,
        gain_two[None],
        grad_rows,
        *second_neighbours(nt, grad_rows),
        jnp.concatenate([ffngate, upproj, downproj], axis=1),
    )
    grad_middle, grad_gain_two, grad_mix_rows, ffn_part, gate_g, up_g, down_g = middle_back(
        nd, nt, grad_gate_up, hidden, rows_two, grad_rows, ffn_w, middle, cot_own, gain_two[None]
    )
    ffn_out = lax.psum_scatter(ffn_part, "tensor", scatter_dimension=0, tiled=True)
    layer_out = from_relative(middle + ffn_out.astype(single), 1, nd)
    grad_main, grad_side, tap_sums, head_sums, mixer_g, attn_g = mixers_backward(
        nd, nt, size, taps, out_w, main_raw, side_raw, segments, flags, tap_rows, head_rows, y_value, states,
        keys, values, grad_mix_rows, mixed_in,
    )
    small = jnp.concatenate(
        [
            jnp.zeros((width,), single),
            grad_gain_two[0],
            tap_sums[:taps, channels:].reshape(-1),
            tap_sums[:taps, :channels].reshape(-1),
            tap_sums[4, :channels],
            head_sums[:2].reshape(-1),
        ]
    )
    shared_length = 2 * width + taps * state_columns
    small = jnp.pad(small, (0, -small.shape[0] % 1024)).reshape(-1, 128)
    grad_residual, small, common_g, gateproj_g, inner_g, query_g, step_g = last_sums(
        nd,
        nt,
        normed,
        grad_main,
        grad_side,
        main,
        side,
        resid_own,
        grad_middle,
        gain_one[None],
        small,
        shared_length // 128,
        (channels, channels, query_columns, heads),
    )
    small = small.reshape(-1)
    place = lax.axis_index("dp") * nt + zed
    gain_one_g = lax.dynamic_slice_in_dim(small, place * small_rows, small_rows, 0)
    gain_two_g = lax.dynamic_slice_in_dim(small, width + place * small_rows, small_rows, 0)
    conv_g = lax.dynamic_slice_in_dim(
        small[2 * width : shared_length].reshape(taps, -1), place * conv_rows, conv_rows, 1
    ).T
    local = small[shared_length:]
    skip_at = taps * channels
    head_at = skip_at + channels
    return (
        layer_out,
        grad_residual,
        gain_one_g,
        gain_two_g,
        gateproj_g,
        inner_g,
        step_g,
        common_g[:, :state_columns],
        local[:skip_at].reshape(taps, channels).T,
        conv_g,
        local[head_at : head_at + heads],
        local[head_at + size.step_lanes : head_at + size.step_lanes + heads],
        local[skip_at:head_at].reshape(heads, -1).sum(axis=1),
        mixer_g,
        query_g,
        common_g[:, state_columns:],
        attn_g,
        gate_g,
        up_g,
        down_g,
    )


def solution(mesh):
    return jax.shard_map(
        functools.partial(per_device, mesh.shape["dp"], mesh.shape["tensor"]),
        mesh=mesh,
        in_specs=(
            P(("dp", "tensor"), None),
            P("dp", None),
            P(("dp", "tensor")),
            P(("dp", "tensor")),
            P("dp", "tensor"),
            P("dp", "tensor"),
            P("dp", "tensor"),
            P(("dp", "tensor"), None),
            P("tensor", None),
            P(("dp", "tensor"), None),
            P("tensor"),
            P("tensor"),
            P("tensor"),
            P("dp", "tensor"),
            P("dp", "tensor"),
            P(("dp", "tensor"), None),
            P("dp", "tensor"),
            P("dp", "tensor"),
            P("dp", "tensor"),
            P("dp", "tensor"),
            P(("dp", "tensor"), None),
        ),
        out_specs=(
            P(("dp", "tensor"), None),
            P(("dp", "tensor"), None),
            P(("dp", "tensor")),
            P(("dp", "tensor")),
            P("dp", "tensor"),
            P("dp", "tensor"),
            P("dp", "tensor"),
            P(("dp", "tensor"), None),
            P("tensor", None),
            P(("dp", "tensor"), None),
            P("tensor"),
            P("tensor"),
            P("tensor"),
            P("dp", "tensor"),
            P("dp", "tensor"),
            P(("dp", "tensor"), None),
            P("dp", "tensor"),
            P("dp", "tensor"),
            P("dp", "tensor"),
            P("dp", "tensor"),
        ),
        check_vma=False,
    )
```

```python
import functools
import math

import jax
import jax.numpy as jnp
import numpy as np
from jax import lax
from jax.experimental import pallas as pl
from jax.experimental.pallas import tpu as pltpu
from jax.sharding import PartitionSpec as P

QUERY_HEADS = 8
KEY_VALUE_HEADS = 2
HEAD_SIZE = 128
SPAN = 256


eps = 1e-05
rope_base = 10000.0


def contract_last(left, right):
    return lax.dot_general(
        left, right, (((1,), (1,)), ((), ())), preferred_element_type=jnp.float32
    )


def bit_orders(size):
    high = list(range(size.bit_length() - 2, 0, -1))
    return high, high[:2][::-1] + high[2:]


def relative_blocks(size):
    both = []
    for half, order in enumerate(bit_orders(size)):
        chain = [0]
        for bit in order:
            chain = chain + [other ^ (1 << bit) for other in chain]
        both = both + [(other, half) for other in chain]
    return both + [(other ^ 1, half) for other, half in both]


def relative_place(other, half, size):
    place = half * (size // 2) + (other & 1) * size
    for digit, bit in enumerate(bit_orders(size)[half]):
        place = place + (((other >> bit) & 1) << digit)
    return place


def to_relative(value, axis, size):
    me = lax.axis_index("dp")
    width = value.shape[axis] // (2 * size)
    return jnp.concatenate(
        [
            lax.dynamic_slice_in_dim(value, ((me ^ other) * 2 + half) * width, width, axis)
            for other, half in relative_blocks(size)
        ],
        axis,
    )


def from_relative(value, axis, size):
    me = lax.axis_index("dp")
    width = value.shape[axis] // (2 * size)
    return jnp.concatenate(
        [
            lax.dynamic_slice_in_dim(value, relative_place(me ^ number, half, size) * width, width, axis)
            for number in range(size)
            for half in range(2)
        ],
        axis,
    )


MESH = pl.DeviceIdType.MESH
VMEM_LIMIT = 56 * 1024 * 1024
LINE_CHUNKS = 4
LARGE_LIMIT = 62 * 1024 * 1024


def flip(value, bit):
    unit = 1 << bit
    return value + unit * (1 - 2 * ((value // unit) % 2))


def mixed_with(value, other, bits):
    for bit in range(bits):
        if (other >> bit) & 1:
            value = flip(value, bit)
    return value


def enter(nt, bits):
    me, zed = lax.axis_index("dp"), lax.axis_index("tensor")
    barrier = pltpu.get_barrier_semaphore()
    for other in range(nt):

        @pl.when(zed != other)
        def _(other=other):
            pl.semaphore_signal(barrier, inc=1, device_id=(me, other), device_id_type=MESH)

    for bit in range(bits):
        pl.semaphore_signal(barrier, inc=1, device_id=(flip(me, bit), zed), device_id_type=MESH)
    pl.semaphore_wait(barrier, bits + nt - 1)
    return me, zed


def aligned(start, size):
    return pl.ds(pl.multiple_of(start, 16), size)


def together(*flows):
    flows = [list(flow) for flow in flows]
    order = sorted(
        ((place + 0.5) / len(flow), number, place)
        for number, flow in enumerate(flows)
        for place in range(len(flow))
    )
    for _, number, place in order:
        flows[number][place]()


def gather_steps(nd, me, zed, own, everything, send, recv, local):
    half = own.shape[0] // 2
    blocks = relative_blocks(nd)
    place = {block: number for number, block in enumerate(blocks)}

    def rows(block):
        return everything.at[pl.ds(place[block] * half, half)]

    def source(block):
        return own.at[pl.ds(block[1] * half, half)] if block[0] == 0 else rows(block)

    hops = []
    for part, order in enumerate(bit_orders(nd)):
        chain = [0]
        for bit in order:
            hops = hops + [((other, part), bit) for other in chain]
            chain = chain + [other ^ (1 << bit) for other in chain]
    hops = hops + [(block, 0) for block in blocks[:nd]]

    def copy(number):
        block, bit = hops[number]
        landed = (block[0] ^ (1 << bit), block[1])
        return pltpu.make_async_remote_copy(
            src_ref=source(block),
            dst_ref=rows(landed),
            send_sem=send.at[number],
            recv_sem=recv.at[place[landed]],
            device_id=(flip(me, bit), zed),
            device_id_type=MESH,
        )

    def arrival(block):
        return pltpu.make_async_remote_copy(
            src_ref=rows(block),
            dst_ref=rows(block),
            send_sem=send.at[0],
            recv_sem=recv.at[place[block]],
            device_id=(flip(me, 0), zed),
            device_id_type=MESH,
        )

    def begin():
        for number, (block, bit) in enumerate(hops):
            if block[0] == 0:
                copy(number).start()
        for part in range(2):
            pltpu.make_async_copy(source((0, part)), rows((0, part)), local.at[part]).start()

    def forward(block):
        def step():
            arrival(block).wait_recv()
            for number, (origin, bit) in enumerate(hops):
                if origin == block:
                    copy(number).start()

        return step

    def end():
        for block in blocks[nd:]:
            arrival(block).wait_recv()
        for number in range(len(hops)):
            copy(number).wait_send()
        for part in range(2):
            pltpu.make_async_copy(source((0, part)), rows((0, part)), local.at[part]).wait()

    first, second = blocks[1 : nd // 2], blocks[nd // 2 + 1 : nd]
    middle = [forward(block) for pair in zip(first, second) for block in pair]
    return [begin] + middle + [end]


def gather_hops(nd):
    return 2 * (nd // 2 - 1) + nd


def gather_semaphores(nd):
    return [
        pltpu.SemaphoreType.DMA((gather_hops(nd),)),
        pltpu.SemaphoreType.DMA((2 * nd,)),
        pltpu.SemaphoreType.DMA((2,)),
    ]


def each_rows(rows, body, unit=16):
    def step(number, carry):
        body(aligned(number * unit, unit))
        return carry

    lax.fori_loop(0, rows // unit, step, 0)


def computed_scatter(nd, me, zed, half, compute, stage, held, landed, totals, core_send, core_recv, send, recv):
    chain_length = nd // 2
    block = 256
    pieces = block // half
    per_part = chain_length // pieces
    turns = [part * per_part + spot for spot in range(per_part - 1, -1, -1) for part in range(2)]

    def piece(ref, number):
        return ref.at[pl.ds(number * half, half)]

    def block_of(ref, number):
        return ref.at[pl.ds(number * block, block)]

    rounds, slot = [], 0
    for part, order in enumerate(bit_orders(nd)):
        length, own_rounds = chain_length, []
        for bit in order[::-1]:
            length = length // 2
            own_rounds.append((bit, length, slot))
            slot = slot + length
        rounds.append(own_rounds)

    def core_copy(number):
        return pltpu.make_async_remote_copy(
            src_ref=block_of(stage, number),
            dst_ref=block_of(held, number),
            send_sem=core_send.at[number],
            recv_sem=core_recv.at[number],
            device_id=(flip(me, 0), zed),
            device_id_type=MESH,
        )

    def hop(bit, number, where):
        return pltpu.make_async_remote_copy(
            src_ref=piece(held, number),
            dst_ref=piece(landed, where),
            send_sem=send.at[where],
            recv_sem=recv.at[where],
            device_id=(flip(me, bit), zed),
            device_id_type=MESH,
        )

    def away(number):
        def step():
            compute(nd * half + number * block, None, block_of(stage, number))
            core_copy(number).start()

        return step

    def near(number):
        def step():
            core_copy(number).wait_recv()
            compute(number * block, block_of(held, number), block_of(held, number))
            for inner in range(pieces):
                place = number * pieces + inner
                part, spot = place // chain_length, place % chain_length
                bit, length, first = rounds[part][0]
                if spot >= length:
                    hop(bit, place, first + spot - length).start()

        return step

    def later_sum(part, turn, spot):
        bit, length, first = rounds[part][turn]
        number = part * chain_length + spot

        def step():
            hop(bit, number, first + spot).wait_recv()
            last = turn == len(rounds[part]) - 1

            def body(rows):
                kept, came = piece(held, number)[rows], piece(landed, first + spot)[rows]
                if last:
                    value = kept.astype(jnp.float32) + came.astype(jnp.float32)
                    for target, start, columns in totals:
                        piece(target, part)[rows] = value[:, start : start + columns]
                else:
                    piece(held, number)[rows] = kept + came

            each_rows(half, body)
            if not last:
                next_bit, next_length, next_first = rounds[part][turn + 1]
                if spot >= next_length:
                    hop(next_bit, number, next_first + spot - next_length).start()

        return step

    def end():
        for number in range(len(turns)):
            core_copy(number).wait_send()
        for part in range(2):
            for bit, length, first in rounds[part]:
                for spot in range(length):
                    hop(bit, part * chain_length + length + spot, first + spot).wait_send()

    later = []
    for turn in range(len(rounds[0])):
        length = rounds[0][turn][1]
        later.append([later_sum(part, turn, spot) for spot in range(length - 1, -1, -1) for part in range(2)])
    return [away(number) for number in turns], [near(number) for number in turns], later, end


def computed_scratch(nd, rows, columns):
    slots = nd - 2
    blocks = nd * rows // 2 // 256
    return [
        pltpu.VMEM((nd * rows // 2, columns), jnp.bfloat16),
        pltpu.VMEM((nd * rows // 2, columns), jnp.bfloat16),
        pltpu.VMEM((slots * rows // 2, columns), jnp.bfloat16),
        pltpu.SemaphoreType.DMA((blocks,)),
        pltpu.SemaphoreType.DMA((blocks,)),
        pltpu.SemaphoreType.DMA((slots,)),
        pltpu.SemaphoreType.DMA((slots,)),
    ]


def products_of(left, rights, tile):
    def compute(start, add, target):
        turned_left = jnp.transpose(left[:, start : start + 256])
        at = 0
        for right, columns in rights:
            for first in range(0, columns, tile):
                extent = slice(first, min(first + tile, columns))
                value = jnp.dot(turned_left, right[:, extent], preferred_element_type=jnp.float32)
                here = slice(at + extent.start, at + extent.stop)
                if add is not None:
                    value = value + add[:, here].astype(jnp.float32)
                target[:, here] = value.astype(jnp.bfloat16)
            at = at + columns

    return compute


def line_gather(nt, me, zed, chunks, own, everything, send, recv, chunked=False, reach=None):
    size = own.shape[0] // chunks
    reach = nt - 1 if reach is None else reach

    def own_rows(chunk):
        return own.at[pl.ds(chunk * size, size)]

    def rows(block, chunk):
        start = (chunk * nt + block) * size if chunked else block * (size * chunks) + chunk * size
        return everything.at[aligned(start, size)]

    def copy(source, block, chunk, side):
        return pltpu.make_async_remote_copy(
            src_ref=source,
            dst_ref=rows(block, chunk),
            send_sem=send.at[side, block, chunk],
            recv_sem=recv.at[block, chunk],
            device_id=(me, zed + 1 - 2 * side),
            device_id_type=MESH,
        )

    def keep(chunk):
        return pltpu.make_async_copy(own_rows(chunk), rows(zed, chunk), recv.at[zed, chunk])

    def first(chunk):
        for side, condition in ((0, zed < nt - 1), (1, zed > 0)):

            @pl.when(condition)
            def _(side=side):
                copy(own_rows(chunk), zed, chunk, side).start()

        keep(chunk).start()

    def onward(chunk, distance):
        for side, block in ((0, zed - distance), (1, zed + distance)):
            inside = (block >= 0) if side == 0 else (block < nt)
            open_end = (zed < nt - 1) if side == 0 else (zed > 0)

            @pl.when(inside)
            def _(block=block, side=side):
                copy(rows(block, chunk), block, chunk, side).wait_recv()

            if distance < reach:

                @pl.when(jnp.logical_and(inside, open_end))
                def _(block=block, side=side):
                    copy(rows(block, chunk), block, chunk, side).start()

    def settle(chunk):
        keep(chunk).wait()

    def end(chunk):
        for side, condition in ((0, zed < nt - 1), (1, zed > 0)):

            @pl.when(condition)
            def _(side=side):
                copy(own_rows(chunk), zed, chunk, side).wait_send()

            for distance in range(1, reach):
                block = zed - distance if side == 0 else zed + distance
                inside = (block >= 0) if side == 0 else (block < nt)

                @pl.when(jnp.logical_and(inside, condition))
                def _(block=block, side=side):
                    copy(rows(block, chunk), block, chunk, side).wait_send()

    return first, onward, settle, end


def line_gather_semaphores(nt, chunks):
    return [pltpu.SemaphoreType.DMA((2, nt, chunks)), pltpu.SemaphoreType.DMA((nt, chunks))]


def line_reduce(nt, me, zed, chunks, parts, held, send, recv, chunked=False):
    block_rows = parts.shape[0] // nt
    size = block_rows // chunks
    def rows(block, chunk):
        if chunked:
            return aligned((chunk * nt + block) * size, size)
        return aligned(block * block_rows + chunk * size, size)

    def held_rows(side, block, chunk):
        return aligned((block + 1 - side) * block_rows + chunk * size, size)

    def copy(own, side, block, chunk):
        place = held_rows(side, block, chunk)
        return pltpu.make_async_remote_copy(
            src_ref=parts.at[rows(block, chunk)] if own else held.at[place],
            dst_ref=held.at[place],
            send_sem=send.at[side, block, chunk],
            recv_sem=recv.at[side, block, chunk],
            device_id=(me, zed + 1 - 2 * side),
            device_id_type=MESH,
        )

    def role(side, turn):
        away = nt - 1 - turn
        if side == 0:
            return zed + away, zed + away < nt, zed == 0
        return zed - away, zed - away >= 0, zed == nt - 1

    def pass_on(chunk, turn):
        for side in range(2):
            block, active, source = role(side, turn)

            @pl.when(jnp.logical_and(active, source))
            def _(side=side, block=block):
                copy(True, side, block, chunk).start()

            @pl.when(jnp.logical_and(active, jnp.logical_not(source)))
            def _(side=side, block=block):
                copy(False, side, block, chunk).wait_recv()
                mine, came = parts.at[rows(block, chunk)], held.at[held_rows(side, block, chunk)]

                def body(inner):
                    came[inner] = mine[inner] + came[inner]

                each_rows(size, body)
                copy(False, side, block, chunk).start()

    def own_sum(chunk, total):
        total[...] = parts[rows(zed, chunk)].astype(jnp.float32)
        for side in range(2):

            @pl.when(zed > 0 if side == 0 else zed < nt - 1)
            def _(side=side):
                copy(False, side, zed, chunk).wait_recv()
                total[...] += held[held_rows(side, zed, chunk)].astype(jnp.float32)

    def end(chunk):
        for turn in range(nt - 1):
            for side in range(2):
                block, active, source = role(side, turn)

                @pl.when(active)
                def _(side=side, block=block):
                    copy(False, side, block, chunk).wait_send()

    return pass_on, own_sum, end


def line_reduce_scratch(nt, block_rows, columns, chunks):
    return [
        pltpu.VMEM(((nt + 1) * block_rows, columns), jnp.bfloat16),
        pltpu.VMEM((block_rows // chunks, columns), jnp.float32),
        pltpu.SemaphoreType.DMA((2, nt, chunks)),
        pltpu.SemaphoreType.DMA((2, nt, chunks)),
    ]


HBM = pl.BlockSpec(memory_space=pl.ANY)
ONCHIP = pl.BlockSpec(memory_space=pltpu.VMEM)


def near_first(nt, zed, turn):
    block = 0
    for mine in range(nt):
        order = sorted(range(nt), key=lambda other: (abs(other - mine), other))
        block = block + jnp.where(zed == mine, order[turn], 0)
    return block


def first_gathers(nd, nt, rows, grad, small, main_own, out_own, shared_columns):
    chunks = LINE_CHUNKS
    bits = nd.bit_length() - 1
    blocks = relative_blocks(nd)
    block_rows, width = rows.shape
    lane = width // len(blocks)
    if lane % 128:
        rows, grad = to_relative(rows, 1, nd), to_relative(grad, 1, nd)
    main_columns, small_columns = main_own.shape[1], small.shape[1]
    side_columns = shared_columns + 2 * HEAD_SIZE
    gains_at = shared_columns + 2 * KEY_VALUE_HEADS * HEAD_SIZE
    tile = 256

    def reorder(me, source, target):
        if lane % 128:
            target[...] = source[...]
            return
        for number, (other, part) in enumerate(blocks):
            start = (mixed_with(me, other, bits) * 2 + part) * lane
            target[:, number * lane : (number + 1) * lane] = source[:, pl.ds(pl.multiple_of(start, lane), lane)]

    def kernel(
        rows_in, grad_in, small_ref, main_ref, out_ref,
        rows_ref, grad_ref, gains_ref, normed_all, grad_all, small_line, main_all, side_all, out_all, main_raw, side_raw,
        row_space, normed, main_space, small_space, side_space, main_stage, side_stage, store_sems, *refs,
    ):
        row_sems, small_sems, grad_sems = refs[:2], refs[2:4], refs[4:6]
        main_sems, small_dp, out_sems = refs[6:9], refs[9:12], refs[12:15]
        me, zed = enter(nt, bits)
        small_first, small_onward, small_settle, small_end = line_gather(
            nt, me, zed, 1, small_ref, small_line, *small_sems
        )
        row_first, row_onward, row_settle, row_end = line_gather(
            nt, me, zed, chunks, rows_ref, row_space, *row_sems
        )
        grad_first, grad_onward, grad_settle, grad_end = line_gather(
            nt, me, zed, chunks, grad_ref, grad_all, *grad_sems, chunked=True, reach=1
        )
        main_flow = gather_steps(nd, me, zed, main_ref, main_space, *main_sems)
        small_flow = gather_steps(nd, me, zed, small_line, small_space, *small_dp)
        out_flow = gather_steps(nd, me, zed, out_ref, out_all, *out_sems)
        head = zed * (QUERY_HEADS // nt) // (QUERY_HEADS // KEY_VALUE_HEADS)

        def columns(turn):
            if turn == 0:
                return small_space.at[:, pl.ds(0, shared_columns)], side_space.at[:, pl.ds(0, shared_columns)]
            start = shared_columns + ((turn - 1) * KEY_VALUE_HEADS + head) * HEAD_SIZE
            target = shared_columns + (turn - 1) * HEAD_SIZE
            return (
                small_space.at[:, pl.ds(pl.multiple_of(start, HEAD_SIZE), HEAD_SIZE)],
                side_space.at[:, pl.ds(target, HEAD_SIZE)],
            )

        def keep(number):
            source, target = ((main_space, main_all), (side_space, side_all), (normed, normed_all))[number]
            return pltpu.make_async_copy(source, target, store_sems.at[number])

        def pick(turn):
            return pltpu.make_async_copy(*columns(turn), store_sems.at[3 + turn])

        def store(turn, number):
            block = near_first(nt, zed, turn)
            stage, target = ((main_stage, main_raw), (side_stage, side_raw))[number]
            return pltpu.make_async_copy(
                stage.at[turn % 2],
                target.at[aligned(block * block_rows, block_rows)],
                store_sems.at[6 + 2 * turn + number],
            )

        def project(turn):
            where = aligned(near_first(nt, zed, turn) * block_rows, block_rows)
            value = (rows_ref[...] if turn == 0 else row_space[where]).astype(jnp.float32)
            scale = lax.rsqrt(jnp.mean(value * value, axis=-1, keepdims=True) + eps)
            mine = (value * scale * gains_ref[0:1]).astype(jnp.bfloat16)
            normed[where] = mine
            if turn >= 2:
                store(turn - 2, 0).wait()
                store(turn - 2, 1).wait()
            for space, stage, number in ((main_space, main_stage, 0), (side_space, side_stage, 1)):
                for start in range(0, space.shape[1], tile):
                    extent = slice(start, min(start + tile, space.shape[1]))
                    stage[turn % 2, :, extent] = jnp.dot(
                        mine, space[:, extent], preferred_element_type=jnp.float32
                    )
                store(turn, number).start()

        small_first(0)
        main_flow[0]()
        reorder(me, rows_in, rows_ref)
        for chunk in range(chunks):
            row_first(chunk)
        for distance in range(1, nt):
            small_onward(0, distance)
        small_settle(0)
        small_end(0)
        small_flow[0]()
        out_flow[0]()
        reorder(me, grad_in, grad_ref)
        near = [
            functools.partial(row_onward, chunk, distance) for distance in range(1, nt - 1) for chunk in range(chunks)
        ]
        for chunk in range(chunks):
            grad_first(chunk)
        together(near, main_flow[1:-1] + small_flow[1:-1])
        small_flow[-1]()
        for turn in range(3):
            pick(turn).start()
        for start in range(0, width, 128):
            turned_block = jnp.transpose(
                small_space[start : start + 128, gains_at : gains_at + 128].astype(jnp.float32)
            )
            gains_ref[:, start : start + 128] = turned_block[:8]
        main_flow[-1]()
        keep(0).start()
        for turn in range(3):
            pick(turn).wait()
        keep(1).start()

        def last_rows():
            for chunk in range(chunks):
                row_onward(chunk, nt - 1)

        def grads_from(distance):
            for chunk in range(chunks):
                grad_onward(chunk, distance)

        compute = [functools.partial(project, turn) for turn in range(nt - 1)] + [last_rows]
        together(compute, out_flow[1:-1])
        project(nt - 1)
        keep(2).start()
        grads_from(1)
        out_flow[-1]()
        for chunk in range(chunks):
            row_settle(chunk)
            row_end(chunk)
            grad_settle(chunk)
            grad_end(chunk)
        for turn in range(max(nt - 2, 0), nt):
            store(turn, 0).wait()
            store(turn, 1).wait()
        for number in range(3):
            keep(number).wait()

    def sized(array, times, dtype=None):
        return jax.ShapeDtypeStruct((array.shape[0] * times, array.shape[1]), dtype or array.dtype)

    tokens = block_rows * nt
    return pl.pallas_call(
        kernel,
        out_shape=[
            sized(rows, 1),
            sized(grad, 1),
            jax.ShapeDtypeStruct((8, width), jnp.float32),
            sized(rows, nt),
            sized(grad, nt),
            sized(small, nt),
            sized(main_own, nd),
            jax.ShapeDtypeStruct((width, side_columns), small.dtype),
            sized(out_own, nd),
            jax.ShapeDtypeStruct((tokens, main_columns), jnp.float32),
            jax.ShapeDtypeStruct((tokens, side_columns), jnp.float32),
        ],
        in_specs=[ONCHIP] * 2 + [HBM] * 3,
        out_specs=[ONCHIP] * 3 + [HBM] * 8,
        scratch_shapes=[
            pltpu.VMEM((tokens, width), jnp.bfloat16),
            pltpu.VMEM((tokens, width), jnp.bfloat16),
            pltpu.VMEM((width, main_columns), jnp.bfloat16),
            pltpu.VMEM((width, small_columns), jnp.bfloat16),
            pltpu.VMEM((width, side_columns), jnp.bfloat16),
            pltpu.VMEM((2, block_rows, main_columns), jnp.float32),
            pltpu.VMEM((2, block_rows, side_columns), jnp.float32),
            pltpu.SemaphoreType.DMA((6 + 2 * nt,)),
        ]
        + line_gather_semaphores(nt, chunks)
        + line_gather_semaphores(nt, 1)
        + line_gather_semaphores(nt, chunks)
        + gather_semaphores(nd) * 3,
        compiler_params=pltpu.CompilerParams(
            collective_id=0, has_side_effects=True, vmem_limit_bytes=VMEM_LIMIT
        ),
        name="first_gathers",
    )(rows, grad, small, main_own, out_own)


def second_neighbours(nt, grads):
    zed = lax.axis_index("tensor")
    width = grads.shape[1]
    blocks = grads.reshape(LINE_CHUNKS, nt, -1, width)
    below = lax.dynamic_slice_in_dim(blocks, jnp.maximum(zed - 1, 0), 1, 1).reshape(-1, width)
    above = lax.dynamic_slice_in_dim(blocks, jnp.minimum(zed + 1, nt - 1), 1, 1).reshape(-1, width)
    return (
        lax.ppermute(below, "tensor", [(i, i + 1) for i in range(1, nt - 1)]),
        lax.ppermute(above, "tensor", [(i, i - 1) for i in range(1, nt - 1)]),
    )


def middle_rows(nd, nt, mixed, out_w, resid, gain, grads, grads_below, grads_above, ffn_own):
    chunks = LINE_CHUNKS
    bits = nd.bit_length() - 1
    block_rows, width = resid.shape
    tokens = block_rows * nt
    size = block_rows // chunks
    ffn_columns = ffn_own.shape[1] // 3
    tile = 512

    def kernel(
        mixed_ref, out_ref, resid_ref, gain_ref, grads_ref, below_ref, above_ref, ffn_ref,
        middle_ref, rows_ref, hidden_ref, slopes_ref, grads_all, ffn_all,
        parts, grad_space, ffn_space, own, held, total, send, recv, gather_send, gather_recv,
        ffn_send, ffn_recv, ffn_local, store_sems, far_send, far_recv, far_space, second_sems,
    ):
        me, zed = enter(nt, bits)
        load = pltpu.make_async_copy(grads_ref, grad_space, store_sems.at[0])
        load.start()
        pass_on, own_sum, reduce_end = line_reduce(nt, me, zed, chunks, parts, held, send, recv)
        first, onward, settle, gather_end = line_gather(
            nt, me, zed, chunks, own, rows_ref, gather_send, gather_recv, chunked=True
        )
        flow = gather_steps(nd, me, zed, ffn_ref, ffn_space, ffn_send, ffn_recv, ffn_local)
        keeps = [
            pltpu.make_async_copy(grad_space, grads_all, store_sems.at[1]),
            pltpu.make_async_copy(ffn_space, ffn_all, store_sems.at[2]),
        ]

        def part(turn):
            where = aligned(near_first(nt, zed, nt - 1 - turn) * block_rows, block_rows)
            left = mixed_ref[where]
            for start in range(0, width, tile):
                extent = slice(start, start + tile)
                parts[where, extent] = product(left, out_ref[extent], LAST).astype(jnp.bfloat16)

        def second(action):
            for side, source in ((0, below_ref), (1, above_ref)):

                @pl.when(zed >= 2 if side == 0 else zed < nt - 2)
                def _(side=side, source=source):
                    block = zed - 2 if side == 0 else zed + 2
                    for chunk in range(chunks):
                        place = aligned((chunk * nt + block) * size, size)
                        action(
                            pltpu.make_async_copy(
                                source.at[pl.ds(chunk * size, size)], grad_space.at[place], second_sems.at[side, chunk]
                            )
                        )

        def far(chunk, up):
            block = 0 if up else nt - 1
            return pltpu.make_async_remote_copy(
                src_ref=grad_space.at[pl.ds((chunk * nt + block) * size, size)],
                dst_ref=far_space.at[pl.ds(chunk * size, size)],
                send_sem=far_send.at[chunk],
                recv_sem=far_recv.at[chunk],
                device_id=(me, nt - 1 if up else 0),
                device_id_type=MESH,
            )

        def far_begin():
            for up, sender in ((True, nt - 2), (False, 1)):

                @pl.when(zed == sender)
                def _(up=up):
                    for chunk in range(chunks):
                        far(chunk, up).start()

        def far_end():
            for up, sender in ((True, nt - 2), (False, 1)):

                @pl.when(zed == sender)
                def _(up=up):
                    for chunk in range(chunks):
                        far(chunk, up).wait_send()

                @pl.when(zed == (nt - 1 if up else 0))
                def _(up=up):
                    for chunk in range(chunks):
                        far(chunk, up).wait_recv()
                        start = (chunk * nt + (0 if up else nt - 1)) * size
                        grad_space[pl.ds(start, size)] = far_space[pl.ds(chunk * size, size)]

        def finish(chunk):
            own_sum(chunk, total)
            where = pl.ds(chunk * size, size)
            value = resid_ref[where].astype(jnp.float32) + total[...]
            middle_ref[where] = value
            scale = lax.rsqrt(jnp.mean(value * value, axis=-1, keepdims=True) + eps)
            own[where] = (value * scale * gain_ref[...]).astype(jnp.bfloat16)
            first(chunk)

        def feed(chunk):
            settle(chunk)
            where = pl.ds(chunk * nt * size, nt * size)
            rows, grads = rows_ref[where], grad_space[where]
            for start in range(0, ffn_columns, tile):
                columns = [slice(turn * ffn_columns + start, turn * ffn_columns + start + tile) for turn in range(3)]
                gate = product(rows, ffn_space[:, columns[0]])
                upper = product(rows, ffn_space[:, columns[1]])
                grad = product(grads, ffn_space[:, columns[2]])
                sigma = jax.nn.sigmoid(gate)
                through = gate * sigma
                hidden_ref[where, columns[0]] = (through * upper).astype(jnp.bfloat16)
                slopes_ref[where, columns[0]] = (grad * upper * silu_slope(gate, sigma)).astype(jnp.bfloat16)
                slopes_ref[where, columns[1]] = (grad * through).astype(jnp.bfloat16)

        flow[0]()
        part(0)
        for chunk in range(chunks):
            pass_on(chunk, 0)
        load.wait()
        second(lambda copy: copy.start())
        for turn in range(1, nt):
            part(turn)
        second(lambda copy: copy.wait())
        far_begin()
        steps = line_steps(nt, chunks, pass_on, finish, onward)
        drain = nt
        together(steps[:-drain], flow[1:] + [far_end])
        for keep in keeps:
            keep.start()
        feeds = [functools.partial(feed, chunk) for chunk in range(chunks)]
        for number, step in enumerate(steps[-drain:]):
            if 0 < number < drain and feeds and number - 1 < chunks - 1:
                feeds.pop(0)()
            step()
        for step in feeds:
            step()
        for chunk in range(chunks):
            reduce_end(chunk)
            gather_end(chunk)
        for keep in keeps:
            keep.wait()

    return pl.pallas_call(
        kernel,
        out_shape=[
            jax.ShapeDtypeStruct((block_rows, width), jnp.float32),
            jax.ShapeDtypeStruct((tokens, width), jnp.bfloat16),
            jax.ShapeDtypeStruct((tokens, ffn_columns), jnp.bfloat16),
            jax.ShapeDtypeStruct((tokens, 2 * ffn_columns), jnp.bfloat16),
            jax.ShapeDtypeStruct((tokens, width), jnp.bfloat16),
            jax.ShapeDtypeStruct((width, 3 * ffn_columns), jnp.bfloat16),
        ],
        in_specs=[ONCHIP] * 4 + [HBM] * 4,
        out_specs=[ONCHIP] * 4 + [HBM] * 2,
        scratch_shapes=[
            pltpu.VMEM((tokens, width), jnp.bfloat16),
            pltpu.VMEM((tokens, width), jnp.bfloat16),
            pltpu.VMEM((width, 3 * ffn_columns), jnp.bfloat16),
            pltpu.VMEM((block_rows, width), jnp.bfloat16),
        ]
        + line_reduce_scratch(nt, block_rows, width, chunks)
        + line_gather_semaphores(nt, chunks)
        + gather_semaphores(nd)
        + [
            pltpu.SemaphoreType.DMA((3,)),
            pltpu.SemaphoreType.DMA((chunks,)),
            pltpu.SemaphoreType.DMA((chunks,)),
            pltpu.VMEM((block_rows, width), jnp.bfloat16),
            pltpu.SemaphoreType.DMA((2, chunks)),
        ],
        compiler_params=pltpu.CompilerParams(
            collective_id=1, has_side_effects=True, vmem_limit_bytes=LARGE_LIMIT
        ),
        name="middle_rows",
    )(mixed, out_w, resid, gain, grads, grads_below, grads_above, ffn_own)


def absolute_lanes(me, bits, blocks, source, target):
    lane = source.shape[1] // len(blocks)
    for number, (other, part) in enumerate(blocks):
        start = (mixed_with(me, other, bits) * 2 + part) * lane
        target[:, pl.ds(pl.multiple_of(start, lane), lane)] = source[:, number * lane : (number + 1) * lane]


def norm_pull(value, gain, grad):
    scale = lax.rsqrt(jnp.mean(value * value, axis=-1, keepdims=True) + eps)
    scaled = grad * gain
    inner = jnp.mean(scaled * value, axis=-1, keepdims=True)
    return scale * (scaled - value * (inner * scale * scale)), grad * value * scale


def line_steps(nt, chunks, pass_on, finish, onward, settle=None):
    steps = []

    def add(function, chunk, *rest):
        if 0 <= chunk < chunks:
            steps.append(functools.partial(function, chunk, *rest))

    for chunk in range(chunks + 2):
        add(finish, chunk - 1)
        add(onward, chunk - 2, nt - 1)
        for turn in range(1, nt - 1):
            add(pass_on, chunk, turn)
            add(onward, chunk - 1, turn)
    return steps


def middle_back(nd, nt, slopes, hidden, rows, grads, ffn_w, middle, cot, gain):
    chunks = LINE_CHUNKS
    bits = nd.bit_length() - 1
    block_rows, width = middle.shape
    tokens = block_rows * nt
    size = block_rows // chunks
    blocks = relative_blocks(nd)
    lane = width // len(blocks)
    ffn_columns = hidden.shape[1]
    out_rows = width // nd
    tile = 512

    def kernel(
        slopes_in, hidden_in, rows_in, grads_in, ffn_ref, middle_ref, cot_ref, gain_ref,
        grad_ref, gain_out, rows_all, out_all, gate_total, up_total, down_total,
        slopes_ref, hidden_ref, rows_ref, grads_ref, weights, down_weights, load_sems, parts, own, gain_grad,
        out_stage, out_sems,
        line_held, total, send, recv, gather_send, gather_recv, *refs,
    ):
        loads = [
            pltpu.make_async_copy(source, target, load_sems.at[number])
            for number, (source, target) in enumerate(
                (
                    (ffn_ref.at[:, pl.ds(0, 2 * ffn_columns)], weights),
                    (slopes_in, slopes_ref),
                    (rows_in, rows_ref),
                    (hidden_in, hidden_ref),
                    (grads_in, grads_ref),
                    (ffn_ref.at[:, pl.ds(2 * ffn_columns, ffn_columns)], down_weights),
                )
            )
        ]
        for load in loads:
            load.start()
        me, zed = enter(nt, bits)
        pass_on, own_sum, reduce_end = line_reduce(nt, me, zed, chunks, parts, line_held, send, recv, chunked=True)
        first, onward, settle, gather_end = line_gather(nt, me, zed, chunks, own, rows_all, gather_send, gather_recv)
        half = nd * out_rows // 2
        scatters = [
            computed_scatter(
                nd, me, zed, out_rows // 2, products_of(rows_ref, ((slopes_ref, 2 * ffn_columns),), tile),
                weights.at[pl.ds(0, half)], *refs[:2],
                ((gate_total, 0, ffn_columns), (up_total, ffn_columns, ffn_columns)), *refs[2:6],
            ),
            computed_scatter(
                nd, me, zed, out_rows // 2, products_of(grads_ref, ((hidden_ref, ffn_columns),), tile),
                weights.at[pl.ds(half, half), pl.ds(0, ffn_columns)], *refs[6:8],
                ((down_total, 0, ffn_columns),), *refs[8:12],
            ),
        ]
        gain_grad[...] = jnp.zeros_like(gain_grad)

        def out_copy(chunk, block):
            return pltpu.make_async_copy(
                out_stage.at[pl.ds(block * size, size)],
                out_all.at[pl.ds(block * block_rows + chunk * size, size)],
                out_sems.at[chunk, block],
            )

        def feed_out(chunk):
            if chunk > 0:
                for block in range(nt):
                    out_copy(chunk - 1, block).wait()
            left = hidden_ref[pl.ds(chunk * nt * size, nt * size)]
            for start in range(0, width, tile):
                extent = slice(start, start + tile)
                out_stage[:, extent] = product(left, down_weights[extent], LAST).astype(jnp.bfloat16)
            for block in range(nt):
                out_copy(chunk, block).start()

        def part(chunk):
            where = pl.ds(chunk * nt * size, nt * size)
            left = slopes_ref[where]
            for start in range(0, width, tile):
                extent = slice(start, start + tile)
                parts[where, extent] = product(left, weights[extent], LAST).astype(jnp.bfloat16)

        def finish(chunk):
            own_sum(chunk, total)
            where = pl.ds(chunk * size, size)
            through, gained = norm_pull(middle_ref[where], gain_ref[...], total[...])
            value = cot_ref[where].astype(jnp.float32) + through
            gain_grad[...] += jnp.sum(gained, axis=0, keepdims=True)
            grad_ref[where] = value
            own[where] = value.astype(jnp.bfloat16)
            first(chunk)

        loads[0].wait()
        loads[1].wait()
        for chunk in range(chunks):
            part(chunk)
            pass_on(chunk, 0)
        for load in loads[2:]:
            load.wait()
        over = []
        for number in range(2):
            over = over + [step for pair in zip(scatters[0][number], scatters[1][number]) for step in pair]
        for number in range(len(scatters[0][2])):
            over = over + scatters[0][2][number] + scatters[1][2][number]
            if number == 0:
                over = over + [functools.partial(feed_out, chunk) for chunk in range(chunks)]
        together(line_steps(nt, chunks, pass_on, finish, onward), over)
        for scatter in scatters:
            scatter[3]()
        for block in range(nt):
            out_copy(chunks - 1, block).wait()
        for chunk in range(chunks):
            reduce_end(chunk)
            settle(chunk)
            gather_end(chunk)
        if lane % 128:
            gain_out[...] = gain_grad[...]
        else:
            absolute_lanes(me, bits, blocks, gain_grad, gain_out)

    results = pl.pallas_call(
        kernel,
        out_shape=[
            jax.ShapeDtypeStruct((block_rows, width), jnp.float32),
            jax.ShapeDtypeStruct((1, width), jnp.float32),
            jax.ShapeDtypeStruct((tokens, width), jnp.bfloat16),
            jax.ShapeDtypeStruct((tokens, width), jnp.bfloat16),
        ]
        + [jax.ShapeDtypeStruct((out_rows, ffn_columns), jnp.float32)] * 3,
        in_specs=[HBM] * 5 + [ONCHIP] * 3,
        out_specs=[ONCHIP, ONCHIP, HBM, HBM] + [ONCHIP] * 3,
        scratch_shapes=[
            pltpu.VMEM(slopes.shape, jnp.bfloat16),
            pltpu.VMEM(hidden.shape, jnp.bfloat16),
            pltpu.VMEM(rows.shape, jnp.bfloat16),
            pltpu.VMEM(grads.shape, jnp.bfloat16),
            pltpu.VMEM((width, 2 * ffn_columns), jnp.bfloat16),
            pltpu.VMEM((width, ffn_columns), jnp.bfloat16),
            pltpu.SemaphoreType.DMA((6,)),
            pltpu.VMEM((tokens, width), jnp.bfloat16),
            pltpu.VMEM((block_rows, width), jnp.bfloat16),
            pltpu.VMEM((1, width), jnp.float32),
            pltpu.VMEM((nt * size, width), jnp.bfloat16),
            pltpu.SemaphoreType.DMA((chunks, nt)),
        ]
        + line_reduce_scratch(nt, block_rows, width, chunks)
        + line_gather_semaphores(nt, chunks)
        + computed_scratch(nd, out_rows, 2 * ffn_columns)[1:]
        + computed_scratch(nd, out_rows, ffn_columns)[1:],
        compiler_params=pltpu.CompilerParams(
            collective_id=2, has_side_effects=True, vmem_limit_bytes=LARGE_LIMIT
        ),
        name="middle_back",
    )(slopes, hidden, rows, grads, ffn_w, middle, cot, gain)
    if lane % 128:
        results = (results[0], from_relative(results[1], 1, nd), *results[2:])
    return results


def last_sums(nd, nt, normed, grad_main, grad_side, main, side, resid, before, gain, small, shared_rows, main_widths):
    chunks = LINE_CHUNKS
    bits, line_bits = nd.bit_length() - 1, nt.bit_length() - 1
    block_rows, width = resid.shape
    tokens = block_rows * nt
    size = block_rows // chunks
    blocks = relative_blocks(nd)
    lane = width // len(blocks)
    main_columns, side_columns = main.shape[1], side.shape[1]
    shared_columns = side_columns - 2 * HEAD_SIZE
    side_rows = width // nd
    owned = side_rows // nt
    common_columns = shared_columns + 2 * KEY_VALUE_HEADS * HEAD_SIZE
    count = len(main_widths)
    if lane % 128:
        gain_part = jnp.sum(
            (contract_last(grad_main, main) + contract_last(grad_side, side)) * normed.astype(jnp.float32), axis=0
        )
        own_gain = from_relative(gain_part / gain[0], 0, nd)
        small = jnp.concatenate([own_gain.reshape(-1, 128), small[width // 128 :]])

    def kernel(normed_ref, grad_main_ref, grad_side_ref, main_ref, side_ref, resid_ref, before_ref, gain_ref, small_ref, *refs):
        grad_ref, small_out, common_ref = refs[:3]
        totals, refs = refs[3 : 3 + count], refs[3 + count :]
        parts_ref, side_total, line_held, total, send, recv = refs[:6]
        sums, landed, small_send, small_recv, gain_grad = refs[6:11]
        side_out, side_in, side_send, side_recv = refs[11:15]
        stage, held, hop_landed, core_send, core_recv, hop_send, hop_recv = refs[15:]
        me, zed = enter(nt, bits)
        pass_on, own_sum, reduce_end = line_reduce(nt, me, zed, chunks, parts_ref, line_held, send, recv)
        targets, at = [], 0
        for target, columns in zip(totals, main_widths):
            targets.append((target, at, columns))
            at = at + columns
        targets.append((side_total, main_columns, side_columns))
        away, near, later, scatter_end = computed_scatter(
            nd, me, zed, side_rows // 2,
            products_of(normed_ref, ((grad_main_ref, main_columns), (grad_side_ref, side_columns)), 512),
            stage, held, hop_landed, targets, core_send, core_recv, hop_send, hop_recv,
        )

        def part(turn):
            def step():
                where = aligned(near_first(nt, zed, nt - 1 - turn) * block_rows, block_rows)
                left, right = grad_main_ref[where], grad_side_ref[where]
                for start in range(0, width, 512):
                    extent = slice(start, start + 512)
                    value = product(left, main_ref[extent], LAST) + product(right, side_ref[extent], LAST)
                    parts_ref[where, extent] = value.astype(jnp.bfloat16)

            return step

        def gain_term(number):
            def step():
                if number == 0:
                    gain_grad[...] = jnp.zeros_like(gain_grad)

                def body(inner, carry):
                    where = aligned(number * block_rows + inner * 16, 16)
                    gain_grad[...] += parts_ref[where].astype(jnp.float32) * normed_ref[where].astype(jnp.float32)
                    return carry

                lax.fori_loop(0, block_rows // 16, body, 0)

            return step

        def small_copy(turn):
            if turn < bits:
                device = (flip(me, turn), zed)
            else:
                device = (me, flip(zed, turn - bits))
            extent = slice(None) if turn < bits else pl.ds(0, shared_rows)
            return pltpu.make_async_remote_copy(
                src_ref=sums.at[turn, extent],
                dst_ref=landed.at[turn, extent],
                send_sem=small_send.at[turn],
                recv_sem=small_recv.at[turn],
                device_id=device,
                device_id_type=MESH,
            )

        def small_begin():
            sums[0] = small_ref[...]
            if lane % 128 == 0:
                whole = jnp.sum(gain_grad[...], axis=0, keepdims=True) / gain_ref[...]
                for number, (other, half) in enumerate(blocks):
                    spot = mixed_with(me, other, bits) * 2 + half
                    sums[0, pl.ds(spot, 1), :] = whole[:, number * lane : (number + 1) * lane]
            small_copy(0).start()

        def small_step(turn):
            def step():
                small_copy(turn).wait_recv()
                if turn < bits:
                    sums[turn + 1] = sums[turn] + landed[turn]
                else:
                    sums[turn + 1] = sums[turn]
                    sums[turn + 1, pl.ds(0, shared_rows)] = (
                        sums[turn, pl.ds(0, shared_rows)] + landed[turn, pl.ds(0, shared_rows)]
                    )
                if turn + 1 < bits + line_bits:
                    small_copy(turn + 1).start()

            return step

        def small_end():
            for turn in range(bits + line_bits):
                small_copy(turn).wait_send()
            small_out[...] = sums[bits + line_bits]

        few = [gain_term(number) for number in range(nt if lane % 128 == 0 else 0)]
        few = few + [small_begin] + [small_step(turn) for turn in range(bits + line_bits)]

        def side_copy(source, target):
            return pltpu.make_async_remote_copy(
                src_ref=side_out.at[pl.ds(target * owned, owned)],
                dst_ref=side_in.at[source],
                send_sem=side_send.at[target],
                recv_sem=side_recv.at[source],
                device_id=(me, target),
                device_id_type=MESH,
            )

        def side_begin():
            side_out[...] = side_total[...].astype(jnp.bfloat16)
            for target in range(nt):

                @pl.when(zed != target)
                def _(target=target):
                    side_copy(zed, target).start()

            side_in[zed] = side_out[aligned(zed * owned, owned)]

        def side_end():
            for source in range(nt):

                @pl.when(zed != source)
                def _(source=source):
                    side_copy(source, source).wait_recv()

            common_ref[...] = jnp.zeros_like(common_ref)
            for source in range(nt):
                value = side_in[source].astype(jnp.float32)
                head = source * (QUERY_HEADS // nt) // (QUERY_HEADS // KEY_VALUE_HEADS)
                common_ref[:, :shared_columns] += value[:, :shared_columns]
                for turn in range(2):
                    at = shared_columns + (turn * KEY_VALUE_HEADS + head) * HEAD_SIZE
                    start = shared_columns + turn * HEAD_SIZE
                    common_ref[:, at : at + HEAD_SIZE] += value[:, start : start + HEAD_SIZE]
            for target in range(nt):

                @pl.when(zed != target)
                def _(target=target):
                    side_copy(zed, target).wait_send()

        def finish(chunk):
            own_sum(chunk, total)
            where = pl.ds(chunk * size, size)
            through, _ = norm_pull(resid_ref[where].astype(jnp.float32), gain_ref[...], total[...])
            value = before_ref[where] + through
            if lane % 128:
                grad_ref[where] = value
                return
            for number, (other, half) in enumerate(blocks):
                start = (mixed_with(me, other, bits) * 2 + half) * lane
                grad_ref[where, pl.ds(pl.multiple_of(start, lane), lane)] = value[:, number * lane : (number + 1) * lane]

        def passes(turn):
            return [functools.partial(pass_on, chunk, turn) for chunk in range(chunks)]

        middle = len(away) // 2
        steps = away[:middle] + [part(0)] + passes(0) + away[middle:] + [part(1)] + near[:middle]
        for turn in range(2, nt):
            steps.append(part(turn))
        steps = steps + passes(1) + near[middle:]
        for stage_steps in later[:-1]:
            steps = steps + stage_steps
        for turn in range(2, nt - 1):
            steps = steps + passes(turn)
        steps = steps + few[: -(bits + line_bits)] + later[-1] + [side_begin]
        ends = [functools.partial(finish, chunk) for chunk in range(chunks)]
        rest = few[-(bits + line_bits) :]
        for step in steps:
            step()
        together(ends, rest)
        side_end()
        small_end()
        scatter_end()
        for chunk in range(chunks):
            reduce_end(chunk)

    turns = bits + line_bits
    results = pl.pallas_call(
        kernel,
        out_shape=[
            jax.ShapeDtypeStruct((block_rows, width), jnp.float32),
            jax.ShapeDtypeStruct(small.shape, jnp.float32),
            jax.ShapeDtypeStruct((owned, common_columns), jnp.float32),
        ]
        + [jax.ShapeDtypeStruct((side_rows, columns), jnp.float32) for columns in main_widths],
        in_specs=[ONCHIP] * 9,
        out_specs=[ONCHIP] * (3 + count),
        scratch_shapes=[
            pltpu.VMEM((tokens, width), jnp.bfloat16),
            pltpu.VMEM((side_rows, side_columns), jnp.float32),
        ]
        + line_reduce_scratch(nt, block_rows, width, chunks)
        + [
            pltpu.VMEM((turns + 1, *small.shape), jnp.float32),
            pltpu.VMEM((turns, *small.shape), jnp.float32),
            pltpu.SemaphoreType.DMA((turns,)),
            pltpu.SemaphoreType.DMA((turns,)),
            pltpu.VMEM((16, width), jnp.float32),
            pltpu.VMEM((side_rows, side_columns), jnp.bfloat16),
            pltpu.VMEM((nt, owned, side_columns), jnp.bfloat16),
            pltpu.SemaphoreType.DMA((nt,)),
            pltpu.SemaphoreType.DMA((nt,)),
        ]
        + computed_scratch(nd, side_rows, main_columns + side_columns),
        compiler_params=pltpu.CompilerParams(
            collective_id=3, has_side_effects=True, vmem_limit_bytes=LARGE_LIMIT
        ),
        name="last_sums",
    )(normed, grad_main, grad_side, main, side, resid, before, gain, small)
    if lane % 128:
        results = (from_relative(results[0], 1, nd), *results[1:])
    return results


def silu_slope(value, sig):
    return sig * (1.0 + value * (1.0 - sig))


def split_dot(value, constant, dims, terms):
    total = None
    for _ in range(terms):
        piece = value.astype(jnp.bfloat16)
        value = value - piece.astype(jnp.float32)
        part = lax.dot_general(*((piece, constant) if dims[0] else (constant, piece)), dims[1], preferred_element_type=jnp.float32)
        total = part if total is None else total + part
    return total


PLAIN = (((1,), (0,)), ((), ()))
LAST = (((1,), (1,)), ((), ()))
FIRST = (((0,), (0,)), ((), ()))


def product(left, right, dims=PLAIN):
    return lax.dot_general(left, right, dims, preferred_element_type=jnp.float32)


def turned(value, cosine, sine):
    return value * cosine + pltpu.roll(value, value.shape[-1] // 2, 1) * sine


class Sizes:
    def __init__(self, channels, state_columns, query_columns, heads, length):
        self.channels, self.states = channels, state_columns // 2
        self.query, self.heads, self.length = query_columns, heads, length
        self.span = SPAN
        self.count = length // SPAN
        self.wide = channels + state_columns
        self.head_width = channels // heads
        self.step_at = 2 * channels + query_columns
        self.main = self.step_at + heads + (-(self.step_at + heads)) % 128
        self.step_lanes = self.main - self.step_at
        self.side = state_columns + 2 * HEAD_SIZE
        self.window = min(length, 3 * SPAN)


def spread_heads(size):
    table = np.zeros((size.step_lanes, size.channels), np.float32)
    for head in range(size.heads):
        table[head, head * size.head_width : (head + 1) * size.head_width] = 1.0
    return table.astype(jnp.bfloat16)


def turn_tables(length):
    half = HEAD_SIZE // 2
    angle = np.arange(length, dtype=np.float64)[:, None] * rope_base ** (-np.arange(half) / half)[None]
    cosine, sine = np.cos(angle), np.sin(angle)
    return (
        np.concatenate([cosine, cosine], 1).astype(np.float32),
        np.concatenate([-sine, sine], 1).astype(np.float32),
    )


def token_flags(segments, taps):
    seg = segments[0]
    length = seg.shape[0]
    ends = jnp.broadcast_to(seg.reshape(-1, SPAN)[:, -1:], (length // SPAN, SPAN)).reshape(-1)
    before = jnp.pad(ends, (SPAN, 0), constant_values=-1)[:length]
    lines = [seg == seg]
    lines = lines + [jnp.pad(seg, (lag, 0), constant_values=-1)[:length] == seg for lag in range(1, taps)]
    lines = lines + [before == seg, ends == seg]
    lines = lines + [jnp.pad(seg, (0, lag), constant_values=-1)[lag:] == seg for lag in range(1, taps)]
    lines = lines + [jnp.zeros((length,), bool)] * (16 - len(lines))
    return jnp.stack(lines).astype(jnp.float32).T


def chunk_values(size, taps, main_ref, wide_ref, flags, spread, taps_ref, heads_ref, segc, segr):
    span = size.span
    pre = wide_ref[pl.ds(8, span), :] * taps_ref[0:1, :]
    for lag in range(1, taps):
        pre = pre + wide_ref[pl.ds(8 - lag, span), :] * (flags[:, lag : lag + 1] * taps_ref[lag : lag + 1, :])
    sig = jax.nn.sigmoid(pre)
    act = pre * sig
    inner = act[:, : size.channels]
    bmat = act[:, size.channels : size.channels + size.states].astype(jnp.bfloat16)
    cmat = act[:, size.channels + size.states :].astype(jnp.bfloat16)
    step_in = main_ref[:, size.step_at :] + heads_ref[0:1, :]
    step = jnp.maximum(step_in, 0.0) + jnp.log1p(jnp.exp(-jnp.abs(step_in)))
    logdec = -step * heads_ref[1:2, :]
    rows = lax.broadcasted_iota(jnp.int32, (span, span), 0)
    columns = lax.broadcasted_iota(jnp.int32, (span, span), 1)
    later = jnp.where(rows >= columns, 1.0, 0.0).astype(jnp.bfloat16)
    cumul = split_dot(logdec, later, (False, PLAIN), 3)
    inside = jnp.logical_and(rows >= columns, segc == segr)
    ending = cumul[span - 1 : span, :]
    reach = jnp.exp(cumul) * flags[:, 4:5]
    tail = jnp.exp(ending - cumul) * flags[:, 5:6]
    step_wide = split_dot(step, spread, (True, PLAIN), 2)
    scaled = inner * step_wide
    return dict(
        pre=pre, sig=sig, inner=inner, bmat=bmat, cmat=cmat, step_in=step_in, step=step, logdec=logdec, later=later,
        cumul=cumul, turned=jnp.transpose(cumul), inside=inside, step_wide=step_wide, scaled=scaled,
        scaled_b=scaled.astype(jnp.bfloat16), meeting=product(cmat, bmat, LAST),
        reach_wide=split_dot(reach, spread, (True, PLAIN), 2), tail_wide=split_dot(tail, spread, (True, PLAIN), 2),
        skip_wide=split_dot(jnp.broadcast_to(heads_ref[2:3, :], (8, size.step_lanes)), spread, (True, PLAIN), 2)[0:1],
    )


def decay_of(values, head):
    spread = values["cumul"][:, head : head + 1] - values["turned"][head : head + 1, :]
    return jnp.exp(jnp.where(values["inside"], spread, -1e30))


def softmax_of(size, query, keys, chunk, start, segc, seg_all):
    scores = product(query, keys, LAST) * (1.0 / math.sqrt(HEAD_SIZE))
    rows = lax.broadcasted_iota(jnp.int32, scores.shape, 0) + chunk * size.span
    columns = lax.broadcasted_iota(jnp.int32, scores.shape, 1) + start
    allowed = jnp.logical_and(rows >= columns, segc == seg_all)
    masked = jnp.where(allowed, scores, -1e30)
    expo = jnp.exp(masked - jnp.max(masked, axis=-1, keepdims=True))
    return expo / jnp.sum(expo, axis=-1, keepdims=True)


def mixers_forward(size, taps, main_raw, side_raw, segments, flags, tap_rows, head_rows):
    span = size.span
    per_head = size.head_width

    def kernel(
        main_ref, side_ref, segc_ref, segr_ref, flags_ref, taps_ref, heads_ref, cos_ref, sin_ref, spread_ref,
        mixed_ref, y_ref, state_ref, keys_ref, values_ref, wide, state,
    ):
        chunk = pl.program_id(0)

        @pl.when(chunk == 0)
        def _():
            wide[0:8, :] = jnp.zeros((8, size.wide), jnp.float32)
            state[...] = jnp.zeros_like(state)
            keys_ref[...] = jnp.zeros_like(keys_ref)
            values_ref[...] = jnp.zeros_like(values_ref)

        wide[pl.ds(8, span), : size.channels] = main_ref[:, size.channels : 2 * size.channels]
        wide[pl.ds(8, span), size.channels :] = side_ref[:, : 2 * size.states]
        flags, spread, segc = flags_ref[...], spread_ref[...], segc_ref[...]
        segr = segr_ref[:, pl.ds(pl.multiple_of(chunk * span, span), span)]
        val = chunk_values(size, taps, main_ref, wide, flags, spread, taps_ref, heads_ref, segc, segr)
        wide[0:8, :] = wide[pl.ds(span, 8), :]
        held = state[...]
        held_b = held.astype(jnp.bfloat16)
        state_ref[...] = held
        across = val["reach_wide"] * product(val["cmat"], held_b)
        lane = lax.broadcasted_iota(jnp.int32, (span, 2 * per_head), 1)
        for pair in range(size.heads // 2):
            where = slice(pair * 2 * per_head, (pair + 1) * 2 * per_head)
            both = []
            for head in (2 * pair, 2 * pair + 1):
                weights = (val["meeting"] * decay_of(val, head)).astype(jnp.bfloat16)
                both.append(product(weights, val["scaled_b"][:, where]))
            result = jnp.where(lane < per_head, both[0], both[1])
            result = result + across[:, where] + val["skip_wide"][:, where] * val["inner"][:, where]
            y_ref[:, where] = result
            gate = main_ref[:, where]
            mixed_ref[:, where] = (result * (gate * jax.nn.sigmoid(gate))).astype(jnp.bfloat16)
        keep = jnp.broadcast_to(val["reach_wide"][span - 1 : span, :], (1, size.channels))
        state[...] = keep * held + product(
            val["bmat"], (val["tail_wide"] * val["scaled"]).astype(jnp.bfloat16), FIRST
        )

        cosine, sine = cos_ref[...], sin_ref[...]
        own = pl.ds(pl.multiple_of(chunk * span, span), span)
        key_at = 2 * size.states
        keys_ref[own, :] = turned(side_ref[:, key_at : key_at + HEAD_SIZE], cosine, sine).astype(jnp.bfloat16)
        values_ref[own, :] = side_ref[:, key_at + HEAD_SIZE :].astype(jnp.bfloat16)
        start = pl.multiple_of(jnp.maximum(chunk + 1 - size.window // span, 0) * span, span)
        seen = pl.ds(start, size.window)
        for head in range(size.query // HEAD_SIZE):
            at = 2 * size.channels + head * HEAD_SIZE
            query = turned(main_ref[:, at : at + HEAD_SIZE], cosine, sine).astype(jnp.bfloat16)
            probs = softmax_of(size, query, keys_ref[seen, :], chunk, start, segc, segr_ref[:, seen])
            result = product(probs.astype(jnp.bfloat16), values_ref[seen, :])
            at = size.channels + head * HEAD_SIZE
            mixed_ref[:, at : at + HEAD_SIZE] = result.astype(jnp.bfloat16)

    def rows(columns):
        return pl.BlockSpec((span, columns), lambda i: (i, 0))

    def whole(array):
        return pl.BlockSpec(array.shape, lambda i: (0, 0))

    cosine, sine = turn_tables(size.length)
    spread = spread_heads(size)
    tokens = size.length
    return pl.pallas_call(
        kernel,
        grid=(size.count,),
        in_specs=[
            rows(size.main), rows(size.side), rows(1), whole(segments), rows(16), whole(tap_rows), whole(head_rows),
            rows(HEAD_SIZE), rows(HEAD_SIZE), whole(spread),
        ],
        out_specs=[
            rows(size.channels + size.query), rows(size.channels),
            pl.BlockSpec((size.states, size.channels), lambda i: (i, 0)),
            pl.BlockSpec((tokens, HEAD_SIZE), lambda i: (0, 0)), pl.BlockSpec((tokens, HEAD_SIZE), lambda i: (0, 0)),
        ],
        out_shape=[
            jax.ShapeDtypeStruct((tokens, size.channels + size.query), jnp.bfloat16),
            jax.ShapeDtypeStruct((tokens, size.channels), jnp.float32),
            jax.ShapeDtypeStruct((size.count * size.states, size.channels), jnp.float32),
            jax.ShapeDtypeStruct((tokens, HEAD_SIZE), jnp.bfloat16),
            jax.ShapeDtypeStruct((tokens, HEAD_SIZE), jnp.bfloat16),
        ],
        scratch_shapes=[
            pltpu.VMEM((span + 8, size.wide), jnp.float32),
            pltpu.VMEM((size.states, size.channels), jnp.float32),
        ],
        compiler_params=pltpu.CompilerParams(
            dimension_semantics=("arbitrary",), vmem_limit_bytes=VMEM_LIMIT
        ),
        cost_estimate=pl.CostEstimate(flops=20 * 10**9, bytes_accessed=25 * 10**6, transcendentals=5 * 10**6),
        name="mixers_forward",
    )(main_raw, side_raw, segments.reshape(tokens, 1), segments, flags, tap_rows, head_rows,
      jnp.asarray(cosine), jnp.asarray(sine), jnp.asarray(spread))


def mixers_backward(
    nd, nt, size, taps, out_w, main_raw, side_raw, segments, flags, tap_rows, head_rows, y_value, states, keys, values,
    grad_rows, mixed,
):
    bits = nd.bit_length() - 1
    out_rows, out_columns = grad_rows.shape[1] // nd, mixed.shape[1]
    span = size.span
    per_head = size.head_width
    count = size.count

    def kernel(
        out_ref, main_ref, side_ref, before_ref, side_before_ref, segc_ref, segr_ref, flags_ref, taps_ref, heads_ref,
        cos_ref, sin_ref, spread_ref, y_ref, state_ref, keys_ref, values_ref, rows_ref, mixed_ref,
        grad_main, grad_side, tap_sums, head_sums, mixer_total, attn_total,
        wide, back, grad_state, grad_keys, grad_values, grad_ref,
        stage, held, landed, core_send, core_recv, hop_send, hop_recv,
    ):
        turn = pl.program_id(0)
        chunk = count - 1 - turn
        me, zed = lax.axis_index("dp"), lax.axis_index("tensor")
        away, near, later, scatter_end = computed_scatter(
            nd, me, zed, out_rows // 2, products_of(rows_ref, ((mixed_ref, out_columns),), 512), stage, held, landed,
            ((mixer_total, 0, size.channels), (attn_total, size.channels, size.query)),
            core_send, core_recv, hop_send, hop_recv,
        )
        stages = [away, near, *later[: count - 3], [step for stage_steps in later[count - 3 :] for step in stage_steps]]
        for number, stage_steps in enumerate(stages):

            @pl.when(turn == number)
            def _(number=number, stage_steps=stage_steps):
                if number == 0:
                    enter(nt, bits)
                for step in stage_steps:
                    step()
                if number == len(stages) - 1:
                    scatter_end()

        @pl.when(turn == 0)
        def _():
            back[pl.ds(span, 8), :] = jnp.zeros((8, size.wide), jnp.float32)
            grad_state[...] = jnp.zeros_like(grad_state)
            grad_keys[...] = jnp.zeros_like(grad_keys)
            grad_values[...] = jnp.zeros_like(grad_values)
            tap_sums[...] = jnp.zeros_like(tap_sums)
            head_sums[...] = jnp.zeros_like(head_sums)

        own_rows = rows_ref[pl.ds(pl.multiple_of(chunk * span, span), span), :]
        for start in range(0, out_columns, 512):
            extent = slice(start, start + 512)
            grad_ref[:, extent] = product(own_rows, out_ref[:, extent])
        wide[0:8, : size.channels] = before_ref[...]
        wide[0:8, size.channels :] = side_before_ref[...]
        wide[pl.ds(8, span), : size.channels] = main_ref[:, size.channels : 2 * size.channels]
        wide[pl.ds(8, span), size.channels :] = side_ref[:, : 2 * size.states]
        flags, spread, segc = flags_ref[...], spread_ref[...], segc_ref[...]
        segr = segr_ref[:, pl.ds(pl.multiple_of(chunk * span, span), span)]
        val = chunk_values(size, taps, main_ref, wide, flags, spread, taps_ref, heads_ref, segc, segr)
        inner, scaled = val["inner"], val["scaled"]

        gate = main_ref[:, : size.channels]
        gate_sig = jax.nn.sigmoid(gate)
        grad = grad_ref[:, : size.channels]
        grad_main[:, : size.channels] = (grad * y_ref[...] * silu_slope(gate, gate_sig)).astype(jnp.bfloat16)
        grad_y = grad * (gate * gate_sig)
        grad_y_b = grad_y.astype(jnp.bfloat16)
        tap_sums[4:5, : size.channels] += jnp.sum(grad_y * inner, axis=0, keepdims=True)

        lane = lax.broadcasted_iota(jnp.int32, (span, 2 * per_head), 1)
        head_lane = lax.broadcasted_iota(jnp.int32, (span, size.step_lanes), 1)
        head_row = lax.broadcasted_iota(jnp.int32, (size.step_lanes, span), 0)
        grad_meeting = jnp.zeros((span, span), jnp.float32)
        by_row = jnp.zeros((span, size.step_lanes), jnp.float32)
        by_column = jnp.zeros((size.step_lanes, span), jnp.float32)
        pieces = []
        for pair in range(size.heads // 2):
            where = slice(pair * 2 * per_head, (pair + 1) * 2 * per_head)
            both = []
            for side in range(2):
                head = 2 * pair + side
                decay = decay_of(val, head)
                weights = val["meeting"] * decay
                mine = (lane < per_head) if side == 0 else (lane >= per_head)
                grad_own = jnp.where(mine, grad_y_b[:, where], jnp.zeros((), jnp.bfloat16))
                grad_weights = product(grad_own, val["scaled_b"][:, where], LAST)
                both.append(product(weights.astype(jnp.bfloat16), grad_y_b[:, where], FIRST))
                grad_meeting = grad_meeting + grad_weights * decay
                moved = grad_weights * weights
                by_row = jnp.where(head_lane == head, jnp.sum(moved, axis=1, keepdims=True), by_row)
                by_column = jnp.where(head_row == head, jnp.sum(moved, axis=0, keepdims=True), by_column)
            pieces.append(jnp.where(lane < per_head, both[0], both[1]))
        grad_scaled = jnp.concatenate(pieces, axis=1)
        grad_cumul = by_row - jnp.transpose(by_column)

        held = state_ref[...]
        held_b = held.astype(jnp.bfloat16)
        grad_held = grad_state[...]
        grad_held_b = grad_held.astype(jnp.bfloat16)
        grad_meeting_b = grad_meeting.astype(jnp.bfloat16)
        reached = val["reach_wide"] * grad_y
        reached_b = reached.astype(jnp.bfloat16)
        grad_cumul = grad_cumul + split_dot(reached * product(val["cmat"], held_b), spread, (True, LAST), 2)
        grad_c = product(reached_b, held_b, LAST) + product(grad_meeting_b, val["bmat"])
        from_state = val["tail_wide"] * product(val["bmat"], grad_held_b)
        grad_b = product(grad_meeting_b, val["cmat"], FIRST) + product(
            (val["tail_wide"] * scaled).astype(jnp.bfloat16), grad_held_b, LAST
        )
        grad_scaled = grad_scaled + from_state
        ended = split_dot(scaled * from_state, spread, (True, LAST), 2)
        keep = val["reach_wide"][span - 1 : span, :]
        kept = jnp.sum(grad_held * held, axis=0, keepdims=True) * keep
        kept = split_dot(jnp.broadcast_to(kept, (8, size.channels)), spread, (True, LAST), 2)[0:1]
        at_end = jnp.sum(ended, axis=0, keepdims=True) + kept
        grad_logdec = split_dot(grad_cumul - ended, val["later"], (False, FIRST), 3) + at_end
        grad_state[...] = keep * grad_held + product(val["cmat"], reached_b, FIRST)

        grad_inner = grad_scaled * val["step_wide"] + grad_y * val["skip_wide"]
        grad_step = split_dot(grad_scaled * inner, spread, (True, LAST), 2) - grad_logdec * heads_ref[1:2, :]
        grad_step_raw = grad_step * jax.nn.sigmoid(val["step_in"])
        head_sums[0:1, :] += jnp.sum(grad_step_raw, axis=0, keepdims=True)
        head_sums[1:2, :] += jnp.sum(grad_logdec * val["logdec"], axis=0, keepdims=True)
        grad_main[:, size.step_at :] = grad_step_raw.astype(jnp.bfloat16)

        slope = silu_slope(val["pre"], val["sig"])
        grad_pre = jnp.concatenate([grad_inner, grad_b, grad_c], axis=1) * slope
        back[pl.ds(0, span), :] = grad_pre
        raw = grad_pre * taps_ref[0:1, :]
        tap_sums[0:1, :] += jnp.sum(grad_pre * wide[pl.ds(8, span), :], axis=0, keepdims=True)
        for lag in range(1, taps):
            tap_sums[lag : lag + 1, :] += jnp.sum(
                grad_pre * (wide[pl.ds(8 - lag, span), :] * flags[:, lag : lag + 1]), axis=0, keepdims=True
            )
            raw = raw + back[pl.ds(lag, span), :] * (flags[:, 5 + lag : 6 + lag] * taps_ref[lag : lag + 1, :])
        back[pl.ds(span, 8), :] = back[0:8, :]
        grad_main[:, size.channels : 2 * size.channels] = raw[:, : size.channels].astype(jnp.bfloat16)
        grad_side[:, : 2 * size.states] = raw[:, size.channels :].astype(jnp.bfloat16)

        cosine, sine = cos_ref[...], sin_ref[...]
        start = pl.multiple_of(jnp.maximum(chunk + 1 - size.window // span, 0) * span, span)
        seen = pl.ds(start, size.window)
        seen_keys, seen_values = keys_ref[seen, :], values_ref[seen, :]
        scale = 1.0 / math.sqrt(HEAD_SIZE)
        for head in range(size.query // HEAD_SIZE):
            at = 2 * size.channels + head * HEAD_SIZE
            query = turned(main_ref[:, at : at + HEAD_SIZE], cosine, sine).astype(jnp.bfloat16)
            probs = softmax_of(size, query, seen_keys, chunk, start, segc, segr_ref[:, seen])
            out_at = size.channels + head * HEAD_SIZE
            grad_out = grad_ref[:, out_at : out_at + HEAD_SIZE].astype(jnp.bfloat16)
            grad_probs = product(grad_out, seen_values, LAST)
            delta = jnp.sum(grad_probs * probs, axis=-1, keepdims=True)
            grad_scores = (probs * (grad_probs - delta)).astype(jnp.bfloat16)
            grad_query = product(grad_scores, seen_keys) * scale
            grad_main[:, at : at + HEAD_SIZE] = turned(grad_query, cosine, -sine).astype(jnp.bfloat16)
            grad_keys[seen, :] += product(grad_scores, query, FIRST) * scale
            grad_values[seen, :] += product(probs.astype(jnp.bfloat16), grad_out, FIRST)
        own = pl.ds(pl.multiple_of(chunk * span, span), span)
        key_at = 2 * size.states
        grad_side[:, key_at : key_at + HEAD_SIZE] = turned(grad_keys[own, :], cosine, -sine).astype(jnp.bfloat16)
        grad_side[:, key_at + HEAD_SIZE :] = grad_values[own, :].astype(jnp.bfloat16)

    def rows(columns):
        return pl.BlockSpec((span, columns), lambda i: (count - 1 - i, 0))

    def previous(columns, column):
        return pl.BlockSpec((8, columns), lambda i: (jnp.maximum((count - 1 - i) * (span // 8) - 1, 0), column))

    def whole(array):
        return pl.BlockSpec(array.shape, lambda i: (0, 0))

    cosine, sine = turn_tables(size.length)
    spread = spread_heads(size)
    tokens = size.length
    return pl.pallas_call(
        kernel,
        grid=(count,),
        in_specs=[
            whole(out_w), rows(size.main), rows(size.side), previous(size.channels, 1),
            previous(2 * size.states, 0), rows(1), whole(segments), rows(16), whole(tap_rows), whole(head_rows),
            rows(HEAD_SIZE), rows(HEAD_SIZE), whole(spread), rows(size.channels),
            pl.BlockSpec((size.states, size.channels), lambda i: (count - 1 - i, 0)), whole(keys), whole(values),
            whole(grad_rows), whole(mixed),
        ],
        out_specs=[
            rows(size.main), rows(size.side), pl.BlockSpec((8, size.wide), lambda i: (0, 0)),
            pl.BlockSpec((8, size.step_lanes), lambda i: (0, 0)),
            pl.BlockSpec((out_rows, size.channels), lambda i: (0, 0)),
            pl.BlockSpec((out_rows, size.query), lambda i: (0, 0)),
        ],
        out_shape=[
            jax.ShapeDtypeStruct((tokens, size.main), jnp.bfloat16),
            jax.ShapeDtypeStruct((tokens, size.side), jnp.bfloat16),
            jax.ShapeDtypeStruct((8, size.wide), jnp.float32),
            jax.ShapeDtypeStruct((8, size.step_lanes), jnp.float32),
            jax.ShapeDtypeStruct((out_rows, size.channels), jnp.float32),
            jax.ShapeDtypeStruct((out_rows, size.query), jnp.float32),
        ],
        scratch_shapes=[
            pltpu.VMEM((span + 8, size.wide), jnp.float32),
            pltpu.VMEM((span + 8, size.wide), jnp.float32),
            pltpu.VMEM((size.states, size.channels), jnp.float32),
            pltpu.VMEM((tokens, HEAD_SIZE), jnp.float32),
            pltpu.VMEM((tokens, HEAD_SIZE), jnp.float32),
            pltpu.VMEM((span, out_columns), jnp.float32),
        ]
        + computed_scratch(nd, out_rows, out_columns),
        compiler_params=pltpu.CompilerParams(
            dimension_semantics=("arbitrary",), vmem_limit_bytes=VMEM_LIMIT, collective_id=4, has_side_effects=True
        ),
        cost_estimate=pl.CostEstimate(flops=40 * 10**9, bytes_accessed=60 * 10**6, transcendentals=10**7),
        name="mixers_backward",
    )(out_w, main_raw, side_raw, main_raw, side_raw, segments.reshape(tokens, 1), segments, flags, tap_rows,
      head_rows, jnp.asarray(cosine), jnp.asarray(sine), jnp.asarray(spread), y_value, states, keys, values, grad_rows, mixed)


def per_device(
    nd,
    nt,
    residual,
    segments,
    mixgain,
    ffngain,
    gateproj,
    innerproj,
    stepproj,
    sharedproj,
    innerconv,
    sharedconv,
    stepbias,
    decaylog,
    skipgain,
    mixerout,
    queryproj,
    keyvalue,
    attnout,
    ffngate,
    upproj,
    downproj,
    cotangent,
):
    bfloat = jnp.bfloat16
    single = jnp.float32
    width = residual.shape[1]
    zed = lax.axis_index("tensor")
    seq_count, length = segments.shape
    token_count = seq_count * length
    channels = innerproj.shape[1]
    state_columns = sharedproj.shape[1]
    heads = stepproj.shape[1]
    query_columns = queryproj.shape[1]
    ffn_columns = ffngate.shape[1]
    small_rows = sharedproj.shape[0]
    conv_rows = sharedconv.shape[0]
    taps = sharedconv.shape[1]

    gains = jnp.concatenate(
        [
            mixgain[:, None],
            ffngain[:, None],
            jnp.pad(sharedconv, ((0, small_rows - conv_rows), (0, 0))),
            jnp.zeros((small_rows, 128 - 2 - taps), bfloat),
        ],
        axis=1,
    )
    main_used = 2 * channels + query_columns + heads
    main_own = jnp.concatenate(
        [
            gateproj,
            innerproj,
            queryproj,
            stepproj,
            jnp.zeros((gateproj.shape[0], -main_used % 128), bfloat),
        ],
        axis=1,
    )
    resid_own, cot_own, gain_rows, normed, grad_rows, _, main, side, out_w, main_raw, side_raw = first_gathers(
        nd,
        nt,
        residual,
        cotangent,
        jnp.concatenate([sharedproj, keyvalue, gains], axis=1),
        main_own,
        jnp.concatenate([mixerout, attnout], axis=1),
        state_columns,
    )
    gain_one, gain_two = gain_rows[0], gain_rows[1]
    conv_shared = from_relative(gain_rows[2 : 2 + taps], 1, nd)
    conv_shared = conv_shared.reshape(taps, nd * nt, small_rows)[:, :, :conv_rows].reshape(taps, -1)

    size = Sizes(channels, state_columns, query_columns, heads, length)
    flags = token_flags(segments, taps)
    tap_rows = jnp.concatenate([innerconv.astype(single).T, conv_shared], axis=1)
    tap_rows = jnp.pad(tap_rows, ((0, 8 - taps), (0, 0)))
    head_rows = jnp.stack([stepbias.astype(single), jnp.exp(decaylog.astype(single)), skipgain.astype(single)])
    head_rows = jnp.pad(head_rows, ((0, 5), (0, size.step_lanes - heads)))
    mixed_in, y_value, states, keys, values = mixers_forward(
        size, taps, main_raw, side_raw, segments, flags, tap_rows, head_rows
    )
    middle, rows_two, hidden, grad_gate_up, grad_rows, ffn_w = middle_rows(
        nd,
        nt,
        mixed_in,
        out_w,
        resid_own,
        gain_two[None],
        grad_rows,
        *second_neighbours(nt, grad_rows),
        jnp.concatenate([ffngate, upproj, downproj], axis=1),
    )
    grad_middle, grad_gain_two, grad_mix_rows, ffn_part, gate_g, up_g, down_g = middle_back(
        nd, nt, grad_gate_up, hidden, rows_two, grad_rows, ffn_w, middle, cot_own, gain_two[None]
    )
    ffn_out = lax.psum_scatter(ffn_part, "tensor", scatter_dimension=0, tiled=True)
    layer_out = from_relative(middle + ffn_out.astype(single), 1, nd)
    grad_main, grad_side, tap_sums, head_sums, mixer_g, attn_g = mixers_backward(
        nd, nt, size, taps, out_w, main_raw, side_raw, segments, flags, tap_rows, head_rows, y_value, states,
        keys, values, grad_mix_rows, mixed_in,
    )
    small = jnp.concatenate(
        [
            jnp.zeros((width,), single),
            grad_gain_two[0],
            tap_sums[:taps, channels:].reshape(-1),
            tap_sums[:taps, :channels].reshape(-1),
            tap_sums[4, :channels],
            head_sums[:2].reshape(-1),
        ]
    )
    shared_length = 2 * width + taps * state_columns
    small = jnp.pad(small, (0, -small.shape[0] % 1024)).reshape(-1, 128)
    grad_residual, small, common_g, gateproj_g, inner_g, query_g, step_g = last_sums(
        nd,
        nt,
        normed,
        grad_main,
        grad_side,
        main,
        side,
        resid_own,
        grad_middle,
        gain_one[None],
        small,
        shared_length // 128,
        (channels, channels, query_columns, heads),
    )
    small = small.reshape(-1)
    place = lax.axis_index("dp") * nt + zed
    gain_one_g = lax.dynamic_slice_in_dim(small, place * small_rows, small_rows, 0)
    gain_two_g = lax.dynamic_slice_in_dim(small, width + place * small_rows, small_rows, 0)
    conv_g = lax.dynamic_slice_in_dim(
        small[2 * width : shared_length].reshape(taps, -1), place * conv_rows, conv_rows, 1
    ).T
    local = small[shared_length:]
    skip_at = taps * channels
    head_at = skip_at + channels
    return (
        layer_out,
        grad_residual,
        gain_one_g,
        gain_two_g,
        gateproj_g,
        inner_g,
        step_g,
        common_g[:, :state_columns],
        local[:skip_at].reshape(taps, channels).T,
        conv_g,
        local[head_at : head_at + heads],
        local[head_at + size.step_lanes : head_at + size.step_lanes + heads],
        local[skip_at:head_at].reshape(heads, -1).sum(axis=1),
        mixer_g,
        query_g,
        common_g[:, state_columns:],
        attn_g,
        gate_g,
        up_g,
        down_g,
    )


def solution(mesh):
    return jax.shard_map(
        functools.partial(per_device, mesh.shape["dp"], mesh.shape["tensor"]),
        mesh=mesh,
        in_specs=(
            P(("dp", "tensor"), None),
            P("dp", None),
            P(("dp", "tensor")),
            P(("dp", "tensor")),
            P("dp", "tensor"),
            P("dp", "tensor"),
            P("dp", "tensor"),
            P(("dp", "tensor"), None),
            P("tensor", None),
            P(("dp", "tensor"), None),
            P("tensor"),
            P("tensor"),
            P("tensor"),
            P("dp", "tensor"),
            P("dp", "tensor"),
            P(("dp", "tensor"), None),
            P("dp", "tensor"),
            P("dp", "tensor"),
            P("dp", "tensor"),
            P("dp", "tensor"),
            P(("dp", "tensor"), None),
        ),
        out_specs=(
            P(("dp", "tensor"), None),
            P(("dp", "tensor"), None),
            P(("dp", "tensor")),
            P(("dp", "tensor")),
            P("dp", "tensor"),
            P("dp", "tensor"),
            P("dp", "tensor"),
            P(("dp", "tensor"), None),
            P("tensor", None),
            P(("dp", "tensor"), None),
            P("tensor"),
            P("tensor"),
            P("tensor"),
            P("dp", "tensor"),
            P("dp", "tensor"),
            P(("dp", "tensor"), None),
            P("dp", "tensor"),
            P("dp", "tensor"),
            P("dp", "tensor"),
            P("dp", "tensor"),
        ),
        check_vma=False,
    )
```
